32 devices in a mesh: groups: 2 (over y), expert: 4 (over z), proj: 4 (over x, core).
Axes of the slice: x: 2, y: 2, z: 4, core: 2. Of those that a mesh axis runs over, the one named last changes fastest.
Arguments:
- activations: bfloat16 [4096, 7168], P(('groups', 'expert'), 'proj'), parts along dimension 0, may hold values from -6 to 6
- grad_hidden: bfloat16 [4096, 8, 2048], P(('groups', 'expert'), None, 'proj'), parts along dimension 0, may hold values from -6 to 6
- routes: int32 [4096, 8], P(('groups', 'expert')), parts along dimension 0, may hold values from 0 to 31, all different within a row; in each aligned block of 512 rows (0 to 511, 512 to 1023, ...) at most 256 rows name the same one
- doc_ids: int32 [4096], P(('groups', 'expert')), parts along dimension 0, may hold values from 0 to 31, never falling along the last dimension, each value on 1 to 256 neighbouring positions
- query_grads: bfloat16 [256, 32, 4096], P(None, 'expert', 'proj'), may hold values from -0.009765625 to 0.009765625
- in_projection: bfloat16 [64, 7168], P(None, 'proj'), may hold values from -0.0625 to 0.0625
- out_projection: bfloat16 [64, 2048], P(None, 'proj'), may hold values from -0.125 to 0.125
- inverse_in: float32 [32, 64, 64], P('expert'), may hold values from -1 to 3, as said below
- inverse_out: float32 [32, 64, 64], P('expert'), may hold values from -1 to 3, as said below
Outputs:
- scores: float32 [256, 64], P('proj', ('groups', 'expert')), parts along dimension 1
The draws below stay inside these ranges and needn't reach their ends.
There are 2 independent parts, one for each index of `groups`. The reference program is written for one: setup_inputs(seed, part) draws one part's arguments, and reference() takes and returns one part's arrays. A program takes and returns all parts, laid end to end along the dimension named above; an argument that names none is the same for every part. Nothing has to cross between parts.
Inputs may be any that keep to these rules, and one draw needn't show every extreme that they name: `routes`: each token names 8 different experts. In each aligned block of 512 tokens (the tokens of one device) no expert is named by more than 256 tokens, a bound that some block reaches. `doc_ids`: never falls along the tokens; each of the 32 documents has 1 to 256 tokens, one exactly 256. `inverse_in`: each matrix is symmetric. `inverse_out`: each matrix is symmetric.
All inputs are finite; a program needn't handle non-finite values.
Results may differ from the reference program's by a relative error of at most 0.0065.
Values may be sent and summed in bfloat16 or wider, within the bound.
No kernel may reach another device: no remote copies, remote signals or barrier semaphores. Data moves between devices by JAX's collectives and lax.ppermute only.
A program may use at most 64 MiB of HBM per device.

```python
import math
import jax
import jax.numpy as jnp
import numpy as np
from jax import lax

D = 7168
FF = 2048
TOP = 8
KIN = 64
KOUT = 64
TOK_DEV = 512
DOC_DEV = 8
QUERIES = 256
EXPERTS = 32
TOKENS = 2048
DOCS = 32
DOC_MOST = 256
CAP = 256


def symmetric_factor(key_diag, noise_draw, matrix_order):
    noise_draw = jnp.clip(noise_draw, -4.0, 4.0)
    mixed_part = (noise_draw + jnp.swapaxes(noise_draw, 1, 2)) * (0.25 / math.sqrt(matrix_order))
    diagonal_part = jax.random.uniform(key_diag, noise_draw.shape[:2], jnp.float32, 0.6, 1.6)
    return mixed_part + diagonal_part[:, :, None] * jnp.eye(matrix_order, dtype=jnp.float32)[None, :, :]


def draw_inverse_in(key, part):
    key = jax.random.fold_in(key, 11)
    key_off, key_diag = jax.random.split(key)
    noise_draw = jax.random.normal(key_off, (EXPERTS, KIN, KIN), jnp.float32)
    return symmetric_factor(key_diag, noise_draw, KIN)


def draw_inverse_out(key, part):
    key = jax.random.fold_in(key, 23)
    key_off, key_diag = jax.random.split(key)
    noise_draw = jax.random.normal(key_off, (EXPERTS, KOUT, KOUT), jnp.float32)
    return symmetric_factor(key_diag, noise_draw, KOUT)


def level_of(key, extent, cuts, low, high):
    gain, own = 1.0, jax.random.fold_in(key, 6)
    for axis_at, blocks in cuts:
        heights = jnp.exp(jax.random.uniform(jax.random.fold_in(own, axis_at), (blocks,), jnp.float32, low / len(cuts), high / len(cuts)))
        gain = gain * jnp.repeat(heights, extent[axis_at] // blocks).reshape([-1 if axis == axis_at else 1 for axis in range(len(extent))])
    return gain


def split_up(amount, total, limit, slope):
    portions = [(1 << 20) // math.isqrt(standing ** slope) + 1 for standing in range(2, amount + 1)]
    surplus, counts = total - limit - (amount - 1), [1] * (amount - 1)
    while surplus > 0:
        movable = [i for i in range(amount - 1) if counts[i] < limit]
        mass, remaining = sum([portions[i] for i in movable]), surplus
        for i in movable:
            extra = min(limit - counts[i], max(1, remaining * portions[i] // mass), surplus)
            counts[i] = counts[i] + extra
            surplus = surplus - extra
    return np.array([limit] + counts)


def ragged_sizes(stream_key, amount, total, reach, slope):
    if amount == 2:
        one = jax.random.randint(stream_key, (), max(1, total - reach), min(reach, total - 1) + 1)
        return jnp.stack([one, total - one])
    tallies = jnp.asarray(split_up(amount, total, reach, slope), jnp.int32)
    pairs = (amount - 1) // 2
    source_of, receiver = tallies[1:1 + 2 * pairs:2], tallies[2:2 + 2 * pairs:2]
    slack = jnp.minimum(source_of - 1, reach - receiver)
    shifted = jax.random.randint(jax.random.fold_in(stream_key, 1), (pairs,), 0, 1 << 20) % (slack + 1)
    tallies = tallies.at[1:1 + 2 * pairs:2].set(source_of - shifted).at[2:2 + 2 * pairs:2].set(receiver + shifted)
    return tallies[jax.random.permutation(jax.random.fold_in(stream_key, 2), amount)]


def routed_block(own_key, own, number, rows, number_of, top, most, skew):
    ranking = jax.random.permutation(own_key, number_of)
    crowded, common = shares(number_of, rows * top, most, skew, True), shares(number_of, rows * top, most, skew, False)
    places = jnp.arange(number_of)

    def named(lengths, turn):
        used = int((lengths > 0).sum())
        fixed = max(1, used // 4)
        passed = fixed + (places - fixed + turn * (used - fixed)) % max(1, number_of - fixed)
        return jnp.zeros((number_of,), jnp.int32).at[ranking[jnp.where(places < fixed, places, passed)]].set(jnp.asarray(lengths, jnp.int32))

    lengths = jnp.where(number % 4 == 0, named(crowded, number // 4), named(common, number - number // 4 - 1))
    mixed = jax.random.permutation(jax.random.fold_in(own, 3), number_of)
    giver, sink = mixed[0:number_of // 2 * 2:2], mixed[1:number_of // 2 * 2:2]
    room = jnp.minimum(lengths[giver] - 1, most - lengths[sink]) // 2
    room = jnp.where((giver == ranking[0]) | (sink == ranking[0]) | (lengths[sink] == 0), 0, jnp.maximum(room, 0))
    passed = jax.random.randint(jax.random.fold_in(own, 4), (number_of // 2,), 0, 1 << 20) % (room + 1)
    lengths = lengths.at[giver].add(-passed).at[sink].add(passed)
    labels = jnp.searchsorted(jnp.cumsum(lengths), jnp.arange(rows * top), side="right").astype(jnp.int32)
    grid = labels.reshape(top, rows).T
    grid = grid[jax.random.permutation(jax.random.fold_in(own, 1), rows)]
    turn = jax.random.randint(jax.random.fold_in(own, 2), (rows, 1), 0, top)
    return jnp.take_along_axis(grid, (jnp.arange(top)[None, :] + turn) % top, axis=1)


def shares(amount, total, limit, skew, full):
    portions = [(1 << 20) // math.isqrt(grade ** skew) + 1 for grade in range(1, amount + 1)]
    largest = limit if full else min(limit, max(-(-total // amount), total * portions[0] // sum(portions)))
    least = 1 if total - largest >= amount - 1 else 0
    given, spare = [largest] + [least] * (amount - 1), total - largest - least * (amount - 1)
    while spare > 0:
        free = [i for i in range(1, amount) if given[i] < largest] or [i for i in range(1, amount) if given[i] < limit]
        whole, remaining = sum([portions[i] for i in free]), spare
        for i in free:
            more = min(limit - given[i], max(1, remaining * portions[i] // whole), spare)
            given[i] = given[i] + more
            spare = spare - more
    return np.array(given)


def scatter_about(rng, extent, width, reach, cuts=(), held_as=jnp.bfloat16):
    result = width * jax.random.normal(rng, extent, jnp.float32)
    if cuts:
        result = result * level_of(rng, extent, cuts, -0.22, 0.18)
    return jnp.clip(result, -reach, reach).astype(held_as)


def setup_inputs(seed: int = 0, part: int = 0) -> dict:
    key_list = jax.random.split(jax.random.key(seed), 10)
    part_splits = jax.random.split(jax.random.fold_in(key_list[9], part), 10)
    activations = scatter_about(part_splits[0], (TOKENS, D), 1.0, 6.0, ((0, 4), (1, 4)))
    grad_hidden = scatter_about(part_splits[1], (TOKENS, TOP, FF), 1.0, 6.0, ((0, 4), (2, 4)))
    routes_keys = jax.random.split(jax.random.fold_in(part_splits[2], 1), TOKENS // TOK_DEV)
    routes_turns = jax.random.permutation(jax.random.fold_in(part_splits[2], 3), TOKENS // TOK_DEV)
    routes = jax.vmap(lambda own, number: routed_block(jax.random.fold_in(part_splits[2], 2), own, number, TOK_DEV, EXPERTS, TOP, CAP, 1))(routes_keys, routes_turns).reshape((TOKENS, TOP))
    doc_ids = jnp.searchsorted(jnp.cumsum(ragged_sizes(part_splits[3], DOCS, TOKENS, DOC_MOST, 1)), jnp.arange(TOKENS), side="right").astype(jnp.int32)
    query_grads = scatter_about(key_list[4], (QUERIES, EXPERTS, KOUT * KIN), ((TOK_DEV * TOP * KIN * KOUT // DOC_DEV) ** -0.5), 0.009765625, ((1, 4), (2, 4)))
    in_projection = scatter_about(key_list[5], (KIN, D), D ** -0.5, 0.0625, ((1, 4),))
    out_projection = scatter_about(key_list[6], (KOUT, FF), FF ** -0.5, 0.125, ((1, 4),))
    inverse_in = draw_inverse_in(jax.random.fold_in(key_list[9], 71), part)
    inverse_out = draw_inverse_out(jax.random.fold_in(key_list[9], 71), part)
    return {"activations": activations, "grad_hidden": grad_hidden, "routes": routes, "doc_ids": doc_ids, "query_grads": query_grads, "in_projection": in_projection, "out_projection": out_projection, "inverse_in": inverse_in, "inverse_out": inverse_out}


PRECISE = lax.Precision.HIGHEST


def reference(activations, grad_hidden, routes, doc_ids, query_grads, in_projection, out_projection, inverse_in, inverse_out):
    projected_in = jnp.dot(activations, in_projection.T, preferred_element_type=jnp.float32).astype(jnp.bfloat16)
    flat_hidden = grad_hidden.reshape(TOKENS * TOP, FF)
    projected_out = jnp.dot(flat_hidden, out_projection.T, preferred_element_type=jnp.float32).astype(jnp.bfloat16)
    route_total = TOKENS * TOP
    route_block = math.gcd(route_total, 4096)
    block_count = route_total // route_block
    expert_flat = routes.reshape(block_count, route_block).astype(jnp.int32)
    docs_flat = jnp.repeat(doc_ids, TOP).reshape(block_count, route_block).astype(jnp.int32)
    in_flat = jnp.repeat(projected_in, TOP, axis=0).reshape(block_count, route_block, KIN)
    out_flat = projected_out.reshape(block_count, route_block, KOUT)

    def accumulate(grad_total, pieces):
        block_experts, block_docs, block_in, block_out = pieces
        conditioned_in = jnp.einsum("rk,rkj->rj", block_in.astype(jnp.float32), inverse_in[block_experts], precision=PRECISE)
        conditioned_in = lax.optimization_barrier(conditioned_in.astype(jnp.bfloat16)).astype(jnp.float32)
        conditioned_out = jnp.einsum("rik,rk->ri", inverse_out[block_experts], block_out.astype(jnp.float32), precision=PRECISE)
        conditioned_out = lax.optimization_barrier(conditioned_out.astype(jnp.bfloat16)).astype(jnp.float32)
        outer_terms = (conditioned_out[:, :, None] * conditioned_in[:, None, :]).reshape(route_block, KOUT * KIN)
        target_rows = (block_experts * DOCS + block_docs).astype(jnp.int32)
        return grad_total.at[target_rows].add(outer_terms), None

    grad_start = jnp.zeros((EXPERTS * DOCS, KOUT * KIN), jnp.float32)
    grad_total, _ = lax.scan(accumulate, grad_start, (expert_flat, docs_flat, in_flat, out_flat))
    example_grads = grad_total.astype(jnp.bfloat16).reshape(EXPERTS, DOCS, KOUT * KIN)

    def add_expert(running, expert_pair):
        expert_queries, expert_grads = expert_pair
        return running + jnp.dot(expert_queries, expert_grads.T, preferred_element_type=jnp.float32), None

    scores, _ = lax.scan(add_expert, jnp.zeros((QUERIES, DOCS), jnp.float32), (jnp.swapaxes(query_grads, 0, 1), example_grads))
    return scores
```

```python
import functools

import jax
import jax.numpy as jnp
from jax import lax
from jax.experimental import pallas as pl
from jax.experimental.pallas import tpu as pltpu
from jax.sharding import PartitionSpec as P

DOC_DEV = 8
VMEM_BYTES = 48 * 1024 * 1024


def half_lanes(shape, width):
    return lax.broadcasted_iota(jnp.int32, shape, len(shape) - 1) < width


def project_kernel(act_ref, hidden_ref, in_proj_ref, out_proj_ref, wire_ref, rows_ref, *, top):
    quarter = act_ref.shape[0]
    width = in_proj_ref.shape[0]
    twice = jnp.concatenate([out_proj_ref[...], out_proj_ref[...]], axis=0)
    rows_ref[...] = lax.dot_general(
        hidden_ref[...], twice, (((1,), (1,)), ((), ())), preferred_element_type=jnp.float32
    )
    first = half_lanes((quarter, 2 * width), width)
    for pair in range(top // 2):
        even = rows_ref[pl.ds(2 * pair, quarter, stride=top), :]
        odd = rows_ref[pl.ds(2 * pair + 1, quarter, stride=top), :]
        wire_ref[0, pair * quarter : (pair + 1) * quarter, :] = jnp.where(first, even, odd).astype(jnp.bfloat16)
    twice_in = jnp.concatenate([in_proj_ref[...], in_proj_ref[...]], axis=0)
    inner = lax.dot_general(
        act_ref[...], twice_in, (((1,), (1,)), ((), ())), preferred_element_type=jnp.float32
    )
    half = quarter // 2
    wire_ref[0, top // 2 * quarter :, :] = jnp.where(
        half_lanes((half, 2 * width), width), inner[:half], inner[half:]
    ).astype(jnp.bfloat16)


def project(activations, flat_hidden, in_projection, out_projection, quarters, top):
    tokens, model = activations.shape
    width = in_projection.shape[0]
    quarter = tokens // quarters
    wire_rows = top // 2 * quarter + quarter // 2
    return pl.pallas_call(
        functools.partial(project_kernel, top=top),
        grid=(quarters,),
        in_specs=[
            pl.BlockSpec((quarter, model), lambda q: (q, 0)),
            pl.BlockSpec((quarter * top, flat_hidden.shape[1]), lambda q: (q, 0)),
            pl.BlockSpec(in_projection.shape, lambda q: (0, 0)),
            pl.BlockSpec(out_projection.shape, lambda q: (0, 0)),
        ],
        out_specs=pl.BlockSpec((1, wire_rows, 2 * width), lambda q: (q, 0, 0)),
        out_shape=jax.ShapeDtypeStruct((quarters, wire_rows, 2 * width), jnp.bfloat16),
        scratch_shapes=[pltpu.VMEM((quarter * top, 2 * width), jnp.float32)],
        compiler_params=pltpu.CompilerParams(vmem_limit_bytes=VMEM_BYTES),
    )(activations, flat_hidden, in_projection, out_projection)


def condition_kernel(parts_ref, routes_ref, weights_ref, payload_ref, value_ref, name_ref, *, top, width):
    quarter = routes_ref.shape[0]
    groups, dense_width, _ = weights_ref.shape
    shares = payload_ref.shape[0] // groups
    lanes = 2 * width
    experts = dense_width // width
    first = half_lanes((quarter, lanes), width)
    second = 1 - first.astype(jnp.int32)

    def summed(start, size):
        total = parts_ref[0, start : start + size, :].astype(jnp.float32)
        for source in range(1, parts_ref.shape[0]):
            total = total + parts_ref[source, start : start + size, :].astype(jnp.float32)
        return total

    for pair in range(top // 2):
        both = summed(pair * quarter, quarter)
        swapped = pltpu.roll(both, width, 1)
        value_ref[2 * pair] = jnp.where(first, both, swapped)
        value_ref[2 * pair + 1] = jnp.where(first, swapped, both)
    for k in range(top):
        name_ref[k] = jnp.broadcast_to(routes_ref[:, k : k + 1], (quarter, lanes)) - second
    half = quarter // 2
    inner = summed(top // 2 * quarter, half)
    inner = jnp.concatenate([inner[:, :width], inner[:, width:]], axis=0)
    inner = jnp.transpose(inner).astype(jnp.bfloat16)

    def one_group(group, carry):
        dense = []
        for pair in range(experts // 2):
            base = group * experts + 2 * pair
            chosen = jnp.zeros((quarter, lanes), jnp.float32)
            for k in range(top):
                chosen = jnp.where(name_ref[k] == base, value_ref[k], chosen)
            dense.append(chosen.astype(jnp.bfloat16))
        result = jnp.dot(
            jnp.concatenate(dense, axis=1), weights_ref[group], preferred_element_type=jnp.float32
        ).astype(jnp.bfloat16)
        share_width = result.shape[1] // shares
        for share in range(shares):
            payload_ref[group * shares + share, :quarter, :] = result[:, share * share_width : (share + 1) * share_width]
            payload_ref[group * shares + share, quarter:, :] = inner
        return carry

    lax.fori_loop(0, groups, one_group, 0, unroll=groups <= 4)


def condition(parts, quarter_routes, weights, shares, width):
    quarter, top = quarter_routes.shape
    groups = weights.shape[0]
    lanes = 2 * width
    return pl.pallas_call(
        functools.partial(condition_kernel, top=top, width=width),
        out_shape=jax.ShapeDtypeStruct((groups * shares, quarter + width, lanes), jnp.bfloat16),
        scratch_shapes=[
            pltpu.VMEM((top, quarter, lanes), jnp.float32),
            pltpu.VMEM((top, quarter, lanes), jnp.int32),
        ],
        compiler_params=pltpu.CompilerParams(vmem_limit_bytes=VMEM_BYTES),
    )(parts, quarter_routes, weights)


def score_kernel(arrived_ref, docs_ref, queries_ref, out_ref, grads_ref, *, width, doc_count):
    sources, rows, lanes = arrived_ref.shape
    quarter = rows - width
    outer = arrived_ref[:, :quarter, :].reshape(sources * quarter, lanes)
    inner = jnp.concatenate([arrived_ref[s, quarter:, :] for s in range(sources)], axis=1)
    docs = jnp.concatenate([docs_ref[s : s + 1, :] for s in range(sources)], axis=1)
    docs = jnp.broadcast_to(docs, (width, sources * quarter))
    doc_group = 8

    def one_group(group, carry):
        masked = [
            jnp.where(docs == group * doc_group + d, inner, jnp.zeros_like(inner)) for d in range(doc_group)
        ]
        start = pl.multiple_of(group * doc_group * width, doc_group * width)
        grads_ref[pl.ds(start, doc_group * width), :] = jnp.dot(
            jnp.concatenate(masked, axis=0), outer, preferred_element_type=jnp.float32
        )
        return carry

    lax.fori_loop(0, doc_count // doc_group, one_group, 0, unroll=doc_count <= 32)
    flat = jnp.concatenate(
        [grads_ref[pl.ds(j, doc_count, stride=width), :].astype(jnp.bfloat16) for j in range(width)], axis=1
    )
    result = jnp.dot(flat, queries_ref[...], preferred_element_type=jnp.float32)
    owners, shares, owned, columns = out_ref.shape
    for owner in range(owners):
        for share in range(shares):
            out_ref[owner, share] = result[
                owner * owned : (owner + 1) * owned, share * columns : (share + 1) * columns
            ]


def score(arrived, docs, queries, width, owners, shares):
    doc_count = DOC_DEV * owners
    return pl.pallas_call(
        functools.partial(score_kernel, width=width, doc_count=doc_count),
        out_shape=jax.ShapeDtypeStruct((owners, shares, DOC_DEV, queries.shape[1] // shares), jnp.float32),
        scratch_shapes=[pltpu.VMEM((doc_count * width, arrived.shape[2]), jnp.float32)],
        compiler_params=pltpu.CompilerParams(vmem_limit_bytes=VMEM_BYTES),
    )(arrived, docs, queries)


def local(
    activations,
    grad_hidden,
    routes,
    doc_ids,
    query_grads,
    in_projection,
    out_projection,
    inverse_in,
    inverse_out,
):
    tokens, top = routes.shape
    experts, width, _ = inverse_in.shape
    owners = lax.axis_size("expert")
    shares = lax.axis_size("proj")
    quarter = tokens // shares
    query_count = query_grads.shape[0]
    share_rows = width // shares
    doc_count = DOC_DEV * owners
    assert doc_count <= 256

    half = experts // 2
    factors = inverse_out.astype(jnp.bfloat16)
    factors = jnp.concatenate([factors[:half], factors[half:]], axis=2).reshape(half * width, 2 * width)
    doc_rows = doc_ids.astype(jnp.bfloat16).reshape(tokens // 128, 128)
    shared = jnp.concatenate([factors, jnp.pad(doc_rows, ((0, 16 - tokens // 128), (0, 0)))], axis=0)
    shared = jnp.broadcast_to(shared[None], (owners, *shared.shape))
    shared = lax.all_to_all(shared, "expert", 0, 0, tiled=True)
    all_docs = shared[:, half * width : half * width + tokens // 128, :].astype(jnp.int32)
    all_docs = all_docs.reshape(owners * shares, quarter)
    factors = shared[:, : half * width, :].reshape(owners, half, width, 2, width)
    factors = factors.transpose(0, 3, 1, 2, 4).reshape(owners * experts * width, width)

    column = jnp.arange(experts * width)
    source_row = column // (experts * share_rows) * share_rows + column % share_rows
    place = (jnp.arange(width)[:, None] == source_row[None, :]).astype(jnp.bfloat16)
    own = column[:, None] // width == (column[None, :] // share_rows) % experts
    weights = jnp.dot(factors, place, preferred_element_type=jnp.float32).reshape(owners, experts * width, experts * width)
    weights = jnp.where(own[None], weights, 0).astype(jnp.bfloat16)

    flat_hidden = grad_hidden.reshape(tokens * top, grad_hidden.shape[2])
    wire = project(activations, flat_hidden, in_projection, out_projection, shares, top)
    parts = lax.all_to_all(wire, "proj", 0, 0, tiled=True)
    quarter_routes = lax.dynamic_slice_in_dim(routes, lax.axis_index("proj") * quarter, quarter, 0)
    payload = condition(parts, quarter_routes, weights, shares, width)
    arrived = lax.all_to_all(payload, ("expert", "proj"), 0, 0, tiled=True)

    queries = jnp.einsum(
        "qeil,ejl->jeiq",
        query_grads.reshape(query_count, experts, share_rows, width),
        inverse_in.astype(jnp.bfloat16),
        preferred_element_type=jnp.float32,
    ).astype(jnp.bfloat16).reshape(width * experts * share_rows, query_count)

    partial_scores = score(arrived, all_docs, queries, width, owners, shares)
    pieces = lax.all_to_all(
        partial_scores.reshape(owners * shares, DOC_DEV, query_count // shares), ("expert", "proj"), 0, 0, tiled=True
    )
    return jnp.sum(pieces, axis=0).T


def solution(mesh):
    in_specs = (
        P(("groups", "expert"), "proj"),
        P(("groups", "expert"), None, "proj"),
        P(("groups", "expert"), None),
        P(("groups", "expert")),
        P(None, "expert", "proj"),
        P(None, "proj"),
        P(None, "proj"),
        P("expert", None, None),
        P("expert", None, None),
    )
    out_specs = P("proj", ("groups", "expert"))
    return jax.shard_map(local, mesh=mesh, in_specs=in_specs, out_specs=out_specs, check_vma=False)
```

```python
import functools

import jax
import jax.numpy as jnp
from jax import lax
from jax.experimental import pallas as pl
from jax.experimental.pallas import tpu as pltpu
from jax.sharding import PartitionSpec as P

DOC_DEV = 8
VMEM_BYTES = 40 * 1024 * 1024


def half_lanes(shape, width):
    return lax.broadcasted_iota(jnp.int32, shape, len(shape) - 1) < width


def project_kernel(act_ref, hidden_ref, in_proj_ref, out_proj_ref, wire_ref, rows_ref, *, top):
    quarter = act_ref.shape[0]
    width = in_proj_ref.shape[0]
    twice = jnp.concatenate([out_proj_ref[...], out_proj_ref[...]], axis=0)
    rows_ref[...] = lax.dot_general(
        hidden_ref[...], twice, (((1,), (1,)), ((), ())), preferred_element_type=jnp.float32
    )
    first = half_lanes((quarter, 2 * width), width)
    for pair in range(top // 2):
        even = rows_ref[pl.ds(2 * pair, quarter, stride=top), :]
        odd = rows_ref[pl.ds(2 * pair + 1, quarter, stride=top), :]
        wire_ref[0, pair * quarter : (pair + 1) * quarter, :] = jnp.where(first, even, odd).astype(jnp.bfloat16)
    twice_in = jnp.concatenate([in_proj_ref[...], in_proj_ref[...]], axis=0)
    inner = lax.dot_general(
        act_ref[...], twice_in, (((1,), (1,)), ((), ())), preferred_element_type=jnp.float32
    )
    half = quarter // 2
    packed = jnp.where(half_lanes((half, 2 * width), width), inner[:half], inner[half:])
    high = packed.astype(jnp.bfloat16)
    start = top // 2 * quarter
    wire_ref[0, start : start + half, :] = high
    wire_ref[0, start + half :, :] = (packed - high.astype(jnp.float32)).astype(jnp.bfloat16)


def project(activations, flat_hidden, in_projection, out_projection, quarters, top):
    tokens, model = activations.shape
    width = in_projection.shape[0]
    quarter = tokens // quarters
    wire_rows = top // 2 * quarter + quarter
    return pl.pallas_call(
        functools.partial(project_kernel, top=top),
        grid=(quarters,),
        in_specs=[
            pl.BlockSpec((quarter, model), lambda q: (q, 0)),
            pl.BlockSpec((quarter * top, flat_hidden.shape[1]), lambda q: (q, 0)),
            pl.BlockSpec(in_projection.shape, lambda q: (0, 0)),
            pl.BlockSpec(out_projection.shape, lambda q: (0, 0)),
        ],
        out_specs=pl.BlockSpec((1, wire_rows, 2 * width), lambda q: (q, 0, 0)),
        out_shape=jax.ShapeDtypeStruct((quarters, wire_rows, 2 * width), jnp.bfloat16),
        scratch_shapes=[pltpu.VMEM((quarter * top, 2 * width), jnp.float32)],
        compiler_params=pltpu.CompilerParams(vmem_limit_bytes=60 * 1024 * 1024),
    )(activations, flat_hidden, in_projection, out_projection)


def condition_kernel(
    place_ref, parts_ref, routes_ref, weights_ref, payload_ref, value_ref, name_ref, *, top, width
):
    quarter = routes_ref.shape[0]
    groups, dense_width, _ = weights_ref.shape
    shares = payload_ref.shape[0] // groups
    lanes = 2 * width
    experts = dense_width // width
    first = half_lanes((quarter, lanes), width)
    second = 1 - first.astype(jnp.int32)

    def summed(start, size):
        total = parts_ref[0, start : start + size, :].astype(jnp.float32)
        for source in range(1, parts_ref.shape[0]):
            total = total + parts_ref[source, start : start + size, :].astype(jnp.float32)
        return total

    for pair in range(top // 2):
        both = summed(pair * quarter, quarter)
        swapped = pltpu.roll(both, width, 1)
        value_ref[2 * pair] = jnp.where(first, both, swapped)
        value_ref[2 * pair + 1] = jnp.where(first, swapped, both)
    for k in range(top):
        name_ref[k] = jnp.broadcast_to(routes_ref[:, k : k + 1], (quarter, lanes)) - second
    half = quarter // 2
    inner = summed(top // 2 * quarter, half) + summed(top // 2 * quarter + half, half)
    inner = jnp.concatenate([inner[:, :width], inner[:, width:]], axis=0)
    inner = jnp.transpose(inner).astype(jnp.bfloat16)

    def one_group(step, carry):
        group = lax.rem(place_ref[0] + groups - step, groups)
        dense = []
        for pair in range(experts // 2):
            base = group * experts + 2 * pair
            chosen = jnp.zeros((quarter, lanes), jnp.float32)
            for k in range(top):
                chosen = jnp.where(name_ref[k] == base, value_ref[k], chosen)
            dense.append(chosen.astype(jnp.bfloat16))
        result = jnp.dot(
            jnp.concatenate(dense, axis=1), weights_ref[step], preferred_element_type=jnp.float32
        ).astype(jnp.bfloat16)
        share_width = result.shape[1] // shares
        for share in range(shares):
            payload_ref[group * shares + share, :quarter, :] = result[:, share * share_width : (share + 1) * share_width]
            payload_ref[group * shares + share, quarter:, :] = inner
        return carry

    lax.fori_loop(0, groups, one_group, 0, unroll=groups <= 4)


def condition(place, parts, quarter_routes, weights, shares, width):
    quarter, top = quarter_routes.shape
    groups = weights.shape[0]
    lanes = 2 * width
    whole = pl.BlockSpec(memory_space=pltpu.VMEM)
    return pl.pallas_call(
        functools.partial(condition_kernel, top=top, width=width),
        in_specs=[pl.BlockSpec(memory_space=pltpu.SMEM), whole, whole, whole],
        out_shape=jax.ShapeDtypeStruct((groups * shares, quarter + width, lanes), jnp.bfloat16),
        scratch_shapes=[
            pltpu.VMEM((top, quarter, lanes), jnp.float32),
            pltpu.VMEM((top, quarter, lanes), jnp.int32),
        ],
        compiler_params=pltpu.CompilerParams(vmem_limit_bytes=VMEM_BYTES),
    )(place, parts, quarter_routes, weights)


def score_kernel(arrived_ref, docs_ref, far_ref, out_ref, grads_ref, queries_ref, sem, *, width, doc_count):
    fetch = pltpu.make_async_copy(far_ref, queries_ref, sem)
    fetch.start()
    sources, rows, lanes = arrived_ref.shape
    quarter = rows - width
    outer = arrived_ref[:, :quarter, :].reshape(sources * quarter, lanes)
    inner = jnp.concatenate([arrived_ref[s, quarter:, :] for s in range(sources)], axis=1)
    docs = jnp.concatenate([docs_ref[s : s + 1, :] for s in range(sources)], axis=1)
    docs = jnp.broadcast_to(docs, (width, sources * quarter))
    doc_group = 8

    def one_group(group, carry):
        masked = [
            jnp.where(docs == group * doc_group + d, inner, jnp.zeros_like(inner)) for d in range(doc_group)
        ]
        start = pl.multiple_of(group * doc_group * width, doc_group * width)
        grads_ref[pl.ds(start, doc_group * width), :] = jnp.dot(
            jnp.concatenate(masked, axis=0), outer, preferred_element_type=jnp.float32
        )
        return carry

    lax.fori_loop(0, doc_count // doc_group, one_group, 0, unroll=doc_count <= 32)
    high, low = [], []
    for j in range(width):
        grads = grads_ref[pl.ds(j, doc_count, stride=width), :]
        high.append(grads.astype(jnp.bfloat16))
        low.append((grads - high[-1].astype(jnp.float32)).astype(jnp.bfloat16))
    flat = jnp.concatenate([jnp.concatenate(high, axis=1), jnp.concatenate(low, axis=1)], axis=0)
    fetch.wait()
    result = jnp.dot(flat, queries_ref[...], preferred_element_type=jnp.float32)
    result = result[:doc_count] + result[doc_count:]
    owners, shares, owned, columns = out_ref.shape
    for owner in range(owners):
        for share in range(shares):
            out_ref[owner, share] = result[
                owner * owned : (owner + 1) * owned, share * columns : (share + 1) * columns
            ]


def score(arrived, docs, queries, width, owners, shares):
    doc_count = DOC_DEV * owners
    return pl.pallas_call(
        functools.partial(score_kernel, width=width, doc_count=doc_count),
        out_shape=jax.ShapeDtypeStruct((owners, shares, DOC_DEV, queries.shape[1] // shares), jnp.float32),
        in_specs=[
            pl.BlockSpec(memory_space=pltpu.VMEM),
            pl.BlockSpec(memory_space=pltpu.VMEM),
            pl.BlockSpec(memory_space=pl.ANY),
        ],
        scratch_shapes=[
            pltpu.VMEM((doc_count * width, arrived.shape[2]), jnp.float32),
            pltpu.VMEM(queries.shape, jnp.bfloat16),
            pltpu.SemaphoreType.DMA,
        ],
        compiler_params=pltpu.CompilerParams(vmem_limit_bytes=VMEM_BYTES),
    )(arrived, docs, queries)


def sum_kernel(pieces_ref, out_ref):
    total = pieces_ref[0]
    for source in range(1, pieces_ref.shape[0]):
        total = total + pieces_ref[source]
    out_ref[...] = total


def sum_pieces(pieces):
    return pl.pallas_call(
        sum_kernel, out_shape=jax.ShapeDtypeStruct(pieces.shape[1:], jnp.float32)
    )(pieces)


def gather_turned(block, axis, size):
    arrived = [block]
    for step in range(1, size):
        arrived.append(lax.ppermute(block, axis, [(i, (i + step) % size) for i in range(size)]))
    return jnp.stack(arrived)


def local(
    activations,
    grad_hidden,
    routes,
    doc_ids,
    query_grads,
    in_projection,
    out_projection,
    inverse_in,
    inverse_out,
):
    tokens, top = routes.shape
    experts, width, _ = inverse_in.shape
    owners = lax.axis_size("expert")
    shares = lax.axis_size("proj")
    quarter = tokens // shares
    query_count = query_grads.shape[0]
    share_rows = width // shares
    doc_count = DOC_DEV * owners
    assert doc_count <= 256

    half = experts // 2
    factors = inverse_out.astype(jnp.bfloat16)
    factors = jnp.concatenate([factors[:half], factors[half:]], axis=2).reshape(half * width, 2 * width)
    doc_rows = doc_ids.astype(jnp.bfloat16).reshape(tokens // 128, 128)
    shared = jnp.concatenate([factors, jnp.pad(doc_rows, ((0, 16 - tokens // 128), (0, 0)))], axis=0)
    place = lax.axis_index("expert")
    shared = gather_turned(shared, "expert", owners)
    all_docs = shared[:, half * width : half * width + tokens // 128, :].astype(jnp.int32)
    all_docs = all_docs[(place - jnp.arange(owners)) % owners]
    all_docs = all_docs.reshape(owners * shares, quarter)
    factors = shared[:, : half * width, :].reshape(owners, half, width, 2, width)
    factors = factors.transpose(0, 3, 1, 2, 4).reshape(owners * experts * width, width)

    column = jnp.arange(experts * width)
    source_row = column // (experts * share_rows) * share_rows + column % share_rows
    spread = (jnp.arange(width)[:, None] == source_row[None, :]).astype(jnp.bfloat16)
    own = column[:, None] // width == (column[None, :] // share_rows) % experts
    weights = jnp.dot(factors, spread, preferred_element_type=jnp.float32).reshape(owners, experts * width, experts * width)
    weights = jnp.where(own[None], weights, 0).astype(jnp.bfloat16)

    flat_hidden = grad_hidden.reshape(tokens * top, grad_hidden.shape[2])
    wire = project(activations, flat_hidden, in_projection, out_projection, shares, top)
    parts = lax.all_to_all(wire, "proj", 0, 0, tiled=True)
    quarter_routes = lax.dynamic_slice_in_dim(routes, lax.axis_index("proj") * quarter, quarter, 0)
    payload = condition(place.reshape(1).astype(jnp.int32), parts, quarter_routes, weights, shares, width)
    arrived = lax.all_to_all(payload, ("expert", "proj"), 0, 0, tiled=True)

    queries = jnp.einsum(
        "qeil,ejl->jeiq",
        query_grads.reshape(query_count, experts, share_rows, width),
        inverse_in.astype(jnp.bfloat16),
        preferred_element_type=jnp.float32,
    ).astype(jnp.bfloat16).reshape(width * experts * share_rows, query_count)

    partial_scores = score(arrived, all_docs, queries, width, owners, shares)
    pieces = lax.all_to_all(
        partial_scores.reshape(owners * shares, DOC_DEV, query_count // shares), ("expert", "proj"), 0, 0, tiled=True
    )
    return sum_pieces(pieces).T


def solution(mesh):
    in_specs = (
        P(("groups", "expert"), "proj"),
        P(("groups", "expert"), None, "proj"),
        P(("groups", "expert"), None),
        P(("groups", "expert")),
        P(None, "expert", "proj"),
        P(None, "proj"),
        P(None, "proj"),
        P("expert", None, None),
        P("expert", None, None),
    )
    out_specs = P("proj", ("groups", "expert"))
    return jax.shard_map(local, mesh=mesh, in_specs=in_specs, out_specs=out_specs, check_vma=False)
```

```python
import functools

import jax
import jax.numpy as jnp
from jax import lax
from jax.experimental import pallas as pl
from jax.experimental.pallas import tpu as pltpu
from jax.sharding import PartitionSpec as P

DOC_DEV = 8
LANES = 128
DOC_ROWS = 16
MIB = 1024 * 1024
VMEM = pl.BlockSpec(memory_space=pltpu.VMEM)
SMEM = pl.BlockSpec(memory_space=pltpu.SMEM)


def low_lanes(rows, width):
    return lax.broadcasted_iota(jnp.int32, (rows, LANES), 1) < width


def split(value):
    high = value.astype(jnp.bfloat16)
    return high, (value - high.astype(jnp.float32)).astype(jnp.bfloat16)


def project_kernel(
    act_ref, hidden_ref, in_proj_ref, out_proj_ref, inverse_ref, docs_ref, wire_ref, shared_ref, rows_ref, *, top
):
    quarter = act_ref.shape[0]
    width = in_proj_ref.shape[0]

    @pl.when(pl.program_id(0) == 0)
    def _():
        half = inverse_ref.shape[0] // 2
        for e in range(half):
            pair = jnp.concatenate([inverse_ref[e], inverse_ref[half + e]], axis=1)
            shared_ref[e * width : (e + 1) * width, :] = pair.astype(jnp.bfloat16)
        docs = docs_ref[...].astype(jnp.float32)
        docs = jnp.concatenate([docs, jnp.zeros((DOC_ROWS - docs.shape[0], LANES), jnp.float32)], axis=0)
        shared_ref[half * width :, :] = docs.astype(jnp.bfloat16)

    twice = jnp.concatenate([out_proj_ref[...], out_proj_ref[...]], axis=0)
    rows_ref[...] = lax.dot_general(
        hidden_ref[...], twice, (((1,), (1,)), ((), ())), preferred_element_type=jnp.float32
    )
    first = low_lanes(quarter, width)
    for pair in range(top // 2):
        even = rows_ref[pl.ds(2 * pair, quarter, stride=top), :]
        odd = rows_ref[pl.ds(2 * pair + 1, quarter, stride=top), :]
        wire_ref[0, pair * quarter : (pair + 1) * quarter, :] = jnp.where(first, even, odd).astype(jnp.bfloat16)
    twice_in = jnp.concatenate([in_proj_ref[...], in_proj_ref[...]], axis=0)
    inner = lax.dot_general(
        act_ref[...], twice_in, (((1,), (1,)), ((), ())), preferred_element_type=jnp.float32
    )
    half = quarter // 2
    high, low = split(jnp.where(low_lanes(half, width), inner[:half], inner[half:]))
    start = top // 2 * quarter
    wire_ref[0, start : start + half, :] = high
    wire_ref[0, start + half :, :] = low


def project(activations, flat_hidden, in_projection, out_projection, inverse_out, doc_rows, quarters, top):
    tokens, model = activations.shape
    width = in_projection.shape[0]
    quarter = tokens // quarters
    wire_rows = top // 2 * quarter + quarter
    shared_rows = inverse_out.shape[0] // 2 * width + DOC_ROWS
    return pl.pallas_call(
        functools.partial(project_kernel, top=top),
        grid=(quarters,),
        in_specs=[
            pl.BlockSpec((quarter, model), lambda q: (q, 0)),
            pl.BlockSpec((quarter * top, flat_hidden.shape[1]), lambda q: (q, 0)),
            pl.BlockSpec(in_projection.shape, lambda q: (0, 0)),
            pl.BlockSpec(out_projection.shape, lambda q: (0, 0)),
            pl.BlockSpec(inverse_out.shape, lambda q: (0, 0, 0)),
            pl.BlockSpec(doc_rows.shape, lambda q: (0, 0)),
        ],
        out_specs=[
            pl.BlockSpec((1, wire_rows, LANES), lambda q: (q, 0, 0)),
            pl.BlockSpec((shared_rows, LANES), lambda q: (0, 0)),
        ],
        out_shape=[
            jax.ShapeDtypeStruct((quarters, wire_rows, LANES), jnp.bfloat16),
            jax.ShapeDtypeStruct((shared_rows, LANES), jnp.bfloat16),
        ],
        scratch_shapes=[pltpu.VMEM((quarter * top, LANES), jnp.float32)],
        compiler_params=pltpu.CompilerParams(vmem_limit_bytes=60 * MIB),
    )(activations, flat_hidden, in_projection, out_projection, inverse_out, doc_rows)


def expand_kernel(place_ref, *refs, width, experts, shares):
    *shared_refs, weights_ref, docs_ref = refs
    owners = len(shared_refs)
    columns = experts * width
    share_rows = width // shares
    half = experts // 2
    lane = lax.broadcasted_iota(jnp.int32, (LANES, columns), 1)
    row = lax.broadcasted_iota(jnp.int32, (LANES, columns), 0)
    source = lane // (experts * share_rows) * share_rows + lane % share_rows
    expert_lane = lax.broadcasted_iota(jnp.int32, (half * width, columns), 1) // share_rows % experts
    expert_row = lax.broadcasted_iota(jnp.int32, (half * width, columns), 0) // width
    for side in range(2):
        spread = (row == source + side * width).astype(jnp.float32).astype(jnp.bfloat16)
        own = expert_lane == expert_row + side * half
        for step in range(owners):
            placed = jnp.dot(
                shared_refs[step][: half * width, :], spread, preferred_element_type=jnp.float32
            )
            weights_ref[step, side * half * width : (side + 1) * half * width, :] = jnp.where(
                own, placed, 0.0
            ).astype(jnp.bfloat16)
    for step in range(owners):
        owner = lax.rem(place_ref[0] + owners - step, owners)
        docs_ref[owner] = shared_refs[step][half * width :, :].astype(jnp.float32).astype(jnp.int32)


def expand(place, shared, width, experts, shares):
    owners = len(shared)
    return pl.pallas_call(
        functools.partial(expand_kernel, width=width, experts=experts, shares=shares),
        in_specs=[SMEM] + [VMEM] * owners,
        out_shape=[
            jax.ShapeDtypeStruct((owners, experts * width, experts * width), jnp.bfloat16),
            jax.ShapeDtypeStruct((owners, DOC_ROWS, LANES), jnp.int32),
        ],
        compiler_params=pltpu.CompilerParams(vmem_limit_bytes=40 * MIB),
    )(place, *shared)


def condition_kernel(
    place_ref, parts_ref, routes_ref, weights_ref, payload_ref, inner_ref, value_ref, name_ref, *, top, width
):
    quarter = routes_ref.shape[0]
    groups, dense_width, _ = weights_ref.shape
    shares = payload_ref.shape[0] // groups
    experts = dense_width // width
    first = low_lanes(quarter, width)
    second = 1 - first.astype(jnp.int32)

    def summed(start, size):
        total = parts_ref[0, start : start + size, :].astype(jnp.float32)
        for source in range(1, parts_ref.shape[0]):
            total = total + parts_ref[source, start : start + size, :].astype(jnp.float32)
        return total

    for pair in range(top // 2):
        both = summed(pair * quarter, quarter)
        swapped = pltpu.roll(both, width, 1)
        value_ref[2 * pair] = jnp.where(first, both, swapped)
        value_ref[2 * pair + 1] = jnp.where(first, swapped, both)
    for k in range(top):
        name_ref[k] = jnp.broadcast_to(routes_ref[:, k : k + 1], (quarter, LANES)) - second
    half = quarter // 2
    inner = summed(top // 2 * quarter, half) + summed(top // 2 * quarter + half, half)
    inner = jnp.concatenate([inner[:, :width], inner[:, width:]], axis=0)
    inner_ref[...] = jnp.transpose(inner).astype(jnp.bfloat16)

    def one_group(step, carry):
        group = lax.rem(place_ref[0] + groups - step, groups)
        dense = []
        for pair in range(experts // 2):
            base = group * experts + 2 * pair
            chosen = jnp.zeros((quarter, LANES), jnp.float32)
            for k in range(top):
                chosen = jnp.where(name_ref[k] == base, value_ref[k], chosen)
            dense.append(chosen.astype(jnp.bfloat16))
        result = jnp.dot(
            jnp.concatenate(dense, axis=1), weights_ref[step], preferred_element_type=jnp.float32
        ).astype(jnp.bfloat16)
        share_width = result.shape[1] // shares
        for share in range(shares):
            payload_ref[group * shares + share] = result[:, share * share_width : (share + 1) * share_width]
        return carry

    lax.fori_loop(0, groups, one_group, 0, unroll=groups <= 4)


def condition(place, parts, quarter_routes, weights, shares, width):
    quarter, top = quarter_routes.shape
    groups = weights.shape[0]
    return pl.pallas_call(
        functools.partial(condition_kernel, top=top, width=width),
        in_specs=[SMEM, VMEM, VMEM, VMEM],
        out_shape=[
            jax.ShapeDtypeStruct((groups * shares, quarter, LANES), jnp.bfloat16),
            jax.ShapeDtypeStruct((width, quarter), jnp.bfloat16),
        ],
        scratch_shapes=[
            pltpu.VMEM((top, quarter, LANES), jnp.float32),
            pltpu.VMEM((top, quarter, LANES), jnp.int32),
        ],
        compiler_params=pltpu.CompilerParams(vmem_limit_bytes=40 * MIB),
    )(place, parts, quarter_routes, weights)


def query_kernel(query_ref, inverse_ref, out_ref, factor_ref, spread_ref, wide_ref):
    count, experts, _ = query_ref.shape
    width = inverse_ref.shape[1]
    step = pl.program_id(0)
    rows = out_ref.shape[0] // width

    @pl.when(step == 0)
    def _():
        zeros = jnp.zeros((width, width), jnp.bfloat16)
        for e in range(experts):
            high, low = split(inverse_ref[e])
            upper = jnp.concatenate([high, zeros, low, zeros], axis=1)
            lower = jnp.concatenate([zeros, high, zeros, low], axis=1)
            factor_ref[e] = jnp.concatenate([upper, lower], axis=0)

    spread_ref[...] = query_ref[...].astype(jnp.float32).reshape(count * experts, LANES)
    for e in range(experts):
        query = spread_ref[pl.ds(e, count, stride=experts), :].astype(jnp.bfloat16)
        result = lax.dot_general(
            factor_ref[e],
            jnp.concatenate([query, query], axis=1),
            (((1,), (1,)), ((), ())),
            preferred_element_type=jnp.float32,
        )
        start = e * (rows // experts) + 2 * step
        for tile in range(wide_ref.shape[0]):
            part = result[:, tile * LANES : (tile + 1) * LANES]
            wide_ref[tile, pl.ds(start, width, stride=rows), :] = part[:width]
            wide_ref[tile, pl.ds(start + 1, width, stride=rows), :] = part[width:]

    @pl.when(step == pl.num_programs(0) - 1)
    def _():
        for tile in range(wide_ref.shape[0]):
            out_ref[:, tile * LANES : (tile + 1) * LANES] = wide_ref[tile].astype(jnp.bfloat16)


def condition_queries(query_grads, inverse_in):
    count, experts, flat = query_grads.shape
    width = inverse_in.shape[1]
    rows = experts * flat
    return pl.pallas_call(
        query_kernel,
        grid=(flat // LANES,),
        in_specs=[
            pl.BlockSpec((count, experts, LANES), lambda c: (0, 0, c)),
            pl.BlockSpec(inverse_in.shape, lambda c: (0, 0, 0)),
        ],
        out_specs=pl.BlockSpec((rows, count), lambda c: (0, 0)),
        out_shape=jax.ShapeDtypeStruct((rows, count), jnp.bfloat16),
        scratch_shapes=[
            pltpu.VMEM((experts, 2 * width, 4 * width), jnp.bfloat16),
            pltpu.VMEM((count * experts, LANES), jnp.float32),
            pltpu.VMEM((count // LANES, rows, LANES), jnp.float32),
        ],
        compiler_params=pltpu.CompilerParams(vmem_limit_bytes=40 * MIB),
    )(query_grads, inverse_in)


def score_kernel(place_ref, arrived_ref, docs_ref, *refs, width, doc_count, shares):
    *inner_refs, queries_ref, out_ref, grads_ref = refs
    owners = arrived_ref.shape[0] // shares
    outer, inner, docs = [], [], []
    for turn in range(shares):
        share = lax.rem(place_ref[1] + shares - turn, shares)
        for step in range(owners):
            owner = lax.rem(place_ref[0] + owners - step, owners)
            outer.append(arrived_ref[owner * shares + share])
            docs.append(docs_ref[owner, pl.ds(share, 1), :])
            inner.append(inner_refs[turn][step])
    outer = jnp.concatenate(outer, axis=0)
    inner = jnp.concatenate(inner, axis=1)
    docs = jnp.broadcast_to(jnp.concatenate(docs, axis=1), inner.shape)
    doc_group = 8

    def one_group(group, carry):
        masked = [
            jnp.where(docs == group * doc_group + d, inner, jnp.zeros_like(inner)) for d in range(doc_group)
        ]
        start = pl.multiple_of(group * doc_group * width, doc_group * width)
        grads_ref[pl.ds(start, doc_group * width), :] = jnp.dot(
            jnp.concatenate(masked, axis=0), outer, preferred_element_type=jnp.float32
        )
        return carry

    lax.fori_loop(0, doc_count // doc_group, one_group, 0, unroll=doc_count <= 32)
    high, low = [], []
    for j in range(width):
        parts = split(grads_ref[pl.ds(j, doc_count, stride=width), :])
        high.append(parts[0])
        low.append(parts[1])
    flat = jnp.concatenate([jnp.concatenate(high, axis=1), jnp.concatenate(low, axis=1)], axis=0)
    result = jnp.dot(flat, queries_ref[...], preferred_element_type=jnp.float32)
    result = result[:doc_count] + result[doc_count:]
    columns = result.shape[1] // shares
    fill = jnp.zeros((DOC_DEV, LANES - columns), jnp.float32)
    for owner in range(owners):
        for share in range(shares):
            piece = result[owner * DOC_DEV : (owner + 1) * DOC_DEV, share * columns : (share + 1) * columns]
            out_ref[owner * shares + share] = jnp.concatenate([piece, fill], axis=1)


def score(place, arrived, docs, inner, queries, width, shares):
    sources = arrived.shape[0]
    doc_count = DOC_DEV * sources // shares
    return pl.pallas_call(
        functools.partial(score_kernel, width=width, doc_count=doc_count, shares=shares),
        in_specs=[SMEM, VMEM, VMEM] + [VMEM] * len(inner) + [VMEM],
        out_shape=jax.ShapeDtypeStruct((sources, DOC_DEV, LANES), jnp.float32),
        scratch_shapes=[pltpu.VMEM((doc_count * width, arrived.shape[2]), jnp.float32)],
        compiler_params=pltpu.CompilerParams(vmem_limit_bytes=40 * MIB),
    )(place, arrived, docs, *inner, queries)


def sum_kernel(pieces_ref, out_ref):
    total = pieces_ref[0]
    for source in range(1, pieces_ref.shape[0]):
        total = total + pieces_ref[source]
    out_ref[...] = total[:, : out_ref.shape[1]]


def sum_pieces(pieces, columns):
    return pl.pallas_call(
        sum_kernel,
        in_specs=[VMEM],
        out_shape=jax.ShapeDtypeStruct((pieces.shape[1], columns), jnp.float32),
    )(pieces)


def gather_turned(block, axis, size):
    arrived = [block]
    for step in range(1, size):
        arrived.append(lax.ppermute(block, axis, [(i, (i + step) % size) for i in range(size)]))
    return arrived


def local(
    activations,
    grad_hidden,
    routes,
    doc_ids,
    query_grads,
    in_projection,
    out_projection,
    inverse_in,
    inverse_out,
):
    tokens, top = routes.shape
    experts, width, _ = inverse_in.shape
    owners = lax.axis_size("expert")
    shares = lax.axis_size("proj")
    quarter = tokens // shares
    assert quarter == LANES and 2 * width == LANES and experts * width // shares == LANES
    assert DOC_DEV * owners <= 256
    place = jnp.stack([lax.axis_index("expert"), lax.axis_index("proj")]).astype(jnp.int32)

    flat_hidden = grad_hidden.reshape(tokens * top, grad_hidden.shape[2])
    wire, shared = project(
        activations,
        flat_hidden,
        in_projection,
        out_projection,
        inverse_out,
        doc_ids.reshape(shares, quarter),
        shares,
        top,
    )
    parts = lax.all_to_all(wire, "proj", 0, 0, tiled=True)
    weights, all_docs = expand(place, gather_turned(shared, "expert", owners), width, experts, shares)
    quarter_routes = lax.dynamic_slice_in_dim(routes, lax.axis_index("proj") * quarter, quarter, 0)
    payload, inner = condition(place, parts, quarter_routes, weights, shares, width)
    arrived = lax.all_to_all(payload, ("expert", "proj"), 0, 0, tiled=True)
    inner = gather_turned(jnp.stack(gather_turned(inner, "expert", owners)), "proj", shares)
    queries = condition_queries(query_grads, inverse_in)
    partial_scores = score(place, arrived, all_docs, inner, queries, width, shares)
    pieces = lax.all_to_all(partial_scores, ("expert", "proj"), 0, 0, tiled=True)
    return sum_pieces(pieces, query_grads.shape[0] // shares).T


def solution(mesh):
    in_specs = (
        P(("groups", "expert"), "proj"),
        P(("groups", "expert"), None, "proj"),
        P(("groups", "expert"), None),
        P(("groups", "expert")),
        P(None, "expert", "proj"),
        P(None, "proj"),
        P(None, "proj"),
        P("expert", None, None),
        P("expert", None, None),
    )
    out_specs = P("proj", ("groups", "expert"))
    return jax.shard_map(local, mesh=mesh, in_specs=in_specs, out_specs=out_specs, check_vma=False)
```

```python
import functools

import jax
import jax.numpy as jnp
from jax import lax
from jax.experimental import pallas as pl
from jax.experimental.pallas import tpu as pltpu
from jax.sharding import PartitionSpec as P

DOC_DEV = 8
LANES = 128
DOC_ROWS = 16
MIB = 1024 * 1024
VMEM = pl.BlockSpec(memory_space=pltpu.VMEM)
SMEM = pl.BlockSpec(memory_space=pltpu.SMEM)


def low_lanes(rows, width):
    return lax.broadcasted_iota(jnp.int32, (rows, LANES), 1) < width


def split(value):
    high = value.astype(jnp.bfloat16)
    return high, (value - high.astype(jnp.float32)).astype(jnp.bfloat16)


def cost(microseconds):
    return pl.CostEstimate(flops=0, bytes_accessed=int(microseconds * 3.3e6), transcendentals=0)


def pack_shared(inverse_ref, docs_ref, shared_ref):
    width = inverse_ref.shape[1]
    half = inverse_ref.shape[0] // 2
    for e in range(half):
        pair = jnp.concatenate([inverse_ref[e], inverse_ref[half + e]], axis=1)
        shared_ref[e * width : (e + 1) * width, :] = pair.astype(jnp.bfloat16)
    docs = docs_ref[...].astype(jnp.float32)
    docs = jnp.concatenate([docs, jnp.zeros((DOC_ROWS - docs.shape[0], LANES), jnp.float32)], axis=0)
    shared_ref[half * width :, :] = docs.astype(jnp.bfloat16)


def project_kernel(place_ref, act_ref, hidden_ref, in_proj_ref, out_proj_ref, *refs, top):
    *pack_refs, rows_ref = refs
    if len(pack_refs) == 1:
        wire_ref = pack_refs[0]
    else:
        inverse_ref, docs_ref, wire_ref, shared_ref = pack_refs

        @pl.when(pl.program_id(0) == 0)
        def _():
            pack_shared(inverse_ref, docs_ref, shared_ref)

    quarter = act_ref.shape[0]
    width = in_proj_ref.shape[0]
    twice = jnp.concatenate([out_proj_ref[...], out_proj_ref[...]], axis=0)
    rows_ref[...] = lax.dot_general(
        hidden_ref[...], twice, (((1,), (1,)), ((), ())), preferred_element_type=jnp.float32
    )
    first = low_lanes(quarter, width)
    for pair in range(top // 2):
        even = rows_ref[pl.ds(2 * pair, quarter, stride=top), :]
        odd = rows_ref[pl.ds(2 * pair + 1, quarter, stride=top), :]
        wire_ref[0, pair * quarter : (pair + 1) * quarter, :] = jnp.where(first, even, odd).astype(jnp.bfloat16)
    twice_in = jnp.concatenate([in_proj_ref[...], in_proj_ref[...]], axis=0)
    inner = lax.dot_general(
        act_ref[...], twice_in, (((1,), (1,)), ((), ())), preferred_element_type=jnp.float32
    )
    half = quarter // 2
    high, low = split(jnp.where(low_lanes(half, width), inner[:half], inner[half:]))
    start = top // 2 * quarter
    wire_ref[0, start : start + half, :] = high
    wire_ref[0, start + half :, :] = low


def project(place, activations, flat_hidden, in_projection, out_projection, quarters, top, turn, packed=()):
    tokens, model = activations.shape
    quarter = tokens // quarters
    wire_rows = top // 2 * quarter + quarter

    def rows(g, place_ref):
        return jnp.bitwise_xor(place_ref[1], turn(g)), 0

    def fixed(array):
        return pl.BlockSpec(array.shape, lambda g, place_ref: (0,) * array.ndim)

    out_specs = [pl.BlockSpec((1, wire_rows, LANES), lambda g, place_ref: (g, 0, 0))]
    out_shape = [jax.ShapeDtypeStruct((quarters // 2, wire_rows, LANES), jnp.bfloat16)]
    if packed:
        experts, width, _ = packed[0].shape
        out_shape.append(jax.ShapeDtypeStruct((experts // 2 * width + DOC_ROWS, LANES), jnp.bfloat16))
        out_specs.append(fixed(out_shape[1]))
    return pl.pallas_call(
        functools.partial(project_kernel, top=top),
        grid_spec=pltpu.PrefetchScalarGridSpec(
            num_scalar_prefetch=1,
            grid=(quarters // 2,),
            in_specs=[
                pl.BlockSpec((quarter, model), rows),
                pl.BlockSpec((quarter * top, flat_hidden.shape[1]), rows),
                fixed(in_projection),
                fixed(out_projection),
            ]
            + [fixed(array) for array in packed],
            out_specs=out_specs,
            scratch_shapes=[pltpu.VMEM((quarter * top, LANES), jnp.float32)],
        ),
        out_shape=out_shape,
        compiler_params=pltpu.CompilerParams(vmem_limit_bytes=57 * MIB),
        cost_estimate=cost(3),
    )(place, activations, flat_hidden, in_projection, out_projection, *packed)


def combine_kernel(own_ref, other_ref, out_ref, *, value_rows):
    total = own_ref[0, :value_rows, :].astype(jnp.float32) + other_ref[1, :value_rows, :].astype(jnp.float32)
    out_ref[:value_rows, :] = total.astype(jnp.bfloat16)
    half = (out_ref.shape[0] - value_rows) // 2
    exact = jnp.zeros((half, LANES), jnp.float32)
    for part in (own_ref[0], other_ref[1]):
        exact = exact + part[value_rows : value_rows + half].astype(jnp.float32)
        exact = exact + part[value_rows + half :].astype(jnp.float32)
    high, low = split(exact)
    out_ref[value_rows : value_rows + half, :] = high
    out_ref[value_rows + half :, :] = low


def combine(own, other, value_rows):
    return pl.pallas_call(
        functools.partial(combine_kernel, value_rows=value_rows),
        in_specs=[VMEM, VMEM],
        out_shape=jax.ShapeDtypeStruct(own.shape[1:], jnp.bfloat16),
        compiler_params=pltpu.CompilerParams(vmem_limit_bytes=40 * MIB),
        cost_estimate=cost(1),
    )(own, other)


def expand_kernel(place_ref, shared_ref, weights_ref, docs_ref, *, width, experts, shares, turns):
    columns = experts * width
    share_rows = width // shares
    half = experts // 2
    lane = lax.broadcasted_iota(jnp.int32, (LANES, columns), 1)
    row = lax.broadcasted_iota(jnp.int32, (LANES, columns), 0)
    source = lane // (experts * share_rows) * share_rows + lane % share_rows
    expert_lane = lax.broadcasted_iota(jnp.int32, (half * width, columns), 1) // share_rows % experts
    expert_row = lax.broadcasted_iota(jnp.int32, (half * width, columns), 0) // width
    for side in range(2):
        spread = (row == source + side * width).astype(jnp.float32).astype(jnp.bfloat16)
        own = expert_lane == expert_row + side * half
        for entry, turn in enumerate(turns):
            placed = jnp.dot(
                shared_ref[entry, : half * width, :], spread, preferred_element_type=jnp.float32
            )
            weights_ref[turn, side * half * width : (side + 1) * half * width, :] = jnp.where(
                own, placed, 0.0
            ).astype(jnp.bfloat16)
    for entry, turn in enumerate(turns):
        owner = jnp.bitwise_xor(place_ref[0], turn)
        docs_ref[owner] = shared_ref[entry, half * width :, :].astype(jnp.float32).astype(jnp.int32)


def expand(place, shared, turns, width, experts, shares):
    owners = shared.shape[0]
    return pl.pallas_call(
        functools.partial(expand_kernel, width=width, experts=experts, shares=shares, turns=turns),
        in_specs=[SMEM, VMEM],
        out_shape=[
            jax.ShapeDtypeStruct((owners, experts * width, experts * width), jnp.bfloat16),
            jax.ShapeDtypeStruct((owners, DOC_ROWS, LANES), jnp.int32),
        ],
        compiler_params=pltpu.CompilerParams(vmem_limit_bytes=40 * MIB),
        cost_estimate=cost(1.3),
    )(place, shared)


def condition_kernel(
    place_ref, own_ref, near_ref, far_ref, routes_ref, weights_ref, payload_ref, value_ref, name_ref, *, top, width
):
    quarter = routes_ref.shape[0]
    groups, dense_width, _ = weights_ref.shape
    shares = payload_ref.shape[0] // groups
    experts = dense_width // width
    first = low_lanes(quarter, width)
    second = 1 - first.astype(jnp.int32)

    def summed(start, size):
        rows = slice(start, start + size)
        total = own_ref[1, rows, :].astype(jnp.float32) + near_ref[0, rows, :].astype(jnp.float32)
        return total + far_ref[rows, :].astype(jnp.float32)

    for pair in range(top // 2):
        both = summed(pair * quarter, quarter)
        swapped = pltpu.roll(both, width, 1)
        value_ref[2 * pair] = jnp.where(first, both, swapped)
        value_ref[2 * pair + 1] = jnp.where(first, swapped, both)
    for k in range(top):
        name_ref[k] = jnp.broadcast_to(routes_ref[:, k : k + 1], (quarter, LANES)) - second
    half = quarter // 2
    inner = summed(top // 2 * quarter, half) + summed(top // 2 * quarter + half, half)
    inner = jnp.concatenate([inner[:, :width], inner[:, width:]], axis=0)
    inner = jnp.transpose(inner).astype(jnp.bfloat16)

    def one_group(step, carry):
        group = jnp.bitwise_xor(place_ref[0], step)
        dense = []
        for pair in range(experts // 2):
            base = group * experts + 2 * pair
            chosen = jnp.zeros((quarter, LANES), jnp.float32)
            for k in range(top):
                chosen = jnp.where(name_ref[k] == base, value_ref[k], chosen)
            dense.append(chosen.astype(jnp.bfloat16))
        result = jnp.dot(
            jnp.concatenate(dense, axis=1), weights_ref[step], preferred_element_type=jnp.float32
        ).astype(jnp.bfloat16)
        share_width = result.shape[1] // shares
        for share in range(shares):
            piece = result[:, share * share_width : (share + 1) * share_width]
            payload_ref[group * shares + share, :quarter, :] = piece
            payload_ref[group * shares + share, quarter:, :] = inner
        return carry

    lax.fori_loop(0, groups, one_group, 0, unroll=groups <= 4)


def condition(place, own, near, far, quarter_routes, weights, shares, width):
    quarter, top = quarter_routes.shape
    groups = weights.shape[0]
    return pl.pallas_call(
        functools.partial(condition_kernel, top=top, width=width),
        in_specs=[SMEM] + [VMEM] * 5,
        out_shape=jax.ShapeDtypeStruct((groups * shares, quarter + width, LANES), jnp.bfloat16),
        scratch_shapes=[
            pltpu.VMEM((top, quarter, LANES), jnp.float32),
            pltpu.VMEM((top, quarter, LANES), jnp.int32),
        ],
        compiler_params=pltpu.CompilerParams(vmem_limit_bytes=40 * MIB),
        cost_estimate=cost(2),
    )(place, own, near, far, quarter_routes, weights)


def query_kernel(query_ref, inverse_ref, out_ref, factor_ref, spread_ref, wide_ref):
    count, experts, _ = query_ref.shape
    width = inverse_ref.shape[1]
    step = pl.program_id(0)
    rows = out_ref.shape[0] // width

    @pl.when(step == 0)
    def _():
        zeros = jnp.zeros((width, width), jnp.bfloat16)
        for e in range(experts):
            high, low = split(inverse_ref[e])
            upper = jnp.concatenate([high, zeros, low, zeros], axis=1)
            lower = jnp.concatenate([zeros, high, zeros, low], axis=1)
            factor_ref[e] = jnp.concatenate([upper, lower], axis=0)

    spread_ref[...] = query_ref[...].astype(jnp.float32).reshape(count * experts, LANES)
    for e in range(experts):
        query = spread_ref[pl.ds(e, count, stride=experts), :].astype(jnp.bfloat16)
        result = lax.dot_general(
            factor_ref[e],
            jnp.concatenate([query, query], axis=1),
            (((1,), (1,)), ((), ())),
            preferred_element_type=jnp.float32,
        )
        start = e * (rows // experts) + 2 * step
        for tile in range(wide_ref.shape[0]):
            part = result[:, tile * LANES : (tile + 1) * LANES]
            wide_ref[tile, pl.ds(start, width, stride=rows), :] = part[:width]
            wide_ref[tile, pl.ds(start + 1, width, stride=rows), :] = part[width:]

    @pl.when(step == pl.num_programs(0) - 1)
    def _():
        for tile in range(wide_ref.shape[0]):
            out_ref[:, tile * LANES : (tile + 1) * LANES] = wide_ref[tile].astype(jnp.bfloat16)


def condition_queries(query_grads, inverse_in):
    count, experts, flat = query_grads.shape
    width = inverse_in.shape[1]
    rows = experts * flat
    return pl.pallas_call(
        query_kernel,
        grid=(flat // LANES,),
        in_specs=[
            pl.BlockSpec((count, experts, LANES), lambda c: (0, 0, c)),
            pl.BlockSpec(inverse_in.shape, lambda c: (0, 0, 0)),
        ],
        out_specs=pl.BlockSpec((rows, count), lambda c: (0, 0)),
        out_shape=jax.ShapeDtypeStruct((rows, count), jnp.bfloat16),
        scratch_shapes=[
            pltpu.VMEM((experts, 2 * width, 4 * width), jnp.bfloat16),
            pltpu.VMEM((count * experts, LANES), jnp.float32),
            pltpu.VMEM((count // LANES, rows, LANES), jnp.float32),
        ],
        compiler_params=pltpu.CompilerParams(vmem_limit_bytes=57 * MIB),
        cost_estimate=cost(10),
    )(query_grads, inverse_in)


def score_kernel(arrived_ref, docs_ref, far_ref, out_ref, grads_ref, queries_ref, sem, *, width, doc_count, shares):
    fetch = pltpu.make_async_copy(far_ref, queries_ref, sem)
    fetch.start()
    sources, rows, lanes = arrived_ref.shape
    owners = sources // shares
    quarter = rows - width
    outer = arrived_ref[:, :quarter, :].reshape(sources * quarter, lanes)
    inner = jnp.concatenate([arrived_ref[s, quarter:, :] for s in range(sources)], axis=1)
    docs = [docs_ref[s // shares, s % shares : s % shares + 1, :] for s in range(sources)]
    docs = jnp.broadcast_to(jnp.concatenate(docs, axis=1), inner.shape)
    doc_group = 8

    def one_group(group, carry):
        masked = [
            jnp.where(docs == group * doc_group + d, inner, jnp.zeros_like(inner)) for d in range(doc_group)
        ]
        start = pl.multiple_of(group * doc_group * width, doc_group * width)
        grads_ref[pl.ds(start, doc_group * width), :] = jnp.dot(
            jnp.concatenate(masked, axis=0), outer, preferred_element_type=jnp.float32
        )
        return carry

    lax.fori_loop(0, doc_count // doc_group, one_group, 0, unroll=doc_count <= 32)
    high, low = [], []
    for j in range(width):
        parts = split(grads_ref[pl.ds(j, doc_count, stride=width), :])
        high.append(parts[0])
        low.append(parts[1])
    flat = jnp.concatenate([jnp.concatenate(high, axis=1), jnp.concatenate(low, axis=1)], axis=0)
    fetch.wait()
    result = jnp.dot(flat, queries_ref[...], preferred_element_type=jnp.float32)
    result = result[:doc_count] + result[doc_count:]
    columns = result.shape[1] // shares
    fill = jnp.zeros((DOC_DEV, LANES - columns), jnp.float32)
    for owner in range(owners):
        for share in range(shares):
            piece = result[owner * DOC_DEV : (owner + 1) * DOC_DEV, share * columns : (share + 1) * columns]
            out_ref[owner * shares + share] = jnp.concatenate([piece, fill], axis=1)


def score(arrived, docs, queries, width, shares):
    sources = arrived.shape[0]
    doc_count = DOC_DEV * sources // shares
    return pl.pallas_call(
        functools.partial(score_kernel, width=width, doc_count=doc_count, shares=shares),
        in_specs=[VMEM, VMEM, pl.BlockSpec(memory_space=pl.ANY)],
        out_shape=jax.ShapeDtypeStruct((sources, DOC_DEV, LANES), jnp.float32),
        scratch_shapes=[
            pltpu.VMEM((doc_count * width, arrived.shape[2]), jnp.float32),
            pltpu.VMEM(queries.shape, jnp.bfloat16),
            pltpu.SemaphoreType.DMA,
        ],
        compiler_params=pltpu.CompilerParams(vmem_limit_bytes=57 * MIB),
        cost_estimate=cost(5),
    )(arrived, docs, queries)


def sum_kernel(pieces_ref, out_ref):
    total = pieces_ref[0]
    for source in range(1, pieces_ref.shape[0]):
        total = total + pieces_ref[source]
    out_ref[...] = total[:, : out_ref.shape[1]]


def sum_pieces(pieces, columns):
    return pl.pallas_call(
        sum_kernel,
        in_specs=[VMEM],
        out_shape=jax.ShapeDtypeStruct((pieces.shape[1], columns), jnp.float32),
    )(pieces)


def exchange(block, axis, size, turn):
    return lax.ppermute(block, axis, [(i, i ^ turn) for i in range(size)])


def double(blocks, turns, axis, size, turn):
    blocks = jnp.concatenate([blocks, exchange(blocks, axis, size, turn)], axis=0)
    return blocks, turns + tuple(t ^ turn for t in turns)


def local(
    activations,
    grad_hidden,
    routes,
    doc_ids,
    query_grads,
    in_projection,
    out_projection,
    inverse_in,
    inverse_out,
):
    tokens, top = routes.shape
    experts, width, _ = inverse_in.shape
    owners = lax.axis_size("expert")
    shares = lax.axis_size("proj")
    quarter = tokens // shares
    assert quarter == LANES and 2 * width == LANES and experts * width // shares == LANES
    assert shares == 4 and owners & (owners - 1) == 0
    assert DOC_DEV * owners <= 256
    place = jnp.stack([lax.axis_index("expert"), lax.axis_index("proj")]).astype(jnp.int32)

    flat_hidden = grad_hidden.reshape(tokens * top, grad_hidden.shape[2])
    factors = (activations, flat_hidden, in_projection, out_projection, shares, top)
    leaving, shared = project(
        place, *factors, lambda g: 2 * g + 1, (inverse_out, doc_ids.reshape(shares, quarter))
    )
    near = exchange(leaving, "proj", shares, 1)
    first = exchange(shared, "expert", owners, owners // 2)
    (own,) = project(place, *factors, lambda g: 2 - 2 * g)
    first, own = lax.optimization_barrier((first, own))
    shared, turns = jnp.stack([shared, first]), (0, owners // 2)
    for bit in reversed(range((owners // 2).bit_length() - 1)):
        shared, turns = double(shared, turns, "expert", owners, 1 << bit)
    far = exchange(combine(own, near, top // 2 * quarter), "proj", shares, 2)
    weights, all_docs = expand(place, shared, turns, width, experts, shares)
    quarter_routes = lax.dynamic_slice_in_dim(routes, lax.axis_index("proj") * quarter, quarter, 0)
    payload = condition(place, own, near, far, quarter_routes, weights, shares, width)
    payload, query_grads = lax.optimization_barrier((payload, query_grads))
    arrived = lax.all_to_all(payload, ("expert", "proj"), 0, 0, tiled=True)
    queries = condition_queries(query_grads, inverse_in)
    partial_scores = score(arrived, all_docs, queries, width, shares)
    pieces = lax.all_to_all(partial_scores, ("expert", "proj"), 0, 0, tiled=True)
    return sum_pieces(pieces, query_grads.shape[0] // shares).T


def solution(mesh):
    in_specs = (
        P(("groups", "expert"), "proj"),
        P(("groups", "expert"), None, "proj"),
        P(("groups", "expert"), None),
        P(("groups", "expert")),
        P(None, "expert", "proj"),
        P(None, "proj"),
        P(None, "proj"),
        P("expert", None, None),
        P("expert", None, None),
    )
    out_specs = P("proj", ("groups", "expert"))
    return jax.shard_map(local, mesh=mesh, in_specs=in_specs, out_specs=out_specs, check_vma=False)
```

```python
import functools

import jax
import jax.numpy as jnp
from jax import lax
from jax.experimental import pallas as pl
from jax.experimental.pallas import tpu as pltpu
from jax.sharding import PartitionSpec as P

DOC_DEV = 8
LANES = 128
DOC_ROWS = 16
MIB = 1024 * 1024
VMEM = pl.BlockSpec(memory_space=pltpu.VMEM)
HBM = pl.BlockSpec(memory_space=pltpu.HBM)


def low_lanes(rows, width):
    return lax.broadcasted_iota(jnp.int32, (rows, LANES), 1) < width


def stay(array):
    return pltpu.with_memory_space_constraint(array, pltpu.HBM)


def split(value):
    high = value.astype(jnp.bfloat16)
    return high, (value - high.astype(jnp.float32)).astype(jnp.bfloat16)


def cost(microseconds):
    return pl.CostEstimate(flops=0, bytes_accessed=int(microseconds * 3.3e6), transcendentals=0)


def pack_shared(inverse_ref, docs_ref, shared_ref):
    width = inverse_ref.shape[1]
    half = inverse_ref.shape[0] // 2
    for e in range(half):
        pair = jnp.concatenate([inverse_ref[e], inverse_ref[half + e]], axis=1)
        shared_ref[e * width : (e + 1) * width, :] = pair.astype(jnp.bfloat16)
    docs = docs_ref[...].astype(jnp.float32)
    docs = jnp.concatenate([docs, jnp.zeros((DOC_ROWS - docs.shape[0], LANES), jnp.float32)], axis=0)
    shared_ref[half * width :, :] = docs.astype(jnp.bfloat16)


def project_kernel(
    act_hbm, hidden_hbm, in_proj_hbm, out_proj_hbm, inverse_hbm, docs_hbm, leaving_ref, own_ref, shared_ref, *refs, top
):
    act_ref, hidden_ref, in_proj_ref, out_proj_ref, inverse_ref, docs_ref, rows_ref, quarter_sems, sems = refs
    turns = (1, 3, 2, 0)
    quarter = act_ref.shape[1]
    width = in_proj_ref.shape[0]
    place = lax.axis_index("proj")
    fixed = [
        pltpu.make_async_copy(source, target, sems.at[i])
        for i, (source, target) in enumerate(
            [(out_proj_hbm, out_proj_ref), (in_proj_hbm, in_proj_ref), (inverse_hbm, inverse_ref), (docs_hbm, docs_ref)]
        )
    ]
    fixed[0].start()
    moving = []
    for g, turn in enumerate(turns):
        start = jnp.bitwise_xor(place, turn) * quarter
        hidden_rows = pl.ds(pl.multiple_of(start * top, quarter * top), quarter * top)
        act_rows = pl.ds(pl.multiple_of(start, quarter), quarter)
        moving.append(
            (
                pltpu.make_async_copy(hidden_hbm.at[hidden_rows], hidden_ref.at[g], quarter_sems.at[g, 0]),
                pltpu.make_async_copy(act_hbm.at[act_rows], act_ref.at[g], quarter_sems.at[g, 1]),
            )
        )
        moving[g][0].start()
        if g == 0:
            fixed[1].start()
        moving[g][1].start()
        if g == 0:
            fixed[2].start()
            fixed[3].start()
    half = quarter // 2
    first = low_lanes(quarter, width)
    fixed[0].wait()
    twice = jnp.concatenate([out_proj_ref[...], out_proj_ref[...]], axis=0)
    for g in range(len(turns)):
        wire_ref = leaving_ref.at[g] if g < 2 else own_ref.at[g - 2]
        moving[g][0].wait()
        rows_ref[g % 2] = lax.dot_general(
            hidden_ref[g], twice, (((1,), (1,)), ((), ())), preferred_element_type=jnp.float32
        )
        for pair in range(top // 2):
            even = rows_ref[g % 2, pl.ds(2 * pair, quarter, stride=top), :]
            odd = rows_ref[g % 2, pl.ds(2 * pair + 1, quarter, stride=top), :]
            wire_ref[pair * quarter : (pair + 1) * quarter, :] = jnp.where(first, even, odd).astype(jnp.bfloat16)
        if g == 0:
            fixed[1].wait()
        twice_in = jnp.concatenate([in_proj_ref[...], in_proj_ref[...]], axis=0)
        moving[g][1].wait()
        inner = lax.dot_general(
            act_ref[g], twice_in, (((1,), (1,)), ((), ())), preferred_element_type=jnp.float32
        )
        high, low = split(jnp.where(low_lanes(half, width), inner[:half], inner[half:]))
        start = top // 2 * quarter
        wire_ref[start : start + half, :] = high
        wire_ref[start + half :, :] = low
        if g == 0:
            fixed[2].wait()
            fixed[3].wait()
            pack_shared(inverse_ref, docs_ref, shared_ref)


def project(activations, flat_hidden, in_projection, out_projection, inverse_out, doc_rows, quarters, top):
    tokens, model = activations.shape
    quarter = tokens // quarters
    wire_rows = top // 2 * quarter + quarter
    experts, width, _ = inverse_out.shape
    wire = jax.ShapeDtypeStruct((quarters // 2, wire_rows, LANES), jnp.bfloat16)
    fixed = (in_projection, out_projection, inverse_out, doc_rows)
    return pl.pallas_call(
        functools.partial(project_kernel, top=top),
        in_specs=[HBM] * 6,
        out_specs=[VMEM] * 3,
        out_shape=[wire, wire, jax.ShapeDtypeStruct((experts // 2 * width + DOC_ROWS, LANES), jnp.bfloat16)],
        scratch_shapes=[
            pltpu.VMEM((quarters, quarter, model), jnp.bfloat16),
            pltpu.VMEM((quarters, quarter * top, flat_hidden.shape[1]), jnp.bfloat16),
        ]
        + [pltpu.VMEM(array.shape, array.dtype) for array in fixed]
        + [
            pltpu.VMEM((2, quarter * top, LANES), jnp.float32),
            pltpu.SemaphoreType.DMA((quarters, 2)),
            pltpu.SemaphoreType.DMA((len(fixed),)),
        ],
        compiler_params=pltpu.CompilerParams(vmem_limit_bytes=40 * MIB),
        cost_estimate=cost(5),
    )(*[stay(array) for array in (activations, flat_hidden, *fixed)])


def combine_kernel(own_ref, other_ref, out_ref, *, value_rows):
    total = own_ref[0, :value_rows, :].astype(jnp.float32) + other_ref[1, :value_rows, :].astype(jnp.float32)
    out_ref[:value_rows, :] = total.astype(jnp.bfloat16)
    half = (out_ref.shape[0] - value_rows) // 2
    exact = jnp.zeros((half, LANES), jnp.float32)
    for part in (own_ref[0], other_ref[1]):
        exact = exact + part[value_rows : value_rows + half].astype(jnp.float32)
        exact = exact + part[value_rows + half :].astype(jnp.float32)
    high, low = split(exact)
    out_ref[value_rows : value_rows + half, :] = high
    out_ref[value_rows + half :, :] = low


def combine(own, other, value_rows):
    return pl.pallas_call(
        functools.partial(combine_kernel, value_rows=value_rows),
        in_specs=[VMEM, VMEM],
        out_shape=jax.ShapeDtypeStruct(own.shape[1:], jnp.bfloat16),
        compiler_params=pltpu.CompilerParams(vmem_limit_bytes=40 * MIB),
        cost_estimate=cost(1),
    )(own, other)


def expand_kernel(shared_ref, weights_ref, docs_ref, *, width, experts, shares, turns):
    columns = experts * width
    share_rows = width // shares
    half = experts // 2
    lane = lax.broadcasted_iota(jnp.int32, (LANES, columns), 1)
    row = lax.broadcasted_iota(jnp.int32, (LANES, columns), 0)
    source = lane // (experts * share_rows) * share_rows + lane % share_rows
    expert_lane = lax.broadcasted_iota(jnp.int32, (half * width, columns), 1) // share_rows % experts
    expert_row = lax.broadcasted_iota(jnp.int32, (half * width, columns), 0) // width
    for side in range(2):
        spread = (row == source + side * width).astype(jnp.float32).astype(jnp.bfloat16)
        own = expert_lane == expert_row + side * half
        for entry, turn in enumerate(turns):
            placed = jnp.dot(
                shared_ref[entry, : half * width, :], spread, preferred_element_type=jnp.float32
            )
            weights_ref[turn, side * half * width : (side + 1) * half * width, :] = jnp.where(
                own, placed, 0.0
            ).astype(jnp.bfloat16)
    for entry, turn in enumerate(turns):
        owner = jnp.bitwise_xor(lax.axis_index("expert"), turn)
        docs_ref[owner] = shared_ref[entry, half * width :, :].astype(jnp.float32).astype(jnp.int32)


def expand(shared, turns, width, experts, shares):
    owners = shared.shape[0]
    return pl.pallas_call(
        functools.partial(expand_kernel, width=width, experts=experts, shares=shares, turns=turns),
        in_specs=[VMEM],
        out_shape=[
            jax.ShapeDtypeStruct((owners, experts * width, experts * width), jnp.bfloat16),
            jax.ShapeDtypeStruct((owners, DOC_ROWS, LANES), jnp.int32),
        ],
        compiler_params=pltpu.CompilerParams(vmem_limit_bytes=40 * MIB),
        cost_estimate=cost(1.3),
    )(shared)


def condition_kernel(
    own_ref, near_ref, far_ref, routes_ref, weights_ref, payload_ref, value_ref, name_ref, *, top, width
):
    quarter = routes_ref.shape[0]
    groups, dense_width, _ = weights_ref.shape
    shares = payload_ref.shape[0] // groups
    experts = dense_width // width
    first = low_lanes(quarter, width)
    second = 1 - first.astype(jnp.int32)

    def summed(start, size):
        rows = slice(start, start + size)
        total = own_ref[1, rows, :].astype(jnp.float32) + near_ref[0, rows, :].astype(jnp.float32)
        return total + far_ref[rows, :].astype(jnp.float32)

    for pair in range(top // 2):
        both = summed(pair * quarter, quarter)
        swapped = pltpu.roll(both, width, 1)
        value_ref[2 * pair] = jnp.where(first, both, swapped)
        value_ref[2 * pair + 1] = jnp.where(first, swapped, both)
    for k in range(top):
        name_ref[k] = jnp.broadcast_to(routes_ref[:, k : k + 1], (quarter, LANES)) - second
    half = quarter // 2
    inner = summed(top // 2 * quarter, half) + summed(top // 2 * quarter + half, half)
    inner = jnp.concatenate([inner[:, :width], inner[:, width:]], axis=0)
    inner = jnp.transpose(inner).astype(jnp.bfloat16)

    def one_group(step, carry):
        group = jnp.bitwise_xor(lax.axis_index("expert"), step)
        dense = []
        for pair in range(experts // 2):
            base = group * experts + 2 * pair
            chosen = jnp.zeros((quarter, LANES), jnp.float32)
            for k in range(top):
                chosen = jnp.where(name_ref[k] == base, value_ref[k], chosen)
            dense.append(chosen.astype(jnp.bfloat16))
        result = jnp.dot(
            jnp.concatenate(dense, axis=1), weights_ref[step], preferred_element_type=jnp.float32
        ).astype(jnp.bfloat16)
        share_width = result.shape[1] // shares
        for share in range(shares):
            piece = result[:, share * share_width : (share + 1) * share_width]
            payload_ref[group * shares + share, :quarter, :] = piece
            payload_ref[group * shares + share, quarter:, :] = inner
        return carry

    lax.fori_loop(0, groups, one_group, 0, unroll=groups <= 4)


def condition(own, near, far, quarter_routes, weights, shares, width):
    quarter, top = quarter_routes.shape
    groups = weights.shape[0]
    return pl.pallas_call(
        functools.partial(condition_kernel, top=top, width=width),
        in_specs=[VMEM] * 5,
        out_shape=jax.ShapeDtypeStruct((groups * shares, quarter + width, LANES), jnp.bfloat16),
        scratch_shapes=[
            pltpu.VMEM((top, quarter, LANES), jnp.float32),
            pltpu.VMEM((top, quarter, LANES), jnp.int32),
        ],
        compiler_params=pltpu.CompilerParams(vmem_limit_bytes=40 * MIB),
        cost_estimate=cost(2),
    )(own, near, far, quarter_routes, weights)


def query_kernel(query_ref, inverse_ref, out_ref, factor_ref, spread_ref, wide_ref):
    count, experts, _ = query_ref.shape
    width = inverse_ref.shape[1]
    step = pl.program_id(0)
    rows = out_ref.shape[0] // width

    @pl.when(step == 0)
    def _():
        zeros = jnp.zeros((width, width), jnp.bfloat16)
        for e in range(experts):
            high, low = split(inverse_ref[e])
            upper = jnp.concatenate([high, zeros, low, zeros], axis=1)
            lower = jnp.concatenate([zeros, high, zeros, low], axis=1)
            factor_ref[e] = jnp.concatenate([upper, lower], axis=0)

    spread_ref[...] = query_ref[...].astype(jnp.float32).reshape(count * experts, LANES)
    for e in range(experts):
        query = spread_ref[pl.ds(e, count, stride=experts), :].astype(jnp.bfloat16)
        result = lax.dot_general(
            factor_ref[e],
            jnp.concatenate([query, query], axis=1),
            (((1,), (1,)), ((), ())),
            preferred_element_type=jnp.float32,
        )
        start = e * (rows // experts) + 2 * step
        for tile in range(wide_ref.shape[0]):
            part = result[:, tile * LANES : (tile + 1) * LANES]
            wide_ref[tile, pl.ds(start, width, stride=rows), :] = part[:width]
            wide_ref[tile, pl.ds(start + 1, width, stride=rows), :] = part[width:]

    @pl.when(step == pl.num_programs(0) - 1)
    def _():
        for tile in range(wide_ref.shape[0]):
            out_ref[:, tile * LANES : (tile + 1) * LANES] = wide_ref[tile].astype(jnp.bfloat16)


def condition_queries(query_grads, inverse_in):
    count, experts, flat = query_grads.shape
    width = inverse_in.shape[1]
    rows = experts * flat
    return pl.pallas_call(
        query_kernel,
        grid=(flat // LANES,),
        in_specs=[
            pl.BlockSpec((count, experts, LANES), lambda c: (0, 0, c)),
            pl.BlockSpec(inverse_in.shape, lambda c: (0, 0, 0)),
        ],
        out_specs=pl.BlockSpec((rows, count), lambda c: (0, 0)),
        out_shape=jax.ShapeDtypeStruct((rows, count), jnp.bfloat16),
        scratch_shapes=[
            pltpu.VMEM((experts, 2 * width, 4 * width), jnp.bfloat16),
            pltpu.VMEM((count * experts, LANES), jnp.float32),
            pltpu.VMEM((count // LANES, rows, LANES), jnp.float32),
        ],
        compiler_params=pltpu.CompilerParams(vmem_limit_bytes=40 * MIB),
        cost_estimate=cost(10),
    )(stay(query_grads), inverse_in)


def score_kernel(arrived_ref, docs_ref, far_ref, out_ref, grads_ref, queries_ref, sem, *, width, doc_count, shares):
    fetch = pltpu.make_async_copy(far_ref, queries_ref, sem)
    fetch.start()
    sources, rows, lanes = arrived_ref.shape
    owners = sources // shares
    quarter = rows - width
    outer = arrived_ref[:, :quarter, :].reshape(sources * quarter, lanes)
    inner = jnp.concatenate([arrived_ref[s, quarter:, :] for s in range(sources)], axis=1)
    docs = [docs_ref[s // shares, s % shares : s % shares + 1, :] for s in range(sources)]
    docs = jnp.broadcast_to(jnp.concatenate(docs, axis=1), inner.shape)
    doc_group = 8

    def one_group(group, carry):
        masked = [
            jnp.where(docs == group * doc_group + d, inner, jnp.zeros_like(inner)) for d in range(doc_group)
        ]
        start = pl.multiple_of(group * doc_group * width, doc_group * width)
        grads_ref[pl.ds(start, doc_group * width), :] = jnp.dot(
            jnp.concatenate(masked, axis=0), outer, preferred_element_type=jnp.float32
        )
        return carry

    lax.fori_loop(0, doc_count // doc_group, one_group, 0, unroll=doc_count <= 32)
    high, low = [], []
    for j in range(width):
        parts = split(grads_ref[pl.ds(j, doc_count, stride=width), :])
        high.append(parts[0])
        low.append(parts[1])
    flat = jnp.concatenate([jnp.concatenate(high, axis=1), jnp.concatenate(low, axis=1)], axis=0)
    fetch.wait()
    result = jnp.dot(flat, queries_ref[...], preferred_element_type=jnp.float32)
    result = result[:doc_count] + result[doc_count:]
    columns = result.shape[1] // shares
    fill = jnp.zeros((DOC_DEV, LANES - columns), jnp.float32)
    for owner in range(owners):
        for share in range(shares):
            piece = result[owner * DOC_DEV : (owner + 1) * DOC_DEV, share * columns : (share + 1) * columns]
            out_ref[owner * shares + share] = jnp.concatenate([piece, fill], axis=1)


def score(arrived, docs, queries, width, shares):
    sources = arrived.shape[0]
    doc_count = DOC_DEV * sources // shares
    return pl.pallas_call(
        functools.partial(score_kernel, width=width, doc_count=doc_count, shares=shares),
        in_specs=[VMEM, VMEM, HBM],
        out_shape=jax.ShapeDtypeStruct((sources, DOC_DEV, LANES), jnp.float32),
        scratch_shapes=[
            pltpu.VMEM((doc_count * width, arrived.shape[2]), jnp.float32),
            pltpu.VMEM(queries.shape, jnp.bfloat16),
            pltpu.SemaphoreType.DMA,
        ],
        compiler_params=pltpu.CompilerParams(vmem_limit_bytes=40 * MIB),
        cost_estimate=cost(5),
    )(arrived, docs, stay(queries))


def sum_kernel(pieces_ref, out_ref):
    total = pieces_ref[0]
    for source in range(1, pieces_ref.shape[0]):
        total = total + pieces_ref[source]
    out_ref[...] = total[:, : out_ref.shape[1]]


def sum_pieces(pieces, columns):
    return pl.pallas_call(
        sum_kernel,
        in_specs=[VMEM],
        out_shape=jax.ShapeDtypeStruct((pieces.shape[1], columns), jnp.float32),
    )(pieces)


def exchange(block, axis, size, turn):
    return lax.ppermute(block, axis, [(i, i ^ turn) for i in range(size)])


def double(blocks, turns, axis, size, turn):
    blocks = jnp.concatenate([blocks, exchange(blocks, axis, size, turn)], axis=0)
    return blocks, turns + tuple(t ^ turn for t in turns)


def local(
    activations,
    grad_hidden,
    routes,
    doc_ids,
    query_grads,
    in_projection,
    out_projection,
    inverse_in,
    inverse_out,
):
    tokens, top = routes.shape
    experts, width, _ = inverse_in.shape
    owners = lax.axis_size("expert")
    shares = lax.axis_size("proj")
    quarter = tokens // shares
    assert quarter == LANES and 2 * width == LANES and experts * width // shares == LANES
    assert shares == 4 and owners & (owners - 1) == 0
    assert DOC_DEV * owners <= 256

    flat_hidden = grad_hidden.reshape(tokens * top, grad_hidden.shape[2])
    doc_rows = doc_ids.reshape(shares, quarter)
    leaving, own, shared = project(
        activations, flat_hidden, in_projection, out_projection, inverse_out, doc_rows, shares, top
    )
    near = exchange(leaving, "proj", shares, 1)
    first = exchange(shared, "expert", owners, owners // 2)
    shared, turns = jnp.stack([shared, first]), (0, owners // 2)
    for bit in reversed(range((owners // 2).bit_length() - 1)):
        shared, turns = double(shared, turns, "expert", owners, 1 << bit)
    far = exchange(combine(own, near, top // 2 * quarter), "proj", shares, 2)
    weights, all_docs = expand(shared, turns, width, experts, shares)
    quarter_routes = lax.dynamic_slice_in_dim(routes, lax.axis_index("proj") * quarter, quarter, 0)
    payload = condition(own, near, far, quarter_routes, weights, shares, width)
    payload, query_grads = lax.optimization_barrier((payload, query_grads))
    arrived = lax.all_to_all(payload, ("expert", "proj"), 0, 0, tiled=True)
    queries = condition_queries(query_grads, inverse_in)
    partial_scores = score(arrived, all_docs, queries, width, shares)
    pieces = lax.all_to_all(partial_scores, ("expert", "proj"), 0, 0, tiled=True)
    return sum_pieces(pieces, query_grads.shape[0] // shares).T


def solution(mesh):
    in_specs = (
        P(("groups", "expert"), "proj"),
        P(("groups", "expert"), None, "proj"),
        P(("groups", "expert"), None),
        P(("groups", "expert")),
        P(None, "expert", "proj"),
        P(None, "proj"),
        P(None, "proj"),
        P("expert", None, None),
        P("expert", None, None),
    )
    out_specs = P("proj", ("groups", "expert"))
    return jax.shard_map(local, mesh=mesh, in_specs=in_specs, out_specs=out_specs, check_vma=False)
```

```python
import functools

import jax
import jax.numpy as jnp
from jax import lax
from jax.experimental import pallas as pl
from jax.experimental.pallas import tpu as pltpu
from jax.sharding import PartitionSpec as P

DOC_DEV = 8
LANES = 128
DOC_ROWS = 16
MIB = 1024 * 1024
VMEM = pl.BlockSpec(memory_space=pltpu.VMEM)
HBM = pl.BlockSpec(memory_space=pltpu.HBM)


def low_lanes(rows, width):
    return lax.broadcasted_iota(jnp.int32, (rows, LANES), 1) < width


def stay(array):
    return pltpu.with_memory_space_constraint(array, pltpu.HBM)


def split(value):
    high = value.astype(jnp.bfloat16)
    return high, (value - high.astype(jnp.float32)).astype(jnp.bfloat16)


def cost(microseconds):
    return pl.CostEstimate(flops=0, bytes_accessed=int(microseconds * 3.3e6), transcendentals=0)


def pack_kernel(inverse_hbm, docs_hbm, shared_ref, inverse_ref, docs_ref, sems):
    copies = [
        pltpu.make_async_copy(inverse_hbm, inverse_ref, sems.at[0]),
        pltpu.make_async_copy(docs_hbm, docs_ref, sems.at[1]),
    ]
    for copy in copies:
        copy.start()
    for copy in copies:
        copy.wait()
    width = inverse_ref.shape[1]
    half = inverse_ref.shape[0] // 2
    for e in range(half):
        pair = jnp.concatenate([inverse_ref[e], inverse_ref[half + e]], axis=1)
        shared_ref[e * width : (e + 1) * width, :] = pair.astype(jnp.bfloat16)
    docs = docs_ref[...].astype(jnp.float32)
    docs = jnp.concatenate([docs, jnp.zeros((DOC_ROWS - docs.shape[0], LANES), jnp.float32)], axis=0)
    shared_ref[half * width :, :] = docs.astype(jnp.bfloat16)


def pack(inverse_out, doc_rows):
    experts, width, _ = inverse_out.shape
    return pl.pallas_call(
        pack_kernel,
        in_specs=[HBM, HBM],
        out_specs=VMEM,
        out_shape=jax.ShapeDtypeStruct((experts // 2 * width + DOC_ROWS, LANES), jnp.bfloat16),
        scratch_shapes=[
            pltpu.VMEM(inverse_out.shape, inverse_out.dtype),
            pltpu.VMEM(doc_rows.shape, doc_rows.dtype),
            pltpu.SemaphoreType.DMA((2,)),
        ],
        cost_estimate=cost(1),
    )(stay(inverse_out), stay(doc_rows))


def project_kernel(act_hbm, hidden_hbm, in_proj_hbm, out_proj_hbm, leaving_ref, own_ref, *refs, top):
    act_ref, hidden_ref, in_proj_ref, out_proj_ref, rows_ref, sems = refs
    turns = (1, 3, 2, 0)
    quarter = act_ref.shape[1]
    width = in_proj_ref.shape[0]
    half = quarter // 2
    place = lax.axis_index("proj")
    pairs = []
    for g, turn in enumerate(turns):
        start = jnp.bitwise_xor(place, turn) * quarter
        for part in range(2):
            rows = pl.ds(pl.multiple_of((start + part * half) * top, half * top), half * top)
            pairs.append((hidden_hbm.at[rows], hidden_ref.at[g, part]))
            if g == 0 and part == 0:
                pairs.append((out_proj_hbm, out_proj_ref))
        rows = pl.ds(pl.multiple_of(start, quarter), quarter)
        if g == 0:
            pairs.append((in_proj_hbm, in_proj_ref))
        pairs.append((act_hbm.at[rows], act_ref.at[g]))
    copies = [pltpu.make_async_copy(source, target, sems.at[i]) for i, (source, target) in enumerate(pairs)]
    ahead = 4
    for copy in copies[:ahead]:
        copy.start()
    arrived = 0

    def take():
        nonlocal arrived
        copies[arrived].wait()
        if arrived + ahead < len(copies):
            copies[arrived + ahead].start()
        arrived += 1

    first = low_lanes(half, width)
    for g in range(len(turns)):
        wire_ref = leaving_ref.at[g] if g < 2 else own_ref.at[g - 2]
        for part in range(2):
            take()
            if g == 0 and part == 0:
                take()
            twice = jnp.concatenate([out_proj_ref[...], out_proj_ref[...]], axis=0)
            rows_ref[part] = lax.dot_general(
                hidden_ref[g, part], twice, (((1,), (1,)), ((), ())), preferred_element_type=jnp.float32
            )
            for pair in range(top // 2):
                even = rows_ref[part, pl.ds(2 * pair, half, stride=top), :]
                odd = rows_ref[part, pl.ds(2 * pair + 1, half, stride=top), :]
                start = pair * quarter + part * half
                wire_ref[start : start + half, :] = jnp.where(first, even, odd).astype(jnp.bfloat16)
        if g == 0:
            take()
        take()
        twice_in = jnp.concatenate([in_proj_ref[...], in_proj_ref[...]], axis=0)
        inner = lax.dot_general(
            act_ref[g], twice_in, (((1,), (1,)), ((), ())), preferred_element_type=jnp.float32
        )
        high, low = split(jnp.where(first, inner[:half], inner[half:]))
        start = top // 2 * quarter
        wire_ref[start : start + half, :] = high
        wire_ref[start + half :, :] = low


def project(activations, flat_hidden, in_projection, out_projection, quarters, top):
    tokens, model = activations.shape
    quarter = tokens // quarters
    wire_rows = top // 2 * quarter + quarter
    wire = jax.ShapeDtypeStruct((quarters // 2, wire_rows, LANES), jnp.bfloat16)
    fixed = (in_projection, out_projection)
    return pl.pallas_call(
        functools.partial(project_kernel, top=top),
        in_specs=[HBM] * 4,
        out_specs=[VMEM] * 2,
        out_shape=[wire, wire],
        scratch_shapes=[
            pltpu.VMEM((quarters, quarter, model), jnp.bfloat16),
            pltpu.VMEM((quarters, 2, quarter // 2 * top, flat_hidden.shape[1]), jnp.bfloat16),
        ]
        + [pltpu.VMEM(array.shape, array.dtype) for array in fixed]
        + [
            pltpu.VMEM((2, quarter // 2 * top, LANES), jnp.float32),
            pltpu.SemaphoreType.DMA((3 * quarters + len(fixed),)),
        ],
        compiler_params=pltpu.CompilerParams(vmem_limit_bytes=40 * MIB),
        cost_estimate=cost(5),
    )(*[stay(array) for array in (activations, flat_hidden, *fixed)])


def combine_kernel(own_ref, other_ref, out_ref, *, value_rows):
    total = own_ref[0, :value_rows, :].astype(jnp.float32) + other_ref[1, :value_rows, :].astype(jnp.float32)
    out_ref[:value_rows, :] = total.astype(jnp.bfloat16)
    half = (out_ref.shape[0] - value_rows) // 2
    exact = jnp.zeros((half, LANES), jnp.float32)
    for part in (own_ref[0], other_ref[1]):
        exact = exact + part[value_rows : value_rows + half].astype(jnp.float32)
        exact = exact + part[value_rows + half :].astype(jnp.float32)
    high, low = split(exact)
    out_ref[value_rows : value_rows + half, :] = high
    out_ref[value_rows + half :, :] = low


def combine(own, other, value_rows):
    return pl.pallas_call(
        functools.partial(combine_kernel, value_rows=value_rows),
        in_specs=[VMEM, VMEM],
        out_shape=jax.ShapeDtypeStruct(own.shape[1:], jnp.bfloat16),
        compiler_params=pltpu.CompilerParams(vmem_limit_bytes=40 * MIB),
        cost_estimate=cost(1),
    )(own, other)


def expand_kernel(shared_ref, weights_ref, docs_ref, *, width, experts, shares, turns):
    columns = experts * width
    share_rows = width // shares
    half = experts // 2
    lane = lax.broadcasted_iota(jnp.int32, (LANES, columns), 1)
    row = lax.broadcasted_iota(jnp.int32, (LANES, columns), 0)
    source = lane // (experts * share_rows) * share_rows + lane % share_rows
    expert_lane = lax.broadcasted_iota(jnp.int32, (half * width, columns), 1) // share_rows % experts
    expert_row = lax.broadcasted_iota(jnp.int32, (half * width, columns), 0) // width
    for side in range(2):
        spread = (row == source + side * width).astype(jnp.float32).astype(jnp.bfloat16)
        own = expert_lane == expert_row + side * half
        for entry, turn in enumerate(turns):
            placed = jnp.dot(
                shared_ref[entry, : half * width, :], spread, preferred_element_type=jnp.float32
            )
            weights_ref[turn, side * half * width : (side + 1) * half * width, :] = jnp.where(
                own, placed, 0.0
            ).astype(jnp.bfloat16)
    for entry, turn in enumerate(turns):
        owner = jnp.bitwise_xor(lax.axis_index("expert"), turn)
        docs_ref[owner] = shared_ref[entry, half * width :, :].astype(jnp.float32).astype(jnp.int32)


def expand(shared, turns, width, experts, shares):
    owners = shared.shape[0]
    return pl.pallas_call(
        functools.partial(expand_kernel, width=width, experts=experts, shares=shares, turns=turns),
        in_specs=[VMEM],
        out_shape=[
            jax.ShapeDtypeStruct((owners, experts * width, experts * width), jnp.bfloat16),
            jax.ShapeDtypeStruct((owners, DOC_ROWS, LANES), jnp.int32),
        ],
        compiler_params=pltpu.CompilerParams(vmem_limit_bytes=40 * MIB),
        cost_estimate=cost(1.3),
    )(shared)


def condition_kernel(
    own_ref, near_ref, far_ref, routes_ref, weights_ref, payload_ref, value_ref, name_ref, *, top, width
):
    quarter = routes_ref.shape[0]
    groups, dense_width, _ = weights_ref.shape
    shares = payload_ref.shape[0] // groups
    experts = dense_width // width
    first = low_lanes(quarter, width)
    second = 1 - first.astype(jnp.int32)

    def summed(start, size):
        rows = slice(start, start + size)
        total = own_ref[1, rows, :].astype(jnp.float32) + near_ref[0, rows, :].astype(jnp.float32)
        return total + far_ref[rows, :].astype(jnp.float32)

    for pair in range(top // 2):
        both = summed(pair * quarter, quarter)
        swapped = pltpu.roll(both, width, 1)
        value_ref[2 * pair] = jnp.where(first, both, swapped)
        value_ref[2 * pair + 1] = jnp.where(first, swapped, both)
    for k in range(top):
        name_ref[k] = jnp.broadcast_to(routes_ref[:, k : k + 1], (quarter, LANES)) - second
    half = quarter // 2
    inner = summed(top // 2 * quarter, half) + summed(top // 2 * quarter + half, half)
    inner = jnp.concatenate([inner[:, :width], inner[:, width:]], axis=0)
    inner = jnp.transpose(inner).astype(jnp.bfloat16)

    def one_group(step, carry):
        group = jnp.bitwise_xor(lax.axis_index("expert"), step)
        dense = []
        for pair in range(experts // 2):
            base = group * experts + 2 * pair
            chosen = jnp.zeros((quarter, LANES), jnp.float32)
            for k in range(top):
                chosen = jnp.where(name_ref[k] == base, value_ref[k], chosen)
            dense.append(chosen.astype(jnp.bfloat16))
        result = jnp.dot(
            jnp.concatenate(dense, axis=1), weights_ref[step], preferred_element_type=jnp.float32
        ).astype(jnp.bfloat16)
        share_width = result.shape[1] // shares
        for share in range(shares):
            piece = result[:, share * share_width : (share + 1) * share_width]
            payload_ref[group * shares + share, :quarter, :] = piece
            payload_ref[group * shares + share, quarter:, :] = inner
        return carry

    lax.fori_loop(0, groups, one_group, 0, unroll=groups <= 4)


def condition(own, near, far, quarter_routes, weights, shares, width):
    quarter, top = quarter_routes.shape
    groups = weights.shape[0]
    return pl.pallas_call(
        functools.partial(condition_kernel, top=top, width=width),
        in_specs=[VMEM] * 5,
        out_shape=jax.ShapeDtypeStruct((groups * shares, quarter + width, LANES), jnp.bfloat16),
        scratch_shapes=[
            pltpu.VMEM((top, quarter, LANES), jnp.float32),
            pltpu.VMEM((top, quarter, LANES), jnp.int32),
        ],
        compiler_params=pltpu.CompilerParams(vmem_limit_bytes=40 * MIB),
        cost_estimate=cost(2),
    )(own, near, far, quarter_routes, weights)


def query_kernel(query_ref, inverse_ref, out_ref, factor_ref, spread_ref, wide_ref):
    count, experts, _ = query_ref.shape
    width = inverse_ref.shape[1]
    step = pl.program_id(0)
    rows = out_ref.shape[0] // width

    @pl.when(step == 0)
    def _():
        zeros = jnp.zeros((width, width), jnp.bfloat16)
        for e in range(experts):
            high, low = split(inverse_ref[e])
            upper = jnp.concatenate([high, zeros, low, zeros], axis=1)
            lower = jnp.concatenate([zeros, high, zeros, low], axis=1)
            factor_ref[e] = jnp.concatenate([upper, lower], axis=0)

    spread_ref[...] = query_ref[...].astype(jnp.float32).reshape(count * experts, LANES)
    for e in range(experts):
        query = spread_ref[pl.ds(e, count, stride=experts), :].astype(jnp.bfloat16)
        result = lax.dot_general(
            factor_ref[e],
            jnp.concatenate([query, query], axis=1),
            (((1,), (1,)), ((), ())),
            preferred_element_type=jnp.float32,
        )
        start = e * (rows // experts) + 2 * step
        for tile in range(wide_ref.shape[0]):
            part = result[:, tile * LANES : (tile + 1) * LANES]
            wide_ref[tile, pl.ds(start, width, stride=rows), :] = part[:width]
            wide_ref[tile, pl.ds(start + 1, width, stride=rows), :] = part[width:]

    @pl.when(step == pl.num_programs(0) - 1)
    def _():
        for tile in range(wide_ref.shape[0]):
            out_ref[:, tile * LANES : (tile + 1) * LANES] = wide_ref[tile].astype(jnp.bfloat16)


def condition_queries(query_grads, inverse_in):
    count, experts, flat = query_grads.shape
    width = inverse_in.shape[1]
    rows = experts * flat
    return pl.pallas_call(
        query_kernel,
        grid=(flat // LANES,),
        in_specs=[
            pl.BlockSpec((count, experts, LANES), lambda c: (0, 0, c)),
            pl.BlockSpec(inverse_in.shape, lambda c: (0, 0, 0)),
        ],
        out_specs=pl.BlockSpec((rows, count), lambda c: (0, 0)),
        out_shape=jax.ShapeDtypeStruct((rows, count), jnp.bfloat16),
        scratch_shapes=[
            pltpu.VMEM((experts, 2 * width, 4 * width), jnp.bfloat16),
            pltpu.VMEM((count * experts, LANES), jnp.float32),
            pltpu.VMEM((count // LANES, rows, LANES), jnp.float32),
        ],
        compiler_params=pltpu.CompilerParams(vmem_limit_bytes=40 * MIB),
        cost_estimate=cost(10),
    )(stay(query_grads), inverse_in)


def score_kernel(arrived_ref, docs_ref, far_ref, out_ref, grads_ref, queries_ref, sem, *, width, doc_count, shares):
    fetch = pltpu.make_async_copy(far_ref, queries_ref, sem)
    fetch.start()
    sources, rows, lanes = arrived_ref.shape
    owners = sources // shares
    quarter = rows - width
    outer = arrived_ref[:, :quarter, :].reshape(sources * quarter, lanes)
    inner = jnp.concatenate([arrived_ref[s, quarter:, :] for s in range(sources)], axis=1)
    docs = [docs_ref[s // shares, s % shares : s % shares + 1, :] for s in range(sources)]
    docs = jnp.broadcast_to(jnp.concatenate(docs, axis=1), inner.shape)
    doc_group = 8

    def one_group(group, carry):
        masked = [
            jnp.where(docs == group * doc_group + d, inner, jnp.zeros_like(inner)) for d in range(doc_group)
        ]
        start = pl.multiple_of(group * doc_group * width, doc_group * width)
        grads_ref[pl.ds(start, doc_group * width), :] = jnp.dot(
            jnp.concatenate(masked, axis=0), outer, preferred_element_type=jnp.float32
        )
        return carry

    lax.fori_loop(0, doc_count // doc_group, one_group, 0, unroll=doc_count <= 32)
    high, low = [], []
    for j in range(width):
        parts = split(grads_ref[pl.ds(j, doc_count, stride=width), :])
        high.append(parts[0])
        low.append(parts[1])
    flat = jnp.concatenate([jnp.concatenate(high, axis=1), jnp.concatenate(low, axis=1)], axis=0)
    fetch.wait()
    result = jnp.dot(flat, queries_ref[...], preferred_element_type=jnp.float32)
    result = result[:doc_count] + result[doc_count:]
    columns = result.shape[1] // shares
    fill = jnp.zeros((DOC_DEV, LANES - columns), jnp.float32)
    for owner in range(owners):
        for share in range(shares):
            piece = result[owner * DOC_DEV : (owner + 1) * DOC_DEV, share * columns : (share + 1) * columns]
            share_turn = jnp.bitwise_xor(lax.axis_index("proj"), share)
            owner_turn = jnp.bitwise_xor(lax.axis_index("expert"), owner)
            out_ref[share_turn, owner_turn] = jnp.concatenate([piece, fill], axis=1)


def score(arrived, docs, queries, width, shares):
    sources = arrived.shape[0]
    doc_count = DOC_DEV * sources // shares
    return pl.pallas_call(
        functools.partial(score_kernel, width=width, doc_count=doc_count, shares=shares),
        in_specs=[VMEM, VMEM, HBM],
        out_shape=jax.ShapeDtypeStruct((shares, sources // shares, DOC_DEV, LANES), jnp.float32),
        scratch_shapes=[
            pltpu.VMEM((doc_count * width, arrived.shape[2]), jnp.float32),
            pltpu.VMEM(queries.shape, jnp.bfloat16),
            pltpu.SemaphoreType.DMA,
        ],
        compiler_params=pltpu.CompilerParams(vmem_limit_bytes=40 * MIB),
        cost_estimate=cost(5),
    )(arrived, docs, stay(queries))


def exchange(block, axis, size, turn):
    return lax.ppermute(block, axis, [(i, i ^ turn) for i in range(size)])


def double(blocks, turns, axis, size, turn):
    blocks = jnp.concatenate([blocks, exchange(blocks, axis, size, turn)], axis=0)
    return blocks, turns + tuple(t ^ turn for t in turns)


def local(
    activations,
    grad_hidden,
    routes,
    doc_ids,
    query_grads,
    in_projection,
    out_projection,
    inverse_in,
    inverse_out,
):
    tokens, top = routes.shape
    experts, width, _ = inverse_in.shape
    owners = lax.axis_size("expert")
    shares = lax.axis_size("proj")
    quarter = tokens // shares
    assert quarter == LANES and 2 * width == LANES and experts * width // shares == LANES
    assert shares == 4 and owners & (owners - 1) == 0
    assert DOC_DEV * owners <= 256

    flat_hidden = grad_hidden.reshape(tokens * top, grad_hidden.shape[2])
    doc_rows = doc_ids.reshape(shares, quarter)
    shared = pack(inverse_out, doc_rows)
    first = exchange(shared, "expert", owners, owners // 2)
    shared, activations = lax.optimization_barrier((shared, activations))
    leaving, own = project(activations, flat_hidden, in_projection, out_projection, shares, top)
    first, leaving = lax.optimization_barrier((first, leaving))
    near = exchange(leaving, "proj", shares, 1)
    shared, turns = jnp.stack([shared, first]), (0, owners // 2)
    for bit in reversed(range((owners // 2).bit_length() - 1)):
        shared, turns = double(shared, turns, "expert", owners, 1 << bit)
    far = exchange(combine(own, near, top // 2 * quarter), "proj", shares, 2)
    weights, all_docs = expand(shared, turns, width, experts, shares)
    quarter_routes = lax.dynamic_slice_in_dim(routes, lax.axis_index("proj") * quarter, quarter, 0)
    payload = condition(own, near, far, quarter_routes, weights, shares, width)
    payload, query_grads = lax.optimization_barrier((payload, query_grads))
    arrived = lax.all_to_all(payload, ("expert", "proj"), 0, 0, tiled=True)
    queries = condition_queries(query_grads, inverse_in)
    pieces = score(arrived, all_docs, queries, width, shares)
    leaving, staying = pieces[1::2], pieces[0::2]
    pieces = staying + exchange(leaving, "proj", shares, 1)
    pieces = pieces[0] + exchange(pieces[1], "proj", shares, 2)
    turn = owners // 2
    while turn:
        pieces = pieces[:turn] + exchange(pieces[turn:], "expert", owners, turn)
        turn //= 2
    return pieces[0, :, : query_grads.shape[0] // shares].T


def solution(mesh):
    in_specs = (
        P(("groups", "expert"), "proj"),
        P(("groups", "expert"), None, "proj"),
        P(("groups", "expert"), None),
        P(("groups", "expert")),
        P(None, "expert", "proj"),
        P(None, "proj"),
        P(None, "proj"),
        P("expert", None, None),
        P("expert", None, None),
    )
    out_specs = P("proj", ("groups", "expert"))
    return jax.shard_map(local, mesh=mesh, in_specs=in_specs, out_specs=out_specs, check_vma=False)
```

```python
import functools

import jax
import jax.numpy as jnp
from jax import lax
from jax.experimental import pallas as pl
from jax.experimental.pallas import tpu as pltpu
from jax.sharding import PartitionSpec as P

DOC_DEV = 8
LANES = 128
DOC_ROWS = 16
MIB = 1024 * 1024
VMEM = pl.BlockSpec(memory_space=pltpu.VMEM)
HBM = pl.BlockSpec(memory_space=pltpu.HBM)


def low_lanes(rows, width):
    return lax.broadcasted_iota(jnp.int32, (rows, LANES), 1) < width


def stay(array):
    return pltpu.with_memory_space_constraint(array, pltpu.HBM)


def split(value):
    high = value.astype(jnp.bfloat16)
    return high, (value - high.astype(jnp.float32)).astype(jnp.bfloat16)


def cost(microseconds):
    return pl.CostEstimate(flops=0, bytes_accessed=int(microseconds * 3.3e6), transcendentals=0)


def in_order(copies, ahead):
    for copy in copies[:ahead]:
        copy.start()
    state = [0]

    def take():
        copies[state[0]].wait()
        if state[0] + ahead < len(copies):
            copies[state[0] + ahead].start()
        state[0] += 1

    return take


def inner_kernel(
    act_hbm, in_proj_hbm, inverse_hbm, docs_hbm, leaving_ref, own_ref, shared_ref, act_ref, in_proj_ref, inverse_ref, docs_ref, sems
):
    turns = (1, 3, 2, 0)
    quarter = act_ref.shape[1]
    width = in_proj_ref.shape[0]
    half = quarter // 2
    place = lax.axis_index("proj")
    pairs = [(in_proj_hbm, in_proj_ref)]
    for g, turn in enumerate(turns):
        rows = pl.ds(pl.multiple_of(jnp.bitwise_xor(place, turn) * quarter, quarter), quarter)
        pairs.append((act_hbm.at[rows], act_ref.at[g]))
        if g == 0:
            pairs += [(inverse_hbm, inverse_ref), (docs_hbm, docs_ref)]
    take = in_order([pltpu.make_async_copy(*pair, sems.at[i]) for i, pair in enumerate(pairs)], 5)
    take()
    first = low_lanes(half, width)
    for g in range(len(turns)):
        wire_ref = leaving_ref.at[g] if g < 2 else own_ref.at[g - 2]
        take()
        if g == 0:
            take()
            take()
            experts = inverse_ref.shape[0] // 2
            for e in range(experts):
                pair = jnp.concatenate([inverse_ref[e], inverse_ref[experts + e]], axis=1)
                shared_ref[e * width : (e + 1) * width, :] = pair.astype(jnp.bfloat16)
            docs = docs_ref[...].astype(jnp.float32)
            docs = jnp.concatenate([docs, jnp.zeros((DOC_ROWS - docs.shape[0], LANES), jnp.float32)], axis=0)
            shared_ref[experts * width :, :] = docs.astype(jnp.bfloat16)
        twice = jnp.concatenate([in_proj_ref[...], in_proj_ref[...]], axis=0)
        inner = lax.dot_general(
            act_ref[g], twice, (((1,), (1,)), ((), ())), preferred_element_type=jnp.float32
        )
        high, low = split(jnp.where(first, inner[:half], inner[half:]))
        wire_ref[:half, :] = high
        wire_ref[half:, :] = low


def project_inner(activations, in_projection, inverse_out, doc_rows, quarters):
    tokens, model = activations.shape
    quarter = tokens // quarters
    experts, width, _ = inverse_out.shape
    wire = jax.ShapeDtypeStruct((quarters // 2, quarter, LANES), jnp.bfloat16)
    fixed = (in_projection, inverse_out, doc_rows)
    return pl.pallas_call(
        inner_kernel,
        in_specs=[HBM] * 4,
        out_specs=[VMEM] * 3,
        out_shape=[wire, wire, jax.ShapeDtypeStruct((experts // 2 * width + DOC_ROWS, LANES), jnp.bfloat16)],
        scratch_shapes=[pltpu.VMEM((quarters, quarter, model), jnp.bfloat16)]
        + [pltpu.VMEM(array.shape, array.dtype) for array in fixed]
        + [pltpu.SemaphoreType.DMA((quarters + len(fixed),))],
        compiler_params=pltpu.CompilerParams(vmem_limit_bytes=40 * MIB),
        cost_estimate=cost(2.5),
    )(*[stay(array) for array in (activations, *fixed)])


def outer_kernel(hidden_hbm, out_proj_hbm, leaving_ref, own_ref, hidden_ref, out_proj_ref, rows_ref, sems, *, top):
    turns = (1, 3, 2, 0)
    chunks, chunk_rows, _ = hidden_ref.shape
    chunk = chunk_rows // top
    split_by = chunks // len(turns)
    quarter = chunk * split_by
    width = out_proj_ref.shape[0]
    place = lax.axis_index("proj")
    pairs = [(out_proj_hbm, out_proj_ref)]
    for i in range(chunks):
        start = (jnp.bitwise_xor(place, turns[i // split_by]) * split_by + i % split_by) * chunk_rows
        pairs.append((hidden_hbm.at[pl.ds(pl.multiple_of(start, chunk_rows), chunk_rows)], hidden_ref.at[i]))
    take = in_order([pltpu.make_async_copy(*pair, sems.at[i]) for i, pair in enumerate(pairs)], 4)
    take()
    first = low_lanes(chunk, width)

    def pack_rows(i):
        g, part = i // split_by, i % split_by
        wire_ref = leaving_ref.at[g] if g < 2 else own_ref.at[g - 2]
        for pair in range(top // 2):
            even = rows_ref[i % 2, pl.ds(2 * pair, chunk, stride=top), :]
            odd = rows_ref[i % 2, pl.ds(2 * pair + 1, chunk, stride=top), :]
            start = pair * quarter + part * chunk
            wire_ref[start : start + chunk, :] = jnp.where(first, even, odd).astype(jnp.bfloat16)

    for i in range(chunks):
        take()
        twice = jnp.concatenate([out_proj_ref[...], out_proj_ref[...]], axis=0)
        rows_ref[i % 2] = lax.dot_general(
            hidden_ref[i], twice, (((1,), (1,)), ((), ())), preferred_element_type=jnp.float32
        )
        if i:
            pack_rows(i - 1)
    pack_rows(chunks - 1)


def project_outer(flat_hidden, out_projection, quarters, top):
    rows, hidden = flat_hidden.shape
    chunks = 2 * quarters
    wire = jax.ShapeDtypeStruct((quarters // 2, rows // quarters // 2, LANES), jnp.bfloat16)
    return pl.pallas_call(
        functools.partial(outer_kernel, top=top),
        in_specs=[HBM] * 2,
        out_specs=[VMEM] * 2,
        out_shape=[wire, wire],
        scratch_shapes=[
            pltpu.VMEM((chunks, rows // chunks, hidden), jnp.bfloat16),
            pltpu.VMEM(out_projection.shape, out_projection.dtype),
            pltpu.VMEM((2, rows // chunks, LANES), jnp.float32),
            pltpu.SemaphoreType.DMA((chunks + 1,)),
        ],
        compiler_params=pltpu.CompilerParams(vmem_limit_bytes=40 * MIB),
        cost_estimate=cost(4),
    )(stay(flat_hidden), stay(out_projection))


def exact_rows(rows):
    half = rows.shape[0] // 2
    return rows[:half].astype(jnp.float32) + rows[half:].astype(jnp.float32)


def combine_inner_kernel(own_ref, near_ref, out_ref):
    high, low = split(exact_rows(own_ref[0]) + exact_rows(near_ref[1]))
    out_ref[: high.shape[0], :] = high
    out_ref[high.shape[0] :, :] = low


def combine_outer_kernel(own_ref, near_ref, out_ref):
    out_ref[...] = (own_ref[0].astype(jnp.float32) + near_ref[1].astype(jnp.float32)).astype(jnp.bfloat16)


def combine(kernel, own, near):
    return pl.pallas_call(
        kernel,
        in_specs=[VMEM, VMEM],
        out_shape=jax.ShapeDtypeStruct(own.shape[1:], jnp.bfloat16),
        compiler_params=pltpu.CompilerParams(vmem_limit_bytes=40 * MIB),
        cost_estimate=cost(0.5),
    )(own, near)


def finish_inner_kernel(own_ref, near_ref, far_ref, out_ref):
    total = exact_rows(own_ref[1]) + exact_rows(near_ref[0]) + exact_rows(far_ref[...])
    width = out_ref.shape[0]
    total = jnp.concatenate([total[:, :width], total[:, width:]], axis=0)
    out_ref[...] = jnp.transpose(total).astype(jnp.bfloat16)


def finish_inner(own, near, far, width):
    return pl.pallas_call(
        finish_inner_kernel,
        in_specs=[VMEM] * 3,
        out_shape=jax.ShapeDtypeStruct((width, own.shape[1]), jnp.bfloat16),
        cost_estimate=cost(0.5),
    )(own, near, far)


def expand_kernel(shared_ref, weights_ref, docs_ref, *, width, experts, shares, turns):
    columns = experts * width
    share_rows = width // shares
    half = experts // 2
    lane = lax.broadcasted_iota(jnp.int32, (LANES, columns), 1)
    row = lax.broadcasted_iota(jnp.int32, (LANES, columns), 0)
    source = lane // (experts * share_rows) * share_rows + lane % share_rows
    expert_lane = lax.broadcasted_iota(jnp.int32, (half * width, columns), 1) // share_rows % experts
    expert_row = lax.broadcasted_iota(jnp.int32, (half * width, columns), 0) // width
    for side in range(2):
        spread = (row == source + side * width).astype(jnp.float32).astype(jnp.bfloat16)
        own = expert_lane == expert_row + side * half
        for entry, turn in enumerate(turns):
            placed = jnp.dot(
                shared_ref[entry, : half * width, :], spread, preferred_element_type=jnp.float32
            )
            weights_ref[turn, side * half * width : (side + 1) * half * width, :] = jnp.where(
                own, placed, 0.0
            ).astype(jnp.bfloat16)
    for entry, turn in enumerate(turns):
        owner = jnp.bitwise_xor(lax.axis_index("expert"), turn)
        docs_ref[owner] = shared_ref[entry, half * width :, :].astype(jnp.float32).astype(jnp.int32)


def expand(shared, turns, width, experts, shares):
    owners = shared.shape[0]
    return pl.pallas_call(
        functools.partial(expand_kernel, width=width, experts=experts, shares=shares, turns=turns),
        in_specs=[VMEM],
        out_shape=[
            jax.ShapeDtypeStruct((owners, experts * width, experts * width), jnp.bfloat16),
            jax.ShapeDtypeStruct((owners, DOC_ROWS, LANES), jnp.int32),
        ],
        compiler_params=pltpu.CompilerParams(vmem_limit_bytes=40 * MIB),
        cost_estimate=cost(1.3),
    )(shared)


def condition_kernel(
    own_ref, near_ref, far_ref, routes_ref, weights_ref, payload_ref, value_ref, name_ref, *, top, width
):
    quarter = routes_ref.shape[0]
    groups, dense_width, _ = weights_ref.shape
    shares = payload_ref.shape[0] // groups
    experts = dense_width // width
    first = low_lanes(quarter, width)
    second = 1 - first.astype(jnp.int32)

    def summed(start, size):
        rows = slice(start, start + size)
        total = own_ref[1, rows, :].astype(jnp.float32) + near_ref[0, rows, :].astype(jnp.float32)
        return total + far_ref[rows, :].astype(jnp.float32)

    for pair in range(top // 2):
        both = summed(pair * quarter, quarter)
        swapped = pltpu.roll(both, width, 1)
        value_ref[2 * pair] = jnp.where(first, both, swapped)
        value_ref[2 * pair + 1] = jnp.where(first, swapped, both)
    for k in range(top):
        name_ref[k] = jnp.broadcast_to(routes_ref[:, k : k + 1], (quarter, LANES)) - second
    def one_group(step, carry):
        group = jnp.bitwise_xor(lax.axis_index("expert"), step)
        dense = []
        for pair in range(experts // 2):
            base = group * experts + 2 * pair
            chosen = jnp.zeros((quarter, LANES), jnp.float32)
            for k in range(top):
                chosen = jnp.where(name_ref[k] == base, value_ref[k], chosen)
            dense.append(chosen.astype(jnp.bfloat16))
        result = jnp.dot(
            jnp.concatenate(dense, axis=1), weights_ref[step], preferred_element_type=jnp.float32
        ).astype(jnp.bfloat16)
        share_width = result.shape[1] // shares
        for share in range(shares):
            payload_ref[group * shares + share] = result[:, share * share_width : (share + 1) * share_width]
        return carry

    lax.fori_loop(0, groups, one_group, 0, unroll=groups <= 4)


def condition(own, near, far, quarter_routes, weights, shares, width):
    quarter, top = quarter_routes.shape
    groups = weights.shape[0]
    return pl.pallas_call(
        functools.partial(condition_kernel, top=top, width=width),
        in_specs=[VMEM] * 5,
        out_shape=jax.ShapeDtypeStruct((groups * shares, quarter, LANES), jnp.bfloat16),
        scratch_shapes=[
            pltpu.VMEM((top, quarter, LANES), jnp.float32),
            pltpu.VMEM((top, quarter, LANES), jnp.int32),
        ],
        compiler_params=pltpu.CompilerParams(vmem_limit_bytes=40 * MIB),
        cost_estimate=cost(2),
    )(own, near, far, quarter_routes, weights)


def query_kernel(query_ref, inverse_ref, out_ref, factor_ref, spread_ref, wide_ref):
    count, experts, _ = query_ref.shape
    width = inverse_ref.shape[1]
    step = pl.program_id(0)
    rows = out_ref.shape[0] // width

    @pl.when(step == 0)
    def _():
        zeros = jnp.zeros((width, width), jnp.bfloat16)
        for e in range(experts):
            high, low = split(inverse_ref[e])
            upper = jnp.concatenate([high, zeros, low, zeros], axis=1)
            lower = jnp.concatenate([zeros, high, zeros, low], axis=1)
            factor_ref[e] = jnp.concatenate([upper, lower], axis=0)

    spread_ref[...] = query_ref[...].astype(jnp.float32).reshape(count * experts, LANES)
    for e in range(experts):
        query = spread_ref[pl.ds(e, count, stride=experts), :].astype(jnp.bfloat16)
        result = lax.dot_general(
            factor_ref[e],
            jnp.concatenate([query, query], axis=1),
            (((1,), (1,)), ((), ())),
            preferred_element_type=jnp.float32,
        )
        start = e * (rows // experts) + 2 * step
        for tile in range(wide_ref.shape[0]):
            part = result[:, tile * LANES : (tile + 1) * LANES]
            wide_ref[tile, pl.ds(start, width, stride=rows), :] = part[:width]
            wide_ref[tile, pl.ds(start + 1, width, stride=rows), :] = part[width:]

    @pl.when(step == pl.num_programs(0) - 1)
    def _():
        for tile in range(wide_ref.shape[0]):
            out_ref[:, tile * LANES : (tile + 1) * LANES] = wide_ref[tile].astype(jnp.bfloat16)


def condition_queries(query_grads, inverse_in):
    count, experts, flat = query_grads.shape
    width = inverse_in.shape[1]
    rows = experts * flat
    return pl.pallas_call(
        query_kernel,
        grid=(flat // LANES,),
        in_specs=[
            pl.BlockSpec((count, experts, LANES), lambda c: (0, 0, c)),
            pl.BlockSpec(inverse_in.shape, lambda c: (0, 0, 0)),
        ],
        out_specs=pl.BlockSpec((rows, count), lambda c: (0, 0)),
        out_shape=jax.ShapeDtypeStruct((rows, count), jnp.bfloat16),
        scratch_shapes=[
            pltpu.VMEM((experts, 2 * width, 4 * width), jnp.bfloat16),
            pltpu.VMEM((count * experts, LANES), jnp.float32),
            pltpu.VMEM((count // LANES, rows, LANES), jnp.float32),
        ],
        compiler_params=pltpu.CompilerParams(vmem_limit_bytes=40 * MIB),
        cost_estimate=cost(10),
    )(stay(query_grads), inverse_in)


def score_kernel(
    arrived_ref, inner_ref, docs_ref, far_ref, out_ref, grads_ref, queries_ref, sem, *, width, doc_count, turns
):
    fetch = pltpu.make_async_copy(far_ref, queries_ref, sem)
    fetch.start()
    sources, quarter, lanes = arrived_ref.shape
    shares = lax.axis_size("proj")
    owners = sources // shares
    outer, inner, docs = [], [], []
    for entry, (owner_turn, share_turn) in enumerate(turns):
        owner = jnp.bitwise_xor(lax.axis_index("expert"), owner_turn)
        share = jnp.bitwise_xor(lax.axis_index("proj"), share_turn)
        outer.append(arrived_ref[owner * shares + share])
        docs.append(docs_ref[owner, pl.ds(share, 1), :])
        inner.append(inner_ref[entry])
    outer = jnp.concatenate(outer, axis=0)
    inner = jnp.concatenate(inner, axis=1)
    docs = jnp.broadcast_to(jnp.concatenate(docs, axis=1), inner.shape)
    doc_group = 8

    def one_group(group, carry):
        masked = [
            jnp.where(docs == group * doc_group + d, inner, jnp.zeros_like(inner)) for d in range(doc_group)
        ]
        start = pl.multiple_of(group * doc_group * width, doc_group * width)
        grads_ref[pl.ds(start, doc_group * width), :] = jnp.dot(
            jnp.concatenate(masked, axis=0), outer, preferred_element_type=jnp.float32
        )
        return carry

    lax.fori_loop(0, doc_count // doc_group, one_group, 0, unroll=doc_count <= 32)
    high, low = [], []
    for j in range(width):
        parts = split(grads_ref[pl.ds(j, doc_count, stride=width), :])
        high.append(parts[0])
        low.append(parts[1])
    flat = jnp.concatenate([jnp.concatenate(high, axis=1), jnp.concatenate(low, axis=1)], axis=0)
    fetch.wait()
    result = jnp.dot(flat, queries_ref[...], preferred_element_type=jnp.float32)
    result = result[:doc_count] + result[doc_count:]
    columns = result.shape[1] // shares
    fill = jnp.zeros((DOC_DEV, LANES - columns), jnp.float32)
    for owner in range(owners):
        for share in range(shares):
            piece = result[owner * DOC_DEV : (owner + 1) * DOC_DEV, share * columns : (share + 1) * columns]
            out_ref[owner * shares + share] = jnp.concatenate([piece, fill], axis=1)


def score(arrived, inner, docs, queries, turns):
    sources = arrived.shape[0]
    width = inner.shape[1]
    doc_count = DOC_DEV * docs.shape[0]
    return pl.pallas_call(
        functools.partial(score_kernel, width=width, doc_count=doc_count, turns=turns),
        in_specs=[VMEM, VMEM, VMEM, HBM],
        out_shape=jax.ShapeDtypeStruct((sources, DOC_DEV, LANES), jnp.float32),
        scratch_shapes=[
            pltpu.VMEM((doc_count * width, arrived.shape[2]), jnp.float32),
            pltpu.VMEM(queries.shape, jnp.bfloat16),
            pltpu.SemaphoreType.DMA,
        ],
        compiler_params=pltpu.CompilerParams(vmem_limit_bytes=40 * MIB),
        cost_estimate=cost(5),
    )(arrived, inner, docs, stay(queries))


def sum_kernel(pieces_ref, out_ref):
    total = pieces_ref[0]
    for source in range(1, pieces_ref.shape[0]):
        total = total + pieces_ref[source]
    out_ref[...] = total[:, : out_ref.shape[1]]


def sum_pieces(pieces, columns):
    return pl.pallas_call(
        sum_kernel,
        in_specs=[VMEM],
        out_shape=jax.ShapeDtypeStruct((pieces.shape[1], columns), jnp.float32),
    )(pieces)


def exchange(block, axis, size, turn):
    return lax.ppermute(block, axis, [(i, i ^ turn) for i in range(size)])


def double(blocks, turns, axis, size, turn):
    blocks = jnp.concatenate([blocks, exchange(blocks, axis, size, turn)], axis=0)
    return blocks, turns + tuple(t ^ turn for t in turns)


def local(
    activations,
    grad_hidden,
    routes,
    doc_ids,
    query_grads,
    in_projection,
    out_projection,
    inverse_in,
    inverse_out,
):
    tokens, top = routes.shape
    experts, width, _ = inverse_in.shape
    owners = lax.axis_size("expert")
    shares = lax.axis_size("proj")
    quarter = tokens // shares
    assert quarter == LANES and 2 * width == LANES and experts * width // shares == LANES
    assert shares == 4 and owners & (owners - 1) == 0
    assert DOC_DEV * owners <= 256

    flat_hidden = grad_hidden.reshape(tokens * top, grad_hidden.shape[2])
    inner_leaving, inner_own, shared = project_inner(
        activations, in_projection, inverse_out, doc_ids.reshape(shares, quarter), shares
    )
    far_shared = exchange(shared, "expert", owners, owners // 2)
    inner_near = exchange(inner_leaving, "proj", shares, 1)
    inner_far = exchange(combine(combine_inner_kernel, inner_own, inner_near), "proj", shares, 2)
    leaving, own = project_outer(flat_hidden, out_projection, shares, top)
    far_shared, inner_far, leaving = lax.optimization_barrier((far_shared, inner_far, leaving))
    near = exchange(leaving, "proj", shares, 1)
    shared, turns = jnp.stack([shared, far_shared]), (0, owners // 2)
    for bit in reversed(range((owners // 2).bit_length() - 1)):
        shared, turns = double(shared, turns, "expert", owners, 1 << bit)
    sent = combine(combine_outer_kernel, own, near)
    far = exchange(sent, "proj", shares, 2)
    inner = finish_inner(inner_own, inner_near, inner_far, width)
    inner, _ = lax.optimization_barrier((inner, sent))
    inner, owner_turns = inner[None], (0,)
    for bit in reversed(range(owners.bit_length() - 1)):
        inner, owner_turns = double(inner, owner_turns, "expert", owners, 1 << bit)
    weights, all_docs = expand(shared, turns, width, experts, shares)
    quarter_routes = lax.dynamic_slice_in_dim(routes, lax.axis_index("proj") * quarter, quarter, 0)
    payload = condition(own, near, far, quarter_routes, weights, shares, width)
    payload, inner = lax.optimization_barrier((payload, inner))
    arrived = lax.all_to_all(payload, ("expert", "proj"), 0, 0, tiled=True)
    inner, share_turns = inner[None], (0,)
    inner, share_turns = double(inner, share_turns, "proj", shares, 1)
    inner, query_grads = lax.optimization_barrier((inner, query_grads))
    inner, share_turns = double(inner, share_turns, "proj", shares, 2)
    inner = inner.reshape(owners * shares, width, quarter)
    all_turns = tuple((o, p) for p in share_turns for o in owner_turns)
    queries = condition_queries(query_grads, inverse_in)
    pieces = score(arrived, inner, all_docs, queries, all_turns)
    pieces = lax.all_to_all(pieces, ("expert", "proj"), 0, 0, tiled=True)
    return sum_pieces(pieces, query_grads.shape[0] // shares).T


def solution(mesh):
    in_specs = (
        P(("groups", "expert"), "proj"),
        P(("groups", "expert"), None, "proj"),
        P(("groups", "expert"), None),
        P(("groups", "expert")),
        P(None, "expert", "proj"),
        P(None, "proj"),
        P(None, "proj"),
        P("expert", None, None),
        P("expert", None, None),
    )
    out_specs = P("proj", ("groups", "expert"))
    return jax.shard_map(local, mesh=mesh, in_specs=in_specs, out_specs=out_specs, check_vma=False)
```

```python
import functools

import jax
import jax.numpy as jnp
from jax import lax
from jax.experimental import pallas as pl
from jax.experimental.pallas import tpu as pltpu
from jax.sharding import PartitionSpec as P

DOC_DEV = 8
LANES = 128
DOC_ROWS = 16
MIB = 1024 * 1024
VMEM = pl.BlockSpec(memory_space=pltpu.VMEM)
HBM = pl.BlockSpec(memory_space=pltpu.HBM)


def low_lanes(rows, width):
    return lax.broadcasted_iota(jnp.int32, (rows, LANES), 1) < width


def stay(array):
    return pltpu.with_memory_space_constraint(array, pltpu.HBM)


def split(value):
    high = value.astype(jnp.bfloat16)
    return high, (value - high.astype(jnp.float32)).astype(jnp.bfloat16)


def cost(microseconds):
    return pl.CostEstimate(flops=0, bytes_accessed=int(microseconds * 3.3e6), transcendentals=0)


def in_order(copies, ahead):
    for copy in copies[:ahead]:
        copy.start()
    state = [0]

    def take():
        copies[state[0]].wait()
        if state[0] + ahead < len(copies):
            copies[state[0] + ahead].start()
        state[0] += 1

    return take


def inner_kernel(
    act_hbm, in_proj_hbm, inverse_hbm, docs_hbm, leaving_ref, own_ref, shared_ref, act_ref, in_proj_ref, inverse_ref, docs_ref, sems
):
    turns = (1, 3, 2, 0)
    quarter = act_ref.shape[1]
    width = in_proj_ref.shape[0]
    half = quarter // 2
    place = lax.axis_index("proj")
    pairs = [(in_proj_hbm, in_proj_ref)]
    for g, turn in enumerate(turns):
        rows = pl.ds(pl.multiple_of(jnp.bitwise_xor(place, turn) * quarter, quarter), quarter)
        pairs.append((act_hbm.at[rows], act_ref.at[g]))
        if g == 0:
            pairs += [(inverse_hbm, inverse_ref), (docs_hbm, docs_ref)]
    take = in_order([pltpu.make_async_copy(*pair, sems.at[i]) for i, pair in enumerate(pairs)], 5)
    take()
    first = low_lanes(half, width)
    for g in range(len(turns)):
        wire_ref = leaving_ref.at[g] if g < 2 else own_ref.at[g - 2]
        take()
        if g == 0:
            take()
            take()
            experts = inverse_ref.shape[0] // 2
            for e in range(experts):
                pair = jnp.concatenate([inverse_ref[e], inverse_ref[experts + e]], axis=1)
                shared_ref[e * width : (e + 1) * width, :] = pair.astype(jnp.bfloat16)
            docs = docs_ref[...].astype(jnp.float32)
            docs = jnp.concatenate([docs, jnp.zeros((DOC_ROWS - docs.shape[0], LANES), jnp.float32)], axis=0)
            shared_ref[experts * width :, :] = docs.astype(jnp.bfloat16)
        twice = jnp.concatenate([in_proj_ref[...], in_proj_ref[...]], axis=0)
        inner = lax.dot_general(
            act_ref[g], twice, (((1,), (1,)), ((), ())), preferred_element_type=jnp.float32
        )
        high, low = split(jnp.where(first, inner[:half], inner[half:]))
        wire_ref[:half, :] = high
        wire_ref[half:, :] = low


def project_inner(activations, in_projection, inverse_out, doc_rows, quarters):
    tokens, model = activations.shape
    quarter = tokens // quarters
    experts, width, _ = inverse_out.shape
    wire = jax.ShapeDtypeStruct((quarters // 2, quarter, LANES), jnp.bfloat16)
    fixed = (in_projection, inverse_out, doc_rows)
    return pl.pallas_call(
        inner_kernel,
        in_specs=[HBM] * 4,
        out_specs=[VMEM] * 3,
        out_shape=[wire, wire, jax.ShapeDtypeStruct((experts // 2 * width + DOC_ROWS, LANES), jnp.bfloat16)],
        scratch_shapes=[pltpu.VMEM((quarters, quarter, model), jnp.bfloat16)]
        + [pltpu.VMEM(array.shape, array.dtype) for array in fixed]
        + [pltpu.SemaphoreType.DMA((quarters + len(fixed),))],
        compiler_params=pltpu.CompilerParams(vmem_limit_bytes=40 * MIB),
        cost_estimate=cost(2.5),
    )(*[stay(array) for array in (activations, *fixed)])


def outer_kernel(hidden_hbm, out_proj_hbm, leaving_ref, own_ref, hidden_ref, out_proj_ref, rows_ref, sems, *, top):
    turns = (1, 3, 2, 0)
    chunks, chunk_rows, _ = hidden_ref.shape
    chunk = chunk_rows // top
    split_by = chunks // len(turns)
    quarter = chunk * split_by
    width = out_proj_ref.shape[0]
    place = lax.axis_index("proj")
    pairs = [(out_proj_hbm, out_proj_ref)]
    for i in range(chunks):
        start = (jnp.bitwise_xor(place, turns[i // split_by]) * split_by + i % split_by) * chunk_rows
        pairs.append((hidden_hbm.at[pl.ds(pl.multiple_of(start, chunk_rows), chunk_rows)], hidden_ref.at[i]))
    take = in_order([pltpu.make_async_copy(*pair, sems.at[i]) for i, pair in enumerate(pairs)], 4)
    take()
    first = low_lanes(chunk, width)

    def pack_rows(i):
        g, part = i // split_by, i % split_by
        wire_ref = leaving_ref.at[g] if g < 2 else own_ref.at[g - 2]
        for pair in range(top // 2):
            even = rows_ref[i % 2, pl.ds(2 * pair, chunk, stride=top), :]
            odd = rows_ref[i % 2, pl.ds(2 * pair + 1, chunk, stride=top), :]
            start = pair * quarter + part * chunk
            wire_ref[start : start + chunk, :] = jnp.where(first, even, odd).astype(jnp.bfloat16)

    for i in range(chunks):
        take()
        twice = jnp.concatenate([out_proj_ref[...], out_proj_ref[...]], axis=0)
        rows_ref[i % 2] = lax.dot_general(
            hidden_ref[i], twice, (((1,), (1,)), ((), ())), preferred_element_type=jnp.float32
        )
        if i:
            pack_rows(i - 1)
    pack_rows(chunks - 1)


def project_outer(flat_hidden, out_projection, quarters, top):
    rows, hidden = flat_hidden.shape
    chunks = 2 * quarters
    wire = jax.ShapeDtypeStruct((quarters // 2, rows // quarters // 2, LANES), jnp.bfloat16)
    return pl.pallas_call(
        functools.partial(outer_kernel, top=top),
        in_specs=[HBM] * 2,
        out_specs=[VMEM] * 2,
        out_shape=[wire, wire],
        scratch_shapes=[
            pltpu.VMEM((chunks, rows // chunks, hidden), jnp.bfloat16),
            pltpu.VMEM(out_projection.shape, out_projection.dtype),
            pltpu.VMEM((2, rows // chunks, LANES), jnp.float32),
            pltpu.SemaphoreType.DMA((chunks + 1,)),
        ],
        compiler_params=pltpu.CompilerParams(vmem_limit_bytes=40 * MIB),
        cost_estimate=cost(4),
    )(stay(flat_hidden), stay(out_projection))


def exact_rows(rows):
    half = rows.shape[0] // 2
    return rows[:half].astype(jnp.float32) + rows[half:].astype(jnp.float32)


def combine_inner_kernel(own_ref, near_ref, out_ref):
    high, low = split(exact_rows(own_ref[0]) + exact_rows(near_ref[1]))
    out_ref[: high.shape[0], :] = high
    out_ref[high.shape[0] :, :] = low


def combine_outer_kernel(own_ref, near_ref, out_ref):
    out_ref[...] = (own_ref[0].astype(jnp.float32) + near_ref[1].astype(jnp.float32)).astype(jnp.bfloat16)


def combine(kernel, own, near):
    return pl.pallas_call(
        kernel,
        in_specs=[VMEM, VMEM],
        out_shape=jax.ShapeDtypeStruct(own.shape[1:], jnp.bfloat16),
        compiler_params=pltpu.CompilerParams(vmem_limit_bytes=40 * MIB),
        cost_estimate=cost(0.5),
    )(own, near)


def finish_inner_kernel(own_ref, near_ref, far_ref, out_ref):
    total = exact_rows(own_ref[1]) + exact_rows(near_ref[0]) + exact_rows(far_ref[...])
    width = out_ref.shape[0]
    total = jnp.concatenate([total[:, :width], total[:, width:]], axis=0)
    out_ref[...] = jnp.transpose(total).astype(jnp.bfloat16)


def finish_inner(own, near, far, width):
    return pl.pallas_call(
        finish_inner_kernel,
        in_specs=[VMEM] * 3,
        out_shape=jax.ShapeDtypeStruct((width, own.shape[1]), jnp.bfloat16),
        compiler_params=pltpu.CompilerParams(vmem_limit_bytes=40 * MIB),
        cost_estimate=cost(0.5),
    )(own, near, far)


def expand_kernel(shared_ref, weights_ref, docs_ref, *, width, experts, shares, turns):
    columns = experts * width
    share_rows = width // shares
    half = experts // 2
    lane = lax.broadcasted_iota(jnp.int32, (LANES, columns), 1)
    row = lax.broadcasted_iota(jnp.int32, (LANES, columns), 0)
    source = lane // (experts * share_rows) * share_rows + lane % share_rows
    expert_lane = lax.broadcasted_iota(jnp.int32, (half * width, columns), 1) // share_rows % experts
    expert_row = lax.broadcasted_iota(jnp.int32, (half * width, columns), 0) // width
    for side in range(2):
        spread = (row == source + side * width).astype(jnp.float32).astype(jnp.bfloat16)
        own = expert_lane == expert_row + side * half
        for entry, turn in enumerate(turns):
            placed = jnp.dot(
                shared_ref[entry, : half * width, :], spread, preferred_element_type=jnp.float32
            )
            weights_ref[turn, side * half * width : (side + 1) * half * width, :] = jnp.where(
                own, placed, 0.0
            ).astype(jnp.bfloat16)
    for entry, turn in enumerate(turns):
        owner = jnp.bitwise_xor(lax.axis_index("expert"), turn)
        docs_ref[owner] = shared_ref[entry, half * width :, :].astype(jnp.float32).astype(jnp.int32)


def expand(shared, turns, width, experts, shares):
    owners = shared.shape[0]
    return pl.pallas_call(
        functools.partial(expand_kernel, width=width, experts=experts, shares=shares, turns=turns),
        in_specs=[VMEM],
        out_shape=[
            jax.ShapeDtypeStruct((owners, experts * width, experts * width), jnp.bfloat16),
            jax.ShapeDtypeStruct((owners, DOC_ROWS, LANES), jnp.int32),
        ],
        compiler_params=pltpu.CompilerParams(vmem_limit_bytes=40 * MIB),
        cost_estimate=cost(1.3),
    )(shared)


def condition_kernel(
    own_ref, near_ref, far_ref, routes_ref, weights_ref, payload_ref, value_ref, name_ref, *, top, width
):
    quarter = routes_ref.shape[0]
    groups, dense_width, _ = weights_ref.shape
    shares = payload_ref.shape[0] // groups
    experts = dense_width // width
    first = low_lanes(quarter, width)
    second = 1 - first.astype(jnp.int32)

    def summed(start, size):
        rows = slice(start, start + size)
        total = own_ref[1, rows, :].astype(jnp.float32) + near_ref[0, rows, :].astype(jnp.float32)
        return total + far_ref[rows, :].astype(jnp.float32)

    for pair in range(top // 2):
        both = summed(pair * quarter, quarter)
        swapped = pltpu.roll(both, width, 1)
        value_ref[2 * pair] = jnp.where(first, both, swapped)
        value_ref[2 * pair + 1] = jnp.where(first, swapped, both)
    for k in range(top):
        name_ref[k] = jnp.broadcast_to(routes_ref[:, k : k + 1], (quarter, LANES)) - second
    def one_group(step, carry):
        group = jnp.bitwise_xor(lax.axis_index("expert"), step)
        dense = []
        for pair in range(experts // 2):
            base = group * experts + 2 * pair
            chosen = jnp.zeros((quarter, LANES), jnp.float32)
            for k in range(top):
                chosen = jnp.where(name_ref[k] == base, value_ref[k], chosen)
            dense.append(chosen.astype(jnp.bfloat16))
        result = jnp.dot(
            jnp.concatenate(dense, axis=1), weights_ref[step], preferred_element_type=jnp.float32
        ).astype(jnp.bfloat16)
        share_width = result.shape[1] // shares
        for share in range(shares):
            payload_ref[group * shares + share] = result[:, share * share_width : (share + 1) * share_width]
        return carry

    lax.fori_loop(0, groups, one_group, 0, unroll=groups <= 4)


def condition(own, near, far, quarter_routes, weights, shares, width):
    quarter, top = quarter_routes.shape
    groups = weights.shape[0]
    return pl.pallas_call(
        functools.partial(condition_kernel, top=top, width=width),
        in_specs=[VMEM] * 5,
        out_shape=jax.ShapeDtypeStruct((groups * shares, quarter, LANES), jnp.bfloat16),
        scratch_shapes=[
            pltpu.VMEM((top, quarter, LANES), jnp.float32),
            pltpu.VMEM((top, quarter, LANES), jnp.int32),
        ],
        compiler_params=pltpu.CompilerParams(vmem_limit_bytes=40 * MIB),
        cost_estimate=cost(2),
    )(own, near, far, quarter_routes, weights)


def query_kernel(query_ref, inverse_ref, out_ref, factor_ref, spread_ref, wide_ref):
    count, experts, _ = query_ref.shape
    width = inverse_ref.shape[1]
    step = pl.program_id(0)
    rows = out_ref.shape[0] // width

    @pl.when(step == 0)
    def _():
        zeros = jnp.zeros((width, width), jnp.bfloat16)
        for e in range(experts):
            high, low = split(inverse_ref[e])
            left = jnp.concatenate([high, zeros, low, zeros], axis=0)
            right = jnp.concatenate([zeros, high, zeros, low], axis=0)
            factor_ref[e] = jnp.concatenate([left, right], axis=1)

    spread_ref[...] = query_ref[...].astype(jnp.float32).reshape(count * experts, LANES)
    for e in range(experts):
        query = spread_ref[pl.ds(e, count, stride=experts), :].astype(jnp.bfloat16)
        result = lax.dot_general(
            factor_ref[e], query, (((1,), (1,)), ((), ())), preferred_element_type=jnp.float32
        )
        result = result[: 2 * width] + result[2 * width :]
        start = e * (rows // experts) + 2 * step
        for tile in range(wide_ref.shape[0]):
            part = result[:, tile * LANES : (tile + 1) * LANES]
            wide_ref[tile, pl.ds(start, width, stride=rows), :] = part[:width]
            wide_ref[tile, pl.ds(start + 1, width, stride=rows), :] = part[width:]

    @pl.when(step == pl.num_programs(0) - 1)
    def _():
        for tile in range(wide_ref.shape[0]):
            out_ref[:, tile * LANES : (tile + 1) * LANES] = wide_ref[tile].astype(jnp.bfloat16)


def condition_queries(query_grads, inverse_in):
    count, experts, flat = query_grads.shape
    width = inverse_in.shape[1]
    rows = experts * flat
    return pl.pallas_call(
        query_kernel,
        grid=(flat // LANES,),
        in_specs=[
            pl.BlockSpec((count, experts, LANES), lambda c: (0, 0, c)),
            pl.BlockSpec(inverse_in.shape, lambda c: (0, 0, 0)),
        ],
        out_specs=pl.BlockSpec((rows, count), lambda c: (0, 0)),
        out_shape=jax.ShapeDtypeStruct((rows, count), jnp.bfloat16),
        scratch_shapes=[
            pltpu.VMEM((experts, 4 * width, 2 * width), jnp.bfloat16),
            pltpu.VMEM((count * experts, LANES), jnp.float32),
            pltpu.VMEM((count // LANES, rows, LANES), jnp.float32),
        ],
        compiler_params=pltpu.CompilerParams(vmem_limit_bytes=40 * MIB),
        cost_estimate=cost(10),
    )(stay(query_grads), inverse_in)


def score_kernel(
    arrived_ref, inner_ref, docs_ref, far_ref, out_ref, grads_ref, queries_ref, sem, *, width, doc_count, turns
):
    fetch = pltpu.make_async_copy(far_ref, queries_ref, sem)
    fetch.start()
    sources, quarter, lanes = arrived_ref.shape
    shares = lax.axis_size("proj")
    owners = sources // shares
    outer, inner, docs = [], [], []
    for entry, (owner_turn, share_turn) in enumerate(turns):
        owner = jnp.bitwise_xor(lax.axis_index("expert"), owner_turn)
        share = jnp.bitwise_xor(lax.axis_index("proj"), share_turn)
        outer.append(arrived_ref[owner * shares + share])
        docs.append(docs_ref[owner, pl.ds(share, 1), :])
        inner.append(inner_ref[entry])
    outer = jnp.concatenate(outer, axis=0)
    inner = jnp.concatenate(inner, axis=1)
    docs = jnp.broadcast_to(jnp.concatenate(docs, axis=1), inner.shape)
    doc_group = 8

    def one_group(group, carry):
        masked = [
            jnp.where(docs == group * doc_group + d, inner, jnp.zeros_like(inner)) for d in range(doc_group)
        ]
        start = pl.multiple_of(group * doc_group * width, doc_group * width)
        grads_ref[pl.ds(start, doc_group * width), :] = jnp.dot(
            jnp.concatenate(masked, axis=0), outer, preferred_element_type=jnp.float32
        )
        return carry

    lax.fori_loop(0, doc_count // doc_group, one_group, 0, unroll=doc_count <= 32)
    high, low = [], []
    for j in range(width):
        parts = split(grads_ref[pl.ds(j, doc_count, stride=width), :])
        high.append(parts[0])
        low.append(parts[1])
    flat = jnp.concatenate([jnp.concatenate(high, axis=1), jnp.concatenate(low, axis=1)], axis=0)
    fetch.wait()
    result = jnp.dot(flat, queries_ref[...], preferred_element_type=jnp.float32)
    result = result[:doc_count] + result[doc_count:]
    columns = result.shape[1] // shares
    fill = jnp.zeros((DOC_DEV, LANES - columns), jnp.float32)
    for owner in range(owners):
        for share in range(shares):
            piece = result[owner * DOC_DEV : (owner + 1) * DOC_DEV, share * columns : (share + 1) * columns]
            out_ref[owner * shares + share] = jnp.concatenate([piece, fill], axis=1)


def score(arrived, inner, docs, queries, turns):
    sources = arrived.shape[0]
    width = inner.shape[1]
    doc_count = DOC_DEV * docs.shape[0]
    return pl.pallas_call(
        functools.partial(score_kernel, width=width, doc_count=doc_count, turns=turns),
        in_specs=[VMEM, VMEM, VMEM, HBM],
        out_shape=jax.ShapeDtypeStruct((sources, DOC_DEV, LANES), jnp.float32),
        scratch_shapes=[
            pltpu.VMEM((doc_count * width, arrived.shape[2]), jnp.float32),
            pltpu.VMEM(queries.shape, jnp.bfloat16),
            pltpu.SemaphoreType.DMA,
        ],
        compiler_params=pltpu.CompilerParams(vmem_limit_bytes=40 * MIB),
        cost_estimate=cost(5),
    )(arrived, inner, docs, stay(queries))


def sum_kernel(pieces_ref, out_ref):
    total = pieces_ref[0]
    for source in range(1, pieces_ref.shape[0]):
        total = total + pieces_ref[source]
    out_ref[...] = total[:, : out_ref.shape[1]]


def sum_pieces(pieces, columns):
    return pl.pallas_call(
        sum_kernel,
        in_specs=[VMEM],
        out_shape=jax.ShapeDtypeStruct((pieces.shape[1], columns), jnp.float32),
        compiler_params=pltpu.CompilerParams(vmem_limit_bytes=40 * MIB),
    )(pieces)


def exchange(block, axis, size, turn):
    return lax.ppermute(block, axis, [(i, i ^ turn) for i in range(size)])


def double(blocks, turns, axis, size, turn):
    blocks = jnp.concatenate([blocks, exchange(blocks, axis, size, turn)], axis=0)
    return blocks, turns + tuple(t ^ turn for t in turns)


def local(
    activations,
    grad_hidden,
    routes,
    doc_ids,
    query_grads,
    in_projection,
    out_projection,
    inverse_in,
    inverse_out,
):
    tokens, top = routes.shape
    experts, width, _ = inverse_in.shape
    owners = lax.axis_size("expert")
    shares = lax.axis_size("proj")
    quarter = tokens // shares
    assert quarter == LANES and 2 * width == LANES and experts * width // shares == LANES
    assert shares == 4 and owners & (owners - 1) == 0
    assert DOC_DEV * owners <= 256

    flat_hidden = grad_hidden.reshape(tokens * top, grad_hidden.shape[2])
    inner_leaving, inner_own, shared = project_inner(
        activations, in_projection, inverse_out, doc_ids.reshape(shares, quarter), shares
    )
    far_shared = exchange(shared, "expert", owners, owners // 2)
    inner_near = exchange(inner_leaving, "proj", shares, 1)
    inner_far = exchange(combine(combine_inner_kernel, inner_own, inner_near), "proj", shares, 2)
    leaving, own = project_outer(flat_hidden, out_projection, shares, top)
    far_shared, inner_far, leaving = lax.optimization_barrier((far_shared, inner_far, leaving))
    near = exchange(leaving, "proj", shares, 1)
    shared, turns = jnp.stack([shared, far_shared]), (0, owners // 2)
    for bit in reversed(range((owners // 2).bit_length() - 1)):
        shared, turns = double(shared, turns, "expert", owners, 1 << bit)
    sent = combine(combine_outer_kernel, own, near)
    far = exchange(sent, "proj", shares, 2)
    inner = finish_inner(inner_own, inner_near, inner_far, width)
    inner, _ = lax.optimization_barrier((inner, sent))
    inner, owner_turns = double(inner[None], (0,), "expert", owners, owners // 2)
    inner, far, shared = lax.optimization_barrier((inner, far, shared))
    for bit in reversed(range((owners // 2).bit_length() - 1)):
        inner, owner_turns = double(inner, owner_turns, "expert", owners, 1 << bit)
    weights, all_docs = expand(shared, turns, width, experts, shares)
    quarter_routes = lax.dynamic_slice_in_dim(routes, lax.axis_index("proj") * quarter, quarter, 0)
    payload = condition(own, near, far, quarter_routes, weights, shares, width)
    arrived = lax.all_to_all(payload, ("expert", "proj"), 0, 0, tiled=True)
    inner, _ = lax.optimization_barrier((inner, payload))
    inner, share_turns = inner[None], (0,)
    inner, share_turns = double(inner, share_turns, "proj", shares, 1)
    inner, query_grads = lax.optimization_barrier((inner, query_grads))
    inner, share_turns = double(inner, share_turns, "proj", shares, 2)
    inner = inner.reshape(owners * shares, width, quarter)
    all_turns = tuple((o, p) for p in share_turns for o in owner_turns)
    queries = condition_queries(query_grads, inverse_in)
    pieces = score(arrived, inner, all_docs, queries, all_turns)
    pieces = lax.all_to_all(pieces, ("expert", "proj"), 0, 0, tiled=True)
    return sum_pieces(pieces, query_grads.shape[0] // shares).T


def solution(mesh):
    in_specs = (
        P(("groups", "expert"), "proj"),
        P(("groups", "expert"), None, "proj"),
        P(("groups", "expert"), None),
        P(("groups", "expert")),
        P(None, "expert", "proj"),
        P(None, "proj"),
        P(None, "proj"),
        P("expert", None, None),
        P("expert", None, None),
    )
    out_specs = P("proj", ("groups", "expert"))
    return jax.shard_map(local, mesh=mesh, in_specs=in_specs, out_specs=out_specs, check_vma=False)
```

```python
import functools

import jax
import jax.numpy as jnp
from jax import lax
from jax.experimental import pallas as pl
from jax.experimental.pallas import tpu as pltpu
from jax.sharding import PartitionSpec as P

DOC_DEV = 8
LANES = 128
DOC_ROWS = 16
MIB = 1024 * 1024
VMEM = pl.BlockSpec(memory_space=pltpu.VMEM)
HBM = pl.BlockSpec(memory_space=pltpu.HBM)


def low_lanes(rows, width):
    return lax.broadcasted_iota(jnp.int32, (rows, LANES), 1) < width


def stay(array):
    return pltpu.with_memory_space_constraint(array, pltpu.HBM)


def split(value):
    high = value.astype(jnp.bfloat16)
    return high, (value - high.astype(jnp.float32)).astype(jnp.bfloat16)


def cost(microseconds):
    return pl.CostEstimate(flops=0, bytes_accessed=int(microseconds * 3.3e6), transcendentals=0)


def in_order(copies, ahead):
    for copy in copies[:ahead]:
        copy.start()
    state = [0]

    def take():
        copies[state[0]].wait()
        if state[0] + ahead < len(copies):
            copies[state[0] + ahead].start()
        state[0] += 1

    return take


def inner_kernel(
    act_hbm, in_proj_hbm, inverse_hbm, docs_hbm, leaving_ref, own_ref, shared_ref, act_ref, in_proj_ref, inverse_ref, docs_ref, sems
):
    turns = (1, 3, 2, 0)
    quarter = act_ref.shape[1]
    width = in_proj_ref.shape[0]
    half = quarter // 2
    place = lax.axis_index("proj")
    pairs = [(in_proj_hbm, in_proj_ref)]
    for g, turn in enumerate(turns):
        rows = pl.ds(pl.multiple_of(jnp.bitwise_xor(place, turn) * quarter, quarter), quarter)
        pairs.append((act_hbm.at[rows], act_ref.at[g]))
        if g == 0:
            pairs += [(inverse_hbm, inverse_ref), (docs_hbm, docs_ref)]
    take = in_order([pltpu.make_async_copy(*pair, sems.at[i]) for i, pair in enumerate(pairs)], 5)
    take()
    first = low_lanes(half, width)
    for g in range(len(turns)):
        wire_ref = leaving_ref.at[g] if g < 2 else own_ref.at[g - 2]
        take()
        if g == 0:
            take()
            take()
            experts = inverse_ref.shape[0] // 2
            for e in range(experts):
                pair = jnp.concatenate([inverse_ref[e], inverse_ref[experts + e]], axis=1)
                shared_ref[e * width : (e + 1) * width, :] = pair.astype(jnp.bfloat16)
            docs = docs_ref[...].astype(jnp.float32)
            docs = jnp.concatenate([docs, jnp.zeros((DOC_ROWS - docs.shape[0], LANES), jnp.float32)], axis=0)
            shared_ref[experts * width :, :] = docs.astype(jnp.bfloat16)
        twice = jnp.concatenate([in_proj_ref[...], in_proj_ref[...]], axis=0)
        inner = lax.dot_general(
            act_ref[g], twice, (((1,), (1,)), ((), ())), preferred_element_type=jnp.float32
        )
        high, low = split(jnp.where(first, inner[:half], inner[half:]))
        wire_ref[:half, :] = high
        wire_ref[half:, :] = low


def project_inner(activations, in_projection, inverse_out, doc_rows, quarters):
    tokens, model = activations.shape
    quarter = tokens // quarters
    experts, width, _ = inverse_out.shape
    wire = jax.ShapeDtypeStruct((quarters // 2, quarter, LANES), jnp.bfloat16)
    fixed = (in_projection, inverse_out, doc_rows)
    return pl.pallas_call(
        inner_kernel,
        in_specs=[HBM] * 4,
        out_specs=[VMEM] * 3,
        out_shape=[wire, wire, jax.ShapeDtypeStruct((experts // 2 * width + DOC_ROWS, LANES), jnp.bfloat16)],
        scratch_shapes=[pltpu.VMEM((quarters, quarter, model), jnp.bfloat16)]
        + [pltpu.VMEM(array.shape, array.dtype) for array in fixed]
        + [pltpu.SemaphoreType.DMA((quarters + len(fixed),))],
        compiler_params=pltpu.CompilerParams(vmem_limit_bytes=40 * MIB),
        cost_estimate=cost(2.5),
    )(*[stay(array) for array in (activations, *fixed)])


def outer_kernel(hidden_hbm, out_proj_hbm, leaving_ref, own_ref, hidden_ref, out_proj_ref, rows_ref, sems, *, top):
    turns = (1, 3, 2, 0)
    chunks, chunk_rows, _ = hidden_ref.shape
    chunk = chunk_rows // top
    split_by = chunks // len(turns)
    quarter = chunk * split_by
    width = out_proj_ref.shape[0]
    place = lax.axis_index("proj")
    pairs = [(out_proj_hbm, out_proj_ref)]
    for i in range(chunks):
        start = (jnp.bitwise_xor(place, turns[i // split_by]) * split_by + i % split_by) * chunk_rows
        pairs.append((hidden_hbm.at[pl.ds(pl.multiple_of(start, chunk_rows), chunk_rows)], hidden_ref.at[i]))
    take = in_order([pltpu.make_async_copy(*pair, sems.at[i]) for i, pair in enumerate(pairs)], 4)
    take()
    first = low_lanes(chunk, width)

    def pack_rows(i):
        g, part = i // split_by, i % split_by
        wire_ref = leaving_ref.at[g] if g < 2 else own_ref.at[g - 2]
        for pair in range(top // 2):
            even = rows_ref[i % 2, pl.ds(2 * pair, chunk, stride=top), :]
            odd = rows_ref[i % 2, pl.ds(2 * pair + 1, chunk, stride=top), :]
            start = pair * quarter + part * chunk
            wire_ref[start : start + chunk, :] = jnp.where(first, even, odd).astype(jnp.bfloat16)

    for i in range(chunks):
        take()
        twice = jnp.concatenate([out_proj_ref[...], out_proj_ref[...]], axis=0)
        rows_ref[i % 2] = lax.dot_general(
            hidden_ref[i], twice, (((1,), (1,)), ((), ())), preferred_element_type=jnp.float32
        )
        if i:
            pack_rows(i - 1)
    pack_rows(chunks - 1)


def project_outer(flat_hidden, out_projection, quarters, top):
    rows, hidden = flat_hidden.shape
    chunks = 2 * quarters
    wire = jax.ShapeDtypeStruct((quarters // 2, rows // quarters // 2, LANES), jnp.bfloat16)
    return pl.pallas_call(
        functools.partial(outer_kernel, top=top),
        in_specs=[HBM] * 2,
        out_specs=[VMEM] * 2,
        out_shape=[wire, wire],
        scratch_shapes=[
            pltpu.VMEM((chunks, rows // chunks, hidden), jnp.bfloat16),
            pltpu.VMEM(out_projection.shape, out_projection.dtype),
            pltpu.VMEM((2, rows // chunks, LANES), jnp.float32),
            pltpu.SemaphoreType.DMA((chunks + 1,)),
        ],
        compiler_params=pltpu.CompilerParams(vmem_limit_bytes=40 * MIB),
        cost_estimate=cost(4),
    )(stay(flat_hidden), stay(out_projection))


def exact_rows(rows):
    half = rows.shape[0] // 2
    return rows[:half].astype(jnp.float32) + rows[half:].astype(jnp.float32)


def combine_inner_kernel(own_ref, near_ref, out_ref):
    high, low = split(exact_rows(own_ref[0]) + exact_rows(near_ref[1]))
    out_ref[: high.shape[0], :] = high
    out_ref[high.shape[0] :, :] = low


def combine_outer_kernel(own_ref, near_ref, out_ref):
    out_ref[...] = (own_ref[0].astype(jnp.float32) + near_ref[1].astype(jnp.float32)).astype(jnp.bfloat16)


def combine(kernel, own, near):
    return pl.pallas_call(
        kernel,
        in_specs=[VMEM, VMEM],
        out_shape=jax.ShapeDtypeStruct(own.shape[1:], jnp.bfloat16),
        compiler_params=pltpu.CompilerParams(vmem_limit_bytes=40 * MIB),
        cost_estimate=cost(0.5),
    )(own, near)


def finish_inner_kernel(own_ref, near_ref, far_ref, out_ref):
    total = exact_rows(own_ref[1]) + exact_rows(near_ref[0]) + exact_rows(far_ref[...])
    width = out_ref.shape[0]
    total = jnp.concatenate([total[:, :width], total[:, width:]], axis=0)
    out_ref[...] = jnp.transpose(total).astype(jnp.bfloat16)


def finish_inner(own, near, far, width):
    return pl.pallas_call(
        finish_inner_kernel,
        in_specs=[VMEM] * 3,
        out_shape=jax.ShapeDtypeStruct((width, own.shape[1]), jnp.bfloat16),
        compiler_params=pltpu.CompilerParams(vmem_limit_bytes=40 * MIB),
        cost_estimate=cost(0.5),
    )(own, near, far)


def expand_kernel(shared_ref, weights_ref, docs_ref, *, width, experts, shares, turns):
    columns = experts * width
    share_rows = width // shares
    half = experts // 2
    lane = lax.broadcasted_iota(jnp.int32, (LANES, columns), 1)
    row = lax.broadcasted_iota(jnp.int32, (LANES, columns), 0)
    source = lane // (experts * share_rows) * share_rows + lane % share_rows
    expert_lane = lax.broadcasted_iota(jnp.int32, (half * width, columns), 1) // share_rows % experts
    expert_row = lax.broadcasted_iota(jnp.int32, (half * width, columns), 0) // width
    for side in range(2):
        spread = (row == source + side * width).astype(jnp.float32).astype(jnp.bfloat16)
        own = expert_lane == expert_row + side * half
        for entry, turn in enumerate(turns):
            placed = jnp.dot(
                shared_ref[entry, : half * width, :], spread, preferred_element_type=jnp.float32
            )
            weights_ref[turn, side * half * width : (side + 1) * half * width, :] = jnp.where(
                own, placed, 0.0
            ).astype(jnp.bfloat16)
    for entry, turn in enumerate(turns):
        owner = jnp.bitwise_xor(lax.axis_index("expert"), turn)
        docs_ref[owner] = shared_ref[entry, half * width :, :].astype(jnp.float32).astype(jnp.int32)


def expand(shared, turns, width, experts, shares):
    owners = shared.shape[0]
    return pl.pallas_call(
        functools.partial(expand_kernel, width=width, experts=experts, shares=shares, turns=turns),
        in_specs=[VMEM],
        out_shape=[
            jax.ShapeDtypeStruct((owners, experts * width, experts * width), jnp.bfloat16),
            jax.ShapeDtypeStruct((owners, DOC_ROWS, LANES), jnp.int32),
        ],
        compiler_params=pltpu.CompilerParams(vmem_limit_bytes=40 * MIB),
        cost_estimate=cost(1.3),
    )(shared)


def condition_kernel(
    own_ref, near_ref, far_ref, routes_ref, weights_ref, payload_ref, value_ref, name_ref, *, top, width
):
    quarter = routes_ref.shape[0]
    groups, dense_width, _ = weights_ref.shape
    shares = payload_ref.shape[0] // groups
    experts = dense_width // width
    first = low_lanes(quarter, width)
    second = 1 - first.astype(jnp.int32)

    def summed(start, size):
        rows = slice(start, start + size)
        total = own_ref[1, rows, :].astype(jnp.float32) + near_ref[0, rows, :].astype(jnp.float32)
        return total + far_ref[rows, :].astype(jnp.float32)

    for pair in range(top // 2):
        both = summed(pair * quarter, quarter)
        swapped = pltpu.roll(both, width, 1)
        value_ref[2 * pair] = jnp.where(first, both, swapped)
        value_ref[2 * pair + 1] = jnp.where(first, swapped, both)
    for k in range(top):
        name_ref[k] = jnp.broadcast_to(routes_ref[:, k : k + 1], (quarter, LANES)) - second
    def one_group(step, carry):
        group = jnp.bitwise_xor(lax.axis_index("expert"), step)
        dense = []
        for pair in range(experts // 2):
            base = group * experts + 2 * pair
            chosen = jnp.zeros((quarter, LANES), jnp.float32)
            for k in range(top):
                chosen = jnp.where(name_ref[k] == base, value_ref[k], chosen)
            dense.append(chosen.astype(jnp.bfloat16))
        result = jnp.dot(
            jnp.concatenate(dense, axis=1), weights_ref[step], preferred_element_type=jnp.float32
        ).astype(jnp.bfloat16)
        share_width = result.shape[1] // shares
        for share in range(shares):
            payload_ref[group * shares + share] = result[:, share * share_width : (share + 1) * share_width]
        return carry

    lax.fori_loop(0, groups, one_group, 0, unroll=groups <= 4)


def condition(own, near, far, quarter_routes, weights, shares, width):
    quarter, top = quarter_routes.shape
    groups = weights.shape[0]
    return pl.pallas_call(
        functools.partial(condition_kernel, top=top, width=width),
        in_specs=[VMEM] * 5,
        out_shape=jax.ShapeDtypeStruct((groups * shares, quarter, LANES), jnp.bfloat16),
        scratch_shapes=[
            pltpu.VMEM((top, quarter, LANES), jnp.float32),
            pltpu.VMEM((top, quarter, LANES), jnp.int32),
        ],
        compiler_params=pltpu.CompilerParams(vmem_limit_bytes=40 * MIB),
        cost_estimate=cost(2),
    )(own, near, far, quarter_routes, weights)


def query_kernel(query_ref, inverse_ref, out_hbm, factor_ref, spread_ref, wide_ref, out_ref, sems):
    count, experts, _ = query_ref.shape
    width = inverse_ref.shape[1]
    step = pl.program_id(0)
    rows = out_ref.shape[0] // width
    pitch = wide_ref.shape[1] // width

    @pl.when(step == 0)
    def _():
        zeros = jnp.zeros((width, width), jnp.bfloat16)
        for e in range(experts):
            high, low = split(inverse_ref[e])
            left = jnp.concatenate([high, zeros, low, zeros], axis=0)
            right = jnp.concatenate([zeros, high, zeros, low], axis=0)
            factor_ref[e] = jnp.concatenate([left, right], axis=1)

    spread_ref[...] = query_ref[...].astype(jnp.float32).reshape(count * experts, LANES)
    for e in range(experts):
        query = spread_ref[pl.ds(e, count, stride=experts), :].astype(jnp.bfloat16)
        result = lax.dot_general(
            factor_ref[e], query, (((1,), (1,)), ((), ())), preferred_element_type=jnp.float32
        )
        result = result[: 2 * width] + result[2 * width :]
        start = e * (rows // experts) + 2 * step
        for tile in range(wide_ref.shape[0]):
            part = result[:, tile * LANES : (tile + 1) * LANES]
            wide_ref[tile, pl.ds(start, width, stride=pitch), :] = part[:width]
            wide_ref[tile, pl.ds(start + 1, width, stride=pitch), :] = part[width:]

    @pl.when(step == pl.num_programs(0) - 1)
    def _():
        copies = []
        for part in range(sems.shape[0]):
            first = part * (width // sems.shape[0])
            for j in range(first, first + width // sems.shape[0]):
                for tile in range(wide_ref.shape[0]):
                    out_ref[j * rows : (j + 1) * rows, tile * LANES : (tile + 1) * LANES] = wide_ref[
                        tile, j * pitch : j * pitch + rows, :
                    ].astype(jnp.bfloat16)
            block = pl.ds(first * rows, width // sems.shape[0] * rows)
            copies.append(pltpu.make_async_copy(out_ref.at[block], out_hbm.at[block], sems.at[part]))
            copies[-1].start()
        for copy in copies:
            copy.wait()


def condition_queries(query_grads, inverse_in):
    count, experts, flat = query_grads.shape
    width = inverse_in.shape[1]
    rows = experts * flat
    return pl.pallas_call(
        query_kernel,
        grid=(flat // LANES,),
        in_specs=[
            pl.BlockSpec((count, experts, LANES), lambda c: (0, 0, c)),
            pl.BlockSpec(inverse_in.shape, lambda c: (0, 0, 0)),
        ],
        out_specs=HBM,
        out_shape=pltpu.HBM((rows, count), jnp.bfloat16),
        scratch_shapes=[
            pltpu.VMEM((experts, 4 * width, 2 * width), jnp.bfloat16),
            pltpu.VMEM((count * experts, LANES), jnp.float32),
            pltpu.VMEM((count // LANES, rows + 8 * width, LANES), jnp.float32),
            pltpu.VMEM((rows, count), jnp.bfloat16),
            pltpu.SemaphoreType.DMA((4,)),
        ],
        compiler_params=pltpu.CompilerParams(vmem_limit_bytes=40 * MIB),
        cost_estimate=cost(10),
    )(stay(query_grads), inverse_in)


def score_kernel(
    arrived_ref, inner_ref, docs_ref, far_ref, out_ref, grads_ref, queries_ref, sem, *, width, doc_count, turns
):
    fetch = pltpu.make_async_copy(far_ref, queries_ref, sem)
    fetch.start()
    sources, quarter, lanes = arrived_ref.shape
    shares = lax.axis_size("proj")
    owners = sources // shares
    outer, inner, docs = [], [], []
    for entry, (owner_turn, share_turn) in enumerate(turns):
        owner = jnp.bitwise_xor(lax.axis_index("expert"), owner_turn)
        share = jnp.bitwise_xor(lax.axis_index("proj"), share_turn)
        outer.append(arrived_ref[owner * shares + share])
        docs.append(docs_ref[owner, pl.ds(share, 1), :])
        inner.append(inner_ref[entry])
    outer = jnp.concatenate(outer, axis=0)
    inner = jnp.concatenate(inner, axis=1)
    docs = jnp.broadcast_to(jnp.concatenate(docs, axis=1), inner.shape)
    doc_group = 8
    pitch = grads_ref.shape[0] // doc_count

    def one_group(group, carry):
        masked = [
            jnp.where(docs == group * doc_group + d, inner, jnp.zeros_like(inner)) for d in range(doc_group)
        ]
        sums = jnp.dot(jnp.concatenate(masked, axis=0), outer, preferred_element_type=jnp.float32)
        for d in range(doc_group):
            start = pl.multiple_of((group * doc_group + d) * pitch, 8)
            grads_ref[pl.ds(start, width), :] = sums[d * width : (d + 1) * width]
        return carry

    lax.fori_loop(0, doc_count // doc_group, one_group, 0, unroll=doc_count <= 32)
    high, low = [], []
    for j in range(width):
        parts = split(grads_ref[pl.ds(j, doc_count, stride=pitch), :])
        high.append(parts[0])
        low.append(parts[1])
    flat = jnp.concatenate([jnp.concatenate(high, axis=1), jnp.concatenate(low, axis=1)], axis=0)
    fetch.wait()
    result = jnp.dot(flat, queries_ref[...], preferred_element_type=jnp.float32)
    result = result[:doc_count] + result[doc_count:]
    columns = result.shape[1] // shares
    fill = jnp.zeros((DOC_DEV, LANES - columns), jnp.float32)
    for owner in range(owners):
        for share in range(shares):
            piece = result[owner * DOC_DEV : (owner + 1) * DOC_DEV, share * columns : (share + 1) * columns]
            out_ref[owner * shares + share] = jnp.concatenate([piece, fill], axis=1)


def score(arrived, inner, docs, queries, turns):
    sources = arrived.shape[0]
    width = inner.shape[1]
    doc_count = DOC_DEV * docs.shape[0]
    return pl.pallas_call(
        functools.partial(score_kernel, width=width, doc_count=doc_count, turns=turns),
        in_specs=[VMEM, VMEM, VMEM, HBM],
        out_shape=jax.ShapeDtypeStruct((sources, DOC_DEV, LANES), jnp.float32),
        scratch_shapes=[
            pltpu.VMEM((doc_count * (width + 8), arrived.shape[2]), jnp.float32),
            pltpu.VMEM(queries.shape, jnp.bfloat16),
            pltpu.SemaphoreType.DMA,
        ],
        compiler_params=pltpu.CompilerParams(vmem_limit_bytes=40 * MIB),
        cost_estimate=cost(5),
    )(arrived, inner, docs, stay(queries))


def sum_kernel(pieces_ref, out_ref):
    total = pieces_ref[0]
    for source in range(1, pieces_ref.shape[0]):
        total = total + pieces_ref[source]
    out_ref[...] = total[:, : out_ref.shape[1]]


def sum_pieces(pieces, columns):
    return pl.pallas_call(
        sum_kernel,
        in_specs=[VMEM],
        out_shape=jax.ShapeDtypeStruct((pieces.shape[1], columns), jnp.float32),
        compiler_params=pltpu.CompilerParams(vmem_limit_bytes=40 * MIB),
    )(pieces)


def exchange(block, axis, size, turn):
    return lax.ppermute(block, axis, [(i, i ^ turn) for i in range(size)])


def double(blocks, turns, axis, size, turn):
    blocks = jnp.concatenate([blocks, exchange(blocks, axis, size, turn)], axis=0)
    return blocks, turns + tuple(t ^ turn for t in turns)


def local(
    activations,
    grad_hidden,
    routes,
    doc_ids,
    query_grads,
    in_projection,
    out_projection,
    inverse_in,
    inverse_out,
):
    tokens, top = routes.shape
    experts, width, _ = inverse_in.shape
    owners = lax.axis_size("expert")
    shares = lax.axis_size("proj")
    quarter = tokens // shares
    assert quarter == LANES and 2 * width == LANES and experts * width // shares == LANES
    assert shares == 4 and owners & (owners - 1) == 0
    assert DOC_DEV * owners <= 256

    flat_hidden = grad_hidden.reshape(tokens * top, grad_hidden.shape[2])
    inner_leaving, inner_own, shared = project_inner(
        activations, in_projection, inverse_out, doc_ids.reshape(shares, quarter), shares
    )
    far_shared = exchange(shared, "expert", owners, owners // 2)
    inner_near = exchange(inner_leaving, "proj", shares, 1)
    inner_far = exchange(combine(combine_inner_kernel, inner_own, inner_near), "proj", shares, 2)
    leaving, own = project_outer(flat_hidden, out_projection, shares, top)
    far_shared, inner_far, leaving = lax.optimization_barrier((far_shared, inner_far, leaving))
    near = exchange(leaving, "proj", shares, 1)
    shared, turns = jnp.stack([shared, far_shared]), (0, owners // 2)
    for bit in reversed(range((owners // 2).bit_length() - 1)):
        shared, turns = double(shared, turns, "expert", owners, 1 << bit)
    sent = combine(combine_outer_kernel, own, near)
    far = exchange(sent, "proj", shares, 2)
    inner = finish_inner(inner_own, inner_near, inner_far, width)
    inner, _ = lax.optimization_barrier((inner, sent))
    inner, owner_turns = double(inner[None], (0,), "expert", owners, owners // 2)
    inner, far, shared = lax.optimization_barrier((inner, far, shared))
    for bit in reversed(range((owners // 2).bit_length() - 1)):
        arriving = exchange(inner, "expert", owners, 1 << bit)
        owner_turns = owner_turns + tuple(t ^ (1 << bit) for t in owner_turns)
        if bit:
            inner = jnp.concatenate([inner, arriving], axis=0)
    weights, all_docs = expand(shared, turns, width, experts, shares)
    quarter_routes = lax.dynamic_slice_in_dim(routes, lax.axis_index("proj") * quarter, quarter, 0)
    payload = condition(own, near, far, quarter_routes, weights, shares, width)
    payload, arriving = lax.optimization_barrier((payload, arriving))
    arrived = lax.all_to_all(payload, ("expert", "proj"), 0, 0, tiled=True)
    inner = jnp.concatenate([inner, arriving], axis=0)
    inner, share_turns = inner[None], (0,)
    inner, share_turns = double(inner, share_turns, "proj", shares, 1)
    inner, query_grads = lax.optimization_barrier((inner, query_grads))
    inner, share_turns = double(inner, share_turns, "proj", shares, 2)
    inner = inner.reshape(owners * shares, width, quarter)
    all_turns = tuple((o, p) for p in share_turns for o in owner_turns)
    queries = condition_queries(query_grads, inverse_in)
    pieces = score(arrived, inner, all_docs, queries, all_turns)
    pieces = lax.all_to_all(pieces, ("expert", "proj"), 0, 0, tiled=True)
    return sum_pieces(pieces, query_grads.shape[0] // shares).T


def solution(mesh):
    in_specs = (
        P(("groups", "expert"), "proj"),
        P(("groups", "expert"), None, "proj"),
        P(("groups", "expert"), None),
        P(("groups", "expert")),
        P(None, "expert", "proj"),
        P(None, "proj"),
        P(None, "proj"),
        P("expert", None, None),
        P("expert", None, None),
    )
    out_specs = P("proj", ("groups", "expert"))
    return jax.shard_map(local, mesh=mesh, in_specs=in_specs, out_specs=out_specs, check_vma=False)
```

```python
import functools

import jax
import jax.numpy as jnp
from jax import lax
from jax.experimental import pallas as pl
from jax.experimental.pallas import tpu as pltpu
from jax.sharding import PartitionSpec as P

DOC_DEV = 8
LANES = 128
DOC_ROWS = 16
MIB = 1024 * 1024
VMEM = pl.BlockSpec(memory_space=pltpu.VMEM)
HBM = pl.BlockSpec(memory_space=pltpu.HBM)


def low_lanes(rows, width):
    return lax.broadcasted_iota(jnp.int32, (rows, LANES), 1) < width


def stay(array):
    return pltpu.with_memory_space_constraint(array, pltpu.HBM)


def split(value):
    high = value.astype(jnp.bfloat16)
    return high, (value - high.astype(jnp.float32)).astype(jnp.bfloat16)


def cost(microseconds):
    return pl.CostEstimate(flops=0, bytes_accessed=int(microseconds * 3.3e6), transcendentals=0)


def in_order(copies, ahead):
    for copy in copies[:ahead]:
        copy.start()
    state = [0]

    def take():
        copies[state[0]].wait()
        if state[0] + ahead < len(copies):
            copies[state[0] + ahead].start()
        state[0] += 1

    return take


def inner_kernel(
    act_hbm, in_proj_hbm, inverse_hbm, docs_hbm, leaving_ref, own_ref, shared_ref, act_ref, in_proj_ref, inverse_ref, docs_ref, sems
):
    turns = (1, 3, 2, 0)
    quarter = act_ref.shape[1]
    width = in_proj_ref.shape[0]
    half = quarter // 2
    place = lax.axis_index("proj")
    pairs = [(in_proj_hbm, in_proj_ref)]
    for g, turn in enumerate(turns):
        rows = pl.ds(pl.multiple_of(jnp.bitwise_xor(place, turn) * quarter, quarter), quarter)
        pairs.append((act_hbm.at[rows], act_ref.at[g]))
        if g == 0:
            pairs += [(inverse_hbm, inverse_ref), (docs_hbm, docs_ref)]
    take = in_order([pltpu.make_async_copy(*pair, sems.at[i]) for i, pair in enumerate(pairs)], 5)
    take()
    first = low_lanes(half, width)
    for wire_ref in (leaving_ref, own_ref):
        take()
        if wire_ref is leaving_ref:
            take()
            take()
            experts = inverse_ref.shape[0] // 2
            for e in range(experts):
                pair = jnp.concatenate([inverse_ref[e], inverse_ref[experts + e]], axis=1)
                shared_ref[e * width : (e + 1) * width, :] = pair.astype(jnp.bfloat16)
            docs = docs_ref[...].astype(jnp.float32)
            docs = jnp.concatenate([docs, jnp.zeros((DOC_ROWS - docs.shape[0], LANES), jnp.float32)], axis=0)
            shared_ref[experts * width :, :] = docs.astype(jnp.bfloat16)
        take()
        twice = jnp.concatenate([in_proj_ref[...], in_proj_ref[...]], axis=0)
        g = 0 if wire_ref is leaving_ref else 2
        rows = act_ref[g : g + 2].reshape(2 * quarter, act_ref.shape[2])
        inner = lax.dot_general(rows, twice, (((1,), (1,)), ((), ())), preferred_element_type=jnp.float32)
        for i in range(2):
            start = i * quarter
            high, low = split(jnp.where(first, inner[start : start + half], inner[start + half : start + quarter]))
            wire_ref[i, :half, :] = high
            wire_ref[i, half:, :] = low


def project_inner(activations, in_projection, inverse_out, doc_rows, quarters):
    tokens, model = activations.shape
    quarter = tokens // quarters
    experts, width, _ = inverse_out.shape
    wire = jax.ShapeDtypeStruct((quarters // 2, quarter, LANES), jnp.bfloat16)
    fixed = (in_projection, inverse_out, doc_rows)
    return pl.pallas_call(
        inner_kernel,
        in_specs=[HBM] * 4,
        out_specs=[VMEM] * 3,
        out_shape=[wire, wire, jax.ShapeDtypeStruct((experts // 2 * width + DOC_ROWS, LANES), jnp.bfloat16)],
        scratch_shapes=[pltpu.VMEM((quarters, quarter, model), jnp.bfloat16)]
        + [pltpu.VMEM(array.shape, array.dtype) for array in fixed]
        + [pltpu.SemaphoreType.DMA((quarters + len(fixed),))],
        compiler_params=pltpu.CompilerParams(vmem_limit_bytes=40 * MIB),
        cost_estimate=cost(2.5),
    )(*[stay(array) for array in (activations, *fixed)])


def outer_kernel(hidden_hbm, out_proj_hbm, leaving_ref, own_ref, hidden_ref, out_proj_ref, rows_ref, sems, *, top):
    turns = (1, 3, 2, 0)
    chunks, chunk_rows, _ = hidden_ref.shape
    chunk = chunk_rows // top
    split_by = chunks // len(turns)
    quarter = chunk * split_by
    width = out_proj_ref.shape[0]
    place = lax.axis_index("proj")
    pairs = [(out_proj_hbm, out_proj_ref)]
    for i in range(chunks):
        start = (jnp.bitwise_xor(place, turns[i // split_by]) * split_by + i % split_by) * chunk_rows
        pairs.append((hidden_hbm.at[pl.ds(pl.multiple_of(start, chunk_rows), chunk_rows)], hidden_ref.at[i]))
    take = in_order([pltpu.make_async_copy(*pair, sems.at[i]) for i, pair in enumerate(pairs)], 3)
    take()
    first = low_lanes(chunk, width)

    def pack_rows(i):
        g, part = i // split_by, i % split_by
        wire_ref = leaving_ref.at[g] if g < 2 else own_ref.at[g - 2]
        for pair in range(top // 2):
            even = rows_ref[i % 2, pl.ds(2 * pair, chunk, stride=top), :]
            odd = rows_ref[i % 2, pl.ds(2 * pair + 1, chunk, stride=top), :]
            start = pair * quarter + part * chunk
            wire_ref[start : start + chunk, :] = jnp.where(first, even, odd).astype(jnp.bfloat16)

    for i in range(chunks):
        take()
        twice = jnp.concatenate([out_proj_ref[...], out_proj_ref[...]], axis=0)
        rows_ref[i % 2] = lax.dot_general(
            hidden_ref[i], twice, (((1,), (1,)), ((), ())), preferred_element_type=jnp.float32
        )
        if i:
            pack_rows(i - 1)
    pack_rows(chunks - 1)


def project_outer(flat_hidden, out_projection, quarters, top):
    rows, hidden = flat_hidden.shape
    chunks = quarters
    wire = jax.ShapeDtypeStruct((quarters // 2, rows // quarters // 2, LANES), jnp.bfloat16)
    return pl.pallas_call(
        functools.partial(outer_kernel, top=top),
        in_specs=[HBM] * 2,
        out_specs=[VMEM] * 2,
        out_shape=[wire, wire],
        scratch_shapes=[
            pltpu.VMEM((chunks, rows // chunks, hidden), jnp.bfloat16),
            pltpu.VMEM(out_projection.shape, out_projection.dtype),
            pltpu.VMEM((2, rows // chunks, LANES), jnp.float32),
            pltpu.SemaphoreType.DMA((chunks + 1,)),
        ],
        compiler_params=pltpu.CompilerParams(vmem_limit_bytes=40 * MIB),
        cost_estimate=cost(4),
    )(stay(flat_hidden), stay(out_projection))


def exact_rows(rows):
    half = rows.shape[0] // 2
    return rows[:half].astype(jnp.float32) + rows[half:].astype(jnp.float32)


def combine_inner_kernel(own_ref, near_ref, out_ref):
    high, low = split(exact_rows(own_ref[0]) + exact_rows(near_ref[1]))
    out_ref[: high.shape[0], :] = high
    out_ref[high.shape[0] :, :] = low


def combine_outer_kernel(own_ref, near_ref, out_ref):
    out_ref[...] = (own_ref[0].astype(jnp.float32) + near_ref[1].astype(jnp.float32)).astype(jnp.bfloat16)


def combine(kernel, own, near):
    return pl.pallas_call(
        kernel,
        in_specs=[VMEM, VMEM],
        out_shape=jax.ShapeDtypeStruct(own.shape[1:], jnp.bfloat16),
        compiler_params=pltpu.CompilerParams(vmem_limit_bytes=40 * MIB),
        cost_estimate=cost(0.5),
    )(own, near)


def finish_inner_kernel(own_ref, near_ref, far_ref, out_ref):
    total = exact_rows(own_ref[1]) + exact_rows(near_ref[0]) + exact_rows(far_ref[...])
    width = out_ref.shape[0]
    total = jnp.concatenate([total[:, :width], total[:, width:]], axis=0)
    out_ref[...] = jnp.transpose(total).astype(jnp.bfloat16)


def finish_inner(own, near, far, width):
    return pl.pallas_call(
        finish_inner_kernel,
        in_specs=[VMEM] * 3,
        out_shape=jax.ShapeDtypeStruct((width, own.shape[1]), jnp.bfloat16),
        compiler_params=pltpu.CompilerParams(vmem_limit_bytes=40 * MIB),
        cost_estimate=cost(0.5),
    )(own, near, far)


def expand_kernel(shared_ref, weights_ref, docs_ref, *, width, experts, shares, turns):
    columns = experts * width
    share_rows = width // shares
    half = experts // 2
    lane = lax.broadcasted_iota(jnp.int32, (LANES, columns), 1)
    row = lax.broadcasted_iota(jnp.int32, (LANES, columns), 0)
    source = lane // (experts * share_rows) * share_rows + lane % share_rows
    expert_lane = lax.broadcasted_iota(jnp.int32, (half * width, columns), 1) // share_rows % experts
    expert_row = lax.broadcasted_iota(jnp.int32, (half * width, columns), 0) // width
    for side in range(2):
        spread = (row == source + side * width).astype(jnp.float32).astype(jnp.bfloat16)
        own = expert_lane == expert_row + side * half
        for entry, turn in enumerate(turns):
            placed = jnp.dot(
                shared_ref[entry, : half * width, :], spread, preferred_element_type=jnp.float32
            )
            weights_ref[turn, side * half * width : (side + 1) * half * width, :] = jnp.where(
                own, placed, 0.0
            ).astype(jnp.bfloat16)
    for entry, turn in enumerate(turns):
        owner = jnp.bitwise_xor(lax.axis_index("expert"), turn)
        docs_ref[owner] = shared_ref[entry, half * width :, :].astype(jnp.float32).astype(jnp.int32)


def expand(shared, turns, width, experts, shares):
    owners = shared.shape[0]
    return pl.pallas_call(
        functools.partial(expand_kernel, width=width, experts=experts, shares=shares, turns=turns),
        in_specs=[VMEM],
        out_shape=[
            jax.ShapeDtypeStruct((owners, experts * width, experts * width), jnp.bfloat16),
            jax.ShapeDtypeStruct((owners, DOC_ROWS, LANES), jnp.int32),
        ],
        compiler_params=pltpu.CompilerParams(vmem_limit_bytes=40 * MIB),
        cost_estimate=cost(1.3),
    )(shared)


def condition_kernel(
    own_ref, near_ref, far_ref, routes_ref, weights_ref, payload_ref, value_ref, name_ref, *, top, width
):
    quarter = routes_ref.shape[0]
    groups, dense_width, _ = weights_ref.shape
    shares = payload_ref.shape[0] // groups
    experts = dense_width // width
    first = low_lanes(quarter, width)
    second = 1 - first.astype(jnp.int32)

    def summed(start, size):
        rows = slice(start, start + size)
        total = own_ref[1, rows, :].astype(jnp.float32) + near_ref[0, rows, :].astype(jnp.float32)
        return total + far_ref[rows, :].astype(jnp.float32)

    for pair in range(top // 2):
        both = summed(pair * quarter, quarter)
        swapped = pltpu.roll(both, width, 1)
        value_ref[2 * pair] = jnp.where(first, both, swapped)
        value_ref[2 * pair + 1] = jnp.where(first, swapped, both)
    for k in range(top):
        name_ref[k] = jnp.broadcast_to(routes_ref[:, k : k + 1], (quarter, LANES)) - second
    def one_group(step, carry):
        group = jnp.bitwise_xor(lax.axis_index("expert"), step)
        dense = []
        for pair in range(experts // 2):
            base = group * experts + 2 * pair
            chosen = jnp.zeros((quarter, LANES), jnp.float32)
            for k in range(top):
                chosen = jnp.where(name_ref[k] == base, value_ref[k], chosen)
            dense.append(chosen.astype(jnp.bfloat16))
        result = jnp.dot(
            jnp.concatenate(dense, axis=1), weights_ref[step], preferred_element_type=jnp.float32
        ).astype(jnp.bfloat16)
        share_width = result.shape[1] // shares
        for share in range(shares):
            payload_ref[group * shares + share] = result[:, share * share_width : (share + 1) * share_width]
        return carry

    lax.fori_loop(0, groups, one_group, 0, unroll=groups <= 4)


def condition(own, near, far, quarter_routes, weights, shares, width):
    quarter, top = quarter_routes.shape
    groups = weights.shape[0]
    return pl.pallas_call(
        functools.partial(condition_kernel, top=top, width=width),
        in_specs=[VMEM] * 5,
        out_shape=jax.ShapeDtypeStruct((groups * shares, quarter, LANES), jnp.bfloat16),
        scratch_shapes=[
            pltpu.VMEM((top, quarter, LANES), jnp.float32),
            pltpu.VMEM((top, quarter, LANES), jnp.int32),
        ],
        compiler_params=pltpu.CompilerParams(vmem_limit_bytes=40 * MIB),
        cost_estimate=cost(2),
    )(own, near, far, quarter_routes, weights)


def query_kernel(query_ref, inverse_ref, out_hbm, factor_ref, spread_ref, wide_ref, out_ref, sems):
    count, experts, _ = query_ref.shape
    width = inverse_ref.shape[1]
    step = pl.program_id(0)
    rows = out_ref.shape[0] // width
    pitch = wide_ref.shape[1] // width

    @pl.when(step == 0)
    def _():
        zeros = jnp.zeros((width, width), jnp.bfloat16)
        for e in range(experts):
            high, low = split(inverse_ref[e])
            left = jnp.concatenate([high, zeros, low, zeros], axis=0)
            right = jnp.concatenate([zeros, high, zeros, low], axis=0)
            factor_ref[e] = jnp.concatenate([left, right], axis=1)

    spread_ref[...] = query_ref[...].astype(jnp.float32).reshape(count * experts, LANES)
    for e in range(experts):
        query = spread_ref[pl.ds(e, count, stride=experts), :].astype(jnp.bfloat16)
        result = lax.dot_general(
            factor_ref[e], query, (((1,), (1,)), ((), ())), preferred_element_type=jnp.float32
        )
        result = result[: 2 * width] + result[2 * width :]
        start = e * (rows // experts) + 2 * step
        for tile in range(wide_ref.shape[0]):
            part = result[:, tile * LANES : (tile + 1) * LANES]
            wide_ref[tile, pl.ds(start, width, stride=pitch), :] = part[:width]
            wide_ref[tile, pl.ds(start + 1, width, stride=pitch), :] = part[width:]

    @pl.when(step == pl.num_programs(0) - 1)
    def _():
        copies = []
        for part in range(sems.shape[0]):
            first = part * (width // sems.shape[0])
            for j in range(first, first + width // sems.shape[0]):
                for tile in range(wide_ref.shape[0]):
                    out_ref[j * rows : (j + 1) * rows, tile * LANES : (tile + 1) * LANES] = wide_ref[
                        tile, j * pitch : j * pitch + rows, :
                    ].astype(jnp.bfloat16)
            block = pl.ds(first * rows, width // sems.shape[0] * rows)
            copies.append(pltpu.make_async_copy(out_ref.at[block], out_hbm.at[block], sems.at[part]))
            copies[-1].start()
        for copy in copies:
            copy.wait()


def condition_queries(query_grads, inverse_in):
    count, experts, flat = query_grads.shape
    width = inverse_in.shape[1]
    rows = experts * flat
    return pl.pallas_call(
        query_kernel,
        grid=(flat // LANES,),
        in_specs=[
            pl.BlockSpec((count, experts, LANES), lambda c: (0, 0, c)),
            pl.BlockSpec(inverse_in.shape, lambda c: (0, 0, 0)),
        ],
        out_specs=HBM,
        out_shape=pltpu.HBM((rows, count), jnp.bfloat16),
        scratch_shapes=[
            pltpu.VMEM((experts, 4 * width, 2 * width), jnp.bfloat16),
            pltpu.VMEM((count * experts, LANES), jnp.float32),
            pltpu.VMEM((count // LANES, rows + 8 * width, LANES), jnp.float32),
            pltpu.VMEM((rows, count), jnp.bfloat16),
            pltpu.SemaphoreType.DMA((4,)),
        ],
        compiler_params=pltpu.CompilerParams(vmem_limit_bytes=40 * MIB),
        cost_estimate=cost(10),
    )(stay(query_grads), inverse_in)


def score_kernel(
    arrived_ref, inner_ref, docs_ref, far_ref, out_ref, grads_ref, queries_ref, sem, *, width, doc_count, turns
):
    fetch = pltpu.make_async_copy(far_ref, queries_ref, sem)
    fetch.start()
    sources, quarter, lanes = arrived_ref.shape
    shares = lax.axis_size("proj")
    owners = sources // shares
    outer, inner, docs = [], [], []
    for entry, (owner_turn, share_turn) in enumerate(turns):
        owner = jnp.bitwise_xor(lax.axis_index("expert"), owner_turn)
        share = jnp.bitwise_xor(lax.axis_index("proj"), share_turn)
        outer.append(arrived_ref[owner * shares + share])
        docs.append(docs_ref[owner, pl.ds(share, 1), :])
        inner.append(inner_ref[entry])
    outer = jnp.concatenate(outer, axis=0)
    inner = jnp.concatenate(inner, axis=1)
    docs = jnp.broadcast_to(jnp.concatenate(docs, axis=1), inner.shape)
    doc_group = 16
    pitch = grads_ref.shape[0] // doc_count

    def one_group(group, carry):
        masked = [
            jnp.where(docs == group * doc_group + d, inner, jnp.zeros_like(inner)) for d in range(doc_group)
        ]
        sums = jnp.dot(jnp.concatenate(masked, axis=0), outer, preferred_element_type=jnp.float32)
        for d in range(doc_group):
            start = pl.multiple_of((group * doc_group + d) * pitch, 8)
            grads_ref[pl.ds(start, width), :] = sums[d * width : (d + 1) * width]
        return carry

    lax.fori_loop(0, doc_count // doc_group, one_group, 0, unroll=doc_count <= 2 * doc_group)
    high, low = [], []
    for j in range(width):
        parts = split(grads_ref[pl.ds(j, doc_count, stride=pitch), :])
        high.append(parts[0])
        low.append(parts[1])
    flat = jnp.concatenate([jnp.concatenate(high, axis=1), jnp.concatenate(low, axis=1)], axis=0)
    fetch.wait()
    result = jnp.dot(flat, queries_ref[...], preferred_element_type=jnp.float32)
    result = result[:doc_count] + result[doc_count:]
    columns = result.shape[1] // shares
    fill = jnp.zeros((DOC_DEV, LANES - columns), jnp.float32)
    for owner in range(owners):
        for share in range(shares):
            piece = result[owner * DOC_DEV : (owner + 1) * DOC_DEV, share * columns : (share + 1) * columns]
            out_ref[owner * shares + share] = jnp.concatenate([piece, fill], axis=1)


def score(arrived, inner, docs, queries, turns):
    sources = arrived.shape[0]
    width = inner.shape[1]
    doc_count = DOC_DEV * docs.shape[0]
    return pl.pallas_call(
        functools.partial(score_kernel, width=width, doc_count=doc_count, turns=turns),
        in_specs=[VMEM, VMEM, VMEM, HBM],
        out_shape=jax.ShapeDtypeStruct((sources, DOC_DEV, LANES), jnp.float32),
        scratch_shapes=[
            pltpu.VMEM((doc_count * (width + 8), arrived.shape[2]), jnp.float32),
            pltpu.VMEM(queries.shape, jnp.bfloat16),
            pltpu.SemaphoreType.DMA,
        ],
        compiler_params=pltpu.CompilerParams(vmem_limit_bytes=40 * MIB),
        cost_estimate=cost(5),
    )(arrived, inner, docs, stay(queries))


def sum_kernel(pieces_ref, out_ref):
    total = pieces_ref[0]
    for source in range(1, pieces_ref.shape[0]):
        total = total + pieces_ref[source]
    out_ref[...] = total[:, : out_ref.shape[1]]


def sum_pieces(pieces, columns):
    return pl.pallas_call(
        sum_kernel,
        in_specs=[VMEM],
        out_shape=jax.ShapeDtypeStruct((pieces.shape[1], columns), jnp.float32),
        compiler_params=pltpu.CompilerParams(vmem_limit_bytes=40 * MIB),
    )(pieces)


def exchange(block, axis, size, turn):
    return lax.ppermute(block, axis, [(i, i ^ turn) for i in range(size)])


def double(blocks, turns, axis, size, turn):
    blocks = jnp.concatenate([blocks, exchange(blocks, axis, size, turn)], axis=0)
    return blocks, turns + tuple(t ^ turn for t in turns)


def local(
    activations,
    grad_hidden,
    routes,
    doc_ids,
    query_grads,
    in_projection,
    out_projection,
    inverse_in,
    inverse_out,
):
    tokens, top = routes.shape
    experts, width, _ = inverse_in.shape
    owners = lax.axis_size("expert")
    shares = lax.axis_size("proj")
    quarter = tokens // shares
    assert quarter == LANES and 2 * width == LANES and experts * width // shares == LANES
    assert shares == 4 and owners & (owners - 1) == 0
    assert DOC_DEV * owners <= 256

    flat_hidden = grad_hidden.reshape(tokens * top, grad_hidden.shape[2])
    inner_leaving, inner_own, shared = project_inner(
        activations, in_projection, inverse_out, doc_ids.reshape(shares, quarter), shares
    )
    far_shared = exchange(shared, "expert", owners, owners // 2)
    inner_near = exchange(inner_leaving, "proj", shares, 1)
    inner_far = exchange(combine(combine_inner_kernel, inner_own, inner_near), "proj", shares, 2)
    leaving, own = project_outer(flat_hidden, out_projection, shares, top)
    far_shared, inner_far, leaving = lax.optimization_barrier((far_shared, inner_far, leaving))
    near = exchange(leaving, "proj", shares, 1)
    shared, turns = jnp.stack([shared, far_shared]), (0, owners // 2)
    for bit in reversed(range((owners // 2).bit_length() - 1)):
        shared, turns = double(shared, turns, "expert", owners, 1 << bit)
    sent = combine(combine_outer_kernel, own, near)
    far = exchange(sent, "proj", shares, 2)
    inner = finish_inner(inner_own, inner_near, inner_far, width)
    inner, _ = lax.optimization_barrier((inner, sent))
    inner, owner_turns = double(inner[None], (0,), "expert", owners, owners // 2)
    weights, all_docs = expand(shared, turns, width, experts, shares)
    inner, far, weights = lax.optimization_barrier((inner, far, weights))
    for bit in reversed(range((owners // 2).bit_length() - 1)):
        arriving = exchange(inner, "expert", owners, 1 << bit)
        owner_turns = owner_turns + tuple(t ^ (1 << bit) for t in owner_turns)
        if bit:
            inner = jnp.concatenate([inner, arriving], axis=0)
    quarter_routes = lax.dynamic_slice_in_dim(routes, lax.axis_index("proj") * quarter, quarter, 0)
    payload = condition(own, near, far, quarter_routes, weights, shares, width)
    payload, arriving = lax.optimization_barrier((payload, arriving))
    arrived = lax.all_to_all(payload, ("expert", "proj"), 0, 0, tiled=True)
    inner = jnp.concatenate([inner, arriving], axis=0)
    inner, share_turns = inner[None], (0,)
    inner, share_turns = double(inner, share_turns, "proj", shares, 1)
    inner, query_grads = lax.optimization_barrier((inner, query_grads))
    inner, share_turns = double(inner, share_turns, "proj", shares, 2)
    inner = inner.reshape(owners * shares, width, quarter)
    all_turns = tuple((o, p) for p in share_turns for o in owner_turns)
    queries = condition_queries(query_grads, inverse_in)
    pieces = score(arrived, inner, all_docs, queries, all_turns)
    pieces = lax.all_to_all(pieces, ("expert", "proj"), 0, 0, tiled=True)
    return sum_pieces(pieces, query_grads.shape[0] // shares).T


def solution(mesh):
    in_specs = (
        P(("groups", "expert"), "proj"),
        P(("groups", "expert"), None, "proj"),
        P(("groups", "expert"), None),
        P(("groups", "expert")),
        P(None, "expert", "proj"),
        P(None, "proj"),
        P(None, "proj"),
        P("expert", None, None),
        P("expert", None, None),
    )
    out_specs = P("proj", ("groups", "expert"))
    return jax.shard_map(local, mesh=mesh, in_specs=in_specs, out_specs=out_specs, check_vma=False)
```

```python
import functools

import jax
import jax.numpy as jnp
from jax import lax
from jax.experimental import pallas as pl
from jax.experimental.pallas import tpu as pltpu
from jax.sharding import PartitionSpec as P

DOC_DEV = 8
LANES = 128
DOC_ROWS = 16
MIB = 1024 * 1024
VMEM = pl.BlockSpec(memory_space=pltpu.VMEM)
HBM = pl.BlockSpec(memory_space=pltpu.HBM)


def low_lanes(rows, width):
    return lax.broadcasted_iota(jnp.int32, (rows, LANES), 1) < width


def stay(array):
    return pltpu.with_memory_space_constraint(array, pltpu.HBM)


def split(value):
    high = value.astype(jnp.bfloat16)
    return high, (value - high.astype(jnp.float32)).astype(jnp.bfloat16)


def cost(microseconds):
    return pl.CostEstimate(flops=0, bytes_accessed=int(microseconds * 3.3e6), transcendentals=0)


def in_order(copies, ahead):
    for copy in copies[:ahead]:
        copy.start()
    state = [0]

    def take():
        copies[state[0]].wait()
        if state[0] + ahead < len(copies):
            copies[state[0] + ahead].start()
        state[0] += 1

    return take


def inner_kernel(
    act_hbm, in_proj_hbm, inverse_hbm, docs_hbm, leaving_ref, own_ref, shared_ref, act_ref, in_proj_ref, inverse_ref, docs_ref, sems
):
    turns = (2, 3, 1, 0)
    quarter = act_ref.shape[1]
    width = in_proj_ref.shape[0]
    half = quarter // 2
    place = lax.axis_index("proj")
    pairs = [(in_proj_hbm, in_proj_ref)]
    for g, turn in enumerate(turns):
        rows = pl.ds(pl.multiple_of(jnp.bitwise_xor(place, turn) * quarter, quarter), quarter)
        pairs.append((act_hbm.at[rows], act_ref.at[g]))
        if g == 0:
            pairs += [(inverse_hbm, inverse_ref), (docs_hbm, docs_ref)]
    take = in_order([pltpu.make_async_copy(*pair, sems.at[i]) for i, pair in enumerate(pairs)], 5)
    take()
    first = low_lanes(half, width)
    for wire_ref in (leaving_ref, own_ref):
        take()
        if wire_ref is leaving_ref:
            take()
            take()
            experts = inverse_ref.shape[0] // 2
            for e in range(experts):
                pair = jnp.concatenate([inverse_ref[e], inverse_ref[experts + e]], axis=1)
                shared_ref[e * width : (e + 1) * width, :] = pair.astype(jnp.bfloat16)
            docs = docs_ref[...].astype(jnp.float32)
            docs = jnp.concatenate([docs, jnp.zeros((DOC_ROWS - docs.shape[0], LANES), jnp.float32)], axis=0)
            shared_ref[experts * width :, :] = docs.astype(jnp.bfloat16)
        take()
        twice = jnp.concatenate([in_proj_ref[...], in_proj_ref[...]], axis=0)
        g = 0 if wire_ref is leaving_ref else 2
        rows = act_ref[g : g + 2].reshape(2 * quarter, act_ref.shape[2])
        inner = lax.dot_general(rows, twice, (((1,), (1,)), ((), ())), preferred_element_type=jnp.float32)
        for i in range(2):
            start = i * quarter
            high, low = split(jnp.where(first, inner[start : start + half], inner[start + half : start + quarter]))
            wire_ref[i, :half, :] = high
            wire_ref[i, half:, :] = low


def project_inner(activations, in_projection, inverse_out, doc_rows, quarters):
    tokens, model = activations.shape
    quarter = tokens // quarters
    experts, width, _ = inverse_out.shape
    wire = jax.ShapeDtypeStruct((quarters // 2, quarter, LANES), jnp.bfloat16)
    fixed = (in_projection, inverse_out, doc_rows)
    return pl.pallas_call(
        inner_kernel,
        in_specs=[HBM] * 4,
        out_specs=[VMEM] * 3,
        out_shape=[wire, wire, jax.ShapeDtypeStruct((experts // 2 * width + DOC_ROWS, LANES), jnp.bfloat16)],
        scratch_shapes=[pltpu.VMEM((quarters, quarter, model), jnp.bfloat16)]
        + [pltpu.VMEM(array.shape, array.dtype) for array in fixed]
        + [pltpu.SemaphoreType.DMA((quarters + len(fixed),))],
        compiler_params=pltpu.CompilerParams(vmem_limit_bytes=40 * MIB),
        cost_estimate=cost(2.5),
    )(*[stay(array) for array in (activations, *fixed)])


def outer_kernel(hidden_hbm, out_proj_hbm, leaving_ref, own_ref, hidden_ref, out_proj_ref, rows_ref, sems, *, top):
    turns = (1, 3, 2, 0)
    chunks, chunk_rows, _ = hidden_ref.shape
    chunk = chunk_rows // top
    split_by = chunks // len(turns)
    quarter = chunk * split_by
    width = out_proj_ref.shape[0]
    place = lax.axis_index("proj")
    pairs = [(out_proj_hbm, out_proj_ref)]
    for i in range(chunks):
        start = (jnp.bitwise_xor(place, turns[i // split_by]) * split_by + i % split_by) * chunk_rows
        pairs.append((hidden_hbm.at[pl.ds(pl.multiple_of(start, chunk_rows), chunk_rows)], hidden_ref.at[i]))
    take = in_order([pltpu.make_async_copy(*pair, sems.at[i]) for i, pair in enumerate(pairs)], 3)
    take()
    first = low_lanes(chunk, width)

    def pack_rows(i):
        g, part = i // split_by, i % split_by
        wire_ref = leaving_ref.at[g] if g < 2 else own_ref.at[g - 2]
        for pair in range(top // 2):
            even = rows_ref[i % 2, pl.ds(2 * pair, chunk, stride=top), :]
            odd = rows_ref[i % 2, pl.ds(2 * pair + 1, chunk, stride=top), :]
            start = pair * quarter + part * chunk
            wire_ref[start : start + chunk, :] = jnp.where(first, even, odd).astype(jnp.bfloat16)

    for i in range(chunks):
        take()
        twice = jnp.concatenate([out_proj_ref[...], out_proj_ref[...]], axis=0)
        rows_ref[i % 2] = lax.dot_general(
            hidden_ref[i], twice, (((1,), (1,)), ((), ())), preferred_element_type=jnp.float32
        )
        if i:
            pack_rows(i - 1)
    pack_rows(chunks - 1)


def project_outer(flat_hidden, out_projection, quarters, top):
    rows, hidden = flat_hidden.shape
    chunks = quarters
    wire = jax.ShapeDtypeStruct((quarters // 2, rows // quarters // 2, LANES), jnp.bfloat16)
    return pl.pallas_call(
        functools.partial(outer_kernel, top=top),
        in_specs=[HBM] * 2,
        out_specs=[VMEM] * 2,
        out_shape=[wire, wire],
        scratch_shapes=[
            pltpu.VMEM((chunks, rows // chunks, hidden), jnp.bfloat16),
            pltpu.VMEM(out_projection.shape, out_projection.dtype),
            pltpu.VMEM((2, rows // chunks, LANES), jnp.float32),
            pltpu.SemaphoreType.DMA((chunks + 1,)),
        ],
        compiler_params=pltpu.CompilerParams(vmem_limit_bytes=40 * MIB),
        cost_estimate=cost(4),
    )(stay(flat_hidden), stay(out_projection))


def exact_rows(rows):
    half = rows.shape[0] // 2
    return rows[:half].astype(jnp.float32) + rows[half:].astype(jnp.float32)


def combine_inner_kernel(own_ref, near_ref, out_ref):
    high, low = split(exact_rows(own_ref[0]) + exact_rows(near_ref[1]))
    out_ref[: high.shape[0], :] = high
    out_ref[high.shape[0] :, :] = low


def combine_outer_kernel(own_ref, near_ref, out_ref):
    out_ref[...] = (own_ref[0].astype(jnp.float32) + near_ref[1].astype(jnp.float32)).astype(jnp.bfloat16)


def combine(kernel, own, near):
    return pl.pallas_call(
        kernel,
        in_specs=[VMEM, VMEM],
        out_shape=jax.ShapeDtypeStruct(own.shape[1:], jnp.bfloat16),
        compiler_params=pltpu.CompilerParams(vmem_limit_bytes=40 * MIB),
        cost_estimate=cost(0.5),
    )(own, near)


def finish_inner_kernel(own_ref, near_ref, far_ref, out_ref):
    total = exact_rows(own_ref[1]) + exact_rows(near_ref[0]) + exact_rows(far_ref[...])
    width = out_ref.shape[0]
    total = jnp.concatenate([total[:, :width], total[:, width:]], axis=0)
    out_ref[...] = jnp.transpose(total).astype(jnp.bfloat16)


def finish_inner(own, near, far, width):
    return pl.pallas_call(
        finish_inner_kernel,
        in_specs=[VMEM] * 3,
        out_shape=jax.ShapeDtypeStruct((width, own.shape[1]), jnp.bfloat16),
        compiler_params=pltpu.CompilerParams(vmem_limit_bytes=40 * MIB),
        cost_estimate=cost(0.5),
    )(own, near, far)


def expand_kernel(shared_ref, weights_ref, docs_ref, *, width, experts, shares, turns):
    columns = experts * width
    share_rows = width // shares
    half = experts // 2
    lane = lax.broadcasted_iota(jnp.int32, (LANES, columns), 1)
    row = lax.broadcasted_iota(jnp.int32, (LANES, columns), 0)
    source = lane // (experts * share_rows) * share_rows + lane % share_rows
    expert_lane = lax.broadcasted_iota(jnp.int32, (half * width, columns), 1) // share_rows % experts
    expert_row = lax.broadcasted_iota(jnp.int32, (half * width, columns), 0) // width
    for side in range(2):
        spread = (row == source + side * width).astype(jnp.float32).astype(jnp.bfloat16)
        own = expert_lane == expert_row + side * half
        for entry, turn in enumerate(turns):
            placed = jnp.dot(
                shared_ref[entry, : half * width, :], spread, preferred_element_type=jnp.float32
            )
            weights_ref[turn, side * half * width : (side + 1) * half * width, :] = jnp.where(
                own, placed, 0.0
            ).astype(jnp.bfloat16)
    for entry, turn in enumerate(turns):
        owner = jnp.bitwise_xor(lax.axis_index("expert"), turn)
        docs_ref[owner] = shared_ref[entry, half * width :, :].astype(jnp.float32).astype(jnp.int32)


def expand(shared, turns, width, experts, shares):
    owners = shared.shape[0]
    return pl.pallas_call(
        functools.partial(expand_kernel, width=width, experts=experts, shares=shares, turns=turns),
        in_specs=[VMEM],
        out_shape=[
            jax.ShapeDtypeStruct((owners, experts * width, experts * width), jnp.bfloat16),
            jax.ShapeDtypeStruct((owners, DOC_ROWS, LANES), jnp.int32),
        ],
        compiler_params=pltpu.CompilerParams(vmem_limit_bytes=40 * MIB),
        cost_estimate=cost(1.3),
    )(shared)


def condition_kernel(
    own_ref, near_ref, far_ref, routes_ref, weights_ref, payload_ref, value_ref, name_ref, *, top, width
):
    quarter = routes_ref.shape[0]
    groups, dense_width, _ = weights_ref.shape
    shares = payload_ref.shape[0] // groups
    experts = dense_width // width
    first = low_lanes(quarter, width)
    second = 1 - first.astype(jnp.int32)

    def summed(start, size):
        rows = slice(start, start + size)
        total = own_ref[1, rows, :].astype(jnp.float32) + near_ref[0, rows, :].astype(jnp.float32)
        return total + far_ref[rows, :].astype(jnp.float32)

    for pair in range(top // 2):
        both = summed(pair * quarter, quarter)
        swapped = pltpu.roll(both, width, 1)
        value_ref[2 * pair] = jnp.where(first, both, swapped)
        value_ref[2 * pair + 1] = jnp.where(first, swapped, both)
    for k in range(top):
        name_ref[k] = jnp.broadcast_to(routes_ref[:, k : k + 1], (quarter, LANES)) - second
    def one_group(step, carry):
        group = jnp.bitwise_xor(lax.axis_index("expert"), step)
        dense = []
        for pair in range(experts // 2):
            base = group * experts + 2 * pair
            chosen = jnp.zeros((quarter, LANES), jnp.float32)
            for k in range(top):
                chosen = jnp.where(name_ref[k] == base, value_ref[k], chosen)
            dense.append(chosen.astype(jnp.bfloat16))
        result = jnp.dot(
            jnp.concatenate(dense, axis=1), weights_ref[step], preferred_element_type=jnp.float32
        ).astype(jnp.bfloat16)
        share_width = result.shape[1] // shares
        for share in range(shares):
            payload_ref[group * shares + share] = result[:, share * share_width : (share + 1) * share_width]
        return carry

    lax.fori_loop(0, groups, one_group, 0, unroll=groups <= 4)


def condition(own, near, far, quarter_routes, weights, shares, width):
    quarter, top = quarter_routes.shape
    groups = weights.shape[0]
    return pl.pallas_call(
        functools.partial(condition_kernel, top=top, width=width),
        in_specs=[VMEM] * 5,
        out_shape=jax.ShapeDtypeStruct((groups * shares, quarter, LANES), jnp.bfloat16),
        scratch_shapes=[
            pltpu.VMEM((top, quarter, LANES), jnp.float32),
            pltpu.VMEM((top, quarter, LANES), jnp.int32),
        ],
        compiler_params=pltpu.CompilerParams(vmem_limit_bytes=40 * MIB),
        cost_estimate=cost(2),
    )(own, near, far, quarter_routes, weights)


def query_kernel(query_ref, inverse_ref, out_hbm, factor_ref, spread_ref, wide_ref, out_ref, sems):
    count, experts, _ = query_ref.shape
    width = inverse_ref.shape[1]
    step = pl.program_id(0)
    rows = out_ref.shape[0] // width
    pitch = wide_ref.shape[1] // width

    @pl.when(step == 0)
    def _():
        zeros = jnp.zeros((width, width), jnp.bfloat16)
        for e in range(experts):
            high, low = split(inverse_ref[e])
            left = jnp.concatenate([high, zeros, low, zeros], axis=0)
            right = jnp.concatenate([zeros, high, zeros, low], axis=0)
            factor_ref[e] = jnp.concatenate([left, right], axis=1)

    spread_ref[...] = query_ref[...].astype(jnp.float32).reshape(count * experts, LANES)
    for e in range(experts):
        query = spread_ref[pl.ds(e, count, stride=experts), :].astype(jnp.bfloat16)
        result = lax.dot_general(
            factor_ref[e], query, (((1,), (1,)), ((), ())), preferred_element_type=jnp.float32
        )
        result = result[: 2 * width] + result[2 * width :]
        start = e * (rows // experts) + 2 * step
        for tile in range(wide_ref.shape[0]):
            part = result[:, tile * LANES : (tile + 1) * LANES]
            wide_ref[tile, pl.ds(start, width, stride=pitch), :] = part[:width]
            wide_ref[tile, pl.ds(start + 1, width, stride=pitch), :] = part[width:]

    @pl.when(step == pl.num_programs(0) - 1)
    def _():
        copies = []
        for part in range(sems.shape[0]):
            first = part * (width // sems.shape[0])
            for j in range(first, first + width // sems.shape[0]):
                for tile in range(wide_ref.shape[0]):
                    out_ref[j * rows : (j + 1) * rows, tile * LANES : (tile + 1) * LANES] = wide_ref[
                        tile, j * pitch : j * pitch + rows, :
                    ].astype(jnp.bfloat16)
            block = pl.ds(first * rows, width // sems.shape[0] * rows)
            copies.append(pltpu.make_async_copy(out_ref.at[block], out_hbm.at[block], sems.at[part]))
            copies[-1].start()
        for copy in copies:
            copy.wait()


def condition_queries(query_grads, inverse_in):
    count, experts, flat = query_grads.shape
    width = inverse_in.shape[1]
    rows = experts * flat
    return pl.pallas_call(
        query_kernel,
        grid=(flat // LANES,),
        in_specs=[
            pl.BlockSpec((count, experts, LANES), lambda c: (0, 0, c)),
            pl.BlockSpec(inverse_in.shape, lambda c: (0, 0, 0)),
        ],
        out_specs=HBM,
        out_shape=pltpu.HBM((rows, count), jnp.bfloat16),
        scratch_shapes=[
            pltpu.VMEM((experts, 4 * width, 2 * width), jnp.bfloat16),
            pltpu.VMEM((count * experts, LANES), jnp.float32),
            pltpu.VMEM((count // LANES, rows + 8 * width, LANES), jnp.float32),
            pltpu.VMEM((rows, count), jnp.bfloat16),
            pltpu.SemaphoreType.DMA((4,)),
        ],
        compiler_params=pltpu.CompilerParams(vmem_limit_bytes=40 * MIB),
        cost_estimate=cost(10),
    )(stay(query_grads), inverse_in)


def score_kernel(
    arrived_ref, inner_ref, docs_ref, far_ref, out_ref, grads_ref, queries_ref, sem, *, width, doc_count, turns
):
    fetch = pltpu.make_async_copy(far_ref, queries_ref, sem)
    fetch.start()
    sources, quarter, lanes = arrived_ref.shape
    shares = lax.axis_size("proj")
    owners = sources // shares
    outer, inner, docs = [], [], []
    for entry, (owner_turn, share_turn) in enumerate(turns):
        owner = jnp.bitwise_xor(lax.axis_index("expert"), owner_turn)
        share = jnp.bitwise_xor(lax.axis_index("proj"), share_turn)
        outer.append(arrived_ref[owner * shares + share])
        docs.append(docs_ref[owner, pl.ds(share, 1), :])
        inner.append(inner_ref[entry])
    outer = jnp.concatenate(outer, axis=0)
    inner = jnp.concatenate(inner, axis=1)
    docs = jnp.broadcast_to(jnp.concatenate(docs, axis=1), inner.shape)
    doc_group = 16
    pitch = grads_ref.shape[0] // doc_count

    def one_group(group, carry):
        masked = [
            jnp.where(docs == group * doc_group + d, inner, jnp.zeros_like(inner)) for d in range(doc_group)
        ]
        sums = jnp.dot(jnp.concatenate(masked, axis=0), outer, preferred_element_type=jnp.float32)
        for d in range(doc_group):
            start = pl.multiple_of((group * doc_group + d) * pitch, 8)
            grads_ref[pl.ds(start, width), :] = sums[d * width : (d + 1) * width]
        return carry

    lax.fori_loop(0, doc_count // doc_group, one_group, 0, unroll=doc_count <= 2 * doc_group)
    high, low = [], []
    for j in range(width):
        parts = split(grads_ref[pl.ds(j, doc_count, stride=pitch), :])
        high.append(parts[0])
        low.append(parts[1])
    flat = jnp.concatenate([jnp.concatenate(high, axis=1), jnp.concatenate(low, axis=1)], axis=0)
    fetch.wait()
    result = jnp.dot(flat, queries_ref[...], preferred_element_type=jnp.float32)
    result = result[:doc_count] + result[doc_count:]
    columns = result.shape[1] // shares
    fill = jnp.zeros((DOC_DEV, LANES - columns), jnp.float32)
    for owner in range(owners):
        for share in range(shares):
            piece = result[owner * DOC_DEV : (owner + 1) * DOC_DEV, share * columns : (share + 1) * columns]
            out_ref[owner * shares + share] = jnp.concatenate([piece, fill], axis=1)


def score(arrived, inner, docs, queries, turns):
    sources = arrived.shape[0]
    width = inner.shape[1]
    doc_count = DOC_DEV * docs.shape[0]
    return pl.pallas_call(
        functools.partial(score_kernel, width=width, doc_count=doc_count, turns=turns),
        in_specs=[VMEM, VMEM, VMEM, HBM],
        out_shape=jax.ShapeDtypeStruct((sources, DOC_DEV, LANES), jnp.float32),
        scratch_shapes=[
            pltpu.VMEM((doc_count * (width + 8), arrived.shape[2]), jnp.float32),
            pltpu.VMEM(queries.shape, jnp.bfloat16),
            pltpu.SemaphoreType.DMA,
        ],
        compiler_params=pltpu.CompilerParams(vmem_limit_bytes=40 * MIB),
        cost_estimate=cost(5),
    )(arrived, inner, docs, stay(queries))


def sum_kernel(pieces_ref, out_ref):
    total = pieces_ref[0]
    for source in range(1, pieces_ref.shape[0]):
        total = total + pieces_ref[source]
    out_ref[...] = total[:, : out_ref.shape[1]]


def sum_pieces(pieces, columns):
    return pl.pallas_call(
        sum_kernel,
        in_specs=[VMEM],
        out_shape=jax.ShapeDtypeStruct((pieces.shape[1], columns), jnp.float32),
        compiler_params=pltpu.CompilerParams(vmem_limit_bytes=40 * MIB),
    )(pieces)


def exchange(block, axis, size, turn):
    return lax.ppermute(block, axis, [(i, i ^ turn) for i in range(size)])


def double(blocks, turns, axis, size, turn):
    blocks = jnp.concatenate([blocks, exchange(blocks, axis, size, turn)], axis=0)
    return blocks, turns + tuple(t ^ turn for t in turns)


def local(
    activations,
    grad_hidden,
    routes,
    doc_ids,
    query_grads,
    in_projection,
    out_projection,
    inverse_in,
    inverse_out,
):
    tokens, top = routes.shape
    experts, width, _ = inverse_in.shape
    owners = lax.axis_size("expert")
    shares = lax.axis_size("proj")
    quarter = tokens // shares
    assert quarter == LANES and 2 * width == LANES and experts * width // shares == LANES
    assert shares == 4 and owners & (owners - 1) == 0
    assert DOC_DEV * owners <= 256

    flat_hidden = grad_hidden.reshape(tokens * top, grad_hidden.shape[2])
    inner_leaving, inner_own, shared = project_inner(
        activations, in_projection, inverse_out, doc_ids.reshape(shares, quarter), shares
    )
    inner_first = exchange(inner_leaving, "proj", shares, 2)
    far_shared = exchange(shared, "expert", owners, owners // 2)
    leaving, own = project_outer(flat_hidden, out_projection, shares, top)
    far_shared, inner_first, leaving = lax.optimization_barrier((far_shared, inner_first, leaving))
    near = exchange(leaving, "proj", shares, 1)
    shared, turns = jnp.stack([shared, far_shared]), (0, owners // 2)
    for bit in reversed(range((owners // 2).bit_length() - 1)):
        shared, turns = double(shared, turns, "expert", owners, 1 << bit)
    inner_second = exchange(combine(combine_inner_kernel, inner_own, inner_first), "proj", shares, 1)
    sent = combine(combine_outer_kernel, own, near)
    far = exchange(sent, "proj", shares, 2)
    inner = finish_inner(inner_own, inner_first, inner_second, width)
    inner, _ = lax.optimization_barrier((inner, sent))
    owner_turns = tuple(reversed(range(owners)))
    arriving = [exchange(inner, "expert", owners, turn) for turn in owner_turns if turn]
    weights, all_docs = expand(shared, turns, width, experts, shares)
    far, weights = lax.optimization_barrier((far, weights))
    quarter_routes = lax.dynamic_slice_in_dim(routes, lax.axis_index("proj") * quarter, quarter, 0)
    payload = condition(own, near, far, quarter_routes, weights, shares, width)
    payload, arriving = lax.optimization_barrier((payload, arriving))
    arrived = lax.all_to_all(payload, ("expert", "proj"), 0, 0, tiled=True)
    inner = jnp.stack(arriving + [inner])
    inner, share_turns = inner[None], (0,)
    inner, share_turns = double(inner, share_turns, "proj", shares, 1)
    inner, query_grads = lax.optimization_barrier((inner, query_grads))
    inner, share_turns = double(inner, share_turns, "proj", shares, 2)
    inner = inner.reshape(owners * shares, width, quarter)
    all_turns = tuple((o, p) for p in share_turns for o in owner_turns)
    queries = condition_queries(query_grads, inverse_in)
    pieces = score(arrived, inner, all_docs, queries, all_turns)
    pieces = lax.all_to_all(pieces, ("expert", "proj"), 0, 0, tiled=True)
    return sum_pieces(pieces, query_grads.shape[0] // shares).T


def solution(mesh):
    in_specs = (
        P(("groups", "expert"), "proj"),
        P(("groups", "expert"), None, "proj"),
        P(("groups", "expert"), None),
        P(("groups", "expert")),
        P(None, "expert", "proj"),
        P(None, "proj"),
        P(None, "proj"),
        P("expert", None, None),
        P("expert", None, None),
    )
    out_specs = P("proj", ("groups", "expert"))
    return jax.shard_map(local, mesh=mesh, in_specs=in_specs, out_specs=out_specs, check_vma=False)
```

```python
import functools

import jax
import jax.numpy as jnp
from jax import lax
from jax.experimental import pallas as pl
from jax.experimental.pallas import tpu as pltpu
from jax.sharding import PartitionSpec as P

DOC_DEV = 8
LANES = 128
DOC_ROWS = 16
MIB = 1024 * 1024
VMEM = pl.BlockSpec(memory_space=pltpu.VMEM)
HBM = pl.BlockSpec(memory_space=pltpu.HBM)


def low_lanes(rows, width):
    return lax.broadcasted_iota(jnp.int32, (rows, LANES), 1) < width


def stay(array):
    return pltpu.with_memory_space_constraint(array, pltpu.HBM)


def split(value):
    high = value.astype(jnp.bfloat16)
    return high, (value - high.astype(jnp.float32)).astype(jnp.bfloat16)


def cost(microseconds):
    return pl.CostEstimate(flops=0, bytes_accessed=int(microseconds * 3.3e6), transcendentals=0)


def in_order(copies, ahead):
    for copy in copies[:ahead]:
        copy.start()
    state = [0]

    def take():
        copies[state[0]].wait()
        if state[0] + ahead < len(copies):
            copies[state[0] + ahead].start()
        state[0] += 1

    return take


def inner_kernel(
    act_hbm, in_proj_hbm, inverse_hbm, leaving_ref, own_ref, shared_ref, act_ref, in_proj_ref, inverse_ref, sems
):
    turns = (2, 3, 1, 0)
    quarter = act_ref.shape[1]
    width = in_proj_ref.shape[0]
    half = quarter // 2
    place = lax.axis_index("proj")
    pairs = [(in_proj_hbm, in_proj_ref)]
    for g, turn in enumerate(turns):
        rows = pl.ds(pl.multiple_of(jnp.bitwise_xor(place, turn) * quarter, quarter), quarter)
        pairs.append((act_hbm.at[rows], act_ref.at[g]))
        if g == 0:
            pairs.append((inverse_hbm, inverse_ref))
    take = in_order([pltpu.make_async_copy(*pair, sems.at[i]) for i, pair in enumerate(pairs)], 5)
    take()
    first = low_lanes(half, width)
    for wire_ref in (leaving_ref, own_ref):
        take()
        if wire_ref is leaving_ref:
            take()
            experts = inverse_ref.shape[0] // 2
            for e in range(experts):
                pair = jnp.concatenate([inverse_ref[e], inverse_ref[experts + e]], axis=1)
                shared_ref[e * width : (e + 1) * width, :] = pair.astype(jnp.bfloat16)
        take()
        twice = jnp.concatenate([in_proj_ref[...], in_proj_ref[...]], axis=0)
        g = 0 if wire_ref is leaving_ref else 2
        rows = act_ref[g : g + 2].reshape(2 * quarter, act_ref.shape[2])
        inner = lax.dot_general(rows, twice, (((1,), (1,)), ((), ())), preferred_element_type=jnp.float32)
        for i in range(2):
            start = i * quarter
            high, low = split(jnp.where(first, inner[start : start + half], inner[start + half : start + quarter]))
            wire_ref[i, :half, :] = high
            wire_ref[i, half:, :] = low


def project_inner(activations, in_projection, inverse_out, quarters):
    tokens, model = activations.shape
    quarter = tokens // quarters
    experts, width, _ = inverse_out.shape
    wire = jax.ShapeDtypeStruct((quarters // 2, quarter, LANES), jnp.bfloat16)
    fixed = (in_projection, inverse_out)
    return pl.pallas_call(
        inner_kernel,
        in_specs=[HBM] * 3,
        out_specs=[VMEM] * 3,
        out_shape=[wire, wire, jax.ShapeDtypeStruct((experts // 2 * width, LANES), jnp.bfloat16)],
        scratch_shapes=[pltpu.VMEM((quarters, quarter, model), jnp.bfloat16)]
        + [pltpu.VMEM(array.shape, array.dtype) for array in fixed]
        + [pltpu.SemaphoreType.DMA((quarters + len(fixed),))],
        compiler_params=pltpu.CompilerParams(vmem_limit_bytes=40 * MIB),
        cost_estimate=cost(2.5),
    )(*[stay(array) for array in (activations, *fixed)])


def outer_kernel(hidden_hbm, out_proj_hbm, leaving_ref, own_ref, hidden_ref, out_proj_ref, rows_ref, sems, *, top):
    turns = (1, 3, 2, 0)
    chunks, chunk_rows, _ = hidden_ref.shape
    chunk = chunk_rows // top
    split_by = chunks // len(turns)
    quarter = chunk * split_by
    width = out_proj_ref.shape[0]
    place = lax.axis_index("proj")
    pairs = [(out_proj_hbm, out_proj_ref)]
    for i in range(chunks):
        start = (jnp.bitwise_xor(place, turns[i // split_by]) * split_by + i % split_by) * chunk_rows
        pairs.append((hidden_hbm.at[pl.ds(pl.multiple_of(start, chunk_rows), chunk_rows)], hidden_ref.at[i]))
    take = in_order([pltpu.make_async_copy(*pair, sems.at[i]) for i, pair in enumerate(pairs)], 3)
    take()
    first = low_lanes(chunk, width)

    def pack_rows(i):
        g, part = i // split_by, i % split_by
        wire_ref = leaving_ref.at[g] if g < 2 else own_ref.at[g - 2]
        for pair in range(top // 2):
            even = rows_ref[i % 2, pl.ds(2 * pair, chunk, stride=top), :]
            odd = rows_ref[i % 2, pl.ds(2 * pair + 1, chunk, stride=top), :]
            start = pair * quarter + part * chunk
            wire_ref[start : start + chunk, :] = jnp.where(first, even, odd).astype(jnp.bfloat16)

    for i in range(chunks):
        take()
        twice = jnp.concatenate([out_proj_ref[...], out_proj_ref[...]], axis=0)
        rows_ref[i % 2] = lax.dot_general(
            hidden_ref[i], twice, (((1,), (1,)), ((), ())), preferred_element_type=jnp.float32
        )
        if i:
            pack_rows(i - 1)
    pack_rows(chunks - 1)


def project_outer(flat_hidden, out_projection, quarters, top):
    rows, hidden = flat_hidden.shape
    chunks = quarters
    wire = jax.ShapeDtypeStruct((quarters // 2, rows // quarters // 2, LANES), jnp.bfloat16)
    return pl.pallas_call(
        functools.partial(outer_kernel, top=top),
        in_specs=[HBM] * 2,
        out_specs=[VMEM] * 2,
        out_shape=[wire, wire],
        scratch_shapes=[
            pltpu.VMEM((chunks, rows // chunks, hidden), jnp.bfloat16),
            pltpu.VMEM(out_projection.shape, out_projection.dtype),
            pltpu.VMEM((2, rows // chunks, LANES), jnp.float32),
            pltpu.SemaphoreType.DMA((chunks + 1,)),
        ],
        compiler_params=pltpu.CompilerParams(vmem_limit_bytes=40 * MIB),
        cost_estimate=cost(4),
    )(stay(flat_hidden), stay(out_projection))


def exact_rows(rows):
    half = rows.shape[0] // 2
    return rows[:half].astype(jnp.float32) + rows[half:].astype(jnp.float32)


def combine_inner_kernel(own_ref, near_ref, out_ref):
    high, low = split(exact_rows(own_ref[0]) + exact_rows(near_ref[1]))
    out_ref[: high.shape[0], :] = high
    out_ref[high.shape[0] :, :] = low


def combine_outer_kernel(own_ref, near_ref, out_ref):
    out_ref[...] = (own_ref[0].astype(jnp.float32) + near_ref[1].astype(jnp.float32)).astype(jnp.bfloat16)


def combine(kernel, own, near):
    return pl.pallas_call(
        kernel,
        in_specs=[VMEM, VMEM],
        out_shape=jax.ShapeDtypeStruct(own.shape[1:], jnp.bfloat16),
        compiler_params=pltpu.CompilerParams(vmem_limit_bytes=40 * MIB),
        cost_estimate=cost(0.5),
    )(own, near)


def finish_inner_kernel(own_ref, first_ref, second_ref, docs_ref, out_ref):
    total = exact_rows(own_ref[1]) + exact_rows(first_ref[0]) + exact_rows(second_ref[...])
    width = out_ref.shape[0] - DOC_ROWS
    total = jnp.concatenate([total[:, :width], total[:, width:]], axis=0)
    out_ref[:width, :] = jnp.transpose(total).astype(jnp.bfloat16)
    docs = docs_ref[pl.ds(lax.axis_index("proj"), 1), :].astype(jnp.float32)
    out_ref[width:, :] = jnp.broadcast_to(docs, (DOC_ROWS, LANES)).astype(jnp.bfloat16)


def finish_inner(own, first, second, doc_rows, width):
    return pl.pallas_call(
        finish_inner_kernel,
        in_specs=[VMEM] * 4,
        out_shape=jax.ShapeDtypeStruct((width + DOC_ROWS, own.shape[1]), jnp.bfloat16),
        compiler_params=pltpu.CompilerParams(vmem_limit_bytes=40 * MIB),
        cost_estimate=cost(0.5),
    )(own, first, second, doc_rows)


def expand_kernel(shared_ref, weights_ref, *, width, experts, shares, turns):
    columns = experts * width
    share_rows = width // shares
    half = experts // 2
    lane = lax.broadcasted_iota(jnp.int32, (LANES, columns), 1)
    row = lax.broadcasted_iota(jnp.int32, (LANES, columns), 0)
    source = lane // (experts * share_rows) * share_rows + lane % share_rows
    expert_lane = lax.broadcasted_iota(jnp.int32, (half * width, columns), 1) // share_rows % experts
    expert_row = lax.broadcasted_iota(jnp.int32, (half * width, columns), 0) // width
    for side in range(2):
        spread = (row == source + side * width).astype(jnp.float32).astype(jnp.bfloat16)
        own = expert_lane == expert_row + side * half
        for entry, turn in enumerate(turns):
            placed = jnp.dot(
                shared_ref[entry], spread, preferred_element_type=jnp.float32
            )
            weights_ref[turn, side * half * width : (side + 1) * half * width, :] = jnp.where(
                own, placed, 0.0
            ).astype(jnp.bfloat16)


def expand(shared, turns, width, experts, shares):
    owners = shared.shape[0]
    return pl.pallas_call(
        functools.partial(expand_kernel, width=width, experts=experts, shares=shares, turns=turns),
        in_specs=[VMEM],
        out_shape=jax.ShapeDtypeStruct((owners, experts * width, experts * width), jnp.bfloat16),
        compiler_params=pltpu.CompilerParams(vmem_limit_bytes=40 * MIB),
        cost_estimate=cost(1.3),
    )(shared)


def condition_kernel(
    own_ref, near_ref, far_ref, routes_ref, weights_ref, payload_ref, value_ref, name_ref, *, top, width
):
    quarter = routes_ref.shape[0]
    groups, dense_width, _ = weights_ref.shape
    shares = payload_ref.shape[0] // groups
    experts = dense_width // width
    first = low_lanes(quarter, width)
    second = 1 - first.astype(jnp.int32)

    def summed(start, size):
        rows = slice(start, start + size)
        total = own_ref[1, rows, :].astype(jnp.float32) + near_ref[0, rows, :].astype(jnp.float32)
        return total + far_ref[rows, :].astype(jnp.float32)

    for pair in range(top // 2):
        both = summed(pair * quarter, quarter)
        swapped = pltpu.roll(both, width, 1)
        value_ref[2 * pair] = jnp.where(first, both, swapped)
        value_ref[2 * pair + 1] = jnp.where(first, swapped, both)
    for k in range(top):
        name_ref[k] = jnp.broadcast_to(routes_ref[:, k : k + 1], (quarter, LANES)) - second
    def one_group(step, carry):
        group = jnp.bitwise_xor(lax.axis_index("expert"), step)
        dense = []
        for pair in range(experts // 2):
            base = group * experts + 2 * pair
            chosen = jnp.zeros((quarter, LANES), jnp.float32)
            for k in range(top):
                chosen = jnp.where(name_ref[k] == base, value_ref[k], chosen)
            dense.append(chosen.astype(jnp.bfloat16))
        result = jnp.dot(
            jnp.concatenate(dense, axis=1), weights_ref[step], preferred_element_type=jnp.float32
        ).astype(jnp.bfloat16)
        share_width = result.shape[1] // shares
        for share in range(shares):
            payload_ref[group * shares + share] = result[:, share * share_width : (share + 1) * share_width]
        return carry

    lax.fori_loop(0, groups, one_group, 0, unroll=groups <= 4)


def condition(own, near, far, quarter_routes, weights, shares, width):
    quarter, top = quarter_routes.shape
    groups = weights.shape[0]
    return pl.pallas_call(
        functools.partial(condition_kernel, top=top, width=width),
        in_specs=[VMEM] * 5,
        out_shape=jax.ShapeDtypeStruct((groups * shares, quarter, LANES), jnp.bfloat16),
        scratch_shapes=[
            pltpu.VMEM((top, quarter, LANES), jnp.float32),
            pltpu.VMEM((top, quarter, LANES), jnp.int32),
        ],
        compiler_params=pltpu.CompilerParams(vmem_limit_bytes=40 * MIB),
        cost_estimate=cost(2),
    )(own, near, far, quarter_routes, weights)


def query_kernel(query_ref, inverse_ref, out_hbm, factor_ref, spread_ref, wide_ref, out_ref, sems):
    count, experts, _ = query_ref.shape
    width = inverse_ref.shape[1]
    step = pl.program_id(0)
    rows = out_ref.shape[0] // width
    pitch = wide_ref.shape[1] // width

    @pl.when(step == 0)
    def _():
        zeros = jnp.zeros((width, width), jnp.bfloat16)
        for e in range(experts):
            high, low = split(inverse_ref[e])
            left = jnp.concatenate([high, zeros, low, zeros], axis=0)
            right = jnp.concatenate([zeros, high, zeros, low], axis=0)
            factor_ref[e] = jnp.concatenate([left, right], axis=1)

    spread_ref[...] = query_ref[...].astype(jnp.float32).reshape(count * experts, LANES)
    for e in range(experts):
        query = spread_ref[pl.ds(e, count, stride=experts), :].astype(jnp.bfloat16)
        result = lax.dot_general(
            factor_ref[e], query, (((1,), (1,)), ((), ())), preferred_element_type=jnp.float32
        )
        result = result[: 2 * width] + result[2 * width :]
        start = e * (rows // experts) + 2 * step
        for tile in range(wide_ref.shape[0]):
            part = result[:, tile * LANES : (tile + 1) * LANES]
            wide_ref[tile, pl.ds(start, width, stride=pitch), :] = part[:width]
            wide_ref[tile, pl.ds(start + 1, width, stride=pitch), :] = part[width:]

    @pl.when(step == pl.num_programs(0) - 1)
    def _():
        copies = []
        for part in range(sems.shape[0]):
            first = part * (width // sems.shape[0])
            for j in range(first, first + width // sems.shape[0]):
                for tile in range(wide_ref.shape[0]):
                    out_ref[j * rows : (j + 1) * rows, tile * LANES : (tile + 1) * LANES] = wide_ref[
                        tile, j * pitch : j * pitch + rows, :
                    ].astype(jnp.bfloat16)
            block = pl.ds(first * rows, width // sems.shape[0] * rows)
            copies.append(pltpu.make_async_copy(out_ref.at[block], out_hbm.at[block], sems.at[part]))
            copies[-1].start()
        for copy in copies:
            copy.wait()


def condition_queries(query_grads, inverse_in):
    count, experts, flat = query_grads.shape
    width = inverse_in.shape[1]
    rows = experts * flat
    return pl.pallas_call(
        query_kernel,
        grid=(flat // LANES,),
        in_specs=[
            pl.BlockSpec((count, experts, LANES), lambda c: (0, 0, c)),
            pl.BlockSpec(inverse_in.shape, lambda c: (0, 0, 0)),
        ],
        out_specs=HBM,
        out_shape=pltpu.HBM((rows, count), jnp.bfloat16),
        scratch_shapes=[
            pltpu.VMEM((experts, 4 * width, 2 * width), jnp.bfloat16),
            pltpu.VMEM((count * experts, LANES), jnp.float32),
            pltpu.VMEM((count // LANES, rows + 8 * width, LANES), jnp.float32),
            pltpu.VMEM((rows, count), jnp.bfloat16),
            pltpu.SemaphoreType.DMA((4,)),
        ],
        compiler_params=pltpu.CompilerParams(vmem_limit_bytes=40 * MIB),
        cost_estimate=cost(10),
    )(stay(query_grads), inverse_in)


def score_kernel(
    arrived_ref, inner_ref, far_ref, out_ref, grads_ref, queries_ref, sem, *, width, doc_count, turns
):
    fetch = pltpu.make_async_copy(far_ref, queries_ref, sem)
    fetch.start()
    sources, quarter, lanes = arrived_ref.shape
    shares = lax.axis_size("proj")
    owners = sources // shares
    outer, inner, docs = [], [], []
    for entry, (owner_turn, share_turn) in enumerate(turns):
        owner = jnp.bitwise_xor(lax.axis_index("expert"), owner_turn)
        share = jnp.bitwise_xor(lax.axis_index("proj"), share_turn)
        outer.append(arrived_ref[owner * shares + share])
        docs.append(inner_ref[entry, width : width + 1, :].astype(jnp.float32).astype(jnp.int32))
        inner.append(inner_ref[entry, :width, :])
    outer = jnp.concatenate(outer, axis=0)
    inner = jnp.concatenate(inner, axis=1)
    docs = jnp.broadcast_to(jnp.concatenate(docs, axis=1), inner.shape)
    doc_group = 16
    pitch = grads_ref.shape[0] // doc_count

    def one_group(group, carry):
        masked = [
            jnp.where(docs == group * doc_group + d, inner, jnp.zeros_like(inner)) for d in range(doc_group)
        ]
        sums = jnp.dot(jnp.concatenate(masked, axis=0), outer, preferred_element_type=jnp.float32)
        for d in range(doc_group):
            start = pl.multiple_of((group * doc_group + d) * pitch, 8)
            grads_ref[pl.ds(start, width), :] = sums[d * width : (d + 1) * width]
        return carry

    lax.fori_loop(0, doc_count // doc_group, one_group, 0, unroll=doc_count <= 2 * doc_group)
    high, low = [], []
    for j in range(width):
        parts = split(grads_ref[pl.ds(j, doc_count, stride=pitch), :])
        high.append(parts[0])
        low.append(parts[1])
    flat = jnp.concatenate([jnp.concatenate(high, axis=1), jnp.concatenate(low, axis=1)], axis=0)
    fetch.wait()
    result = jnp.dot(flat, queries_ref[...], preferred_element_type=jnp.float32)
    result = result[:doc_count] + result[doc_count:]
    columns = result.shape[1] // shares
    fill = jnp.zeros((DOC_DEV, LANES - columns), jnp.float32)
    for owner in range(owners):
        for share in range(shares):
            piece = result[owner * DOC_DEV : (owner + 1) * DOC_DEV, share * columns : (share + 1) * columns]
            out_ref[owner * shares + share] = jnp.concatenate([piece, fill], axis=1)


def score(arrived, inner, queries, turns, owners):
    sources = arrived.shape[0]
    width = inner.shape[1] - DOC_ROWS
    doc_count = DOC_DEV * owners
    return pl.pallas_call(
        functools.partial(score_kernel, width=width, doc_count=doc_count, turns=turns),
        in_specs=[VMEM, VMEM, HBM],
        out_shape=jax.ShapeDtypeStruct((sources, DOC_DEV, LANES), jnp.float32),
        scratch_shapes=[
            pltpu.VMEM((doc_count * (width + 8), arrived.shape[2]), jnp.float32),
            pltpu.VMEM(queries.shape, jnp.bfloat16),
            pltpu.SemaphoreType.DMA,
        ],
        compiler_params=pltpu.CompilerParams(vmem_limit_bytes=40 * MIB),
        cost_estimate=cost(5),
    )(arrived, inner, stay(queries))


def sum_kernel(pieces_ref, out_ref):
    total = pieces_ref[0]
    for source in range(1, pieces_ref.shape[0]):
        total = total + pieces_ref[source]
    out_ref[...] = total[:, : out_ref.shape[1]]


def sum_pieces(pieces, columns):
    return pl.pallas_call(
        sum_kernel,
        in_specs=[VMEM],
        out_shape=jax.ShapeDtypeStruct((pieces.shape[1], columns), jnp.float32),
        compiler_params=pltpu.CompilerParams(vmem_limit_bytes=40 * MIB),
    )(pieces)


def exchange(block, axis, size, turn):
    return lax.ppermute(block, axis, [(i, i ^ turn) for i in range(size)])


def double(blocks, turns, axis, size, turn):
    blocks = jnp.concatenate([blocks, exchange(blocks, axis, size, turn)], axis=0)
    return blocks, turns + tuple(t ^ turn for t in turns)


def local(
    activations,
    grad_hidden,
    routes,
    doc_ids,
    query_grads,
    in_projection,
    out_projection,
    inverse_in,
    inverse_out,
):
    tokens, top = routes.shape
    experts, width, _ = inverse_in.shape
    owners = lax.axis_size("expert")
    shares = lax.axis_size("proj")
    quarter = tokens // shares
    assert quarter == LANES and 2 * width == LANES and experts * width // shares == LANES
    assert shares == 4 and owners & (owners - 1) == 0
    assert DOC_DEV * owners <= 256

    flat_hidden = grad_hidden.reshape(tokens * top, grad_hidden.shape[2])
    inner_leaving, inner_own, shared = project_inner(activations, in_projection, inverse_out, shares)
    inner_first = exchange(inner_leaving, "proj", shares, 2)
    far_shared = exchange(shared, "expert", owners, owners // 2)
    leaving, own = project_outer(flat_hidden, out_projection, shares, top)
    far_shared, inner_first, leaving = lax.optimization_barrier((far_shared, inner_first, leaving))
    near = exchange(leaving, "proj", shares, 1)
    shared, turns = jnp.stack([shared, far_shared]), (0, owners // 2)
    for bit in reversed(range((owners // 2).bit_length() - 1)):
        shared, turns = double(shared, turns, "expert", owners, 1 << bit)
    inner_second = exchange(combine(combine_inner_kernel, inner_own, inner_first), "proj", shares, 1)
    sent = combine(combine_outer_kernel, own, near)
    far = exchange(sent, "proj", shares, 2)
    inner = finish_inner(inner_own, inner_first, inner_second, doc_ids.reshape(shares, quarter), width)
    inner, _ = lax.optimization_barrier((inner, sent))
    owner_turns = tuple(reversed(range(owners)))
    arriving = [exchange(inner, "expert", owners, turn) for turn in owner_turns if turn]
    weights = expand(shared, turns, width, experts, shares)
    far, weights = lax.optimization_barrier((far, weights))
    quarter_routes = lax.dynamic_slice_in_dim(routes, lax.axis_index("proj") * quarter, quarter, 0)
    payload = condition(own, near, far, quarter_routes, weights, shares, width)
    payload, arriving = lax.optimization_barrier((payload, arriving))
    arrived = lax.all_to_all(payload, ("expert", "proj"), 0, 0, tiled=True)
    inner = jnp.stack(arriving + [inner])
    inner, share_turns = inner[None], (0,)
    inner, share_turns = double(inner, share_turns, "proj", shares, 1)
    inner, query_grads = lax.optimization_barrier((inner, query_grads))
    inner, share_turns = double(inner, share_turns, "proj", shares, 2)
    inner = inner.reshape(owners * shares, width + DOC_ROWS, quarter)
    all_turns = tuple((o, p) for p in share_turns for o in owner_turns)
    queries = condition_queries(query_grads, inverse_in)
    pieces = score(arrived, inner, queries, all_turns, owners)
    pieces = lax.all_to_all(pieces, ("expert", "proj"), 0, 0, tiled=True)
    return sum_pieces(pieces, query_grads.shape[0] // shares).T


def solution(mesh):
    in_specs = (
        P(("groups", "expert"), "proj"),
        P(("groups", "expert"), None, "proj"),
        P(("groups", "expert"), None),
        P(("groups", "expert")),
        P(None, "expert", "proj"),
        P(None, "proj"),
        P(None, "proj"),
        P("expert", None, None),
        P("expert", None, None),
    )
    out_specs = P("proj", ("groups", "expert"))
    return jax.shard_map(local, mesh=mesh, in_specs=in_specs, out_specs=out_specs, check_vma=False)
```

```python
import functools

import jax
import jax.numpy as jnp
from jax import lax
from jax.experimental import pallas as pl
from jax.experimental.pallas import tpu as pltpu
from jax.sharding import PartitionSpec as P

DOC_DEV = 8
LANES = 128
DOC_ROWS = 16
MIB = 1024 * 1024
VMEM = pl.BlockSpec(memory_space=pltpu.VMEM)
HBM = pl.BlockSpec(memory_space=pltpu.HBM)


def low_lanes(rows, width):
    return lax.broadcasted_iota(jnp.int32, (rows, LANES), 1) < width


def stay(array):
    return pltpu.with_memory_space_constraint(array, pltpu.HBM)


def listed(owner, owners):
    return (owner + owners // 2) % owners


def send_to_all(blocks, owners, shares):
    members = [(i + owners // 2 * shares) % (owners * shares) for i in range(owners * shares)]
    return lax.all_to_all(blocks, ("expert", "proj"), 0, 0, tiled=True, axis_index_groups=[members])


def split(value):
    high = value.astype(jnp.bfloat16)
    return high, (value - high.astype(jnp.float32)).astype(jnp.bfloat16)


def cost(microseconds):
    return pl.CostEstimate(flops=0, bytes_accessed=int(microseconds * 3.3e6), transcendentals=0)


def in_order(copies, ahead):
    for copy in copies[:ahead]:
        copy.start()
    state = [0]

    def take():
        copies[state[0]].wait()
        if state[0] + ahead < len(copies):
            copies[state[0] + ahead].start()
        state[0] += 1

    return take


def inner_kernel(
    act_hbm, in_proj_hbm, inverse_hbm, leaving_ref, own_ref, shared_ref, act_ref, in_proj_ref, inverse_ref, sems
):
    turns = (2, 3, 1, 0)
    quarter = act_ref.shape[1]
    width = in_proj_ref.shape[0]
    half = quarter // 2
    place = lax.axis_index("proj")
    pairs = [(in_proj_hbm, in_proj_ref)]
    for g, turn in enumerate(turns):
        rows = pl.ds(pl.multiple_of(jnp.bitwise_xor(place, turn) * quarter, quarter), quarter)
        pairs.append((act_hbm.at[rows], act_ref.at[g]))
        if g == 0:
            pairs.append((inverse_hbm, inverse_ref))
    take = in_order([pltpu.make_async_copy(*pair, sems.at[i]) for i, pair in enumerate(pairs)], 5)
    take()
    first = low_lanes(half, width)
    for wire_ref in (leaving_ref, own_ref):
        take()
        if wire_ref is leaving_ref:
            take()
            experts = inverse_ref.shape[0] // 2
            for e in range(experts):
                pair = jnp.concatenate([inverse_ref[e], inverse_ref[experts + e]], axis=1)
                shared_ref[e * width : (e + 1) * width, :] = pair.astype(jnp.bfloat16)
        take()
        twice = jnp.concatenate([in_proj_ref[...], in_proj_ref[...]], axis=0)
        g = 0 if wire_ref is leaving_ref else 2
        rows = act_ref[g : g + 2].reshape(2 * quarter, act_ref.shape[2])
        inner = lax.dot_general(rows, twice, (((1,), (1,)), ((), ())), preferred_element_type=jnp.float32)
        for i in range(2):
            start = i * quarter
            high, low = split(jnp.where(first, inner[start : start + half], inner[start + half : start + quarter]))
            wire_ref[i, :half, :] = high
            wire_ref[i, half:, :] = low


def project_inner(activations, in_projection, inverse_out, quarters):
    tokens, model = activations.shape
    quarter = tokens // quarters
    experts, width, _ = inverse_out.shape
    wire = jax.ShapeDtypeStruct((quarters // 2, quarter, LANES), jnp.bfloat16)
    fixed = (in_projection, inverse_out)
    return pl.pallas_call(
        inner_kernel,
        in_specs=[HBM] * 3,
        out_specs=[VMEM] * 3,
        out_shape=[wire, wire, jax.ShapeDtypeStruct((experts // 2 * width, LANES), jnp.bfloat16)],
        scratch_shapes=[pltpu.VMEM((quarters, quarter, model), jnp.bfloat16)]
        + [pltpu.VMEM(array.shape, array.dtype) for array in fixed]
        + [pltpu.SemaphoreType.DMA((quarters + len(fixed),))],
        compiler_params=pltpu.CompilerParams(vmem_limit_bytes=40 * MIB),
        cost_estimate=cost(2.5),
    )(*[stay(array) for array in (activations, *fixed)])


def outer_kernel(hidden_hbm, out_proj_hbm, leaving_ref, own_ref, hidden_ref, out_proj_ref, rows_ref, sems, *, top):
    turns = (1, 3, 2, 0)
    chunks, chunk_rows, _ = hidden_ref.shape
    chunk = chunk_rows // top
    split_by = chunks // len(turns)
    quarter = chunk * split_by
    width = out_proj_ref.shape[0]
    place = lax.axis_index("proj")
    pairs = [(out_proj_hbm, out_proj_ref)]
    for i in range(chunks):
        start = (jnp.bitwise_xor(place, turns[i // split_by]) * split_by + i % split_by) * chunk_rows
        pairs.append((hidden_hbm.at[pl.ds(pl.multiple_of(start, chunk_rows), chunk_rows)], hidden_ref.at[i]))
    take = in_order([pltpu.make_async_copy(*pair, sems.at[i]) for i, pair in enumerate(pairs)], 3)
    take()
    first = low_lanes(chunk, width)

    def pack_rows(i):
        g, part = i // split_by, i % split_by
        wire_ref = leaving_ref.at[g] if g < 2 else own_ref.at[g - 2]
        for pair in range(top // 2):
            even = rows_ref[i % 2, pl.ds(2 * pair, chunk, stride=top), :]
            odd = rows_ref[i % 2, pl.ds(2 * pair + 1, chunk, stride=top), :]
            start = pair * quarter + part * chunk
            wire_ref[start : start + chunk, :] = jnp.where(first, even, odd).astype(jnp.bfloat16)

    for i in range(chunks):
        take()
        twice = jnp.concatenate([out_proj_ref[...], out_proj_ref[...]], axis=0)
        rows_ref[i % 2] = lax.dot_general(
            hidden_ref[i], twice, (((1,), (1,)), ((), ())), preferred_element_type=jnp.float32
        )
        if i:
            pack_rows(i - 1)
    pack_rows(chunks - 1)


def project_outer(flat_hidden, out_projection, quarters, top):
    rows, hidden = flat_hidden.shape
    chunks = quarters
    wire = jax.ShapeDtypeStruct((quarters // 2, rows // quarters // 2, LANES), jnp.bfloat16)
    return pl.pallas_call(
        functools.partial(outer_kernel, top=top),
        in_specs=[HBM] * 2,
        out_specs=[VMEM] * 2,
        out_shape=[wire, wire],
        scratch_shapes=[
            pltpu.VMEM((chunks, rows // chunks, hidden), jnp.bfloat16),
            pltpu.VMEM(out_projection.shape, out_projection.dtype),
            pltpu.VMEM((2, rows // chunks, LANES), jnp.float32),
            pltpu.SemaphoreType.DMA((chunks + 1,)),
        ],
        compiler_params=pltpu.CompilerParams(vmem_limit_bytes=40 * MIB),
        cost_estimate=cost(4),
    )(stay(flat_hidden), stay(out_projection))


def exact_rows(rows):
    half = rows.shape[0] // 2
    return rows[:half].astype(jnp.float32) + rows[half:].astype(jnp.float32)


def combine_inner_kernel(own_ref, near_ref, out_ref):
    high, low = split(exact_rows(own_ref[0]) + exact_rows(near_ref[1]))
    out_ref[: high.shape[0], :] = high
    out_ref[high.shape[0] :, :] = low


def combine_outer_kernel(own_ref, near_ref, out_ref):
    out_ref[...] = (own_ref[0].astype(jnp.float32) + near_ref[1].astype(jnp.float32)).astype(jnp.bfloat16)


def combine(kernel, own, near):
    return pl.pallas_call(
        kernel,
        in_specs=[VMEM, VMEM],
        out_shape=jax.ShapeDtypeStruct(own.shape[1:], jnp.bfloat16),
        compiler_params=pltpu.CompilerParams(vmem_limit_bytes=40 * MIB),
        cost_estimate=cost(0.5),
    )(own, near)


def finish_inner_kernel(own_ref, first_ref, second_ref, docs_ref, out_ref):
    total = exact_rows(own_ref[1]) + exact_rows(first_ref[0]) + exact_rows(second_ref[...])
    width = out_ref.shape[0] - DOC_ROWS
    total = jnp.concatenate([total[:, :width], total[:, width:]], axis=0)
    out_ref[:width, :] = jnp.transpose(total).astype(jnp.bfloat16)
    docs = docs_ref[pl.ds(lax.axis_index("proj"), 1), :].astype(jnp.float32)
    out_ref[width:, :] = jnp.broadcast_to(docs, (DOC_ROWS, LANES)).astype(jnp.bfloat16)


def finish_inner(own, first, second, doc_rows, width):
    return pl.pallas_call(
        finish_inner_kernel,
        in_specs=[VMEM] * 4,
        out_shape=jax.ShapeDtypeStruct((width + DOC_ROWS, own.shape[1]), jnp.bfloat16),
        compiler_params=pltpu.CompilerParams(vmem_limit_bytes=40 * MIB),
        cost_estimate=cost(0.5),
    )(own, first, second, doc_rows)


def expand_kernel(shared_ref, weights_ref, *, width, experts, shares, turns):
    columns = experts * width
    share_rows = width // shares
    half = experts // 2
    lane = lax.broadcasted_iota(jnp.int32, (LANES, columns), 1)
    row = lax.broadcasted_iota(jnp.int32, (LANES, columns), 0)
    source = lane // (experts * share_rows) * share_rows + lane % share_rows
    expert_lane = lax.broadcasted_iota(jnp.int32, (half * width, columns), 1) // share_rows % experts
    expert_row = lax.broadcasted_iota(jnp.int32, (half * width, columns), 0) // width
    for side in range(2):
        spread = (row == source + side * width).astype(jnp.float32).astype(jnp.bfloat16)
        own = expert_lane == expert_row + side * half
        for entry, turn in enumerate(turns):
            placed = jnp.dot(
                shared_ref[entry], spread, preferred_element_type=jnp.float32
            )
            weights_ref[turn, side * half * width : (side + 1) * half * width, :] = jnp.where(
                own, placed, 0.0
            ).astype(jnp.bfloat16)


def expand(shared, turns, width, experts, shares):
    owners = shared.shape[0]
    return pl.pallas_call(
        functools.partial(expand_kernel, width=width, experts=experts, shares=shares, turns=turns),
        in_specs=[VMEM],
        out_shape=jax.ShapeDtypeStruct((owners, experts * width, experts * width), jnp.bfloat16),
        compiler_params=pltpu.CompilerParams(vmem_limit_bytes=40 * MIB),
        cost_estimate=cost(1.3),
    )(shared)


def condition_kernel(
    own_ref, near_ref, far_ref, routes_ref, weights_ref, payload_ref, value_ref, name_ref, *, top, width
):
    quarter = routes_ref.shape[0]
    groups, dense_width, _ = weights_ref.shape
    shares = payload_ref.shape[0] // groups
    experts = dense_width // width
    first = low_lanes(quarter, width)
    second = 1 - first.astype(jnp.int32)

    def summed(start, size):
        rows = slice(start, start + size)
        total = own_ref[1, rows, :].astype(jnp.float32) + near_ref[0, rows, :].astype(jnp.float32)
        return total + far_ref[rows, :].astype(jnp.float32)

    for pair in range(top // 2):
        both = summed(pair * quarter, quarter)
        swapped = pltpu.roll(both, width, 1)
        value_ref[2 * pair] = jnp.where(first, both, swapped)
        value_ref[2 * pair + 1] = jnp.where(first, swapped, both)
    for k in range(top):
        name_ref[k] = jnp.broadcast_to(routes_ref[:, k : k + 1], (quarter, LANES)) - second
    def one_group(step, carry):
        group = jnp.bitwise_xor(lax.axis_index("expert"), step)
        dense = []
        for pair in range(experts // 2):
            base = group * experts + 2 * pair
            chosen = jnp.zeros((quarter, LANES), jnp.float32)
            for k in range(top):
                chosen = jnp.where(name_ref[k] == base, value_ref[k], chosen)
            dense.append(chosen.astype(jnp.bfloat16))
        result = jnp.dot(
            jnp.concatenate(dense, axis=1), weights_ref[step], preferred_element_type=jnp.float32
        ).astype(jnp.bfloat16)
        share_width = result.shape[1] // shares
        for share in range(shares):
            payload_ref[listed(group, groups) * shares + share] = result[:, share * share_width : (share + 1) * share_width]
        return carry

    lax.fori_loop(0, groups, one_group, 0, unroll=groups <= 4)


def condition(own, near, far, quarter_routes, weights, shares, width):
    quarter, top = quarter_routes.shape
    groups = weights.shape[0]
    return pl.pallas_call(
        functools.partial(condition_kernel, top=top, width=width),
        in_specs=[VMEM] * 5,
        out_shape=jax.ShapeDtypeStruct((groups * shares, quarter, LANES), jnp.bfloat16),
        scratch_shapes=[
            pltpu.VMEM((top, quarter, LANES), jnp.float32),
            pltpu.VMEM((top, quarter, LANES), jnp.int32),
        ],
        compiler_params=pltpu.CompilerParams(vmem_limit_bytes=40 * MIB),
        cost_estimate=cost(2),
    )(own, near, far, quarter_routes, weights)


def query_kernel(query_ref, inverse_ref, out_hbm, factor_ref, spread_ref, wide_ref, out_ref, sems):
    count, experts, _ = query_ref.shape
    width = inverse_ref.shape[1]
    step = pl.program_id(0)
    rows = out_ref.shape[0] // width
    pitch = wide_ref.shape[1] // width

    @pl.when(step == 0)
    def _():
        zeros = jnp.zeros((width, width), jnp.bfloat16)
        for e in range(experts):
            high, low = split(inverse_ref[e])
            left = jnp.concatenate([high, zeros, low, zeros], axis=0)
            right = jnp.concatenate([zeros, high, zeros, low], axis=0)
            factor_ref[e] = jnp.concatenate([left, right], axis=1)

    spread_ref[...] = query_ref[...].astype(jnp.float32).reshape(count * experts, LANES)
    for e in range(experts):
        query = spread_ref[pl.ds(e, count, stride=experts), :].astype(jnp.bfloat16)
        result = lax.dot_general(
            factor_ref[e], query, (((1,), (1,)), ((), ())), preferred_element_type=jnp.float32
        )
        result = result[: 2 * width] + result[2 * width :]
        start = e * (rows // experts) + 2 * step
        for tile in range(wide_ref.shape[0]):
            part = result[:, tile * LANES : (tile + 1) * LANES]
            wide_ref[tile, pl.ds(start, width, stride=pitch), :] = part[:width]
            wide_ref[tile, pl.ds(start + 1, width, stride=pitch), :] = part[width:]

    @pl.when(step == pl.num_programs(0) - 1)
    def _():
        copies = []
        for part in range(sems.shape[0]):
            first = part * (width // sems.shape[0])
            for j in range(first, first + width // sems.shape[0]):
                for tile in range(wide_ref.shape[0]):
                    out_ref[j * rows : (j + 1) * rows, tile * LANES : (tile + 1) * LANES] = wide_ref[
                        tile, j * pitch : j * pitch + rows, :
                    ].astype(jnp.bfloat16)
            block = pl.ds(first * rows, width // sems.shape[0] * rows)
            copies.append(pltpu.make_async_copy(out_ref.at[block], out_hbm.at[block], sems.at[part]))
            copies[-1].start()
        for copy in copies:
            copy.wait()


def condition_queries(query_grads, inverse_in):
    count, experts, flat = query_grads.shape
    width = inverse_in.shape[1]
    rows = experts * flat
    return pl.pallas_call(
        query_kernel,
        grid=(flat // LANES,),
        in_specs=[
            pl.BlockSpec((count, experts, LANES), lambda c: (0, 0, c)),
            pl.BlockSpec(inverse_in.shape, lambda c: (0, 0, 0)),
        ],
        out_specs=HBM,
        out_shape=pltpu.HBM((rows, count), jnp.bfloat16),
        scratch_shapes=[
            pltpu.VMEM((experts, 4 * width, 2 * width), jnp.bfloat16),
            pltpu.VMEM((count * experts, LANES), jnp.float32),
            pltpu.VMEM((count // LANES, rows + 8 * width, LANES), jnp.float32),
            pltpu.VMEM((rows, count), jnp.bfloat16),
            pltpu.SemaphoreType.DMA((4,)),
        ],
        compiler_params=pltpu.CompilerParams(vmem_limit_bytes=40 * MIB),
        cost_estimate=cost(10),
    )(stay(query_grads), inverse_in)


def score_kernel(
    arrived_ref, inner_ref, far_ref, out_ref, grads_ref, queries_ref, sem, *, width, doc_count, turns
):
    fetch = pltpu.make_async_copy(far_ref, queries_ref, sem)
    fetch.start()
    sources, quarter, lanes = arrived_ref.shape
    shares = lax.axis_size("proj")
    owners = sources // shares
    outer, inner, docs = [], [], []
    for entry, (owner_turn, share_turn) in enumerate(turns):
        owner = jnp.bitwise_xor(lax.axis_index("expert"), owner_turn)
        share = jnp.bitwise_xor(lax.axis_index("proj"), share_turn)
        outer.append(arrived_ref[listed(owner, owners) * shares + share])
        docs.append(inner_ref[entry, width : width + 1, :].astype(jnp.float32).astype(jnp.int32))
        inner.append(inner_ref[entry, :width, :])
    outer = jnp.concatenate(outer, axis=0)
    inner = jnp.concatenate(inner, axis=1)
    docs = jnp.broadcast_to(jnp.concatenate(docs, axis=1), inner.shape)
    doc_group = 16
    pitch = grads_ref.shape[0] // doc_count

    def one_group(group, carry):
        masked = [
            jnp.where(docs == group * doc_group + d, inner, jnp.zeros_like(inner)) for d in range(doc_group)
        ]
        sums = jnp.dot(jnp.concatenate(masked, axis=0), outer, preferred_element_type=jnp.float32)
        for d in range(doc_group):
            start = pl.multiple_of((group * doc_group + d) * pitch, 8)
            grads_ref[pl.ds(start, width), :] = sums[d * width : (d + 1) * width]
        return carry

    lax.fori_loop(0, doc_count // doc_group, one_group, 0, unroll=doc_count <= 2 * doc_group)
    high, low = [], []
    for j in range(width):
        parts = split(grads_ref[pl.ds(j, doc_count, stride=pitch), :])
        high.append(parts[0])
        low.append(parts[1])
    flat = jnp.concatenate([jnp.concatenate(high, axis=1), jnp.concatenate(low, axis=1)], axis=0)
    fetch.wait()
    result = jnp.dot(flat, queries_ref[...], preferred_element_type=jnp.float32)
    result = result[:doc_count] + result[doc_count:]
    columns = result.shape[1] // shares
    fill = jnp.zeros((DOC_DEV, LANES - columns), jnp.float32)
    for owner in range(owners):
        for share in range(shares):
            piece = result[owner * DOC_DEV : (owner + 1) * DOC_DEV, share * columns : (share + 1) * columns]
            out_ref[listed(owner, owners) * shares + share] = jnp.concatenate([piece, fill], axis=1)


def score(arrived, inner, queries, turns, owners):
    sources = arrived.shape[0]
    width = inner.shape[1] - DOC_ROWS
    doc_count = DOC_DEV * owners
    return pl.pallas_call(
        functools.partial(score_kernel, width=width, doc_count=doc_count, turns=turns),
        in_specs=[VMEM, VMEM, HBM],
        out_shape=jax.ShapeDtypeStruct((sources, DOC_DEV, LANES), jnp.float32),
        scratch_shapes=[
            pltpu.VMEM((doc_count * (width + 8), arrived.shape[2]), jnp.float32),
            pltpu.VMEM(queries.shape, jnp.bfloat16),
            pltpu.SemaphoreType.DMA,
        ],
        compiler_params=pltpu.CompilerParams(vmem_limit_bytes=40 * MIB),
        cost_estimate=cost(5),
    )(arrived, inner, stay(queries))


def sum_kernel(pieces_ref, out_ref):
    total = pieces_ref[0]
    for source in range(1, pieces_ref.shape[0]):
        total = total + pieces_ref[source]
    out_ref[...] = total[:, : out_ref.shape[1]]


def sum_pieces(pieces, columns):
    return pl.pallas_call(
        sum_kernel,
        in_specs=[VMEM],
        out_shape=jax.ShapeDtypeStruct((pieces.shape[1], columns), jnp.float32),
        compiler_params=pltpu.CompilerParams(vmem_limit_bytes=40 * MIB),
    )(pieces)


def exchange(block, axis, size, turn):
    return lax.ppermute(block, axis, [(i, i ^ turn) for i in range(size)])


def double(blocks, turns, axis, size, turn):
    blocks = jnp.concatenate([blocks, exchange(blocks, axis, size, turn)], axis=0)
    return blocks, turns + tuple(t ^ turn for t in turns)


def local(
    activations,
    grad_hidden,
    routes,
    doc_ids,
    query_grads,
    in_projection,
    out_projection,
    inverse_in,
    inverse_out,
):
    tokens, top = routes.shape
    experts, width, _ = inverse_in.shape
    owners = lax.axis_size("expert")
    shares = lax.axis_size("proj")
    quarter = tokens // shares
    assert quarter == LANES and 2 * width == LANES and experts * width // shares == LANES
    assert shares == 4 and owners & (owners - 1) == 0
    assert DOC_DEV * owners <= 256

    flat_hidden = grad_hidden.reshape(tokens * top, grad_hidden.shape[2])
    inner_leaving, inner_own, shared = project_inner(activations, in_projection, inverse_out, shares)
    inner_first = exchange(inner_leaving, "proj", shares, 2)
    far_shared = exchange(shared, "expert", owners, owners // 2)
    leaving, own = project_outer(flat_hidden, out_projection, shares, top)
    far_shared, inner_first, leaving = lax.optimization_barrier((far_shared, inner_first, leaving))
    near = exchange(leaving, "proj", shares, 1)
    shared, turns = jnp.stack([shared, far_shared]), (0, owners // 2)
    for bit in reversed(range((owners // 2).bit_length() - 1)):
        shared, turns = double(shared, turns, "expert", owners, 1 << bit)
    inner_second = exchange(combine(combine_inner_kernel, inner_own, inner_first), "proj", shares, 1)
    sent = combine(combine_outer_kernel, own, near)
    far = exchange(sent, "proj", shares, 2)
    inner = finish_inner(inner_own, inner_first, inner_second, doc_ids.reshape(shares, quarter), width)
    inner, _ = lax.optimization_barrier((inner, sent))
    owner_turns = tuple(reversed(range(owners)))
    arriving = [exchange(inner, "expert", owners, turn) for turn in owner_turns if turn]
    weights = expand(shared, turns, width, experts, shares)
    far, weights = lax.optimization_barrier((far, weights))
    quarter_routes = lax.dynamic_slice_in_dim(routes, lax.axis_index("proj") * quarter, quarter, 0)
    payload = condition(own, near, far, quarter_routes, weights, shares, width)
    payload, arriving = lax.optimization_barrier((payload, arriving))
    arrived = send_to_all(payload, owners, shares)
    inner = jnp.stack(arriving + [inner])
    inner, share_turns = inner[None], (0,)
    inner, share_turns = double(inner, share_turns, "proj", shares, 1)
    inner, query_grads = lax.optimization_barrier((inner, query_grads))
    inner, share_turns = double(inner, share_turns, "proj", shares, 2)
    inner = inner.reshape(owners * shares, width + DOC_ROWS, quarter)
    all_turns = tuple((o, p) for p in share_turns for o in owner_turns)
    queries = condition_queries(query_grads, inverse_in)
    pieces = score(arrived, inner, queries, all_turns, owners)
    pieces = send_to_all(pieces, owners, shares)
    return sum_pieces(pieces, query_grads.shape[0] // shares).T


def solution(mesh):
    in_specs = (
        P(("groups", "expert"), "proj"),
        P(("groups", "expert"), None, "proj"),
        P(("groups", "expert"), None),
        P(("groups", "expert")),
        P(None, "expert", "proj"),
        P(None, "proj"),
        P(None, "proj"),
        P("expert", None, None),
        P("expert", None, None),
    )
    out_specs = P("proj", ("groups", "expert"))
    return jax.shard_map(local, mesh=mesh, in_specs=in_specs, out_specs=out_specs, check_vma=False)
```

```python
import functools

import jax
import jax.numpy as jnp
from jax import lax
from jax.experimental import pallas as pl
from jax.experimental.pallas import tpu as pltpu
from jax.sharding import PartitionSpec as P

DOC_DEV = 8
LANES = 128
DOC_ROWS = 16
MIB = 1024 * 1024
VMEM = pl.BlockSpec(memory_space=pltpu.VMEM)
HBM = pl.BlockSpec(memory_space=pltpu.HBM)


def low_lanes(rows, width):
    return lax.broadcasted_iota(jnp.int32, (rows, LANES), 1) < width


def stay(array):
    return pltpu.with_memory_space_constraint(array, pltpu.HBM)


def listed(owner, owners, first):
    return (owner + owners - first) % owners


def send_to_all(blocks, owners, shares, first):
    members = [(i + first * shares) % (owners * shares) for i in range(owners * shares)]
    return lax.all_to_all(blocks, ("expert", "proj"), 0, 0, tiled=True, axis_index_groups=[members])


def split(value):
    high = value.astype(jnp.bfloat16)
    return high, (value - high.astype(jnp.float32)).astype(jnp.bfloat16)


def cost(microseconds):
    return pl.CostEstimate(flops=0, bytes_accessed=int(microseconds * 3.3e6), transcendentals=0)


def in_order(copies, ahead):
    for copy in copies[:ahead]:
        copy.start()
    state = [0]

    def take():
        copies[state[0]].wait()
        if state[0] + ahead < len(copies):
            copies[state[0] + ahead].start()
        state[0] += 1

    return take


def inner_kernel(
    act_hbm, in_proj_hbm, inverse_hbm, leaving_ref, own_ref, shared_ref, act_ref, in_proj_ref, inverse_ref, sems
):
    turns = (2, 3, 1, 0)
    quarter = act_ref.shape[1]
    width = in_proj_ref.shape[0]
    half = quarter // 2
    place = lax.axis_index("proj")
    pairs = [(in_proj_hbm, in_proj_ref)]
    for g, turn in enumerate(turns):
        rows = pl.ds(pl.multiple_of(jnp.bitwise_xor(place, turn) * quarter, quarter), quarter)
        pairs.append((act_hbm.at[rows], act_ref.at[g]))
        if g == 0:
            pairs.append((inverse_hbm, inverse_ref))
    take = in_order([pltpu.make_async_copy(*pair, sems.at[i]) for i, pair in enumerate(pairs)], 5)
    take()
    first = low_lanes(half, width)
    for wire_ref in (leaving_ref, own_ref):
        take()
        if wire_ref is leaving_ref:
            take()
            experts = inverse_ref.shape[0] // 2
            for e in range(experts):
                pair = jnp.concatenate([inverse_ref[e], inverse_ref[experts + e]], axis=1)
                shared_ref[e * width : (e + 1) * width, :] = pair.astype(jnp.bfloat16)
        take()
        twice = jnp.concatenate([in_proj_ref[...], in_proj_ref[...]], axis=0)
        g = 0 if wire_ref is leaving_ref else 2
        rows = act_ref[g : g + 2].reshape(2 * quarter, act_ref.shape[2])
        inner = lax.dot_general(rows, twice, (((1,), (1,)), ((), ())), preferred_element_type=jnp.float32)
        for i in range(2):
            start = i * quarter
            high, low = split(jnp.where(first, inner[start : start + half], inner[start + half : start + quarter]))
            wire_ref[i, :half, :] = high
            wire_ref[i, half:, :] = low


def project_inner(activations, in_projection, inverse_out, quarters):
    tokens, model = activations.shape
    quarter = tokens // quarters
    experts, width, _ = inverse_out.shape
    wire = jax.ShapeDtypeStruct((quarters // 2, quarter, LANES), jnp.bfloat16)
    fixed = (in_projection, inverse_out)
    return pl.pallas_call(
        inner_kernel,
        in_specs=[HBM] * 3,
        out_specs=[VMEM] * 3,
        out_shape=[wire, wire, jax.ShapeDtypeStruct((experts // 2 * width, LANES), jnp.bfloat16)],
        scratch_shapes=[pltpu.VMEM((quarters, quarter, model), jnp.bfloat16)]
        + [pltpu.VMEM(array.shape, array.dtype) for array in fixed]
        + [pltpu.SemaphoreType.DMA((quarters + len(fixed),))],
        compiler_params=pltpu.CompilerParams(vmem_limit_bytes=40 * MIB),
        cost_estimate=cost(2.5),
    )(*[stay(array) for array in (activations, *fixed)])


def outer_kernel(hidden_hbm, out_proj_hbm, leaving_ref, own_ref, hidden_ref, out_proj_ref, rows_ref, sems, *, top):
    turns = (1, 3, 2, 0)
    quarter_rows = hidden_ref.shape[1]
    quarter = quarter_rows // top
    half = quarter // 2
    chunks = [(0, 0, half), (0, half, half), (1, 0, quarter), (2, 0, quarter), (3, 0, half), (3, half, half)]
    width = out_proj_ref.shape[0]
    place = lax.axis_index("proj")
    pairs = [(out_proj_hbm, out_proj_ref)]
    for g, token, size in chunks:
        start = jnp.bitwise_xor(place, turns[g]) * quarter_rows + token * top
        rows = pl.ds(pl.multiple_of(start, half * top), size * top)
        pairs.append((hidden_hbm.at[rows], hidden_ref.at[g, pl.ds(token * top, size * top)]))
    take = in_order([pltpu.make_async_copy(*pair, sems.at[i]) for i, pair in enumerate(pairs)], 3)
    take()

    def pack_rows(i):
        g, token, size = chunks[i]
        wire_ref = leaving_ref.at[g] if g < 2 else own_ref.at[g - 2]
        first = low_lanes(size, width)
        for pair in range(top // 2):
            even = rows_ref[i % 2, pl.ds(2 * pair, size, stride=top), :]
            odd = rows_ref[i % 2, pl.ds(2 * pair + 1, size, stride=top), :]
            start = pair * quarter + token
            wire_ref[start : start + size, :] = jnp.where(first, even, odd).astype(jnp.bfloat16)

    for i, (g, token, size) in enumerate(chunks):
        take()
        twice = jnp.concatenate([out_proj_ref[...], out_proj_ref[...]], axis=0)
        rows_ref[i % 2, : size * top, :] = lax.dot_general(
            hidden_ref[g, token * top : (token + size) * top, :],
            twice,
            (((1,), (1,)), ((), ())),
            preferred_element_type=jnp.float32,
        )
        if i:
            pack_rows(i - 1)
    pack_rows(len(chunks) - 1)


def project_outer(flat_hidden, out_projection, quarters, top):
    rows, hidden = flat_hidden.shape
    wire = jax.ShapeDtypeStruct((quarters // 2, rows // quarters // 2, LANES), jnp.bfloat16)
    return pl.pallas_call(
        functools.partial(outer_kernel, top=top),
        in_specs=[HBM] * 2,
        out_specs=[VMEM] * 2,
        out_shape=[wire, wire],
        scratch_shapes=[
            pltpu.VMEM((quarters, rows // quarters, hidden), jnp.bfloat16),
            pltpu.VMEM(out_projection.shape, out_projection.dtype),
            pltpu.VMEM((2, rows // quarters, LANES), jnp.float32),
            pltpu.SemaphoreType.DMA((quarters + 3,)),
        ],
        compiler_params=pltpu.CompilerParams(vmem_limit_bytes=40 * MIB),
        cost_estimate=cost(4),
    )(stay(flat_hidden), stay(out_projection))


def exact_rows(rows):
    half = rows.shape[0] // 2
    return rows[:half].astype(jnp.float32) + rows[half:].astype(jnp.float32)


def combine_inner_kernel(own_ref, near_ref, out_ref):
    high, low = split(exact_rows(own_ref[0]) + exact_rows(near_ref[1]))
    out_ref[: high.shape[0], :] = high
    out_ref[high.shape[0] :, :] = low


def combine_outer_kernel(own_ref, near_ref, out_ref):
    out_ref[...] = (own_ref[0].astype(jnp.float32) + near_ref[1].astype(jnp.float32)).astype(jnp.bfloat16)


def combine(kernel, own, near):
    return pl.pallas_call(
        kernel,
        in_specs=[VMEM, VMEM],
        out_shape=jax.ShapeDtypeStruct(own.shape[1:], jnp.bfloat16),
        compiler_params=pltpu.CompilerParams(vmem_limit_bytes=40 * MIB),
        cost_estimate=cost(0.5),
    )(own, near)


def finish_inner_kernel(own_ref, first_ref, second_ref, docs_ref, out_ref):
    total = exact_rows(own_ref[1]) + exact_rows(first_ref[0]) + exact_rows(second_ref[...])
    width = out_ref.shape[0] - DOC_ROWS
    total = jnp.concatenate([total[:, :width], total[:, width:]], axis=0)
    out_ref[:width, :] = jnp.transpose(total).astype(jnp.bfloat16)
    docs = docs_ref[pl.ds(lax.axis_index("proj"), 1), :].astype(jnp.float32)
    out_ref[width:, :] = jnp.broadcast_to(docs, (DOC_ROWS, LANES)).astype(jnp.bfloat16)


def finish_inner(own, first, second, doc_rows, width):
    return pl.pallas_call(
        finish_inner_kernel,
        in_specs=[VMEM] * 4,
        out_shape=jax.ShapeDtypeStruct((width + DOC_ROWS, own.shape[1]), jnp.bfloat16),
        compiler_params=pltpu.CompilerParams(vmem_limit_bytes=40 * MIB),
        cost_estimate=cost(0.5),
    )(own, first, second, doc_rows)


def expand_kernel(shared_ref, weights_ref, *, width, experts, shares, turns):
    columns = experts * width
    share_rows = width // shares
    half = experts // 2
    lane = lax.broadcasted_iota(jnp.int32, (LANES, columns), 1)
    row = lax.broadcasted_iota(jnp.int32, (LANES, columns), 0)
    source = lane // (experts * share_rows) * share_rows + lane % share_rows
    expert_lane = lax.broadcasted_iota(jnp.int32, (half * width, columns), 1) // share_rows % experts
    expert_row = lax.broadcasted_iota(jnp.int32, (half * width, columns), 0) // width
    for side in range(2):
        spread = (row == source + side * width).astype(jnp.float32).astype(jnp.bfloat16)
        own = expert_lane == expert_row + side * half
        for entry, turn in enumerate(turns):
            placed = jnp.dot(
                shared_ref[entry], spread, preferred_element_type=jnp.float32
            )
            weights_ref[turn, side * half * width : (side + 1) * half * width, :] = jnp.where(
                own, placed, 0.0
            ).astype(jnp.bfloat16)


def expand(shared, turns, width, experts, shares):
    owners = shared.shape[0]
    return pl.pallas_call(
        functools.partial(expand_kernel, width=width, experts=experts, shares=shares, turns=turns),
        in_specs=[VMEM],
        out_shape=jax.ShapeDtypeStruct((owners, experts * width, experts * width), jnp.bfloat16),
        compiler_params=pltpu.CompilerParams(vmem_limit_bytes=40 * MIB),
        cost_estimate=cost(1.3),
    )(shared)


def condition_kernel(
    own_ref, near_ref, far_ref, routes_ref, weights_ref, payload_ref, value_ref, name_ref, *, top, width
):
    quarter = routes_ref.shape[0]
    groups, dense_width, _ = weights_ref.shape
    shares = payload_ref.shape[0] // groups
    experts = dense_width // width
    first = low_lanes(quarter, width)
    second = 1 - first.astype(jnp.int32)

    def summed(start, size):
        rows = slice(start, start + size)
        total = own_ref[1, rows, :].astype(jnp.float32) + near_ref[0, rows, :].astype(jnp.float32)
        return total + far_ref[rows, :].astype(jnp.float32)

    for pair in range(top // 2):
        both = summed(pair * quarter, quarter)
        swapped = pltpu.roll(both, width, 1)
        value_ref[2 * pair] = jnp.where(first, both, swapped)
        value_ref[2 * pair + 1] = jnp.where(first, swapped, both)
    for k in range(top):
        name_ref[k] = jnp.broadcast_to(routes_ref[:, k : k + 1], (quarter, LANES)) - second
    def one_group(step, carry):
        group = jnp.bitwise_xor(lax.axis_index("expert"), step)
        dense = []
        for pair in range(experts // 2):
            base = group * experts + 2 * pair
            chosen = jnp.zeros((quarter, LANES), jnp.float32)
            for k in range(top):
                chosen = jnp.where(name_ref[k] == base, value_ref[k], chosen)
            dense.append(chosen.astype(jnp.bfloat16))
        result = jnp.dot(
            jnp.concatenate(dense, axis=1), weights_ref[step], preferred_element_type=jnp.float32
        ).astype(jnp.bfloat16)
        share_width = result.shape[1] // shares
        for share in range(shares):
            payload_ref[listed(group, groups, groups // 2) * shares + share] = result[:, share * share_width : (share + 1) * share_width]
        return carry

    lax.fori_loop(0, groups, one_group, 0, unroll=groups <= 4)


def condition(own, near, far, quarter_routes, weights, shares, width):
    quarter, top = quarter_routes.shape
    groups = weights.shape[0]
    return pl.pallas_call(
        functools.partial(condition_kernel, top=top, width=width),
        in_specs=[VMEM] * 5,
        out_shape=jax.ShapeDtypeStruct((groups * shares, quarter, LANES), jnp.bfloat16),
        scratch_shapes=[
            pltpu.VMEM((top, quarter, LANES), jnp.float32),
            pltpu.VMEM((top, quarter, LANES), jnp.int32),
        ],
        compiler_params=pltpu.CompilerParams(vmem_limit_bytes=40 * MIB),
        cost_estimate=cost(2),
    )(own, near, far, quarter_routes, weights)


def query_kernel(query_ref, inverse_ref, out_hbm, factor_ref, spread_ref, wide_ref, out_ref, sems):
    count, experts, _ = query_ref.shape
    width = inverse_ref.shape[1]
    step = pl.program_id(0)
    rows = out_ref.shape[0] // width
    pitch = wide_ref.shape[1] // width

    @pl.when(step == 0)
    def _():
        zeros = jnp.zeros((width, width), jnp.bfloat16)
        for e in range(experts):
            high, low = split(inverse_ref[e])
            left = jnp.concatenate([high, zeros, low, zeros], axis=0)
            right = jnp.concatenate([zeros, high, zeros, low], axis=0)
            factor_ref[e] = jnp.concatenate([left, right], axis=1)

    spread_ref[...] = query_ref[...].astype(jnp.float32).reshape(count * experts, LANES)
    for e in range(experts):
        query = spread_ref[pl.ds(e, count, stride=experts), :].astype(jnp.bfloat16)
        result = lax.dot_general(
            factor_ref[e], query, (((1,), (1,)), ((), ())), preferred_element_type=jnp.float32
        )
        result = result[: 2 * width] + result[2 * width :]
        start = e * (rows // experts) + 2 * step
        for tile in range(wide_ref.shape[0]):
            part = result[:, tile * LANES : (tile + 1) * LANES]
            wide_ref[tile, pl.ds(start, width, stride=pitch), :] = part[:width]
            wide_ref[tile, pl.ds(start + 1, width, stride=pitch), :] = part[width:]

    @pl.when(step == pl.num_programs(0) - 1)
    def _():
        copies = []
        for part in range(sems.shape[0]):
            first = part * (width // sems.shape[0])
            for j in range(first, first + width // sems.shape[0]):
                for tile in range(wide_ref.shape[0]):
                    out_ref[j * rows : (j + 1) * rows, tile * LANES : (tile + 1) * LANES] = wide_ref[
                        tile, j * pitch : j * pitch + rows, :
                    ].astype(jnp.bfloat16)
            block = pl.ds(first * rows, width // sems.shape[0] * rows)
            copies.append(pltpu.make_async_copy(out_ref.at[block], out_hbm.at[block], sems.at[part]))
            copies[-1].start()
        for copy in copies:
            copy.wait()


def condition_queries(query_grads, inverse_in):
    count, experts, flat = query_grads.shape
    width = inverse_in.shape[1]
    rows = experts * flat
    return pl.pallas_call(
        query_kernel,
        grid=(flat // LANES,),
        in_specs=[
            pl.BlockSpec((count, experts, LANES), lambda c: (0, 0, c)),
            pl.BlockSpec(inverse_in.shape, lambda c: (0, 0, 0)),
        ],
        out_specs=HBM,
        out_shape=pltpu.HBM((rows, count), jnp.bfloat16),
        scratch_shapes=[
            pltpu.VMEM((experts, 4 * width, 2 * width), jnp.bfloat16),
            pltpu.VMEM((count * experts, LANES), jnp.float32),
            pltpu.VMEM((count // LANES, rows + 8 * width, LANES), jnp.float32),
            pltpu.VMEM((rows, count), jnp.bfloat16),
            pltpu.SemaphoreType.DMA((4,)),
        ],
        compiler_params=pltpu.CompilerParams(vmem_limit_bytes=40 * MIB),
        cost_estimate=cost(10),
    )(stay(query_grads), inverse_in)


def score_kernel(
    arrived_ref, inner_ref, far_ref, out_ref, grads_ref, queries_ref, sem, *, width, doc_count, turns
):
    fetch = pltpu.make_async_copy(far_ref, queries_ref, sem)
    fetch.start()
    sources, quarter, lanes = arrived_ref.shape
    shares = lax.axis_size("proj")
    owners = sources // shares
    outer, inner, docs = [], [], []
    for entry, (owner_turn, share_turn) in enumerate(turns):
        owner = jnp.bitwise_xor(lax.axis_index("expert"), owner_turn)
        share = jnp.bitwise_xor(lax.axis_index("proj"), share_turn)
        outer.append(arrived_ref[listed(owner, owners, owners // 2) * shares + share])
        docs.append(inner_ref[entry, width:, :])
        inner.append(inner_ref[entry, :width, :])
    outer = jnp.concatenate(outer, axis=0)
    inner = jnp.concatenate(inner, axis=1)
    docs = jnp.concatenate(docs, axis=1)
    ones = jnp.ones_like(docs)
    doc_group = min(doc_count, max(4, 8 * MIB // (2 * inner.size)))
    pitch = grads_ref.shape[0] // doc_count

    def one_group(group, carry):
        masked = []
        for d in range(doc_group):
            named = jnp.full_like(docs, group * doc_group + d)
            own = jnp.where(docs == named, ones, jnp.zeros_like(docs))
            masked += [inner[r : r + DOC_ROWS] * own for r in range(0, width, DOC_ROWS)]
        sums = jnp.dot(jnp.concatenate(masked, axis=0), outer, preferred_element_type=jnp.float32)
        for d in range(doc_group):
            start = pl.multiple_of((group * doc_group + d) * pitch, 8)
            grads_ref[pl.ds(start, width), :] = sums[d * width : (d + 1) * width]
        return carry

    lax.fori_loop(0, doc_count // doc_group, one_group, 0, unroll=doc_count <= 2 * doc_group)
    high, low = [], []
    for j in range(width):
        parts = split(grads_ref[pl.ds(j, doc_count, stride=pitch), :])
        high.append(parts[0])
        low.append(parts[1])
    flat = jnp.concatenate([jnp.concatenate(high, axis=1), jnp.concatenate(low, axis=1)], axis=0)
    fetch.wait()
    result = jnp.dot(flat, queries_ref[...], preferred_element_type=jnp.float32)
    result = result[:doc_count] + result[doc_count:]
    columns = result.shape[1] // shares
    fill = jnp.zeros((DOC_DEV, LANES - columns), jnp.float32)
    for owner in range(owners):
        for share in range(shares):
            piece = result[owner * DOC_DEV : (owner + 1) * DOC_DEV, share * columns : (share + 1) * columns]
            out_ref[listed(owner, owners, owners - 1) * shares + share] = jnp.concatenate([piece, fill], axis=1)


def score(arrived, inner, queries, turns, owners):
    sources = arrived.shape[0]
    width = inner.shape[1] - DOC_ROWS
    doc_count = DOC_DEV * owners
    return pl.pallas_call(
        functools.partial(score_kernel, width=width, doc_count=doc_count, turns=turns),
        in_specs=[VMEM, VMEM, HBM],
        out_shape=jax.ShapeDtypeStruct((sources, DOC_DEV, LANES), jnp.float32),
        scratch_shapes=[
            pltpu.VMEM((doc_count * (width + 8), arrived.shape[2]), jnp.float32),
            pltpu.VMEM(queries.shape, jnp.bfloat16),
            pltpu.SemaphoreType.DMA,
        ],
        compiler_params=pltpu.CompilerParams(vmem_limit_bytes=40 * MIB),
        cost_estimate=cost(5),
    )(arrived, inner, stay(queries))


def sum_kernel(pieces_ref, out_ref):
    total = pieces_ref[0]
    for source in range(1, pieces_ref.shape[0]):
        total = total + pieces_ref[source]
    out_ref[...] = total[:, : out_ref.shape[1]]


def sum_pieces(pieces, columns):
    return pl.pallas_call(
        sum_kernel,
        in_specs=[VMEM],
        out_shape=jax.ShapeDtypeStruct((pieces.shape[1], columns), jnp.float32),
        compiler_params=pltpu.CompilerParams(vmem_limit_bytes=40 * MIB),
    )(pieces)


def exchange(block, axis, size, turn):
    return lax.ppermute(block, axis, [(i, i ^ turn) for i in range(size)])


def double(blocks, turns, axis, size, turn):
    blocks = jnp.concatenate([blocks, exchange(blocks, axis, size, turn)], axis=0)
    return blocks, turns + tuple(t ^ turn for t in turns)


def local(
    activations,
    grad_hidden,
    routes,
    doc_ids,
    query_grads,
    in_projection,
    out_projection,
    inverse_in,
    inverse_out,
):
    tokens, top = routes.shape
    experts, width, _ = inverse_in.shape
    owners = lax.axis_size("expert")
    shares = lax.axis_size("proj")
    quarter = tokens // shares
    assert quarter == LANES and 2 * width == LANES and experts * width // shares == LANES
    assert shares == 4 and owners & (owners - 1) == 0
    assert DOC_DEV * owners <= 256

    flat_hidden = grad_hidden.reshape(tokens * top, grad_hidden.shape[2])
    inner_leaving, inner_own, shared = project_inner(activations, in_projection, inverse_out, shares)
    inner_first = exchange(inner_leaving, "proj", shares, 2)
    far_shared = exchange(shared, "expert", owners, owners // 2)
    leaving, own = project_outer(flat_hidden, out_projection, shares, top)
    far_shared, inner_first, leaving = lax.optimization_barrier((far_shared, inner_first, leaving))
    near = exchange(leaving, "proj", shares, 1)
    shared, turns = jnp.stack([shared, far_shared]), (0, owners // 2)
    for bit in reversed(range((owners // 2).bit_length() - 1)):
        shared, turns = double(shared, turns, "expert", owners, 1 << bit)
    inner_second = exchange(combine(combine_inner_kernel, inner_own, inner_first), "proj", shares, 1)
    sent = combine(combine_outer_kernel, own, near)
    far = exchange(sent, "proj", shares, 2)
    inner = finish_inner(inner_own, inner_first, inner_second, doc_ids.reshape(shares, quarter), width)
    inner, _ = lax.optimization_barrier((inner, sent))
    owner_turns = tuple(reversed(range(owners)))
    arriving = [exchange(inner, "expert", owners, turn) for turn in owner_turns if turn]
    weights = expand(shared, turns, width, experts, shares)
    far, weights = lax.optimization_barrier((far, weights))
    quarter_routes = lax.dynamic_slice_in_dim(routes, lax.axis_index("proj") * quarter, quarter, 0)
    payload = condition(own, near, far, quarter_routes, weights, shares, width)
    payload, arriving = lax.optimization_barrier((payload, arriving))
    arrived = send_to_all(payload, owners, shares, owners // 2)
    inner = jnp.stack(arriving + [inner])
    inner, share_turns = inner[None], (0,)
    inner, share_turns = double(inner, share_turns, "proj", shares, 1)
    inner, query_grads = lax.optimization_barrier((inner, query_grads))
    inner, share_turns = double(inner, share_turns, "proj", shares, 2)
    inner = inner.reshape(owners * shares, width + DOC_ROWS, quarter)
    all_turns = tuple((o, p) for p in share_turns for o in owner_turns)
    queries = condition_queries(query_grads, inverse_in)
    pieces = score(arrived, inner, queries, all_turns, owners)
    pieces = send_to_all(pieces, owners, shares, owners - 1)
    return sum_pieces(pieces, query_grads.shape[0] // shares).T


def solution(mesh):
    in_specs = (
        P(("groups", "expert"), "proj"),
        P(("groups", "expert"), None, "proj"),
        P(("groups", "expert"), None),
        P(("groups", "expert")),
        P(None, "expert", "proj"),
        P(None, "proj"),
        P(None, "proj"),
        P("expert", None, None),
        P("expert", None, None),
    )
    out_specs = P("proj", ("groups", "expert"))
    return jax.shard_map(local, mesh=mesh, in_specs=in_specs, out_specs=out_specs, check_vma=False)
```

```python
import functools

import jax
import jax.numpy as jnp
from jax import lax
from jax.experimental import pallas as pl
from jax.experimental.pallas import tpu as pltpu
from jax.sharding import PartitionSpec as P

DOC_DEV = 8
LANES = 128
DOC_ROWS = 16
MIB = 1024 * 1024
VMEM = pl.BlockSpec(memory_space=pltpu.VMEM)
HBM = pl.BlockSpec(memory_space=pltpu.HBM)


def low_lanes(rows, width):
    return lax.broadcasted_iota(jnp.int32, (rows, LANES), 1) < width


def stay(array):
    return pltpu.with_memory_space_constraint(array, pltpu.HBM)


def listed(owner, owners, first):
    return (owner + owners - first) % owners


def send_to_all(blocks, owners, shares, first):
    members = [(i + first * shares) % (owners * shares) for i in range(owners * shares)]
    return lax.all_to_all(blocks, ("expert", "proj"), 0, 0, tiled=True, axis_index_groups=[members])


def split(value):
    high = value.astype(jnp.bfloat16)
    return high, (value - high.astype(jnp.float32)).astype(jnp.bfloat16)


def cost(microseconds):
    return pl.CostEstimate(flops=0, bytes_accessed=int(microseconds * 3.3e6), transcendentals=0)


def in_order(copies, ahead):
    for copy in copies[:ahead]:
        copy.start()
    state = [0]

    def take():
        copies[state[0]].wait()
        if state[0] + ahead < len(copies):
            copies[state[0] + ahead].start()
        state[0] += 1

    return take


def twice_transposed(projection):
    once = jnp.transpose(projection.astype(jnp.float32))
    return jnp.concatenate([once, once], axis=1).astype(jnp.bfloat16)


def inner_kernel(
    act_hbm, in_proj_hbm, inverse_hbm, leaving_ref, own_ref, shared_ref, act_ref, in_proj_ref, inverse_ref, sems
):
    turns = (2, 3, 1, 0)
    quarter = act_ref.shape[1]
    width = in_proj_ref.shape[0]
    half = quarter // 2
    place = lax.axis_index("proj")
    pairs = [(in_proj_hbm, in_proj_ref)]
    for g, turn in enumerate(turns):
        rows = pl.ds(pl.multiple_of(jnp.bitwise_xor(place, turn) * quarter, quarter), quarter)
        pairs.append((act_hbm.at[rows], act_ref.at[g]))
        if g == 0:
            pairs.append((inverse_hbm, inverse_ref))
    take = in_order([pltpu.make_async_copy(*pair, sems.at[i]) for i, pair in enumerate(pairs)], 5)
    take()
    first = low_lanes(half, width)
    weights = twice_transposed(in_proj_ref[...])
    for wire_ref in (leaving_ref, own_ref):
        take()
        if wire_ref is leaving_ref:
            take()
            experts = inverse_ref.shape[0] // 2
            for e in range(experts):
                pair = jnp.concatenate([inverse_ref[e], inverse_ref[experts + e]], axis=1)
                shared_ref[e * width : (e + 1) * width, :] = pair.astype(jnp.bfloat16)
        take()
        g = 0 if wire_ref is leaving_ref else 2
        rows = act_ref[g : g + 2].reshape(2 * quarter, act_ref.shape[2])
        inner = jnp.dot(rows, weights, preferred_element_type=jnp.float32)
        for i in range(2):
            start = i * quarter
            high, low = split(jnp.where(first, inner[start : start + half], inner[start + half : start + quarter]))
            wire_ref[i, :half, :] = high
            wire_ref[i, half:, :] = low


def project_inner(activations, in_projection, inverse_out, quarters):
    tokens, model = activations.shape
    quarter = tokens // quarters
    experts, width, _ = inverse_out.shape
    wire = jax.ShapeDtypeStruct((quarters // 2, quarter, LANES), jnp.bfloat16)
    fixed = (in_projection, inverse_out)
    return pl.pallas_call(
        inner_kernel,
        in_specs=[HBM] * 3,
        out_specs=[VMEM] * 3,
        out_shape=[wire, wire, jax.ShapeDtypeStruct((experts // 2 * width, LANES), jnp.bfloat16)],
        scratch_shapes=[pltpu.VMEM((quarters, quarter, model), jnp.bfloat16)]
        + [pltpu.VMEM(array.shape, array.dtype) for array in fixed]
        + [pltpu.SemaphoreType.DMA((quarters + len(fixed),))],
        compiler_params=pltpu.CompilerParams(vmem_limit_bytes=40 * MIB),
        cost_estimate=cost(2.5),
    )(*[stay(array) for array in (activations, *fixed)])


def outer_kernel(hidden_hbm, out_proj_hbm, leaving_ref, own_ref, hidden_ref, out_proj_ref, rows_ref, sems, *, top):
    turns = (1, 3, 2, 0)
    chunks, chunk_rows, _ = hidden_ref.shape
    chunk = chunk_rows // top
    split_by = chunks // len(turns)
    quarter = chunk * split_by
    width = out_proj_ref.shape[0]
    place = lax.axis_index("proj")
    pairs = [(out_proj_hbm, out_proj_ref)]
    for i in range(chunks):
        start = (jnp.bitwise_xor(place, turns[i // split_by]) * split_by + i % split_by) * chunk_rows
        pairs.append((hidden_hbm.at[pl.ds(pl.multiple_of(start, chunk_rows), chunk_rows)], hidden_ref.at[i]))
    take = in_order([pltpu.make_async_copy(*pair, sems.at[i]) for i, pair in enumerate(pairs)], 3)
    take()
    first = low_lanes(chunk, width)
    weights = twice_transposed(out_proj_ref[...])

    def pack_rows(i):
        g, part = i // split_by, i % split_by
        wire_ref = leaving_ref.at[g] if g < 2 else own_ref.at[g - 2]
        for pair in range(top // 2):
            even = rows_ref[i % 2, pl.ds(2 * pair, chunk, stride=top), :]
            odd = rows_ref[i % 2, pl.ds(2 * pair + 1, chunk, stride=top), :]
            start = pair * quarter + part * chunk
            wire_ref[start : start + chunk, :] = jnp.where(first, even, odd).astype(jnp.bfloat16)

    for i in range(chunks):
        take()
        rows_ref[i % 2] = jnp.dot(hidden_ref[i], weights, preferred_element_type=jnp.float32)
        if i:
            pack_rows(i - 1)
    pack_rows(chunks - 1)


def project_outer(flat_hidden, out_projection, quarters, top):
    rows, hidden = flat_hidden.shape
    chunks = quarters
    wire = jax.ShapeDtypeStruct((quarters // 2, rows // quarters // 2, LANES), jnp.bfloat16)
    return pl.pallas_call(
        functools.partial(outer_kernel, top=top),
        in_specs=[HBM] * 2,
        out_specs=[VMEM] * 2,
        out_shape=[wire, wire],
        scratch_shapes=[
            pltpu.VMEM((chunks, rows // chunks, hidden), jnp.bfloat16),
            pltpu.VMEM(out_projection.shape, out_projection.dtype),
            pltpu.VMEM((2, rows // chunks, LANES), jnp.float32),
            pltpu.SemaphoreType.DMA((chunks + 1,)),
        ],
        compiler_params=pltpu.CompilerParams(vmem_limit_bytes=40 * MIB),
        cost_estimate=cost(4),
    )(stay(flat_hidden), stay(out_projection))


def exact_rows(rows):
    half = rows.shape[0] // 2
    return rows[:half].astype(jnp.float32) + rows[half:].astype(jnp.float32)


def combine_inner_kernel(own_ref, near_ref, out_ref):
    high, low = split(exact_rows(own_ref[0]) + exact_rows(near_ref[1]))
    out_ref[: high.shape[0], :] = high
    out_ref[high.shape[0] :, :] = low


def combine_outer_kernel(own_ref, near_ref, out_ref):
    out_ref[...] = (own_ref[0].astype(jnp.float32) + near_ref[1].astype(jnp.float32)).astype(jnp.bfloat16)


def combine(kernel, own, near):
    return pl.pallas_call(
        kernel,
        in_specs=[VMEM, VMEM],
        out_shape=jax.ShapeDtypeStruct(own.shape[1:], jnp.bfloat16),
        compiler_params=pltpu.CompilerParams(vmem_limit_bytes=40 * MIB),
        cost_estimate=cost(0.5),
    )(own, near)


def finish_inner_kernel(own_ref, first_ref, second_ref, docs_ref, out_ref):
    total = exact_rows(own_ref[1]) + exact_rows(first_ref[0]) + exact_rows(second_ref[...])
    width = out_ref.shape[0] - DOC_ROWS
    total = jnp.concatenate([total[:, :width], total[:, width:]], axis=0)
    out_ref[:width, :] = jnp.transpose(total).astype(jnp.bfloat16)
    docs = docs_ref[pl.ds(lax.axis_index("proj"), 1), :].astype(jnp.float32)
    out_ref[width:, :] = jnp.broadcast_to(docs, (DOC_ROWS, LANES)).astype(jnp.bfloat16)


def finish_inner(own, first, second, doc_rows, width):
    return pl.pallas_call(
        finish_inner_kernel,
        in_specs=[VMEM] * 4,
        out_shape=jax.ShapeDtypeStruct((width + DOC_ROWS, own.shape[1]), jnp.bfloat16),
        compiler_params=pltpu.CompilerParams(vmem_limit_bytes=40 * MIB),
        cost_estimate=cost(0.5),
    )(own, first, second, doc_rows)


def expand_kernel(shared_ref, weights_ref, *, width, experts, shares, turns):
    columns = experts * width
    share_rows = width // shares
    half = experts // 2
    lane = lax.broadcasted_iota(jnp.int32, (LANES, columns), 1)
    row = lax.broadcasted_iota(jnp.int32, (LANES, columns), 0)
    source = lane // (experts * share_rows) * share_rows + lane % share_rows
    expert_lane = lax.broadcasted_iota(jnp.int32, (half * width, columns), 1) // share_rows % experts
    expert_row = lax.broadcasted_iota(jnp.int32, (half * width, columns), 0) // width
    for side in range(2):
        spread = (row == source + side * width).astype(jnp.float32).astype(jnp.bfloat16)
        own = expert_lane == expert_row + side * half
        for entry, turn in enumerate(turns):
            placed = jnp.dot(
                shared_ref[entry], spread, preferred_element_type=jnp.float32
            )
            weights_ref[turn, side * half * width : (side + 1) * half * width, :] = jnp.where(
                own, placed, 0.0
            ).astype(jnp.bfloat16)


def expand(shared, turns, width, experts, shares):
    owners = shared.shape[0]
    return pl.pallas_call(
        functools.partial(expand_kernel, width=width, experts=experts, shares=shares, turns=turns),
        in_specs=[VMEM],
        out_shape=jax.ShapeDtypeStruct((owners, experts * width, experts * width), jnp.bfloat16),
        compiler_params=pltpu.CompilerParams(vmem_limit_bytes=40 * MIB),
        cost_estimate=cost(1.3),
    )(shared)


def condition_kernel(
    own_ref, near_ref, far_ref, routes_ref, weights_ref, payload_ref, value_ref, name_ref, *, top, width
):
    quarter = routes_ref.shape[0]
    groups, dense_width, _ = weights_ref.shape
    shares = payload_ref.shape[0] // groups
    experts = dense_width // width
    first = low_lanes(quarter, width)
    second = 1 - first.astype(jnp.int32)

    def summed(start, size):
        rows = slice(start, start + size)
        total = own_ref[1, rows, :].astype(jnp.float32) + near_ref[0, rows, :].astype(jnp.float32)
        return total + far_ref[rows, :].astype(jnp.float32)

    for pair in range(top // 2):
        both = summed(pair * quarter, quarter)
        swapped = pltpu.roll(both, width, 1)
        value_ref[2 * pair] = jnp.where(first, both, swapped)
        value_ref[2 * pair + 1] = jnp.where(first, swapped, both)
    for k in range(top):
        name_ref[k] = jnp.broadcast_to(routes_ref[:, k : k + 1], (quarter, LANES)) - second
    def one_group(step, carry):
        group = jnp.bitwise_xor(lax.axis_index("expert"), step)
        dense = []
        for pair in range(experts // 2):
            base = group * experts + 2 * pair
            chosen = jnp.zeros((quarter, LANES), jnp.float32)
            for k in range(top):
                chosen = jnp.where(name_ref[k] == base, value_ref[k], chosen)
            dense.append(chosen.astype(jnp.bfloat16))
        result = jnp.dot(
            jnp.concatenate(dense, axis=1), weights_ref[step], preferred_element_type=jnp.float32
        ).astype(jnp.bfloat16)
        share_width = result.shape[1] // shares
        for share in range(shares):
            payload_ref[listed(group, groups, groups // 2) * shares + share] = result[:, share * share_width : (share + 1) * share_width]
        return carry

    lax.fori_loop(0, groups, one_group, 0, unroll=groups <= 4)


def condition(own, near, far, quarter_routes, weights, shares, width):
    quarter, top = quarter_routes.shape
    groups = weights.shape[0]
    return pl.pallas_call(
        functools.partial(condition_kernel, top=top, width=width),
        in_specs=[VMEM] * 5,
        out_shape=jax.ShapeDtypeStruct((groups * shares, quarter, LANES), jnp.bfloat16),
        scratch_shapes=[
            pltpu.VMEM((top, quarter, LANES), jnp.float32),
            pltpu.VMEM((top, quarter, LANES), jnp.int32),
        ],
        compiler_params=pltpu.CompilerParams(vmem_limit_bytes=40 * MIB),
        cost_estimate=cost(2),
    )(own, near, far, quarter_routes, weights)


def query_kernel(query_ref, inverse_ref, out_hbm, factor_ref, spread_ref, wide_ref, out_ref, sems):
    count, experts, _ = query_ref.shape
    width = inverse_ref.shape[1]
    step = pl.program_id(0)
    rows = out_ref.shape[0] // width
    pitch = wide_ref.shape[1] // width

    @pl.when(step == 0)
    def _():
        zeros = jnp.zeros((width, width), jnp.bfloat16)
        for e in range(experts):
            high, low = split(inverse_ref[e])
            left = jnp.concatenate([high, zeros, low, zeros], axis=0)
            right = jnp.concatenate([zeros, high, zeros, low], axis=0)
            factor_ref[e] = jnp.concatenate([left, right], axis=1)

    spread_ref[...] = query_ref[...].astype(jnp.float32).reshape(count * experts, LANES)
    for e in range(experts):
        query = spread_ref[pl.ds(e, count, stride=experts), :].astype(jnp.bfloat16)
        result = lax.dot_general(
            factor_ref[e], query, (((1,), (1,)), ((), ())), preferred_element_type=jnp.float32
        )
        result = result[: 2 * width] + result[2 * width :]
        start = e * (rows // experts) + 2 * step
        for tile in range(wide_ref.shape[0]):
            part = result[:, tile * LANES : (tile + 1) * LANES]
            wide_ref[tile, pl.ds(start, width, stride=pitch), :] = part[:width]
            wide_ref[tile, pl.ds(start + 1, width, stride=pitch), :] = part[width:]

    @pl.when(step == pl.num_programs(0) - 1)
    def _():
        copies = []
        for part in range(sems.shape[0]):
            first = part * (width // sems.shape[0])
            for j in range(first, first + width // sems.shape[0]):
                for tile in range(wide_ref.shape[0]):
                    out_ref[j * rows : (j + 1) * rows, tile * LANES : (tile + 1) * LANES] = wide_ref[
                        tile, j * pitch : j * pitch + rows, :
                    ].astype(jnp.bfloat16)
            block = pl.ds(first * rows, width // sems.shape[0] * rows)
            copies.append(pltpu.make_async_copy(out_ref.at[block], out_hbm.at[block], sems.at[part]))
            copies[-1].start()
        for copy in copies:
            copy.wait()


def condition_queries(query_grads, inverse_in):
    count, experts, flat = query_grads.shape
    width = inverse_in.shape[1]
    rows = experts * flat
    return pl.pallas_call(
        query_kernel,
        grid=(flat // LANES,),
        in_specs=[
            pl.BlockSpec((count, experts, LANES), lambda c: (0, 0, c)),
            pl.BlockSpec(inverse_in.shape, lambda c: (0, 0, 0)),
        ],
        out_specs=HBM,
        out_shape=pltpu.HBM((rows, count), jnp.bfloat16),
        scratch_shapes=[
            pltpu.VMEM((experts, 4 * width, 2 * width), jnp.bfloat16),
            pltpu.VMEM((count * experts, LANES), jnp.float32),
            pltpu.VMEM((count // LANES, rows + 8 * width, LANES), jnp.float32),
            pltpu.VMEM((rows, count), jnp.bfloat16),
            pltpu.SemaphoreType.DMA((4,)),
        ],
        compiler_params=pltpu.CompilerParams(vmem_limit_bytes=40 * MIB),
        cost_estimate=cost(10),
    )(stay(query_grads), inverse_in)


def score_kernel(
    arrived_ref, inner_ref, far_ref, out_ref, grads_ref, queries_ref, sem, *, width, doc_count, turns
):
    fetch = pltpu.make_async_copy(far_ref, queries_ref, sem)
    fetch.start()
    sources, quarter, lanes = arrived_ref.shape
    shares = lax.axis_size("proj")
    owners = sources // shares
    outer, inner, docs = [], [], []
    for entry, (owner_turn, share_turn) in enumerate(turns):
        owner = jnp.bitwise_xor(lax.axis_index("expert"), owner_turn)
        share = jnp.bitwise_xor(lax.axis_index("proj"), share_turn)
        outer.append(arrived_ref[listed(owner, owners, owners // 2) * shares + share])
        docs.append(inner_ref[entry, width : width + 1, :].astype(jnp.float32).astype(jnp.int32))
        inner.append(inner_ref[entry, :width, :])
    outer = jnp.concatenate(outer, axis=0)
    inner = jnp.concatenate(inner, axis=1)
    docs = jnp.broadcast_to(jnp.concatenate(docs, axis=1), inner.shape)
    doc_group = 16
    pitch = grads_ref.shape[0] // doc_count

    def one_group(group, carry):
        masked = [
            jnp.where(docs == group * doc_group + d, inner, jnp.zeros_like(inner)) for d in range(doc_group)
        ]
        sums = jnp.dot(jnp.concatenate(masked, axis=0), outer, preferred_element_type=jnp.float32)
        for d in range(doc_group):
            start = pl.multiple_of((group * doc_group + d) * pitch, 8)
            grads_ref[pl.ds(start, width), :] = sums[d * width : (d + 1) * width]
        return carry

    lax.fori_loop(0, doc_count // doc_group, one_group, 0, unroll=doc_count <= 2 * doc_group)
    high, low = [], []
    for j in range(width):
        parts = split(grads_ref[pl.ds(j, doc_count, stride=pitch), :])
        high.append(parts[0])
        low.append(parts[1])
    flat = jnp.concatenate([jnp.concatenate(high, axis=1), jnp.concatenate(low, axis=1)], axis=0)
    fetch.wait()
    result = jnp.dot(flat, queries_ref[...], preferred_element_type=jnp.float32)
    result = result[:doc_count] + result[doc_count:]
    columns = result.shape[1] // shares
    fill = jnp.zeros((DOC_DEV, LANES - columns), jnp.float32)
    for owner in range(owners):
        for share in range(shares):
            piece = result[owner * DOC_DEV : (owner + 1) * DOC_DEV, share * columns : (share + 1) * columns]
            out_ref[listed(owner, owners, owners - 1) * shares + share] = jnp.concatenate([piece, fill], axis=1)


def score(arrived, inner, queries, turns, owners):
    sources = arrived.shape[0]
    width = inner.shape[1] - DOC_ROWS
    doc_count = DOC_DEV * owners
    return pl.pallas_call(
        functools.partial(score_kernel, width=width, doc_count=doc_count, turns=turns),
        in_specs=[VMEM, VMEM, HBM],
        out_shape=jax.ShapeDtypeStruct((sources, DOC_DEV, LANES), jnp.float32),
        scratch_shapes=[
            pltpu.VMEM((doc_count * (width + 8), arrived.shape[2]), jnp.float32),
            pltpu.VMEM(queries.shape, jnp.bfloat16),
            pltpu.SemaphoreType.DMA,
        ],
        compiler_params=pltpu.CompilerParams(vmem_limit_bytes=40 * MIB),
        cost_estimate=cost(5),
    )(arrived, inner, stay(queries))


def sum_kernel(pieces_ref, out_ref):
    total = pieces_ref[0]
    for source in range(1, pieces_ref.shape[0]):
        total = total + pieces_ref[source]
    out_ref[...] = total[:, : out_ref.shape[1]]


def sum_pieces(pieces, columns):
    return pl.pallas_call(
        sum_kernel,
        in_specs=[VMEM],
        out_shape=jax.ShapeDtypeStruct((pieces.shape[1], columns), jnp.float32),
        compiler_params=pltpu.CompilerParams(vmem_limit_bytes=40 * MIB),
    )(pieces)


def exchange(block, axis, size, turn):
    return lax.ppermute(block, axis, [(i, i ^ turn) for i in range(size)])


def double(blocks, turns, axis, size, turn):
    blocks = jnp.concatenate([blocks, exchange(blocks, axis, size, turn)], axis=0)
    return blocks, turns + tuple(t ^ turn for t in turns)


def local(
    activations,
    grad_hidden,
    routes,
    doc_ids,
    query_grads,
    in_projection,
    out_projection,
    inverse_in,
    inverse_out,
):
    tokens, top = routes.shape
    experts, width, _ = inverse_in.shape
    owners = lax.axis_size("expert")
    shares = lax.axis_size("proj")
    quarter = tokens // shares
    assert quarter == LANES and 2 * width == LANES and experts * width // shares == LANES
    assert shares == 4 and owners & (owners - 1) == 0
    assert DOC_DEV * owners <= 256

    flat_hidden = grad_hidden.reshape(tokens * top, grad_hidden.shape[2])
    inner_leaving, inner_own, shared = project_inner(activations, in_projection, inverse_out, shares)
    inner_first = exchange(inner_leaving, "proj", shares, 2)
    far_shared = exchange(shared, "expert", owners, owners // 2)
    leaving, own = project_outer(flat_hidden, out_projection, shares, top)
    far_shared, inner_first, leaving = lax.optimization_barrier((far_shared, inner_first, leaving))
    near = exchange(leaving, "proj", shares, 1)
    shared, turns = jnp.stack([shared, far_shared]), (0, owners // 2)
    for bit in reversed(range((owners // 2).bit_length() - 1)):
        shared, turns = double(shared, turns, "expert", owners, 1 << bit)
    inner_second = exchange(combine(combine_inner_kernel, inner_own, inner_first), "proj", shares, 1)
    sent = combine(combine_outer_kernel, own, near)
    far = exchange(sent, "proj", shares, 2)
    inner = finish_inner(inner_own, inner_first, inner_second, doc_ids.reshape(shares, quarter), width)
    inner, _ = lax.optimization_barrier((inner, sent))
    owner_turns = tuple(reversed(range(owners)))
    arriving = [exchange(inner, "expert", owners, turn) for turn in owner_turns if turn]
    weights = expand(shared, turns, width, experts, shares)
    far, weights = lax.optimization_barrier((far, weights))
    quarter_routes = lax.dynamic_slice_in_dim(routes, lax.axis_index("proj") * quarter, quarter, 0)
    payload = condition(own, near, far, quarter_routes, weights, shares, width)
    payload, arriving = lax.optimization_barrier((payload, arriving))
    arrived = send_to_all(payload, owners, shares, owners // 2)
    inner = jnp.stack(arriving + [inner])
    inner, share_turns = inner[None], (0,)
    inner, share_turns = double(inner, share_turns, "proj", shares, 1)
    inner, query_grads = lax.optimization_barrier((inner, query_grads))
    inner, share_turns = double(inner, share_turns, "proj", shares, 2)
    inner = inner.reshape(owners * shares, width + DOC_ROWS, quarter)
    all_turns = tuple((o, p) for p in share_turns for o in owner_turns)
    queries = condition_queries(query_grads, inverse_in)
    pieces = score(arrived, inner, queries, all_turns, owners)
    pieces = send_to_all(pieces, owners, shares, owners - 1)
    return sum_pieces(pieces, query_grads.shape[0] // shares).T


def solution(mesh):
    in_specs = (
        P(("groups", "expert"), "proj"),
        P(("groups", "expert"), None, "proj"),
        P(("groups", "expert"), None),
        P(("groups", "expert")),
        P(None, "expert", "proj"),
        P(None, "proj"),
        P(None, "proj"),
        P("expert", None, None),
        P("expert", None, None),
    )
    out_specs = P("proj", ("groups", "expert"))
    return jax.shard_map(local, mesh=mesh, in_specs=in_specs, out_specs=out_specs, check_vma=False)
```

```python
import functools

import jax
import jax.numpy as jnp
from jax import lax
from jax.experimental import pallas as pl
from jax.experimental.pallas import tpu as pltpu
from jax.sharding import PartitionSpec as P

DOC_DEV = 8
LANES = 128
DOC_ROWS = 16
MIB = 1024 * 1024
VMEM = pl.BlockSpec(memory_space=pltpu.VMEM)
HBM = pl.BlockSpec(memory_space=pltpu.HBM)


def low_lanes(rows, width):
    return lax.broadcasted_iota(jnp.int32, (rows, LANES), 1) < width


def stay(array):
    return pltpu.with_memory_space_constraint(array, pltpu.HBM)


def listed(owner, owners, first):
    return (owner + owners - first) % owners


def send_to_all(blocks, owners, shares, first):
    members = [(i + first * shares) % (owners * shares) for i in range(owners * shares)]
    return lax.all_to_all(blocks, ("expert", "proj"), 0, 0, tiled=True, axis_index_groups=[members])


def split(value):
    high = value.astype(jnp.bfloat16)
    return high, (value - high.astype(jnp.float32)).astype(jnp.bfloat16)


def cost(microseconds):
    return pl.CostEstimate(flops=0, bytes_accessed=int(microseconds * 3.3e6), transcendentals=0)


def in_order(copies, ahead):
    for copy in copies[:ahead]:
        copy.start()
    state = [0]

    def take():
        copies[state[0]].wait()
        if state[0] + ahead < len(copies):
            copies[state[0] + ahead].start()
        state[0] += 1

    return take


def twice_transposed(projection):
    once = jnp.transpose(projection.astype(jnp.float32))
    return jnp.concatenate([once, once], axis=1).astype(jnp.bfloat16)


def inner_kernel(
    act_hbm, in_proj_hbm, inverse_hbm, leaving_ref, own_ref, shared_ref, act_ref, in_proj_ref, inverse_ref, sems
):
    turns = (2, 3, 1, 0)
    quarter = act_ref.shape[1]
    width = in_proj_ref.shape[0]
    half = quarter // 2
    place = lax.axis_index("proj")
    pairs = [(in_proj_hbm, in_proj_ref)]
    for g, turn in enumerate(turns):
        rows = pl.ds(pl.multiple_of(jnp.bitwise_xor(place, turn) * quarter, quarter), quarter)
        pairs.append((act_hbm.at[rows], act_ref.at[g]))
        if g == 0:
            pairs.append((inverse_hbm, inverse_ref))
    take = in_order([pltpu.make_async_copy(*pair, sems.at[i]) for i, pair in enumerate(pairs)], 5)
    take()
    first = low_lanes(half, width)
    weights = twice_transposed(in_proj_ref[...])
    for wire_ref in (leaving_ref, own_ref):
        take()
        if wire_ref is leaving_ref:
            take()
            experts = inverse_ref.shape[0] // 2
            for e in range(experts):
                pair = jnp.concatenate([inverse_ref[e], inverse_ref[experts + e]], axis=1)
                shared_ref[e * width : (e + 1) * width, :] = pair.astype(jnp.bfloat16)
        take()
        g = 0 if wire_ref is leaving_ref else 2
        rows = act_ref[g : g + 2].reshape(2 * quarter, act_ref.shape[2])
        inner = jnp.dot(rows, weights, preferred_element_type=jnp.float32)
        for i in range(2):
            start = i * quarter
            high, low = split(jnp.where(first, inner[start : start + half], inner[start + half : start + quarter]))
            wire_ref[i, :half, :] = high
            wire_ref[i, half:, :] = low


def project_inner(activations, in_projection, inverse_out, quarters):
    tokens, model = activations.shape
    quarter = tokens // quarters
    experts, width, _ = inverse_out.shape
    wire = jax.ShapeDtypeStruct((quarters // 2, quarter, LANES), jnp.bfloat16)
    fixed = (in_projection, inverse_out)
    return pl.pallas_call(
        inner_kernel,
        in_specs=[HBM] * 3,
        out_specs=[VMEM] * 3,
        out_shape=[wire, wire, jax.ShapeDtypeStruct((experts // 2 * width, LANES), jnp.bfloat16)],
        scratch_shapes=[pltpu.VMEM((quarters, quarter, model), jnp.bfloat16)]
        + [pltpu.VMEM(array.shape, array.dtype) for array in fixed]
        + [pltpu.SemaphoreType.DMA((quarters + len(fixed),))],
        compiler_params=pltpu.CompilerParams(vmem_limit_bytes=40 * MIB),
        cost_estimate=cost(2.5),
    )(*[stay(array) for array in (activations, *fixed)])


def outer_kernel(hidden_hbm, out_proj_hbm, leaving_ref, own_ref, hidden_ref, out_proj_ref, rows_ref, sems, *, top):
    turns = (1, 3, 2, 0)
    chunks, chunk_rows, _ = hidden_ref.shape
    chunk = chunk_rows // top
    split_by = chunks // len(turns)
    quarter = chunk * split_by
    width = out_proj_ref.shape[0]
    place = lax.axis_index("proj")
    pairs = [(out_proj_hbm, out_proj_ref)]
    for i in range(chunks):
        start = (jnp.bitwise_xor(place, turns[i // split_by]) * split_by + i % split_by) * chunk_rows
        pairs.append((hidden_hbm.at[pl.ds(pl.multiple_of(start, chunk_rows), chunk_rows)], hidden_ref.at[i]))
    take = in_order([pltpu.make_async_copy(*pair, sems.at[i]) for i, pair in enumerate(pairs)], 3)
    take()
    first = low_lanes(chunk, width)
    weights = twice_transposed(out_proj_ref[...])

    def pack_rows(i):
        g, part = i // split_by, i % split_by
        wire_ref = leaving_ref.at[g] if g < 2 else own_ref.at[g - 2]
        for pair in range(top // 2):
            even = rows_ref[i % 2, pl.ds(2 * pair, chunk, stride=top), :]
            odd = rows_ref[i % 2, pl.ds(2 * pair + 1, chunk, stride=top), :]
            start = pair * quarter + part * chunk
            wire_ref[start : start + chunk, :] = jnp.where(first, even, odd).astype(jnp.bfloat16)

    for i in range(chunks):
        take()
        rows_ref[i % 2] = jnp.dot(hidden_ref[i], weights, preferred_element_type=jnp.float32)
        if i:
            pack_rows(i - 1)
    pack_rows(chunks - 1)


def project_outer(flat_hidden, out_projection, quarters, top):
    rows, hidden = flat_hidden.shape
    chunks = quarters
    wire = jax.ShapeDtypeStruct((quarters // 2, rows // quarters // 2, LANES), jnp.bfloat16)
    return pl.pallas_call(
        functools.partial(outer_kernel, top=top),
        in_specs=[HBM] * 2,
        out_specs=[VMEM] * 2,
        out_shape=[wire, wire],
        scratch_shapes=[
            pltpu.VMEM((chunks, rows // chunks, hidden), jnp.bfloat16),
            pltpu.VMEM(out_projection.shape, out_projection.dtype),
            pltpu.VMEM((2, rows // chunks, LANES), jnp.float32),
            pltpu.SemaphoreType.DMA((chunks + 1,)),
        ],
        compiler_params=pltpu.CompilerParams(vmem_limit_bytes=40 * MIB),
        cost_estimate=cost(4),
    )(stay(flat_hidden), stay(out_projection))


def exact_rows(rows):
    half = rows.shape[0] // 2
    return rows[:half].astype(jnp.float32) + rows[half:].astype(jnp.float32)


def combine_inner_kernel(own_ref, near_ref, out_ref):
    high, low = split(exact_rows(own_ref[0]) + exact_rows(near_ref[1]))
    out_ref[: high.shape[0], :] = high
    out_ref[high.shape[0] :, :] = low


def combine_outer_kernel(own_ref, near_ref, out_ref):
    out_ref[...] = (own_ref[0].astype(jnp.float32) + near_ref[1].astype(jnp.float32)).astype(jnp.bfloat16)


def combine(kernel, own, near):
    return pl.pallas_call(
        kernel,
        in_specs=[VMEM, VMEM],
        out_shape=jax.ShapeDtypeStruct(own.shape[1:], jnp.bfloat16),
        compiler_params=pltpu.CompilerParams(vmem_limit_bytes=40 * MIB),
        cost_estimate=cost(0.5),
    )(own, near)


def finish_inner_kernel(own_ref, first_ref, second_ref, docs_ref, out_ref):
    total = exact_rows(own_ref[1]) + exact_rows(first_ref[0]) + exact_rows(second_ref[...])
    width = out_ref.shape[0] - DOC_ROWS
    total = jnp.concatenate([total[:, :width], total[:, width:]], axis=0)
    out_ref[:width, :] = jnp.transpose(total).astype(jnp.bfloat16)
    docs = docs_ref[pl.ds(lax.axis_index("proj"), 1), :].astype(jnp.float32)
    out_ref[width:, :] = jnp.broadcast_to(docs, (DOC_ROWS, LANES)).astype(jnp.bfloat16)


def finish_inner(own, first, second, doc_rows, width):
    return pl.pallas_call(
        finish_inner_kernel,
        in_specs=[VMEM] * 4,
        out_shape=jax.ShapeDtypeStruct((width + DOC_ROWS, own.shape[1]), jnp.bfloat16),
        compiler_params=pltpu.CompilerParams(vmem_limit_bytes=40 * MIB),
        cost_estimate=cost(0.5),
    )(own, first, second, doc_rows)


def expand_kernel(shared_ref, weights_ref, *, width, experts, shares, turns):
    columns = experts * width
    share_rows = width // shares
    half = experts // 2
    lane = lax.broadcasted_iota(jnp.int32, (LANES, columns), 1)
    row = lax.broadcasted_iota(jnp.int32, (LANES, columns), 0)
    source = lane // (experts * share_rows) * share_rows + lane % share_rows
    expert_lane = lax.broadcasted_iota(jnp.int32, (half * width, columns), 1) // share_rows % experts
    expert_row = lax.broadcasted_iota(jnp.int32, (half * width, columns), 0) // width
    for side in range(2):
        spread = (row == source + side * width).astype(jnp.float32).astype(jnp.bfloat16)
        own = expert_lane == expert_row + side * half
        for entry, turn in enumerate(turns):
            placed = jnp.dot(
                shared_ref[entry], spread, preferred_element_type=jnp.float32
            )
            weights_ref[turn, side * half * width : (side + 1) * half * width, :] = jnp.where(
                own, placed, 0.0
            ).astype(jnp.bfloat16)


def expand(shared, turns, width, experts, shares):
    owners = shared.shape[0]
    return pl.pallas_call(
        functools.partial(expand_kernel, width=width, experts=experts, shares=shares, turns=turns),
        in_specs=[VMEM],
        out_shape=jax.ShapeDtypeStruct((owners, experts * width, experts * width), jnp.bfloat16),
        compiler_params=pltpu.CompilerParams(vmem_limit_bytes=40 * MIB),
        cost_estimate=cost(1.3),
    )(shared)


def condition_kernel(
    own_ref, near_ref, far_ref, routes_ref, weights_ref, payload_ref, value_ref, name_ref, *, top, width
):
    quarter = routes_ref.shape[0]
    groups, dense_width, _ = weights_ref.shape
    shares = payload_ref.shape[0] // groups
    experts = dense_width // width
    first = low_lanes(quarter, width)
    second = 1 - first.astype(jnp.int32)

    def summed(start, size):
        rows = slice(start, start + size)
        total = own_ref[1, rows, :].astype(jnp.float32) + near_ref[0, rows, :].astype(jnp.float32)
        return total + far_ref[rows, :].astype(jnp.float32)

    for pair in range(top // 2):
        both = summed(pair * quarter, quarter)
        swapped = pltpu.roll(both, width, 1)
        value_ref[2 * pair] = jnp.where(first, both, swapped)
        value_ref[2 * pair + 1] = jnp.where(first, swapped, both)
    for k in range(top):
        name_ref[k] = jnp.broadcast_to(routes_ref[:, k : k + 1], (quarter, LANES)) - second
    def one_group(step, carry):
        group = jnp.bitwise_xor(lax.axis_index("expert"), step)
        dense = []
        for pair in range(experts // 2):
            base = group * experts + 2 * pair
            chosen = jnp.zeros((quarter, LANES), jnp.float32)
            for k in range(top):
                chosen = jnp.where(name_ref[k] == base, value_ref[k], chosen)
            dense.append(chosen.astype(jnp.bfloat16))
        result = jnp.dot(
            jnp.concatenate(dense, axis=1), weights_ref[step], preferred_element_type=jnp.float32
        ).astype(jnp.bfloat16)
        share_width = result.shape[1] // shares
        for share in range(shares):
            payload_ref[listed(group, groups, groups // 2) * shares + share] = result[:, share * share_width : (share + 1) * share_width]
        return carry

    lax.fori_loop(0, groups, one_group, 0, unroll=groups <= 4)


def condition(own, near, far, quarter_routes, weights, shares, width):
    quarter, top = quarter_routes.shape
    groups = weights.shape[0]
    return pl.pallas_call(
        functools.partial(condition_kernel, top=top, width=width),
        in_specs=[VMEM] * 5,
        out_shape=jax.ShapeDtypeStruct((groups * shares, quarter, LANES), jnp.bfloat16),
        scratch_shapes=[
            pltpu.VMEM((top, quarter, LANES), jnp.float32),
            pltpu.VMEM((top, quarter, LANES), jnp.int32),
        ],
        compiler_params=pltpu.CompilerParams(vmem_limit_bytes=40 * MIB),
        cost_estimate=cost(2),
    )(own, near, far, quarter_routes, weights)


def query_kernel(query_ref, inverse_ref, out_hbm, factor_ref, spread_ref, wide_ref, out_ref, sems):
    count, experts, _ = query_ref.shape
    width = inverse_ref.shape[1]
    step = pl.program_id(0)
    rows = out_ref.shape[0] // width
    pitch = wide_ref.shape[1] // width

    @pl.when(step == 0)
    def _():
        zeros = jnp.zeros((width, width), jnp.bfloat16)
        for e in range(experts):
            high, low = split(inverse_ref[e])
            left = jnp.concatenate([high, zeros, low, zeros], axis=0)
            right = jnp.concatenate([zeros, high, zeros, low], axis=0)
            factor_ref[e] = jnp.concatenate([left, right], axis=1)

    spread_ref[...] = query_ref[...].astype(jnp.float32).reshape(count * experts, LANES)
    for e in range(experts):
        query = spread_ref[pl.ds(e, count, stride=experts), :].astype(jnp.bfloat16)
        result = lax.dot_general(
            factor_ref[e], query, (((1,), (1,)), ((), ())), preferred_element_type=jnp.float32
        )
        result = result[: 2 * width] + result[2 * width :]
        start = e * (rows // experts) + 2 * step
        for tile in range(wide_ref.shape[0]):
            part = result[:, tile * LANES : (tile + 1) * LANES]
            wide_ref[tile, pl.ds(start, width, stride=pitch), :] = part[:width]
            wide_ref[tile, pl.ds(start + 1, width, stride=pitch), :] = part[width:]

    @pl.when(step == pl.num_programs(0) - 1)
    def _():
        copies = []
        for part in range(sems.shape[0]):
            first = part * (width // sems.shape[0])
            for j in range(first, first + width // sems.shape[0]):
                for tile in range(wide_ref.shape[0]):
                    out_ref[j * rows : (j + 1) * rows, tile * LANES : (tile + 1) * LANES] = wide_ref[
                        tile, j * pitch : j * pitch + rows, :
                    ].astype(jnp.bfloat16)
            block = pl.ds(first * rows, width // sems.shape[0] * rows)
            copies.append(pltpu.make_async_copy(out_ref.at[block], out_hbm.at[block], sems.at[part]))
            copies[-1].start()
        for copy in copies:
            copy.wait()


def condition_queries(query_grads, inverse_in):
    count, experts, flat = query_grads.shape
    width = inverse_in.shape[1]
    rows = experts * flat
    return pl.pallas_call(
        query_kernel,
        grid=(flat // LANES,),
        in_specs=[
            pl.BlockSpec((count, experts, LANES), lambda c: (0, 0, c)),
            pl.BlockSpec(inverse_in.shape, lambda c: (0, 0, 0)),
        ],
        out_specs=HBM,
        out_shape=pltpu.HBM((rows, count), jnp.bfloat16),
        scratch_shapes=[
            pltpu.VMEM((experts, 4 * width, 2 * width), jnp.bfloat16),
            pltpu.VMEM((count * experts, LANES), jnp.float32),
            pltpu.VMEM((count // LANES, rows + 8 * width, LANES), jnp.float32),
            pltpu.VMEM((rows, count), jnp.bfloat16),
            pltpu.SemaphoreType.DMA((4,)),
        ],
        compiler_params=pltpu.CompilerParams(vmem_limit_bytes=40 * MIB),
        cost_estimate=cost(10),
    )(stay(query_grads), inverse_in)


def score_kernel(
    arrived_ref, inner_ref, far_ref, out_ref, grads_ref, queries_ref, sem, *, width, doc_count, turns
):
    fetch = pltpu.make_async_copy(far_ref, queries_ref, sem)
    fetch.start()
    sources, quarter, lanes = arrived_ref.shape
    shares = lax.axis_size("proj")
    owners = sources // shares
    outer, inner, docs = [], [], []
    for entry, (owner_turn, share_turn) in enumerate(turns):
        owner = jnp.bitwise_xor(lax.axis_index("expert"), owner_turn)
        share = jnp.bitwise_xor(lax.axis_index("proj"), share_turn)
        outer.append(arrived_ref[listed(owner, owners, owners // 2) * shares + share])
        docs.append(inner_ref[entry, width:, :].astype(jnp.float32).astype(jnp.int32))
        inner.append(inner_ref[entry, :width, :])
    outer = jnp.concatenate(outer, axis=0)
    inner = jnp.concatenate(inner, axis=1)
    docs = jnp.concatenate(docs, axis=1)
    odd = lax.dot_general(
        (docs & 1).astype(jnp.float32).astype(jnp.bfloat16),
        jnp.full((DOC_ROWS, lanes), 1 / DOC_ROWS, jnp.bfloat16),
        (((0,), (0,)), ((), ())),
        preferred_element_type=jnp.float32,
    ).astype(jnp.bfloat16)
    odd_outer = outer * odd
    outer = jnp.concatenate([outer - odd_outer, odd_outer], axis=1)
    pairs = jnp.broadcast_to(docs[:1] >> 1, inner.shape)
    pair_group = min(16, doc_count // 2)
    pitch = grads_ref.shape[0] // doc_count

    def one_group(group, carry):
        masked = [
            jnp.where(pairs == group * pair_group + p, inner, jnp.zeros_like(inner)) for p in range(pair_group)
        ]
        sums = jnp.dot(jnp.concatenate(masked, axis=0), outer, preferred_element_type=jnp.float32)
        for p in range(pair_group):
            for parity in range(2):
                start = pl.multiple_of((2 * (group * pair_group + p) + parity) * pitch, 8)
                grads_ref[pl.ds(start, width), :] = sums[
                    p * width : (p + 1) * width, parity * lanes : (parity + 1) * lanes
                ]
        return carry

    groups = doc_count // (2 * pair_group)
    lax.fori_loop(0, groups, one_group, 0, unroll=groups == 1)
    high, low = [], []
    for j in range(width):
        parts = split(grads_ref[pl.ds(j, doc_count, stride=pitch), :])
        high.append(parts[0])
        low.append(parts[1])
    flat = jnp.concatenate([jnp.concatenate(high, axis=1), jnp.concatenate(low, axis=1)], axis=0)
    fetch.wait()
    result = jnp.dot(flat, queries_ref[...], preferred_element_type=jnp.float32)
    result = result[:doc_count] + result[doc_count:]
    columns = result.shape[1] // shares
    fill = jnp.zeros((DOC_DEV, LANES - columns), jnp.float32)
    for owner in range(owners):
        for share in range(shares):
            piece = result[owner * DOC_DEV : (owner + 1) * DOC_DEV, share * columns : (share + 1) * columns]
            out_ref[listed(owner, owners, owners - 1) * shares + share] = jnp.concatenate([piece, fill], axis=1)


def score(arrived, inner, queries, turns, owners):
    sources = arrived.shape[0]
    width = inner.shape[1] - DOC_ROWS
    doc_count = DOC_DEV * owners
    return pl.pallas_call(
        functools.partial(score_kernel, width=width, doc_count=doc_count, turns=turns),
        in_specs=[VMEM, VMEM, HBM],
        out_shape=jax.ShapeDtypeStruct((sources, DOC_DEV, LANES), jnp.float32),
        scratch_shapes=[
            pltpu.VMEM((doc_count * (width + 8), arrived.shape[2]), jnp.float32),
            pltpu.VMEM(queries.shape, jnp.bfloat16),
            pltpu.SemaphoreType.DMA,
        ],
        compiler_params=pltpu.CompilerParams(vmem_limit_bytes=40 * MIB),
        cost_estimate=cost(5),
    )(arrived, inner, stay(queries))


def sum_kernel(pieces_ref, out_ref):
    total = pieces_ref[0]
    for source in range(1, pieces_ref.shape[0]):
        total = total + pieces_ref[source]
    out_ref[...] = total[:, : out_ref.shape[1]]


def sum_pieces(pieces, columns):
    return pl.pallas_call(
        sum_kernel,
        in_specs=[VMEM],
        out_shape=jax.ShapeDtypeStruct((pieces.shape[1], columns), jnp.float32),
        compiler_params=pltpu.CompilerParams(vmem_limit_bytes=40 * MIB),
    )(pieces)


def exchange(block, axis, size, turn):
    return lax.ppermute(block, axis, [(i, i ^ turn) for i in range(size)])


def double(blocks, turns, axis, size, turn):
    blocks = jnp.concatenate([blocks, exchange(blocks, axis, size, turn)], axis=0)
    return blocks, turns + tuple(t ^ turn for t in turns)


def local(
    activations,
    grad_hidden,
    routes,
    doc_ids,
    query_grads,
    in_projection,
    out_projection,
    inverse_in,
    inverse_out,
):
    tokens, top = routes.shape
    experts, width, _ = inverse_in.shape
    owners = lax.axis_size("expert")
    shares = lax.axis_size("proj")
    quarter = tokens // shares
    assert quarter == LANES and 2 * width == LANES and experts * width // shares == LANES
    assert shares == 4 and owners & (owners - 1) == 0
    assert DOC_DEV * owners <= 256

    flat_hidden = grad_hidden.reshape(tokens * top, grad_hidden.shape[2])
    inner_leaving, inner_own, shared = project_inner(activations, in_projection, inverse_out, shares)
    inner_first = exchange(inner_leaving, "proj", shares, 2)
    far_shared = exchange(shared, "expert", owners, owners // 2)
    leaving, own = project_outer(flat_hidden, out_projection, shares, top)
    far_shared, inner_first, leaving = lax.optimization_barrier((far_shared, inner_first, leaving))
    near = exchange(leaving, "proj", shares, 1)
    shared, turns = jnp.stack([shared, far_shared]), (0, owners // 2)
    for bit in reversed(range((owners // 2).bit_length() - 1)):
        shared, turns = double(shared, turns, "expert", owners, 1 << bit)
    inner_second = exchange(combine(combine_inner_kernel, inner_own, inner_first), "proj", shares, 1)
    sent = combine(combine_outer_kernel, own, near)
    far = exchange(sent, "proj", shares, 2)
    inner = finish_inner(inner_own, inner_first, inner_second, doc_ids.reshape(shares, quarter), width)
    inner, _ = lax.optimization_barrier((inner, sent))
    owner_turns = tuple(reversed(range(owners)))
    arriving = [exchange(inner, "expert", owners, turn) for turn in owner_turns if turn]
    weights = expand(shared, turns, width, experts, shares)
    far, weights = lax.optimization_barrier((far, weights))
    quarter_routes = lax.dynamic_slice_in_dim(routes, lax.axis_index("proj") * quarter, quarter, 0)
    payload = condition(own, near, far, quarter_routes, weights, shares, width)
    payload, arriving = lax.optimization_barrier((payload, arriving))
    arrived = send_to_all(payload, owners, shares, owners // 2)
    inner = jnp.stack(arriving + [inner])
    inner, share_turns = inner[None], (0,)
    inner, share_turns = double(inner, share_turns, "proj", shares, 1)
    inner, query_grads = lax.optimization_barrier((inner, query_grads))
    inner, share_turns = double(inner, share_turns, "proj", shares, 2)
    inner = inner.reshape(owners * shares, width + DOC_ROWS, quarter)
    all_turns = tuple((o, p) for p in share_turns for o in owner_turns)
    queries = condition_queries(query_grads, inverse_in)
    pieces = score(arrived, inner, queries, all_turns, owners)
    pieces = send_to_all(pieces, owners, shares, owners - 1)
    return sum_pieces(pieces, query_grads.shape[0] // shares).T


def solution(mesh):
    in_specs = (
        P(("groups", "expert"), "proj"),
        P(("groups", "expert"), None, "proj"),
        P(("groups", "expert"), None),
        P(("groups", "expert")),
        P(None, "expert", "proj"),
        P(None, "proj"),
        P(None, "proj"),
        P("expert", None, None),
        P("expert", None, None),
    )
    out_specs = P("proj", ("groups", "expert"))
    return jax.shard_map(local, mesh=mesh, in_specs=in_specs, out_specs=out_specs, check_vma=False)
```

```python
import functools

import jax
import jax.numpy as jnp
from jax import lax
from jax.experimental import pallas as pl
from jax.experimental.pallas import tpu as pltpu
from jax.sharding import PartitionSpec as P

DOC_DEV = 8
LANES = 128
DOC_ROWS = 16
MIB = 1024 * 1024
VMEM = pl.BlockSpec(memory_space=pltpu.VMEM)
HBM = pl.BlockSpec(memory_space=pltpu.HBM)


def low_lanes(rows, width):
    return lax.broadcasted_iota(jnp.int32, (rows, LANES), 1) < width


def stay(array):
    return pltpu.with_memory_space_constraint(array, pltpu.HBM)


def listed(owner, owners, first):
    return (owner + owners - first) % owners


def send_to_all(blocks, owners, shares, first):
    members = [(i + first * shares) % (owners * shares) for i in range(owners * shares)]
    return lax.all_to_all(blocks, ("expert", "proj"), 0, 0, tiled=True, axis_index_groups=[members])


def split(value):
    high = value.astype(jnp.bfloat16)
    return high, (value - high.astype(jnp.float32)).astype(jnp.bfloat16)


def cost(microseconds):
    return pl.CostEstimate(flops=0, bytes_accessed=int(microseconds * 3.3e6), transcendentals=0)


def in_order(copies, ahead):
    for copy in copies[:ahead]:
        copy.start()
    state = [0]

    def take():
        copies[state[0]].wait()
        if state[0] + ahead < len(copies):
            copies[state[0] + ahead].start()
        state[0] += 1

    return take


def twice_transposed(projection):
    once = jnp.transpose(projection.astype(jnp.float32))
    return jnp.concatenate([once, once], axis=1).astype(jnp.bfloat16)


def inner_kernel(
    act_hbm, in_proj_hbm, inverse_hbm, leaving_ref, own_ref, shared_ref, act_ref, in_proj_ref, inverse_ref, sems
):
    turns = (2, 3, 1, 0)
    quarter = act_ref.shape[1]
    width = in_proj_ref.shape[0]
    half = quarter // 2
    place = lax.axis_index("proj")
    pairs = [(in_proj_hbm, in_proj_ref)]
    for g, turn in enumerate(turns):
        rows = pl.ds(pl.multiple_of(jnp.bitwise_xor(place, turn) * quarter, quarter), quarter)
        pairs.append((act_hbm.at[rows], act_ref.at[g]))
        if g == 0:
            pairs.append((inverse_hbm, inverse_ref))
    take = in_order([pltpu.make_async_copy(*pair, sems.at[i]) for i, pair in enumerate(pairs)], 5)
    take()
    first = low_lanes(half, width)
    weights = twice_transposed(in_proj_ref[...])
    for wire_ref in (leaving_ref, own_ref):
        take()
        if wire_ref is leaving_ref:
            take()
            experts = inverse_ref.shape[0] // 2
            for e in range(experts):
                pair = jnp.concatenate([inverse_ref[e], inverse_ref[experts + e]], axis=1)
                shared_ref[e * width : (e + 1) * width, :] = pair.astype(jnp.bfloat16)
        take()
        g = 0 if wire_ref is leaving_ref else 2
        rows = act_ref[g : g + 2].reshape(2 * quarter, act_ref.shape[2])
        inner = jnp.dot(rows, weights, preferred_element_type=jnp.float32)
        for i in range(2):
            start = i * quarter
            high, low = split(jnp.where(first, inner[start : start + half], inner[start + half : start + quarter]))
            wire_ref[i, :half, :] = high
            wire_ref[i, half:, :] = low


def project_inner(activations, in_projection, inverse_out, quarters):
    tokens, model = activations.shape
    quarter = tokens // quarters
    experts, width, _ = inverse_out.shape
    wire = jax.ShapeDtypeStruct((quarters // 2, quarter, LANES), jnp.bfloat16)
    fixed = (in_projection, inverse_out)
    return pl.pallas_call(
        inner_kernel,
        in_specs=[HBM] * 3,
        out_specs=[VMEM] * 3,
        out_shape=[wire, wire, jax.ShapeDtypeStruct((experts // 2 * width, LANES), jnp.bfloat16)],
        scratch_shapes=[pltpu.VMEM((quarters, quarter, model), jnp.bfloat16)]
        + [pltpu.VMEM(array.shape, array.dtype) for array in fixed]
        + [pltpu.SemaphoreType.DMA((quarters + len(fixed),))],
        compiler_params=pltpu.CompilerParams(vmem_limit_bytes=40 * MIB),
        cost_estimate=cost(2.5),
    )(*[stay(array) for array in (activations, *fixed)])


def outer_kernel(hidden_hbm, out_proj_hbm, leaving_ref, own_ref, hidden_ref, out_proj_ref, rows_ref, sems, *, top):
    turns = (1, 3, 2, 0)
    chunks, chunk_rows, _ = hidden_ref.shape
    chunk = chunk_rows // top
    split_by = chunks // len(turns)
    quarter = chunk * split_by
    width = out_proj_ref.shape[0]
    place = lax.axis_index("proj")
    pairs = [(out_proj_hbm, out_proj_ref)]
    for i in range(chunks):
        start = (jnp.bitwise_xor(place, turns[i // split_by]) * split_by + i % split_by) * chunk_rows
        pairs.append((hidden_hbm.at[pl.ds(pl.multiple_of(start, chunk_rows), chunk_rows)], hidden_ref.at[i]))
    take = in_order([pltpu.make_async_copy(*pair, sems.at[i]) for i, pair in enumerate(pairs)], 3)
    take()
    first = low_lanes(chunk, width)
    weights = twice_transposed(out_proj_ref[...])

    def pack_rows(i):
        g, part = i // split_by, i % split_by
        wire_ref = leaving_ref.at[g] if g < 2 else own_ref.at[g - 2]
        for pair in range(top // 2):
            even = rows_ref[i % 2, pl.ds(2 * pair, chunk, stride=top), :]
            odd = rows_ref[i % 2, pl.ds(2 * pair + 1, chunk, stride=top), :]
            start = pair * quarter + part * chunk
            wire_ref[start : start + chunk, :] = jnp.where(first, even, odd).astype(jnp.bfloat16)

    for i in range(chunks):
        take()
        rows_ref[i % 2] = jnp.dot(hidden_ref[i], weights, preferred_element_type=jnp.float32)
        if i:
            pack_rows(i - 1)
    pack_rows(chunks - 1)


def project_outer(flat_hidden, out_projection, quarters, top):
    rows, hidden = flat_hidden.shape
    chunks = quarters
    wire = jax.ShapeDtypeStruct((quarters // 2, rows // quarters // 2, LANES), jnp.bfloat16)
    return pl.pallas_call(
        functools.partial(outer_kernel, top=top),
        in_specs=[HBM] * 2,
        out_specs=[VMEM] * 2,
        out_shape=[wire, wire],
        scratch_shapes=[
            pltpu.VMEM((chunks, rows // chunks, hidden), jnp.bfloat16),
            pltpu.VMEM(out_projection.shape, out_projection.dtype),
            pltpu.VMEM((2, rows // chunks, LANES), jnp.float32),
            pltpu.SemaphoreType.DMA((chunks + 1,)),
        ],
        compiler_params=pltpu.CompilerParams(vmem_limit_bytes=40 * MIB),
        cost_estimate=cost(4),
    )(stay(flat_hidden), stay(out_projection))


def exact_rows(rows):
    half = rows.shape[0] // 2
    return rows[:half].astype(jnp.float32) + rows[half:].astype(jnp.float32)


def combine_inner_kernel(own_ref, near_ref, out_ref):
    high, low = split(exact_rows(own_ref[0]) + exact_rows(near_ref[1]))
    out_ref[: high.shape[0], :] = high
    out_ref[high.shape[0] :, :] = low


def combine_outer_kernel(own_ref, near_ref, out_ref):
    out_ref[...] = (own_ref[0].astype(jnp.float32) + near_ref[1].astype(jnp.float32)).astype(jnp.bfloat16)


def combine(kernel, own, near):
    return pl.pallas_call(
        kernel,
        in_specs=[VMEM, VMEM],
        out_shape=jax.ShapeDtypeStruct(own.shape[1:], jnp.bfloat16),
        compiler_params=pltpu.CompilerParams(vmem_limit_bytes=40 * MIB),
        cost_estimate=cost(0.5),
    )(own, near)


def finish_inner_kernel(own_ref, first_ref, second_ref, docs_ref, out_ref):
    total = exact_rows(own_ref[1]) + exact_rows(first_ref[0]) + exact_rows(second_ref[...])
    width = out_ref.shape[0] - DOC_ROWS
    total = jnp.concatenate([total[:, :width], total[:, width:]], axis=0)
    out_ref[:width, :] = jnp.transpose(total).astype(jnp.bfloat16)
    docs = docs_ref[pl.ds(lax.axis_index("proj"), 1), :].astype(jnp.float32)
    out_ref[width:, :] = jnp.broadcast_to(docs, (DOC_ROWS, LANES)).astype(jnp.bfloat16)


def finish_inner(own, first, second, doc_rows, width):
    return pl.pallas_call(
        finish_inner_kernel,
        in_specs=[VMEM] * 4,
        out_shape=jax.ShapeDtypeStruct((width + DOC_ROWS, own.shape[1]), jnp.bfloat16),
        compiler_params=pltpu.CompilerParams(vmem_limit_bytes=40 * MIB),
        cost_estimate=cost(0.5),
    )(own, first, second, doc_rows)


def expand_kernel(shared_ref, weights_ref, *, width, experts, shares, turns):
    half = experts // 2
    share_rows = width // shares
    columns = shares * half * share_rows
    lane = lax.broadcasted_iota(jnp.int32, (LANES, columns), 1)
    row = lax.broadcasted_iota(jnp.int32, (LANES, columns), 0)
    expert_lane = lax.broadcasted_iota(jnp.int32, (half * width, columns), 1) // share_rows % half
    expert_row = lax.broadcasted_iota(jnp.int32, (half * width, columns), 0) // width
    own = expert_lane == expert_row
    for side in range(2):
        share = jnp.bitwise_xor(lane // (half * share_rows), side)
        source = share * share_rows + lane % share_rows
        spread = (row == source + side * width).astype(jnp.float32).astype(jnp.bfloat16)
        for entry, turn in enumerate(turns):
            placed = jnp.dot(shared_ref[entry], spread, preferred_element_type=jnp.float32)
            weights_ref[turn, side] = jnp.where(own, placed, 0.0).astype(jnp.bfloat16)


def expand(shared, turns, width, experts, shares):
    owners = shared.shape[0]
    return pl.pallas_call(
        functools.partial(expand_kernel, width=width, experts=experts, shares=shares, turns=turns),
        in_specs=[VMEM],
        out_shape=jax.ShapeDtypeStruct((owners, 2, experts // 2 * width, experts // 2 * width), jnp.bfloat16),
        compiler_params=pltpu.CompilerParams(vmem_limit_bytes=40 * MIB),
        cost_estimate=cost(1.3),
    )(shared)


def condition_kernel(
    own_ref, near_ref, far_ref, routes_ref, weights_ref, payload_ref, value_ref, name_ref, *, top, width
):
    quarter = routes_ref.shape[0]
    groups, sides, dense_width, _ = weights_ref.shape
    shares = payload_ref.shape[0] // groups
    experts = sides * dense_width // width
    first = low_lanes(quarter, width)
    second = 1 - first.astype(jnp.int32)

    def summed(start, size):
        rows = slice(start, start + size)
        total = own_ref[1, rows, :].astype(jnp.float32) + near_ref[0, rows, :].astype(jnp.float32)
        return total + far_ref[rows, :].astype(jnp.float32)

    for pair in range(top // 2):
        both = summed(pair * quarter, quarter)
        swapped = pltpu.roll(both, width, 1)
        value_ref[2 * pair] = jnp.where(first, both, swapped)
        value_ref[2 * pair + 1] = jnp.where(first, swapped, both)
    for k in range(top):
        name_ref[k] = jnp.broadcast_to(routes_ref[:, k : k + 1], (quarter, LANES)) - second

    def one_group(step, carry):
        group = jnp.bitwise_xor(lax.axis_index("expert"), step)
        dense = []
        for pair in range(experts // 2):
            base = group * experts + 2 * pair
            chosen = jnp.zeros((quarter, LANES), jnp.float32)
            for k in range(top):
                chosen = jnp.where(name_ref[k] == base, value_ref[k], chosen)
            dense.append(chosen.astype(jnp.bfloat16))
        per_side = len(dense) // sides
        results = [
            jnp.dot(
                jnp.concatenate(dense[side * per_side : (side + 1) * per_side], axis=1),
                weights_ref[step, side],
                preferred_element_type=jnp.float32,
            )
            for side in range(sides)
        ]
        for share in range(shares):
            lanes = slice(share // 2 * LANES, (share // 2 + 1) * LANES)
            low, high = (results[side][:, lanes] for side in ((0, 1) if share % 2 == 0 else (1, 0)))
            place = listed(group, groups, groups // 2) * shares + share
            payload_ref[place] = jnp.where(first, low, high).astype(jnp.bfloat16)
        return carry

    lax.fori_loop(0, groups, one_group, 0, unroll=groups <= 4)


def condition(own, near, far, quarter_routes, weights, shares, width):
    quarter, top = quarter_routes.shape
    groups = weights.shape[0]
    return pl.pallas_call(
        functools.partial(condition_kernel, top=top, width=width),
        in_specs=[VMEM] * 5,
        out_shape=jax.ShapeDtypeStruct((groups * shares, quarter, LANES), jnp.bfloat16),
        scratch_shapes=[
            pltpu.VMEM((top, quarter, LANES), jnp.float32),
            pltpu.VMEM((top, quarter, LANES), jnp.int32),
        ],
        compiler_params=pltpu.CompilerParams(vmem_limit_bytes=40 * MIB),
        cost_estimate=cost(2),
    )(own, near, far, quarter_routes, weights)


def query_kernel(query_ref, inverse_ref, out_hbm, factor_ref, spread_ref, wide_ref, out_ref, sems):
    count, experts, _ = query_ref.shape
    width = inverse_ref.shape[1]
    step = pl.program_id(0)
    rows = out_ref.shape[0] // width
    pitch = wide_ref.shape[1] // width

    @pl.when(step == 0)
    def _():
        zeros = jnp.zeros((width, width), jnp.bfloat16)
        for e in range(experts):
            high, low = split(inverse_ref[e])
            left = jnp.concatenate([high, zeros, low, zeros], axis=0)
            right = jnp.concatenate([zeros, high, zeros, low], axis=0)
            factor_ref[e] = jnp.concatenate([left, right], axis=1)

    spread_ref[...] = query_ref[...].astype(jnp.float32).reshape(count * experts, LANES)
    for e in range(experts):
        query = spread_ref[pl.ds(e, count, stride=experts), :].astype(jnp.bfloat16)
        result = lax.dot_general(
            factor_ref[e], query, (((1,), (1,)), ((), ())), preferred_element_type=jnp.float32
        )
        result = result[: 2 * width] + result[2 * width :]
        slot = (e + experts // 2 * (lax.axis_index("proj") % 2)) % experts
        start = slot * (rows // experts) + 2 * step
        for tile in range(wide_ref.shape[0]):
            part = result[:, tile * LANES : (tile + 1) * LANES]
            wide_ref[tile, pl.ds(start, width, stride=pitch), :] = part[:width]
            wide_ref[tile, pl.ds(start + 1, width, stride=pitch), :] = part[width:]

    @pl.when(step == pl.num_programs(0) - 1)
    def _():
        copies = []
        for part in range(sems.shape[0]):
            first = part * (width // sems.shape[0])
            for j in range(first, first + width // sems.shape[0]):
                for tile in range(wide_ref.shape[0]):
                    out_ref[j * rows : (j + 1) * rows, tile * LANES : (tile + 1) * LANES] = wide_ref[
                        tile, j * pitch : j * pitch + rows, :
                    ].astype(jnp.bfloat16)
            block = pl.ds(first * rows, width // sems.shape[0] * rows)
            copies.append(pltpu.make_async_copy(out_ref.at[block], out_hbm.at[block], sems.at[part]))
            copies[-1].start()
        for copy in copies:
            copy.wait()


def condition_queries(query_grads, inverse_in):
    count, experts, flat = query_grads.shape
    width = inverse_in.shape[1]
    rows = experts * flat
    return pl.pallas_call(
        query_kernel,
        grid=(flat // LANES,),
        in_specs=[
            pl.BlockSpec((count, experts, LANES), lambda c: (0, 0, c)),
            pl.BlockSpec(inverse_in.shape, lambda c: (0, 0, 0)),
        ],
        out_specs=HBM,
        out_shape=pltpu.HBM((rows, count), jnp.bfloat16),
        scratch_shapes=[
            pltpu.VMEM((experts, 4 * width, 2 * width), jnp.bfloat16),
            pltpu.VMEM((count * experts, LANES), jnp.float32),
            pltpu.VMEM((count // LANES, rows + 8 * width, LANES), jnp.float32),
            pltpu.VMEM((rows, count), jnp.bfloat16),
            pltpu.SemaphoreType.DMA((4,)),
        ],
        compiler_params=pltpu.CompilerParams(vmem_limit_bytes=40 * MIB),
        cost_estimate=cost(10),
    )(stay(query_grads), inverse_in)


def score_kernel(
    arrived_ref, inner_ref, far_ref, out_ref, grads_ref, queries_ref, sem, *, width, doc_count, turns
):
    fetch = pltpu.make_async_copy(far_ref, queries_ref, sem)
    fetch.start()
    sources, quarter, lanes = arrived_ref.shape
    shares = lax.axis_size("proj")
    owners = sources // shares
    outer, inner, docs = [], [], []
    for entry, (owner_turn, share_turn) in enumerate(turns):
        owner = jnp.bitwise_xor(lax.axis_index("expert"), owner_turn)
        share = jnp.bitwise_xor(lax.axis_index("proj"), share_turn)
        outer.append(arrived_ref[listed(owner, owners, owners // 2) * shares + share])
        docs.append(inner_ref[entry, width:, :].astype(jnp.float32).astype(jnp.int32))
        inner.append(inner_ref[entry, :width, :])
    outer = jnp.concatenate(outer, axis=0)
    inner = jnp.concatenate(inner, axis=1)
    docs = jnp.concatenate(docs, axis=1)
    odd = lax.dot_general(
        (docs & 1).astype(jnp.float32).astype(jnp.bfloat16),
        jnp.full((DOC_ROWS, lanes), 1 / DOC_ROWS, jnp.bfloat16),
        (((0,), (0,)), ((), ())),
        preferred_element_type=jnp.float32,
    ).astype(jnp.bfloat16)
    odd_outer = outer * odd
    outer = jnp.concatenate([outer - odd_outer, odd_outer], axis=1)
    pairs = jnp.broadcast_to(docs[:1] >> 1, inner.shape)
    pair_group = min(16, doc_count // 2)
    pitch = grads_ref.shape[0] // doc_count

    def one_group(group, carry):
        masked = [
            jnp.where(pairs == group * pair_group + p, inner, jnp.zeros_like(inner)) for p in range(pair_group)
        ]
        sums = jnp.dot(jnp.concatenate(masked, axis=0), outer, preferred_element_type=jnp.float32)
        for p in range(pair_group):
            for parity in range(2):
                start = pl.multiple_of((2 * (group * pair_group + p) + parity) * pitch, 8)
                grads_ref[pl.ds(start, width), :] = sums[
                    p * width : (p + 1) * width, parity * lanes : (parity + 1) * lanes
                ]
        return carry

    groups = doc_count // (2 * pair_group)
    lax.fori_loop(0, groups, one_group, 0, unroll=groups == 1)
    high, low = [], []
    for j in range(width):
        parts = split(grads_ref[pl.ds(j, doc_count, stride=pitch), :])
        high.append(parts[0])
        low.append(parts[1])
    flat = jnp.concatenate([jnp.concatenate(high, axis=1), jnp.concatenate(low, axis=1)], axis=0)
    fetch.wait()
    result = jnp.dot(flat, queries_ref[...], preferred_element_type=jnp.float32)
    result = result[:doc_count] + result[doc_count:]
    columns = result.shape[1] // shares
    fill = jnp.zeros((DOC_DEV, LANES - columns), jnp.float32)
    for owner in range(owners):
        for share in range(shares):
            piece = result[owner * DOC_DEV : (owner + 1) * DOC_DEV, share * columns : (share + 1) * columns]
            out_ref[listed(owner, owners, owners - 1) * shares + share] = jnp.concatenate([piece, fill], axis=1)


def score(arrived, inner, queries, turns, owners):
    sources = arrived.shape[0]
    width = inner.shape[1] - DOC_ROWS
    doc_count = DOC_DEV * owners
    return pl.pallas_call(
        functools.partial(score_kernel, width=width, doc_count=doc_count, turns=turns),
        in_specs=[VMEM, VMEM, HBM],
        out_shape=jax.ShapeDtypeStruct((sources, DOC_DEV, LANES), jnp.float32),
        scratch_shapes=[
            pltpu.VMEM((doc_count * (width + 8), arrived.shape[2]), jnp.float32),
            pltpu.VMEM(queries.shape, jnp.bfloat16),
            pltpu.SemaphoreType.DMA,
        ],
        compiler_params=pltpu.CompilerParams(vmem_limit_bytes=40 * MIB),
        cost_estimate=cost(5),
    )(arrived, inner, stay(queries))


def sum_kernel(pieces_ref, out_ref):
    total = pieces_ref[0]
    for source in range(1, pieces_ref.shape[0]):
        total = total + pieces_ref[source]
    out_ref[...] = total[:, : out_ref.shape[1]]


def sum_pieces(pieces, columns):
    return pl.pallas_call(
        sum_kernel,
        in_specs=[VMEM],
        out_shape=jax.ShapeDtypeStruct((pieces.shape[1], columns), jnp.float32),
        compiler_params=pltpu.CompilerParams(vmem_limit_bytes=40 * MIB),
    )(pieces)


def exchange(block, axis, size, turn):
    return lax.ppermute(block, axis, [(i, i ^ turn) for i in range(size)])


def double(blocks, turns, axis, size, turn):
    blocks = jnp.concatenate([blocks, exchange(blocks, axis, size, turn)], axis=0)
    return blocks, turns + tuple(t ^ turn for t in turns)


def local(
    activations,
    grad_hidden,
    routes,
    doc_ids,
    query_grads,
    in_projection,
    out_projection,
    inverse_in,
    inverse_out,
):
    tokens, top = routes.shape
    experts, width, _ = inverse_in.shape
    owners = lax.axis_size("expert")
    shares = lax.axis_size("proj")
    quarter = tokens // shares
    assert quarter == LANES and 2 * width == LANES and experts * width // shares == LANES
    assert shares == 4 and owners & (owners - 1) == 0
    assert DOC_DEV * owners <= 256

    flat_hidden = grad_hidden.reshape(tokens * top, grad_hidden.shape[2])
    inner_leaving, inner_own, shared = project_inner(activations, in_projection, inverse_out, shares)
    inner_first = exchange(inner_leaving, "proj", shares, 2)
    far_shared = exchange(shared, "expert", owners, owners // 2)
    leaving, own = project_outer(flat_hidden, out_projection, shares, top)
    far_shared, inner_first, leaving = lax.optimization_barrier((far_shared, inner_first, leaving))
    near = exchange(leaving, "proj", shares, 1)
    shared, turns = jnp.stack([shared, far_shared]), (0, owners // 2)
    for bit in reversed(range((owners // 2).bit_length() - 1)):
        shared, turns = double(shared, turns, "expert", owners, 1 << bit)
    inner_second = exchange(combine(combine_inner_kernel, inner_own, inner_first), "proj", shares, 1)
    sent = combine(combine_outer_kernel, own, near)
    far = exchange(sent, "proj", shares, 2)
    inner = finish_inner(inner_own, inner_first, inner_second, doc_ids.reshape(shares, quarter), width)
    inner, _ = lax.optimization_barrier((inner, sent))
    owner_turns = tuple(reversed(range(owners)))
    arriving = [exchange(inner, "expert", owners, turn) for turn in owner_turns if turn]
    weights = expand(shared, turns, width, experts, shares)
    far, weights = lax.optimization_barrier((far, weights))
    quarter_routes = lax.dynamic_slice_in_dim(routes, lax.axis_index("proj") * quarter, quarter, 0)
    payload = condition(own, near, far, quarter_routes, weights, shares, width)
    payload, arriving = lax.optimization_barrier((payload, arriving))
    arrived = send_to_all(payload, owners, shares, owners // 2)
    inner = jnp.stack(arriving + [inner])
    inner, share_turns = inner[None], (0,)
    inner, share_turns = double(inner, share_turns, "proj", shares, 1)
    inner, query_grads = lax.optimization_barrier((inner, query_grads))
    inner, share_turns = double(inner, share_turns, "proj", shares, 2)
    inner = inner.reshape(owners * shares, width + DOC_ROWS, quarter)
    all_turns = tuple((o, p) for p in share_turns for o in owner_turns)
    queries = condition_queries(query_grads, inverse_in)
    pieces = score(arrived, inner, queries, all_turns, owners)
    pieces = send_to_all(pieces, owners, shares, owners - 1)
    return sum_pieces(pieces, query_grads.shape[0] // shares).T


def solution(mesh):
    in_specs = (
        P(("groups", "expert"), "proj"),
        P(("groups", "expert"), None, "proj"),
        P(("groups", "expert"), None),
        P(("groups", "expert")),
        P(None, "expert", "proj"),
        P(None, "proj"),
        P(None, "proj"),
        P("expert", None, None),
        P("expert", None, None),
    )
    out_specs = P("proj", ("groups", "expert"))
    return jax.shard_map(local, mesh=mesh, in_specs=in_specs, out_specs=out_specs, check_vma=False)
```

```python
import functools

import jax
import jax.numpy as jnp
from jax import lax
from jax.experimental import pallas as pl
from jax.experimental.pallas import tpu as pltpu
from jax.sharding import PartitionSpec as P

DOC_DEV = 8
LANES = 128
DOC_ROWS = 16
MIB = 1024 * 1024
VMEM = pl.BlockSpec(memory_space=pltpu.VMEM)
HBM = pl.BlockSpec(memory_space=pltpu.HBM)


def low_lanes(rows, width):
    return lax.broadcasted_iota(jnp.int32, (rows, LANES), 1) < width


def stay(array):
    return pltpu.with_memory_space_constraint(array, pltpu.HBM)


def listed(owner, owners, first):
    return (owner + owners - first) % owners


def send_to_all(blocks, owners, shares, first):
    members = [(i + first * shares) % (owners * shares) for i in range(owners * shares)]
    return lax.all_to_all(blocks, ("expert", "proj"), 0, 0, tiled=True, axis_index_groups=[members])


def split(value):
    high = value.astype(jnp.bfloat16)
    return high, (value - high.astype(jnp.float32)).astype(jnp.bfloat16)


def cost(microseconds):
    return pl.CostEstimate(flops=0, bytes_accessed=int(microseconds * 3.3e6), transcendentals=0)


def in_order(copies, ahead):
    for copy in copies[:ahead]:
        copy.start()
    state = [0]

    def take():
        copies[state[0]].wait()
        if state[0] + ahead < len(copies):
            copies[state[0] + ahead].start()
        state[0] += 1

    return take


def twice_transposed(projection):
    once = jnp.transpose(projection.astype(jnp.float32))
    return jnp.concatenate([once, once], axis=1).astype(jnp.bfloat16)


def inner_kernel(act_hbm, in_proj_hbm, inverse_hbm, wire_ref, shared_ref, act_ref, in_proj_ref, inverse_ref, sems):
    quarters, quarter, model = act_ref.shape
    width = in_proj_ref.shape[0]
    half = quarter // 2
    pairs = [(in_proj_hbm, in_proj_ref)]
    for q in range(quarters):
        pairs.append((act_hbm.at[pl.ds(q * quarter, quarter)], act_ref.at[q]))
        if q == 0:
            pairs.append((inverse_hbm, inverse_ref))
    take = in_order([pltpu.make_async_copy(*pair, sems.at[i]) for i, pair in enumerate(pairs)], 5)
    take()
    first = low_lanes(half, width)
    weights = twice_transposed(in_proj_ref[...])
    for q in range(0, quarters, 2):
        take()
        if q == 0:
            take()
            experts = inverse_ref.shape[0] // 2
            for e in range(experts):
                pair = jnp.concatenate([inverse_ref[e], inverse_ref[experts + e]], axis=1)
                shared_ref[e * width : (e + 1) * width, :] = pair.astype(jnp.bfloat16)
        take()
        rows = act_ref[q : q + 2].reshape(2 * quarter, model)
        inner = jnp.dot(rows, weights, preferred_element_type=jnp.float32)
        for i in range(2):
            start = i * quarter
            high, low = split(jnp.where(first, inner[start : start + half], inner[start + half : start + quarter]))
            wire_ref[q + i, :half, :] = high
            wire_ref[q + i, half:, :] = low


def project_inner(activations, in_projection, inverse_out, quarters):
    tokens, model = activations.shape
    quarter = tokens // quarters
    experts, width, _ = inverse_out.shape
    fixed = (in_projection, inverse_out)
    return pl.pallas_call(
        inner_kernel,
        in_specs=[HBM] * 3,
        out_specs=[VMEM] * 2,
        out_shape=[
            jax.ShapeDtypeStruct((quarters, quarter, LANES), jnp.bfloat16),
            jax.ShapeDtypeStruct((experts // 2 * width, LANES), jnp.bfloat16),
        ],
        scratch_shapes=[pltpu.VMEM((quarters, quarter, model), jnp.bfloat16)]
        + [pltpu.VMEM(array.shape, array.dtype) for array in fixed]
        + [pltpu.SemaphoreType.DMA((quarters + len(fixed),))],
        compiler_params=pltpu.CompilerParams(vmem_limit_bytes=40 * MIB),
        cost_estimate=cost(2.5),
    )(*[stay(array) for array in (activations, *fixed)])


def outer_kernel(hidden_hbm, out_proj_hbm, leaving_ref, own_ref, hidden_ref, out_proj_ref, rows_ref, sems, *, top):
    turns = (1, 3, 2, 0)
    chunks, chunk_rows, _ = hidden_ref.shape
    chunk = chunk_rows // top
    split_by = chunks // len(turns)
    quarter = chunk * split_by
    width = out_proj_ref.shape[0]
    place = lax.axis_index("proj")
    pairs = [(out_proj_hbm, out_proj_ref)]
    for i in range(chunks):
        start = (jnp.bitwise_xor(place, turns[i // split_by]) * split_by + i % split_by) * chunk_rows
        pairs.append((hidden_hbm.at[pl.ds(pl.multiple_of(start, chunk_rows), chunk_rows)], hidden_ref.at[i]))
    take = in_order([pltpu.make_async_copy(*pair, sems.at[i]) for i, pair in enumerate(pairs)], 3)
    take()
    first = low_lanes(chunk, width)
    weights = twice_transposed(out_proj_ref[...])

    def pack_rows(i):
        g, part = i // split_by, i % split_by
        wire_ref = leaving_ref.at[g] if g < 2 else own_ref.at[g - 2]
        for pair in range(top // 2):
            even = rows_ref[i % 2, pl.ds(2 * pair, chunk, stride=top), :]
            odd = rows_ref[i % 2, pl.ds(2 * pair + 1, chunk, stride=top), :]
            start = pair * quarter + part * chunk
            wire_ref[start : start + chunk, :] = jnp.where(first, even, odd).astype(jnp.bfloat16)

    for i in range(chunks):
        take()
        rows_ref[i % 2] = jnp.dot(hidden_ref[i], weights, preferred_element_type=jnp.float32)
        if i:
            pack_rows(i - 1)
    pack_rows(chunks - 1)


def project_outer(flat_hidden, out_projection, quarters, top):
    rows, hidden = flat_hidden.shape
    chunks = quarters
    wire = jax.ShapeDtypeStruct((quarters // 2, rows // quarters // 2, LANES), jnp.bfloat16)
    return pl.pallas_call(
        functools.partial(outer_kernel, top=top),
        in_specs=[HBM] * 2,
        out_specs=[VMEM] * 2,
        out_shape=[wire, wire],
        scratch_shapes=[
            pltpu.VMEM((chunks, rows // chunks, hidden), jnp.bfloat16),
            pltpu.VMEM(out_projection.shape, out_projection.dtype),
            pltpu.VMEM((2, rows // chunks, LANES), jnp.float32),
            pltpu.SemaphoreType.DMA((chunks + 1,)),
        ],
        compiler_params=pltpu.CompilerParams(vmem_limit_bytes=40 * MIB),
        cost_estimate=cost(4),
    )(stay(flat_hidden), stay(out_projection))


def exact_rows(rows):
    half = rows.shape[0] // 2
    return rows[:half].astype(jnp.float32) + rows[half:].astype(jnp.float32)


def combine_inner_kernel(own_ref, other_ref, out_ref):
    half = out_ref.shape[1] // 2
    for q in range(out_ref.shape[0]):
        high, low = split(exact_rows(own_ref[q]) + exact_rows(other_ref[q]))
        out_ref[q, :half, :] = high
        out_ref[q, half:, :] = low


def combine_outer_kernel(own_ref, near_ref, out_ref):
    out_ref[...] = (own_ref[0].astype(jnp.float32) + near_ref[1].astype(jnp.float32)).astype(jnp.bfloat16)


def combine(kernel, own, near, shape):
    return pl.pallas_call(
        kernel,
        in_specs=[VMEM, VMEM],
        out_shape=jax.ShapeDtypeStruct(shape, jnp.bfloat16),
        compiler_params=pltpu.CompilerParams(vmem_limit_bytes=40 * MIB),
        cost_estimate=cost(0.5),
    )(own, near)


def finish_inner_kernel(own_ref, other_ref, docs_ref, out_ref):
    width = out_ref.shape[1] - DOC_ROWS
    for q in range(out_ref.shape[0]):
        total = exact_rows(own_ref[q]) + exact_rows(other_ref[q])
        total = jnp.concatenate([total[:, :width], total[:, width:]], axis=0)
        out_ref[q, :width, :] = jnp.transpose(total).astype(jnp.bfloat16)
        docs = docs_ref[q : q + 1, :].astype(jnp.float32)
        out_ref[q, width:, :] = jnp.broadcast_to(docs, (DOC_ROWS, LANES)).astype(jnp.bfloat16)


def finish_inner(own, other, doc_rows, width):
    return pl.pallas_call(
        finish_inner_kernel,
        in_specs=[VMEM] * 3,
        out_shape=jax.ShapeDtypeStruct((own.shape[0], width + DOC_ROWS, own.shape[1]), jnp.bfloat16),
        compiler_params=pltpu.CompilerParams(vmem_limit_bytes=40 * MIB),
        cost_estimate=cost(0.5),
    )(own, other, doc_rows)


def expand_kernel(shared_ref, weights_ref, *, width, experts, shares, turns):
    half = experts // 2
    share_rows = width // shares
    columns = shares * half * share_rows
    lane = lax.broadcasted_iota(jnp.int32, (LANES, columns), 1)
    row = lax.broadcasted_iota(jnp.int32, (LANES, columns), 0)
    expert_lane = lax.broadcasted_iota(jnp.int32, (half * width, columns), 1) // share_rows % half
    expert_row = lax.broadcasted_iota(jnp.int32, (half * width, columns), 0) // width
    own = expert_lane == expert_row
    for side in range(2):
        share = jnp.bitwise_xor(lane // (half * share_rows), side)
        source = share * share_rows + lane % share_rows
        spread = (row == source + side * width).astype(jnp.float32).astype(jnp.bfloat16)
        for entry, turn in enumerate(turns):
            placed = jnp.dot(shared_ref[entry], spread, preferred_element_type=jnp.float32)
            weights_ref[turn, side] = jnp.where(own, placed, 0.0).astype(jnp.bfloat16)


def expand(shared, turns, width, experts, shares):
    owners = shared.shape[0]
    return pl.pallas_call(
        functools.partial(expand_kernel, width=width, experts=experts, shares=shares, turns=turns),
        in_specs=[VMEM],
        out_shape=jax.ShapeDtypeStruct((owners, 2, experts // 2 * width, experts // 2 * width), jnp.bfloat16),
        compiler_params=pltpu.CompilerParams(vmem_limit_bytes=40 * MIB),
        cost_estimate=cost(1.3),
    )(shared)


def condition_kernel(
    own_ref, near_ref, far_ref, routes_ref, weights_ref, payload_ref, value_ref, name_ref, *, top, width
):
    quarter = routes_ref.shape[0]
    groups, sides, dense_width, _ = weights_ref.shape
    shares = payload_ref.shape[0] // groups
    experts = sides * dense_width // width
    first = low_lanes(quarter, width)
    second = 1 - first.astype(jnp.int32)

    def summed(start, size):
        rows = slice(start, start + size)
        total = own_ref[1, rows, :].astype(jnp.float32) + near_ref[0, rows, :].astype(jnp.float32)
        return total + far_ref[rows, :].astype(jnp.float32)

    for pair in range(top // 2):
        both = summed(pair * quarter, quarter)
        swapped = pltpu.roll(both, width, 1)
        value_ref[2 * pair] = jnp.where(first, both, swapped)
        value_ref[2 * pair + 1] = jnp.where(first, swapped, both)
    for k in range(top):
        name_ref[k] = jnp.broadcast_to(routes_ref[:, k : k + 1], (quarter, LANES)) - second

    def one_group(step, carry):
        group = jnp.bitwise_xor(lax.axis_index("expert"), step)
        dense = []
        for pair in range(experts // 2):
            base = group * experts + 2 * pair
            chosen = jnp.zeros((quarter, LANES), jnp.float32)
            for k in range(top):
                chosen = jnp.where(name_ref[k] == base, value_ref[k], chosen)
            dense.append(chosen.astype(jnp.bfloat16))
        per_side = len(dense) // sides
        results = [
            jnp.dot(
                jnp.concatenate(dense[side * per_side : (side + 1) * per_side], axis=1),
                weights_ref[step, side],
                preferred_element_type=jnp.float32,
            )
            for side in range(sides)
        ]
        for share in range(shares):
            lanes = slice(share // 2 * LANES, (share // 2 + 1) * LANES)
            low, high = (results[side][:, lanes] for side in ((0, 1) if share % 2 == 0 else (1, 0)))
            place = listed(group, groups, groups // 2) * shares + share
            payload_ref[place] = jnp.where(first, low, high).astype(jnp.bfloat16)
        return carry

    lax.fori_loop(0, groups, one_group, 0, unroll=groups <= 4)


def condition(own, near, far, quarter_routes, weights, shares, width):
    quarter, top = quarter_routes.shape
    groups = weights.shape[0]
    return pl.pallas_call(
        functools.partial(condition_kernel, top=top, width=width),
        in_specs=[VMEM] * 5,
        out_shape=jax.ShapeDtypeStruct((groups * shares, quarter, LANES), jnp.bfloat16),
        scratch_shapes=[
            pltpu.VMEM((top, quarter, LANES), jnp.float32),
            pltpu.VMEM((top, quarter, LANES), jnp.int32),
        ],
        compiler_params=pltpu.CompilerParams(vmem_limit_bytes=40 * MIB),
        cost_estimate=cost(2),
    )(own, near, far, quarter_routes, weights)


def query_kernel(query_ref, inverse_ref, out_hbm, factor_ref, spread_ref, wide_ref, out_ref, sems):
    count, experts, _ = query_ref.shape
    width = inverse_ref.shape[1]
    step = pl.program_id(0)
    rows = out_ref.shape[0] // width
    pitch = wide_ref.shape[1] // width

    @pl.when(step == 0)
    def _():
        zeros = jnp.zeros((width, width), jnp.bfloat16)
        for e in range(experts):
            high, low = split(inverse_ref[e])
            left = jnp.concatenate([high, zeros, low, zeros], axis=0)
            right = jnp.concatenate([zeros, high, zeros, low], axis=0)
            factor_ref[e] = jnp.concatenate([left, right], axis=1)

    spread_ref[...] = query_ref[...].astype(jnp.float32).reshape(count * experts, LANES)
    for e in range(experts):
        query = spread_ref[pl.ds(e, count, stride=experts), :].astype(jnp.bfloat16)
        result = lax.dot_general(
            factor_ref[e], query, (((1,), (1,)), ((), ())), preferred_element_type=jnp.float32
        )
        result = result[: 2 * width] + result[2 * width :]
        slot = (e + experts // 2 * (lax.axis_index("proj") % 2)) % experts
        start = slot * (rows // experts) + 2 * step
        for tile in range(wide_ref.shape[0]):
            part = result[:, tile * LANES : (tile + 1) * LANES]
            wide_ref[tile, pl.ds(start, width, stride=pitch), :] = part[:width]
            wide_ref[tile, pl.ds(start + 1, width, stride=pitch), :] = part[width:]

    @pl.when(step == pl.num_programs(0) - 1)
    def _():
        copies = []
        for part in range(sems.shape[0]):
            first = part * (width // sems.shape[0])
            for j in range(first, first + width // sems.shape[0]):
                for tile in range(wide_ref.shape[0]):
                    out_ref[j * rows : (j + 1) * rows, tile * LANES : (tile + 1) * LANES] = wide_ref[
                        tile, j * pitch : j * pitch + rows, :
                    ].astype(jnp.bfloat16)
            block = pl.ds(first * rows, width // sems.shape[0] * rows)
            copies.append(pltpu.make_async_copy(out_ref.at[block], out_hbm.at[block], sems.at[part]))
            copies[-1].start()
        for copy in copies:
            copy.wait()


def condition_queries(query_grads, inverse_in):
    count, experts, flat = query_grads.shape
    width = inverse_in.shape[1]
    rows = experts * flat
    return pl.pallas_call(
        query_kernel,
        grid=(flat // LANES,),
        in_specs=[
            pl.BlockSpec((count, experts, LANES), lambda c: (0, 0, c)),
            pl.BlockSpec(inverse_in.shape, lambda c: (0, 0, 0)),
        ],
        out_specs=HBM,
        out_shape=pltpu.HBM((rows, count), jnp.bfloat16),
        scratch_shapes=[
            pltpu.VMEM((experts, 4 * width, 2 * width), jnp.bfloat16),
            pltpu.VMEM((count * experts, LANES), jnp.float32),
            pltpu.VMEM((count // LANES, rows + 8 * width, LANES), jnp.float32),
            pltpu.VMEM((rows, count), jnp.bfloat16),
            pltpu.SemaphoreType.DMA((4,)),
        ],
        compiler_params=pltpu.CompilerParams(vmem_limit_bytes=40 * MIB),
        cost_estimate=cost(10),
    )(stay(query_grads), inverse_in)


def score_kernel(
    arrived_ref, inner_ref, far_ref, out_ref, grads_ref, queries_ref, sem, *, width, doc_count, turns
):
    fetch = pltpu.make_async_copy(far_ref, queries_ref, sem)
    fetch.start()
    sources, quarter, lanes = arrived_ref.shape
    shares = lax.axis_size("proj")
    owners = sources // shares
    outer, inner, docs = [], [], []
    for t, turn in enumerate(turns):
        for k in range(inner_ref.shape[1]):
            away = k * shares + jnp.bitwise_xor(lax.axis_index("proj"), turn)
            owner = jnp.bitwise_xor(lax.axis_index("expert"), away)
            for q in range(shares):
                outer.append(arrived_ref[listed(owner, owners, owners // 2) * shares + q])
                docs.append(inner_ref[t, k, q, width:, :].astype(jnp.float32).astype(jnp.int32))
                inner.append(inner_ref[t, k, q, :width, :])
    outer = jnp.concatenate(outer, axis=0)
    inner = jnp.concatenate(inner, axis=1)
    docs = jnp.concatenate(docs, axis=1)
    odd = lax.dot_general(
        (docs & 1).astype(jnp.float32).astype(jnp.bfloat16),
        jnp.full((DOC_ROWS, lanes), 1 / DOC_ROWS, jnp.bfloat16),
        (((0,), (0,)), ((), ())),
        preferred_element_type=jnp.float32,
    ).astype(jnp.bfloat16)
    odd_outer = outer * odd
    outer = jnp.concatenate([outer - odd_outer, odd_outer], axis=1)
    pairs = jnp.broadcast_to(docs[:1] >> 1, inner.shape)
    pair_group = min(16, doc_count // 2)
    pitch = grads_ref.shape[0] // doc_count

    def one_group(group, carry):
        masked = [
            jnp.where(pairs == group * pair_group + p, inner, jnp.zeros_like(inner)) for p in range(pair_group)
        ]
        sums = jnp.dot(jnp.concatenate(masked, axis=0), outer, preferred_element_type=jnp.float32)
        for p in range(pair_group):
            for parity in range(2):
                start = pl.multiple_of((2 * (group * pair_group + p) + parity) * pitch, 8)
                grads_ref[pl.ds(start, width), :] = sums[
                    p * width : (p + 1) * width, parity * lanes : (parity + 1) * lanes
                ]
        return carry

    groups = doc_count // (2 * pair_group)
    lax.fori_loop(0, groups, one_group, 0, unroll=groups == 1)
    high, low = [], []
    for j in range(width):
        parts = split(grads_ref[pl.ds(j, doc_count, stride=pitch), :])
        high.append(parts[0])
        low.append(parts[1])
    flat = jnp.concatenate([jnp.concatenate(high, axis=1), jnp.concatenate(low, axis=1)], axis=0)
    fetch.wait()
    result = jnp.dot(flat, queries_ref[...], preferred_element_type=jnp.float32)
    result = result[:doc_count] + result[doc_count:]
    columns = result.shape[1] // shares
    fill = jnp.zeros((DOC_DEV, LANES - columns), jnp.float32)
    for owner in range(owners):
        for share in range(shares):
            piece = result[owner * DOC_DEV : (owner + 1) * DOC_DEV, share * columns : (share + 1) * columns]
            out_ref[listed(owner, owners, owners - 1) * shares + share] = jnp.concatenate([piece, fill], axis=1)


def score(arrived, inner, queries, turns, owners):
    sources = arrived.shape[0]
    width = inner.shape[3] - DOC_ROWS
    doc_count = DOC_DEV * owners
    return pl.pallas_call(
        functools.partial(score_kernel, width=width, doc_count=doc_count, turns=turns),
        in_specs=[VMEM, VMEM, HBM],
        out_shape=jax.ShapeDtypeStruct((sources, DOC_DEV, LANES), jnp.float32),
        scratch_shapes=[
            pltpu.VMEM((doc_count * (width + 8), arrived.shape[2]), jnp.float32),
            pltpu.VMEM(queries.shape, jnp.bfloat16),
            pltpu.SemaphoreType.DMA,
        ],
        compiler_params=pltpu.CompilerParams(vmem_limit_bytes=40 * MIB),
        cost_estimate=cost(5),
    )(arrived, inner, stay(queries))


def sum_kernel(pieces_ref, out_ref):
    total = pieces_ref[0]
    for source in range(1, pieces_ref.shape[0]):
        total = total + pieces_ref[source]
    out_ref[...] = total[:, : out_ref.shape[1]]


def sum_pieces(pieces, columns):
    return pl.pallas_call(
        sum_kernel,
        in_specs=[VMEM],
        out_shape=jax.ShapeDtypeStruct((pieces.shape[1], columns), jnp.float32),
        compiler_params=pltpu.CompilerParams(vmem_limit_bytes=40 * MIB),
    )(pieces)


def exchange(block, axis, size, turn):
    return lax.ppermute(block, axis, [(i, i ^ turn) for i in range(size)])


def double(blocks, turns, axis, size, turn):
    blocks = jnp.concatenate([blocks, exchange(blocks, axis, size, turn)], axis=0)
    return blocks, turns + tuple(t ^ turn for t in turns)


def local(
    activations,
    grad_hidden,
    routes,
    doc_ids,
    query_grads,
    in_projection,
    out_projection,
    inverse_in,
    inverse_out,
):
    tokens, top = routes.shape
    experts, width, _ = inverse_in.shape
    owners = lax.axis_size("expert")
    shares = lax.axis_size("proj")
    quarter = tokens // shares
    assert quarter == LANES and 2 * width == LANES and experts * width // shares == LANES
    assert shares == 4 and owners & (owners - 1) == 0 and owners >= shares
    assert DOC_DEV * owners <= 256

    flat_hidden = grad_hidden.reshape(tokens * top, grad_hidden.shape[2])
    inner_wire, shared = project_inner(activations, in_projection, inverse_out, shares)
    inner_other = exchange(inner_wire, "proj", shares, 2)
    far_shared = exchange(shared, "expert", owners, owners // 2)
    leaving, own = project_outer(flat_hidden, out_projection, shares, top)
    far_shared, inner_other, leaving = lax.optimization_barrier((far_shared, inner_other, leaving))
    near = exchange(leaving, "proj", shares, 1)
    shared, turns = jnp.stack([shared, far_shared]), (0, owners // 2)
    for bit in reversed(range((owners // 2).bit_length() - 1)):
        shared, turns = double(shared, turns, "expert", owners, 1 << bit)
    inner_half = combine(combine_inner_kernel, inner_wire, inner_other, inner_wire.shape)
    inner_other = exchange(inner_half, "proj", shares, 1)
    sent = combine(combine_outer_kernel, own, near, own.shape[1:])
    far = exchange(sent, "proj", shares, 2)
    inner = finish_inner(inner_half, inner_other, doc_ids.reshape(shares, quarter), width)
    inner, _ = lax.optimization_barrier((inner, sent))
    arriving = []
    for k in range(owners // shares):
        pairs = [
            (o * shares + p, (o ^ (k * shares + p)) * shares + p)
            for o in range(owners)
            for p in range(shares)
            if k or p
        ]
        arriving.append(lax.ppermute(inner, ("expert", "proj"), pairs))
    weights = expand(shared, turns, width, experts, shares)
    far, weights = lax.optimization_barrier((far, weights))
    quarter_routes = lax.dynamic_slice_in_dim(routes, lax.axis_index("proj") * quarter, quarter, 0)
    payload = condition(own, near, far, quarter_routes, weights, shares, width)
    payload, arriving = lax.optimization_barrier((payload, arriving))
    arrived = send_to_all(payload, owners, shares, owners // 2)
    arriving[0] = jnp.where(lax.axis_index("proj") == 0, inner, arriving[0])
    inner, share_turns = jnp.stack(arriving)[None], (0,)
    inner, share_turns = double(inner, share_turns, "proj", shares, 1)
    inner, query_grads = lax.optimization_barrier((inner, query_grads))
    inner, share_turns = double(inner, share_turns, "proj", shares, 2)
    queries = condition_queries(query_grads, inverse_in)
    pieces = score(arrived, inner, queries, share_turns, owners)
    pieces = send_to_all(pieces, owners, shares, owners - 1)
    return sum_pieces(pieces, query_grads.shape[0] // shares).T


def solution(mesh):
    in_specs = (
        P(("groups", "expert"), "proj"),
        P(("groups", "expert"), None, "proj"),
        P(("groups", "expert"), None),
        P(("groups", "expert")),
        P(None, "expert", "proj"),
        P(None, "proj"),
        P(None, "proj"),
        P("expert", None, None),
        P("expert", None, None),
    )
    out_specs = P("proj", ("groups", "expert"))
    return jax.shard_map(local, mesh=mesh, in_specs=in_specs, out_specs=out_specs, check_vma=False)
```

```python
import functools

import jax
import jax.numpy as jnp
from jax import lax
from jax.experimental import pallas as pl
from jax.experimental.pallas import tpu as pltpu
from jax.sharding import PartitionSpec as P

DOC_DEV = 8
LANES = 128
DOC_ROWS = 16
DIAGONAL_ROWS = 16
MIB = 1024 * 1024
VMEM = pl.BlockSpec(memory_space=pltpu.VMEM)
HBM = pl.BlockSpec(memory_space=pltpu.HBM)


def low_lanes(rows, width):
    return lax.broadcasted_iota(jnp.int32, (rows, LANES), 1) < width


def stay(array):
    return pltpu.with_memory_space_constraint(array, pltpu.HBM)


def listed(owner, owners, first):
    return (owner + owners - first) % owners


def send_to_all(blocks, owners, shares, first):
    members = [(i + first * shares) % (owners * shares) for i in range(owners * shares)]
    return lax.all_to_all(blocks, ("expert", "proj"), 0, 0, tiled=True, axis_index_groups=[members])


def split(value):
    high = value.astype(jnp.bfloat16)
    return high, (value - high.astype(jnp.float32)).astype(jnp.bfloat16)


def cost(microseconds):
    return pl.CostEstimate(flops=0, bytes_accessed=int(microseconds * 3.3e6), transcendentals=0)


def in_order(copies, ahead):
    for copy in copies[:ahead]:
        copy.start()
    state = [0]

    def take():
        copies[state[0]].wait()
        if state[0] + ahead < len(copies):
            copies[state[0] + ahead].start()
        state[0] += 1

    return take


def twice_transposed(projection):
    once = jnp.transpose(projection.astype(jnp.float32))
    return jnp.concatenate([once, once], axis=1).astype(jnp.bfloat16)


def triangles(width):
    row = lax.broadcasted_iota(jnp.int32, (width, LANES), 0)
    column = lax.broadcasted_iota(jnp.int32, (width, LANES), 1) % width
    return row, column


def pack_factors(inverse_ref, shared_ref):
    experts, width, _ = inverse_ref.shape
    quarter = experts // 4
    row, column = triangles(width)
    diagonals = []
    for e in range(quarter):
        lower, upper = (
            jnp.concatenate([inverse_ref[first], inverse_ref[first + 2 * quarter]], axis=1) for first in (e, e + quarter)
        )
        shared_ref[e * width : (e + 1) * width, :] = jnp.where(row >= column, lower, upper).astype(jnp.bfloat16)
        diagonals.append(jnp.sum(jnp.where(row == column, upper, 0.0), axis=0, keepdims=True))
    fill = jnp.zeros((DIAGONAL_ROWS - quarter, LANES), jnp.float32)
    shared_ref[quarter * width :, :] = jnp.concatenate(diagonals + [fill], axis=0).astype(jnp.bfloat16)


def unpack_factors(packed, width, quarter):
    row, column = triangles(width)
    packed = packed.astype(jnp.float32)
    lower, upper = [], []
    for e in range(quarter):
        square = packed[e * width : (e + 1) * width]
        turned = jnp.transpose(square)
        turned = jnp.concatenate([turned[:width], turned[width:]], axis=1)
        diagonal = packed[quarter * width + e : quarter * width + e + 1]
        lower.append(jnp.where(row >= column, square, turned))
        upper.append(jnp.where(row == column, diagonal, jnp.where(row < column, square, turned)))
    return jnp.concatenate(lower + upper, axis=0).astype(jnp.bfloat16)


OUTER_TURNS = (1, 3, 2, 0)


def quarter_rows(place, turn, rows):
    return pl.ds(pl.multiple_of(jnp.bitwise_xor(place, turn) * rows, rows), rows)


def inner_kernel(
    act_hbm,
    in_proj_hbm,
    inverse_hbm,
    hidden_hbm,
    leaving_ref,
    own_ref,
    shared_ref,
    hidden_ref,
    act_ref,
    in_proj_ref,
    inverse_ref,
    sems,
):
    turns = (2, 3, 1, 0)
    quarter = act_ref.shape[1]
    width = in_proj_ref.shape[0]
    half = quarter // 2
    place = lax.axis_index("proj")
    pairs = [(in_proj_hbm, in_proj_ref)]
    for g, turn in enumerate(turns):
        rows = pl.ds(pl.multiple_of(jnp.bitwise_xor(place, turn) * quarter, quarter), quarter)
        pairs.append((act_hbm.at[rows], act_ref.at[g]))
        if g == 0:
            pairs.append((inverse_hbm, inverse_ref))
    for g in range(hidden_ref.shape[0]):
        pairs.append((hidden_hbm.at[quarter_rows(place, OUTER_TURNS[g], hidden_ref.shape[1])], hidden_ref.at[g]))
    take = in_order([pltpu.make_async_copy(*pair, sems.at[i]) for i, pair in enumerate(pairs)], 4)
    take()
    first = low_lanes(half, width)
    weights = twice_transposed(in_proj_ref[...])
    for wire_ref in (leaving_ref, own_ref):
        take()
        if wire_ref is leaving_ref:
            take()
            pack_factors(inverse_ref, shared_ref)
        take()
        g = 0 if wire_ref is leaving_ref else 2
        rows = act_ref[g : g + 2].reshape(2 * quarter, act_ref.shape[2])
        inner = jnp.dot(rows, weights, preferred_element_type=jnp.float32)
        for i in range(2):
            start = i * quarter
            high, low = split(jnp.where(first, inner[start : start + half], inner[start + half : start + quarter]))
            wire_ref[i, :half, :] = high
            wire_ref[i, half:, :] = low
    for _ in range(hidden_ref.shape[0]):
        take()


def project_inner(activations, in_projection, inverse_out, flat_hidden, quarters):
    tokens, model = activations.shape
    quarter = tokens // quarters
    experts, width, _ = inverse_out.shape
    wire = jax.ShapeDtypeStruct((quarters // 2, quarter, LANES), jnp.bfloat16)
    fixed = (in_projection, inverse_out)
    return pl.pallas_call(
        inner_kernel,
        in_specs=[HBM] * 4,
        out_specs=[VMEM] * 4,
        out_shape=[
            wire,
            wire,
            jax.ShapeDtypeStruct((experts // 4 * width + DIAGONAL_ROWS, LANES), jnp.bfloat16),
            jax.ShapeDtypeStruct((quarters // 2, flat_hidden.shape[0] // quarters, flat_hidden.shape[1]), jnp.bfloat16),
        ],
        scratch_shapes=[pltpu.VMEM((quarters, quarter, model), jnp.bfloat16)]
        + [pltpu.VMEM(array.shape, array.dtype) for array in fixed]
        + [pltpu.SemaphoreType.DMA((quarters + len(fixed) + quarters // 2,))],
        compiler_params=pltpu.CompilerParams(vmem_limit_bytes=40 * MIB),
        cost_estimate=cost(2.5),
    )(*[stay(array) for array in (activations, *fixed, flat_hidden)])


def outer_kernel(near_ref, hidden_hbm, out_proj_hbm, leaving_ref, own_ref, hidden_ref, out_proj_ref, rows_ref, sems, *, top):
    ready, rows, _ = near_ref.shape
    quarter = rows // top
    width = out_proj_ref.shape[0]
    place = lax.axis_index("proj")
    pairs = [(out_proj_hbm, out_proj_ref)]
    for i, turn in enumerate(OUTER_TURNS[ready:]):
        pairs.append((hidden_hbm.at[quarter_rows(place, turn, rows)], hidden_ref.at[i]))
    take = in_order([pltpu.make_async_copy(*pair, sems.at[i]) for i, pair in enumerate(pairs)], len(pairs))
    take()
    first = low_lanes(quarter, width)
    weights = twice_transposed(out_proj_ref[...])

    def pack_rows(g):
        wire_ref = leaving_ref.at[g] if g < 2 else own_ref.at[g - 2]
        for pair in range(top // 2):
            even = rows_ref[g % 2, pl.ds(2 * pair, quarter, stride=top), :]
            odd = rows_ref[g % 2, pl.ds(2 * pair + 1, quarter, stride=top), :]
            wire_ref[pair * quarter : (pair + 1) * quarter, :] = jnp.where(first, even, odd).astype(jnp.bfloat16)

    for g in range(len(OUTER_TURNS)):
        if g >= ready:
            take()
        hidden = near_ref[g] if g < ready else hidden_ref[g - ready]
        rows_ref[g % 2] = jnp.dot(hidden, weights, preferred_element_type=jnp.float32)
        if g:
            pack_rows(g - 1)
    pack_rows(len(OUTER_TURNS) - 1)


def project_outer(near_hidden, flat_hidden, out_projection, quarters, top):
    rows, hidden = flat_hidden.shape
    wire = jax.ShapeDtypeStruct((quarters // 2, rows // quarters // 2, LANES), jnp.bfloat16)
    return pl.pallas_call(
        functools.partial(outer_kernel, top=top),
        in_specs=[VMEM, HBM, HBM],
        out_specs=[VMEM] * 2,
        out_shape=[wire, wire],
        scratch_shapes=[
            pltpu.VMEM((quarters // 2, rows // quarters, hidden), jnp.bfloat16),
            pltpu.VMEM(out_projection.shape, out_projection.dtype),
            pltpu.VMEM((2, rows // quarters, LANES), jnp.float32),
            pltpu.SemaphoreType.DMA((quarters // 2 + 1,)),
        ],
        compiler_params=pltpu.CompilerParams(vmem_limit_bytes=40 * MIB),
        cost_estimate=cost(4),
    )(near_hidden, stay(flat_hidden), stay(out_projection))


def exact_rows(rows):
    half = rows.shape[0] // 2
    return rows[:half].astype(jnp.float32) + rows[half:].astype(jnp.float32)


def combine_inner_kernel(own_ref, near_ref, out_ref):
    high, low = split(exact_rows(own_ref[0]) + exact_rows(near_ref[1]))
    out_ref[: high.shape[0], :] = high
    out_ref[high.shape[0] :, :] = low


def combine_outer_kernel(own_ref, near_ref, out_ref):
    out_ref[...] = (own_ref[0].astype(jnp.float32) + near_ref[1].astype(jnp.float32)).astype(jnp.bfloat16)


def combine(kernel, own, near):
    return pl.pallas_call(
        kernel,
        in_specs=[VMEM, VMEM],
        out_shape=jax.ShapeDtypeStruct(own.shape[1:], jnp.bfloat16),
        compiler_params=pltpu.CompilerParams(vmem_limit_bytes=40 * MIB),
        cost_estimate=cost(0.5),
    )(own, near)


def finish_inner_kernel(own_ref, first_ref, second_ref, docs_ref, out_ref):
    total = exact_rows(own_ref[1]) + exact_rows(first_ref[0]) + exact_rows(second_ref[...])
    width = out_ref.shape[0] - DOC_ROWS
    total = jnp.concatenate([total[:, :width], total[:, width:]], axis=0)
    out_ref[:width, :] = jnp.transpose(total).astype(jnp.bfloat16)
    docs = docs_ref[pl.ds(lax.axis_index("proj"), 1), :].astype(jnp.float32)
    out_ref[width:, :] = jnp.broadcast_to(docs, (DOC_ROWS, LANES)).astype(jnp.bfloat16)


def finish_inner(own, first, second, doc_rows, width):
    return pl.pallas_call(
        finish_inner_kernel,
        in_specs=[VMEM] * 4,
        out_shape=jax.ShapeDtypeStruct((width + DOC_ROWS, own.shape[1]), jnp.bfloat16),
        compiler_params=pltpu.CompilerParams(vmem_limit_bytes=40 * MIB),
        cost_estimate=cost(0.5),
    )(own, first, second, doc_rows)


def expand_kernel(shared_ref, weights_ref, *, width, experts, shares, turns):
    half = experts // 2
    share_rows = width // shares
    columns = shares * half * share_rows
    lane = lax.broadcasted_iota(jnp.int32, (LANES, columns), 1)
    row = lax.broadcasted_iota(jnp.int32, (LANES, columns), 0)
    expert_lane = lax.broadcasted_iota(jnp.int32, (half * width, columns), 1) // share_rows % half
    expert_row = lax.broadcasted_iota(jnp.int32, (half * width, columns), 0) // width
    own = expert_lane == expert_row
    factors = [unpack_factors(shared_ref[entry], width, half // 2) for entry in range(len(turns))]
    for side in range(2):
        share = jnp.bitwise_xor(lane // (half * share_rows), side)
        source = share * share_rows + lane % share_rows
        spread = (row == source + side * width).astype(jnp.float32).astype(jnp.bfloat16)
        for entry, turn in enumerate(turns):
            placed = jnp.dot(factors[entry], spread, preferred_element_type=jnp.float32)
            weights_ref[turn // 2, side] = jnp.where(own, placed, 0.0).astype(jnp.bfloat16)


def expand(shared, turns, width, experts, shares):
    owners = shared.shape[0]
    return pl.pallas_call(
        functools.partial(expand_kernel, width=width, experts=experts, shares=shares, turns=turns),
        in_specs=[VMEM],
        out_shape=jax.ShapeDtypeStruct((owners, 2, experts // 2 * width, experts // 2 * width), jnp.bfloat16),
        compiler_params=pltpu.CompilerParams(vmem_limit_bytes=40 * MIB),
        cost_estimate=cost(1),
    )(shared)


def condition_kernel(
    own_ref, near_ref, far_ref, routes_ref, even_ref, odd_ref, payload_ref, value_ref, name_ref, *, top, width
):
    quarter = routes_ref.shape[0]
    pairs, sides, dense_width, _ = even_ref.shape
    groups = 2 * pairs
    shares = payload_ref.shape[0] // groups
    experts = sides * dense_width // width
    first = low_lanes(quarter, width)
    second = 1 - first.astype(jnp.int32)

    def summed(start, size):
        rows = slice(start, start + size)
        total = own_ref[1, rows, :].astype(jnp.float32) + near_ref[0, rows, :].astype(jnp.float32)
        return total + far_ref[rows, :].astype(jnp.float32)

    for pair in range(top // 2):
        both = summed(pair * quarter, quarter)
        swapped = pltpu.roll(both, width, 1)
        value_ref[2 * pair] = jnp.where(first, both, swapped)
        value_ref[2 * pair + 1] = jnp.where(first, swapped, both)
    for k in range(top):
        name_ref[k] = jnp.broadcast_to(routes_ref[:, k : k + 1], (quarter, LANES)) - second

    def one_group(step, carry, parity):
        weights_ref = odd_ref if parity else even_ref
        group = jnp.bitwise_xor(lax.axis_index("expert"), 2 * step + parity)
        dense = []
        for pair in range(experts // 2):
            base = group * experts + 2 * pair
            chosen = jnp.zeros((quarter, LANES), jnp.float32)
            for k in range(top):
                chosen = jnp.where(name_ref[k] == base, value_ref[k], chosen)
            dense.append(chosen.astype(jnp.bfloat16))
        per_side = len(dense) // sides
        results = [
            jnp.dot(
                jnp.concatenate(dense[side * per_side : (side + 1) * per_side], axis=1),
                weights_ref[step, side],
                preferred_element_type=jnp.float32,
            )
            for side in range(sides)
        ]
        for share in range(shares):
            lanes = slice(share // 2 * LANES, (share // 2 + 1) * LANES)
            low, high = (results[side][:, lanes] for side in ((0, 1) if share % 2 == 0 else (1, 0)))
            place = listed(group, groups, groups // 2) * shares + share
            payload_ref[place] = jnp.where(first, low, high).astype(jnp.bfloat16)
        return carry

    for parity in range(2):
        lax.fori_loop(0, pairs, functools.partial(one_group, parity=parity), 0, unroll=pairs <= 2)


def condition(own, near, far, quarter_routes, even, odd, shares, width):
    quarter, top = quarter_routes.shape
    groups = 2 * even.shape[0]
    return pl.pallas_call(
        functools.partial(condition_kernel, top=top, width=width),
        in_specs=[VMEM] * 6,
        out_shape=jax.ShapeDtypeStruct((groups * shares, quarter, LANES), jnp.bfloat16),
        scratch_shapes=[
            pltpu.VMEM((top, quarter, LANES), jnp.float32),
            pltpu.VMEM((top, quarter, LANES), jnp.int32),
        ],
        compiler_params=pltpu.CompilerParams(vmem_limit_bytes=40 * MIB),
        cost_estimate=cost(2),
    )(own, near, far, quarter_routes, even, odd)


def query_kernel(query_ref, inverse_ref, out_hbm, factor_ref, spread_ref, wide_ref, out_ref, sems):
    count, experts, _ = query_ref.shape
    width = inverse_ref.shape[1]
    step = pl.program_id(0)
    rows = out_ref.shape[0] // width
    pitch = wide_ref.shape[1] // width

    @pl.when(step == 0)
    def _():
        zeros = jnp.zeros((width, width), jnp.bfloat16)
        for e in range(experts):
            high, low = split(inverse_ref[e])
            left = jnp.concatenate([high, zeros, low, zeros], axis=0)
            right = jnp.concatenate([zeros, high, zeros, low], axis=0)
            factor_ref[e] = jnp.concatenate([left, right], axis=1)

    spread_ref[...] = query_ref[...].astype(jnp.float32).reshape(count * experts, LANES)
    for e in range(experts):
        query = spread_ref[pl.ds(e, count, stride=experts), :].astype(jnp.bfloat16)
        result = lax.dot_general(
            factor_ref[e], query, (((1,), (1,)), ((), ())), preferred_element_type=jnp.float32
        )
        result = result[: 2 * width] + result[2 * width :]
        slot = (e + experts // 2 * (lax.axis_index("proj") % 2)) % experts
        start = slot * (rows // experts) + 2 * step
        for tile in range(wide_ref.shape[0]):
            part = result[:, tile * LANES : (tile + 1) * LANES]
            wide_ref[tile, pl.ds(start, width, stride=pitch), :] = part[:width]
            wide_ref[tile, pl.ds(start + 1, width, stride=pitch), :] = part[width:]

    @pl.when(step == pl.num_programs(0) - 1)
    def _():
        copies = []
        for part in range(sems.shape[0]):
            first = part * (width // sems.shape[0])
            for j in range(first, first + width // sems.shape[0]):
                for tile in range(wide_ref.shape[0]):
                    out_ref[j * rows : (j + 1) * rows, tile * LANES : (tile + 1) * LANES] = wide_ref[
                        tile, j * pitch : j * pitch + rows, :
                    ].astype(jnp.bfloat16)
            block = pl.ds(first * rows, width // sems.shape[0] * rows)
            copies.append(pltpu.make_async_copy(out_ref.at[block], out_hbm.at[block], sems.at[part]))
            copies[-1].start()
        for copy in copies:
            copy.wait()


def condition_queries(query_grads, inverse_in):
    count, experts, flat = query_grads.shape
    width = inverse_in.shape[1]
    rows = experts * flat
    return pl.pallas_call(
        query_kernel,
        grid=(flat // LANES,),
        in_specs=[
            pl.BlockSpec((count, experts, LANES), lambda c: (0, 0, c)),
            pl.BlockSpec(inverse_in.shape, lambda c: (0, 0, 0)),
        ],
        out_specs=HBM,
        out_shape=pltpu.HBM((rows, count), jnp.bfloat16),
        scratch_shapes=[
            pltpu.VMEM((experts, 4 * width, 2 * width), jnp.bfloat16),
            pltpu.VMEM((count * experts, LANES), jnp.float32),
            pltpu.VMEM((count // LANES, rows + 8 * width, LANES), jnp.float32),
            pltpu.VMEM((rows, count), jnp.bfloat16),
            pltpu.SemaphoreType.DMA((4,)),
        ],
        compiler_params=pltpu.CompilerParams(vmem_limit_bytes=40 * MIB),
        cost_estimate=cost(10),
    )(stay(query_grads), inverse_in)


def score_kernel(
    arrived_ref, inner_ref, far_ref, out_ref, grads_ref, queries_ref, sem, *, width, doc_count, turns
):
    fetch = pltpu.make_async_copy(far_ref, queries_ref, sem)
    fetch.start()
    sources, quarter, lanes = arrived_ref.shape
    shares = lax.axis_size("proj")
    owners = sources // shares
    outer, inner, docs = [], [], []
    for entry, (owner_turn, share_turn) in enumerate(turns):
        owner = jnp.bitwise_xor(lax.axis_index("expert"), owner_turn)
        share = jnp.bitwise_xor(lax.axis_index("proj"), share_turn)
        outer.append(arrived_ref[listed(owner, owners, owners // 2) * shares + share])
        docs.append(inner_ref[entry, width:, :].astype(jnp.float32).astype(jnp.int32))
        inner.append(inner_ref[entry, :width, :])
    outer = jnp.concatenate(outer, axis=0)
    inner = jnp.concatenate(inner, axis=1)
    docs = jnp.concatenate(docs, axis=1)
    odd = lax.dot_general(
        (docs & 1).astype(jnp.float32).astype(jnp.bfloat16),
        jnp.full((DOC_ROWS, lanes), 1 / DOC_ROWS, jnp.bfloat16),
        (((0,), (0,)), ((), ())),
        preferred_element_type=jnp.float32,
    ).astype(jnp.bfloat16)
    odd_outer = outer * odd
    outer = jnp.concatenate([outer - odd_outer, odd_outer], axis=1)
    pairs = jnp.broadcast_to(docs[:1] >> 1, inner.shape)
    pair_group = min(16, doc_count // 2)
    pitch = grads_ref.shape[0] // doc_count

    def one_group(group, carry):
        masked = [
            jnp.where(pairs == group * pair_group + p, inner, jnp.zeros_like(inner)) for p in range(pair_group)
        ]
        sums = jnp.dot(jnp.concatenate(masked, axis=0), outer, preferred_element_type=jnp.float32)
        for p in range(pair_group):
            for parity in range(2):
                start = pl.multiple_of((2 * (group * pair_group + p) + parity) * pitch, 8)
                grads_ref[pl.ds(start, width), :] = sums[
                    p * width : (p + 1) * width, parity * lanes : (parity + 1) * lanes
                ]
        return carry

    groups = doc_count // (2 * pair_group)
    lax.fori_loop(0, groups, one_group, 0, unroll=groups == 1)
    high, low = [], []
    for j in range(width):
        parts = split(grads_ref[pl.ds(j, doc_count, stride=pitch), :])
        high.append(parts[0])
        low.append(parts[1])
    flat = jnp.concatenate([jnp.concatenate(high, axis=1), jnp.concatenate(low, axis=1)], axis=0)
    fetch.wait()
    result = jnp.dot(flat, queries_ref[...], preferred_element_type=jnp.float32)
    result = result[:doc_count] + result[doc_count:]
    columns = result.shape[1] // shares
    fill = jnp.zeros((DOC_DEV, LANES - columns), jnp.float32)
    for owner in range(owners):
        for share in range(shares):
            piece = result[owner * DOC_DEV : (owner + 1) * DOC_DEV, share * columns : (share + 1) * columns]
            out_ref[listed(owner, owners, owners - 1) * shares + share] = jnp.concatenate([piece, fill], axis=1)


def score(arrived, inner, queries, turns, owners):
    sources = arrived.shape[0]
    width = inner.shape[1] - DOC_ROWS
    doc_count = DOC_DEV * owners
    return pl.pallas_call(
        functools.partial(score_kernel, width=width, doc_count=doc_count, turns=turns),
        in_specs=[VMEM, VMEM, HBM],
        out_shape=jax.ShapeDtypeStruct((sources, DOC_DEV, LANES), jnp.float32),
        scratch_shapes=[
            pltpu.VMEM((doc_count * (width + 8), arrived.shape[2]), jnp.float32),
            pltpu.VMEM(queries.shape, jnp.bfloat16),
            pltpu.SemaphoreType.DMA,
        ],
        compiler_params=pltpu.CompilerParams(vmem_limit_bytes=40 * MIB),
        cost_estimate=cost(5),
    )(arrived, inner, stay(queries))


def sum_kernel(pieces_ref, out_ref):
    total = pieces_ref[0]
    for source in range(1, pieces_ref.shape[0]):
        total = total + pieces_ref[source]
    out_ref[...] = total[:, : out_ref.shape[1]]


def sum_pieces(pieces, columns):
    return pl.pallas_call(
        sum_kernel,
        in_specs=[VMEM],
        out_shape=jax.ShapeDtypeStruct((pieces.shape[1], columns), jnp.float32),
        compiler_params=pltpu.CompilerParams(vmem_limit_bytes=40 * MIB),
    )(pieces)


def exchange(block, axis, size, turn):
    return lax.ppermute(block, axis, [(i, i ^ turn) for i in range(size)])


def double(blocks, turns, axis, size, turn):
    blocks = jnp.concatenate([blocks, exchange(blocks, axis, size, turn)], axis=0)
    return blocks, turns + tuple(t ^ turn for t in turns)


def local(
    activations,
    grad_hidden,
    routes,
    doc_ids,
    query_grads,
    in_projection,
    out_projection,
    inverse_in,
    inverse_out,
):
    tokens, top = routes.shape
    experts, width, _ = inverse_in.shape
    owners = lax.axis_size("expert")
    shares = lax.axis_size("proj")
    quarter = tokens // shares
    assert quarter == LANES and 2 * width == LANES and experts * width // shares == LANES
    assert experts % 4 == 0 and experts // 4 <= DIAGONAL_ROWS
    assert shares == 4 and owners & (owners - 1) == 0
    assert DOC_DEV * owners <= 256

    flat_hidden = grad_hidden.reshape(tokens * top, grad_hidden.shape[2])
    inner_leaving, inner_own, shared, near_hidden = project_inner(
        activations, in_projection, inverse_out, flat_hidden, shares
    )
    inner_first = exchange(inner_leaving, "proj", shares, 2)
    far_shared = exchange(shared, "expert", owners, owners // 2)
    leaving, own = project_outer(near_hidden, flat_hidden, out_projection, shares, top)
    far_shared, inner_first, leaving = lax.optimization_barrier((far_shared, inner_first, leaving))
    near = exchange(leaving, "proj", shares, 1)
    shared, turns = jnp.stack([shared, far_shared]), (0, owners // 2)
    for bit in reversed(range(1, (owners // 2).bit_length() - 1)):
        shared, turns = double(shared, turns, "expert", owners, 1 << bit)
    even = expand(shared, turns, width, experts, shares)
    shared = exchange(shared, "expert", owners, 1)
    near, even = lax.optimization_barrier((near, even))
    inner_second = exchange(combine(combine_inner_kernel, inner_own, inner_first), "proj", shares, 1)
    sent = combine(combine_outer_kernel, own, near)
    far = exchange(sent, "proj", shares, 2)
    inner = finish_inner(inner_own, inner_first, inner_second, doc_ids.reshape(shares, quarter), width)
    inner, _ = lax.optimization_barrier((inner, sent))
    owner_turns = tuple(reversed(range(owners)))
    arriving = [exchange(inner, "expert", owners, turn) for turn in owner_turns if turn]
    odd = expand(shared, turns, width, experts, shares)
    far, odd = lax.optimization_barrier((far, odd))
    quarter_routes = lax.dynamic_slice_in_dim(routes, lax.axis_index("proj") * quarter, quarter, 0)
    payload = condition(own, near, far, quarter_routes, even, odd, shares, width)
    payload, arriving = lax.optimization_barrier((payload, arriving))
    arrived = send_to_all(payload, owners, shares, owners // 2)
    inner = jnp.stack(arriving + [inner])
    inner, share_turns = inner[None], (0,)
    inner, share_turns = double(inner, share_turns, "proj", shares, 1)
    inner, query_grads = lax.optimization_barrier((inner, query_grads))
    inner, share_turns = double(inner, share_turns, "proj", shares, 2)
    inner = inner.reshape(owners * shares, width + DOC_ROWS, quarter)
    all_turns = tuple((o, p) for p in share_turns for o in owner_turns)
    queries = condition_queries(query_grads, inverse_in)
    pieces = score(arrived, inner, queries, all_turns, owners)
    pieces = send_to_all(pieces, owners, shares, owners - 1)
    return sum_pieces(pieces, query_grads.shape[0] // shares).T


def solution(mesh):
    in_specs = (
        P(("groups", "expert"), "proj"),
        P(("groups", "expert"), None, "proj"),
        P(("groups", "expert"), None),
        P(("groups", "expert")),
        P(None, "expert", "proj"),
        P(None, "proj"),
        P(None, "proj"),
        P("expert", None, None),
        P("expert", None, None),
    )
    out_specs = P("proj", ("groups", "expert"))
    return jax.shard_map(local, mesh=mesh, in_specs=in_specs, out_specs=out_specs, check_vma=False)
```

```python
import functools

import jax
import jax.numpy as jnp
from jax import lax
from jax.experimental import pallas as pl
from jax.experimental.pallas import tpu as pltpu
from jax.sharding import PartitionSpec as P

DOC_DEV = 8
LANES = 128
DOC_ROWS = 16
DIAGONAL_ROWS = 16
MIB = 1024 * 1024
VMEM = pl.BlockSpec(memory_space=pltpu.VMEM)
HBM = pl.BlockSpec(memory_space=pltpu.HBM)


def low_lanes(rows, width):
    return lax.broadcasted_iota(jnp.int32, (rows, LANES), 1) < width


def stay(array):
    return pltpu.with_memory_space_constraint(array, pltpu.HBM)


def listed(owner, owners, first):
    return (owner + owners - first) % owners


def send_to_all(blocks, owners, shares, first):
    members = [(i + first * shares) % (owners * shares) for i in range(owners * shares)]
    return lax.all_to_all(blocks, ("expert", "proj"), 0, 0, tiled=True, axis_index_groups=[members])


def split(value):
    high = value.astype(jnp.bfloat16)
    return high, (value - high.astype(jnp.float32)).astype(jnp.bfloat16)


def cost(microseconds):
    return pl.CostEstimate(flops=0, bytes_accessed=int(microseconds * 3.3e6), transcendentals=0)


def in_order(copies, ahead):
    for copy in copies[:ahead]:
        copy.start()
    state = [0]

    def take():
        copies[state[0]].wait()
        if state[0] + ahead < len(copies):
            copies[state[0] + ahead].start()
        state[0] += 1

    return take


def twice_transposed(projection):
    once = jnp.transpose(projection.astype(jnp.float32))
    return jnp.concatenate([once, once], axis=1).astype(jnp.bfloat16)


def triangles(width):
    row = lax.broadcasted_iota(jnp.int32, (width, LANES), 0)
    column = lax.broadcasted_iota(jnp.int32, (width, LANES), 1) % width
    return row, column


def pack_factors(inverse_ref, shared_ref):
    experts, width, _ = inverse_ref.shape
    quarter = experts // 4
    row, column = triangles(width)
    diagonals = []
    for e in range(quarter):
        lower, upper = (
            jnp.concatenate([inverse_ref[first], inverse_ref[first + 2 * quarter]], axis=1) for first in (e, e + quarter)
        )
        shared_ref[e * width : (e + 1) * width, :] = jnp.where(row >= column, lower, upper).astype(jnp.bfloat16)
        diagonals.append(jnp.sum(jnp.where(row == column, upper, 0.0), axis=0, keepdims=True))
    fill = jnp.zeros((DIAGONAL_ROWS - quarter, LANES), jnp.float32)
    shared_ref[quarter * width :, :] = jnp.concatenate(diagonals + [fill], axis=0).astype(jnp.bfloat16)


def unpack_factors(packed, width, quarter):
    row, column = triangles(width)
    packed = packed.astype(jnp.float32)
    lower, upper = [], []
    for e in range(quarter):
        square = packed[e * width : (e + 1) * width]
        turned = jnp.transpose(square)
        turned = jnp.concatenate([turned[:width], turned[width:]], axis=1)
        diagonal = packed[quarter * width + e : quarter * width + e + 1]
        lower.append(jnp.where(row >= column, square, turned))
        upper.append(jnp.where(row == column, diagonal, jnp.where(row < column, square, turned)))
    return jnp.concatenate(lower + upper, axis=0).astype(jnp.bfloat16)


OUTER_TURNS = (1, 3, 2, 0)


def quarter_rows(place, turn, rows):
    return pl.ds(pl.multiple_of(jnp.bitwise_xor(place, turn) * rows, rows), rows)


def inner_kernel(
    act_hbm,
    in_proj_hbm,
    inverse_hbm,
    hidden_hbm,
    leaving_ref,
    own_ref,
    shared_ref,
    hidden_ref,
    act_ref,
    in_proj_ref,
    inverse_ref,
    sems,
):
    turns = (2, 3, 1, 0)
    quarter = act_ref.shape[1]
    width = in_proj_ref.shape[0]
    half = quarter // 2
    place = lax.axis_index("proj")
    pairs = [(in_proj_hbm, in_proj_ref)]
    for g, turn in enumerate(turns):
        rows = pl.ds(pl.multiple_of(jnp.bitwise_xor(place, turn) * quarter, quarter), quarter)
        pairs.append((act_hbm.at[rows], act_ref.at[g]))
        if g == 0:
            pairs.append((inverse_hbm, inverse_ref))
    for g in range(hidden_ref.shape[0]):
        pairs.append((hidden_hbm.at[quarter_rows(place, OUTER_TURNS[g], hidden_ref.shape[1])], hidden_ref.at[g]))
    take = in_order([pltpu.make_async_copy(*pair, sems.at[i]) for i, pair in enumerate(pairs)], 4)
    take()
    first = low_lanes(half, width)
    weights = twice_transposed(in_proj_ref[...])
    for wire_ref in (leaving_ref, own_ref):
        take()
        if wire_ref is leaving_ref:
            take()
            pack_factors(inverse_ref, shared_ref)
        take()
        g = 0 if wire_ref is leaving_ref else 2
        rows = act_ref[g : g + 2].reshape(2 * quarter, act_ref.shape[2])
        inner = jnp.dot(rows, weights, preferred_element_type=jnp.float32)
        for i in range(2):
            start = i * quarter
            high, low = split(jnp.where(first, inner[start : start + half], inner[start + half : start + quarter]))
            wire_ref[i, :half, :] = high
            wire_ref[i, half:, :] = low
    for _ in range(hidden_ref.shape[0]):
        take()


def project_inner(activations, in_projection, inverse_out, flat_hidden, quarters):
    tokens, model = activations.shape
    quarter = tokens // quarters
    experts, width, _ = inverse_out.shape
    wire = jax.ShapeDtypeStruct((quarters // 2, quarter, LANES), jnp.bfloat16)
    fixed = (in_projection, inverse_out)
    return pl.pallas_call(
        inner_kernel,
        in_specs=[HBM] * 4,
        out_specs=[VMEM] * 4,
        out_shape=[
            wire,
            wire,
            jax.ShapeDtypeStruct((experts // 4 * width + DIAGONAL_ROWS, LANES), jnp.bfloat16),
            jax.ShapeDtypeStruct((quarters // 2, flat_hidden.shape[0] // quarters, flat_hidden.shape[1]), jnp.bfloat16),
        ],
        scratch_shapes=[pltpu.VMEM((quarters, quarter, model), jnp.bfloat16)]
        + [pltpu.VMEM(array.shape, array.dtype) for array in fixed]
        + [pltpu.SemaphoreType.DMA((quarters + len(fixed) + quarters // 2,))],
        compiler_params=pltpu.CompilerParams(vmem_limit_bytes=40 * MIB),
        cost_estimate=cost(2.5),
    )(*[stay(array) for array in (activations, *fixed, flat_hidden)])


def outer_kernel(near_ref, hidden_hbm, out_proj_hbm, leaving_ref, own_ref, hidden_ref, out_proj_ref, rows_ref, sems, *, top):
    ready, rows, _ = near_ref.shape
    quarter = rows // top
    width = out_proj_ref.shape[0]
    place = lax.axis_index("proj")
    pairs = [(out_proj_hbm, out_proj_ref)]
    for i, turn in enumerate(OUTER_TURNS[ready:]):
        pairs.append((hidden_hbm.at[quarter_rows(place, turn, rows)], hidden_ref.at[i]))
    take = in_order([pltpu.make_async_copy(*pair, sems.at[i]) for i, pair in enumerate(pairs)], len(pairs))
    take()
    first = low_lanes(quarter, width)
    weights = twice_transposed(out_proj_ref[...])

    def pack_rows(g):
        wire_ref = leaving_ref.at[g] if g < 2 else own_ref.at[g - 2]
        for pair in range(top // 2):
            even = rows_ref[g % 2, pl.ds(2 * pair, quarter, stride=top), :]
            odd = rows_ref[g % 2, pl.ds(2 * pair + 1, quarter, stride=top), :]
            wire_ref[pair * quarter : (pair + 1) * quarter, :] = jnp.where(first, even, odd).astype(jnp.bfloat16)

    for g in range(len(OUTER_TURNS)):
        if g >= ready:
            take()
        hidden = near_ref[g] if g < ready else hidden_ref[g - ready]
        rows_ref[g % 2] = jnp.dot(hidden, weights, preferred_element_type=jnp.float32)
        if g:
            pack_rows(g - 1)
    pack_rows(len(OUTER_TURNS) - 1)


def project_outer(near_hidden, flat_hidden, out_projection, quarters, top):
    rows, hidden = flat_hidden.shape
    wire = jax.ShapeDtypeStruct((quarters // 2, rows // quarters // 2, LANES), jnp.bfloat16)
    return pl.pallas_call(
        functools.partial(outer_kernel, top=top),
        in_specs=[VMEM, HBM, HBM],
        out_specs=[VMEM] * 2,
        out_shape=[wire, wire],
        scratch_shapes=[
            pltpu.VMEM((quarters // 2, rows // quarters, hidden), jnp.bfloat16),
            pltpu.VMEM(out_projection.shape, out_projection.dtype),
            pltpu.VMEM((2, rows // quarters, LANES), jnp.float32),
            pltpu.SemaphoreType.DMA((quarters // 2 + 1,)),
        ],
        compiler_params=pltpu.CompilerParams(vmem_limit_bytes=40 * MIB),
        cost_estimate=cost(4),
    )(near_hidden, stay(flat_hidden), stay(out_projection))


def exact_rows(rows):
    half = rows.shape[0] // 2
    return rows[:half].astype(jnp.float32) + rows[half:].astype(jnp.float32)


def combine_inner_kernel(own_ref, near_ref, out_ref):
    high, low = split(exact_rows(own_ref[0]) + exact_rows(near_ref[1]))
    out_ref[: high.shape[0], :] = high
    out_ref[high.shape[0] :, :] = low


def combine_outer_kernel(own_ref, near_ref, out_ref):
    out_ref[...] = (own_ref[0].astype(jnp.float32) + near_ref[1].astype(jnp.float32)).astype(jnp.bfloat16)


def combine(kernel, own, near):
    return pl.pallas_call(
        kernel,
        in_specs=[VMEM, VMEM],
        out_shape=jax.ShapeDtypeStruct(own.shape[1:], jnp.bfloat16),
        compiler_params=pltpu.CompilerParams(vmem_limit_bytes=40 * MIB),
        cost_estimate=cost(0.5),
    )(own, near)


def finish_inner_kernel(own_ref, first_ref, second_ref, docs_ref, out_ref):
    total = exact_rows(own_ref[1]) + exact_rows(first_ref[0]) + exact_rows(second_ref[...])
    width = out_ref.shape[0] - DOC_ROWS
    total = jnp.concatenate([total[:, :width], total[:, width:]], axis=0)
    out_ref[:width, :] = jnp.transpose(total).astype(jnp.bfloat16)
    docs = docs_ref[pl.ds(lax.axis_index("proj"), 1), :].astype(jnp.float32)
    out_ref[width:, :] = jnp.broadcast_to(docs, (DOC_ROWS, LANES)).astype(jnp.bfloat16)


def finish_inner(own, first, second, doc_rows, width):
    return pl.pallas_call(
        finish_inner_kernel,
        in_specs=[VMEM] * 4,
        out_shape=jax.ShapeDtypeStruct((width + DOC_ROWS, own.shape[1]), jnp.bfloat16),
        compiler_params=pltpu.CompilerParams(vmem_limit_bytes=40 * MIB),
        cost_estimate=cost(0.5),
    )(own, first, second, doc_rows)


def expand_kernel(shared_ref, weights_ref, *, width, experts, shares, turns):
    half = experts // 2
    share_rows = width // shares
    columns = shares * half * share_rows
    lane = lax.broadcasted_iota(jnp.int32, (LANES, columns), 1)
    row = lax.broadcasted_iota(jnp.int32, (LANES, columns), 0)
    expert_lane = lax.broadcasted_iota(jnp.int32, (half * width, columns), 1) // share_rows % half
    expert_row = lax.broadcasted_iota(jnp.int32, (half * width, columns), 0) // width
    own = expert_lane == expert_row
    rows = half // 2 * width + DIAGONAL_ROWS
    factors = [
        unpack_factors(shared_ref[entry * rows : (entry + 1) * rows], width, half // 2) for entry in range(len(turns))
    ]
    for side in range(2):
        share = jnp.bitwise_xor(lane // (half * share_rows), side)
        source = share * share_rows + lane % share_rows
        spread = (row == source + side * width).astype(jnp.float32).astype(jnp.bfloat16)
        for entry, turn in enumerate(turns):
            placed = jnp.dot(factors[entry], spread, preferred_element_type=jnp.float32)
            weights_ref[turn // 2, side] = jnp.where(own, placed, 0.0).astype(jnp.bfloat16)


def expand(shared, turns, width, experts, shares):
    owners = len(turns)
    return pl.pallas_call(
        functools.partial(expand_kernel, width=width, experts=experts, shares=shares, turns=turns),
        in_specs=[VMEM],
        out_shape=jax.ShapeDtypeStruct((owners, 2, experts // 2 * width, experts // 2 * width), jnp.bfloat16),
        compiler_params=pltpu.CompilerParams(vmem_limit_bytes=40 * MIB),
        cost_estimate=cost(1),
    )(shared)


def condition_kernel(
    own_ref, near_ref, far_ref, routes_ref, even_ref, odd_ref, payload_ref, value_ref, name_ref, *, top, width
):
    quarter = routes_ref.shape[0]
    pairs, sides, dense_width, _ = even_ref.shape
    groups = 2 * pairs
    shares = payload_ref.shape[0] // groups
    experts = sides * dense_width // width
    first = low_lanes(quarter, width)
    second = 1 - first.astype(jnp.int32)

    def summed(start, size):
        rows = slice(start, start + size)
        total = own_ref[1, rows, :].astype(jnp.float32) + near_ref[0, rows, :].astype(jnp.float32)
        return total + far_ref[rows, :].astype(jnp.float32)

    for pair in range(top // 2):
        both = summed(pair * quarter, quarter)
        swapped = pltpu.roll(both, width, 1)
        value_ref[2 * pair] = jnp.where(first, both, swapped)
        value_ref[2 * pair + 1] = jnp.where(first, swapped, both)
    for k in range(top):
        name_ref[k] = jnp.broadcast_to(routes_ref[:, k : k + 1], (quarter, LANES)) - second

    def one_group(step, carry, parity):
        weights_ref = odd_ref if parity else even_ref
        group = jnp.bitwise_xor(lax.axis_index("expert"), 2 * step + parity)
        dense = []
        for pair in range(experts // 2):
            base = group * experts + 2 * pair
            chosen = jnp.zeros((quarter, LANES), jnp.float32)
            for k in range(top):
                chosen = jnp.where(name_ref[k] == base, value_ref[k], chosen)
            dense.append(chosen.astype(jnp.bfloat16))
        per_side = len(dense) // sides
        results = [
            jnp.dot(
                jnp.concatenate(dense[side * per_side : (side + 1) * per_side], axis=1),
                weights_ref[step, side],
                preferred_element_type=jnp.float32,
            )
            for side in range(sides)
        ]
        for share in range(shares):
            lanes = slice(share // 2 * LANES, (share // 2 + 1) * LANES)
            low, high = (results[side][:, lanes] for side in ((0, 1) if share % 2 == 0 else (1, 0)))
            place = listed(group, groups, groups // 2) * shares + share
            payload_ref[place] = jnp.where(first, low, high).astype(jnp.bfloat16)
        return carry

    for parity in range(2):
        lax.fori_loop(0, pairs, functools.partial(one_group, parity=parity), 0, unroll=pairs <= 2)


def condition(own, near, far, quarter_routes, even, odd, shares, width):
    quarter, top = quarter_routes.shape
    groups = 2 * even.shape[0]
    return pl.pallas_call(
        functools.partial(condition_kernel, top=top, width=width),
        in_specs=[VMEM] * 6,
        out_shape=jax.ShapeDtypeStruct((groups * shares, quarter, LANES), jnp.bfloat16),
        scratch_shapes=[
            pltpu.VMEM((top, quarter, LANES), jnp.float32),
            pltpu.VMEM((top, quarter, LANES), jnp.int32),
        ],
        compiler_params=pltpu.CompilerParams(vmem_limit_bytes=40 * MIB),
        cost_estimate=cost(2),
    )(own, near, far, quarter_routes, even, odd)


def query_kernel(query_ref, inverse_ref, out_hbm, factor_ref, spread_ref, wide_ref, out_ref, sems):
    count, experts, _ = query_ref.shape
    width = inverse_ref.shape[1]
    step = pl.program_id(0)
    rows = out_ref.shape[0] // width
    pitch = wide_ref.shape[1] // width

    @pl.when(step == 0)
    def _():
        zeros = jnp.zeros((width, width), jnp.bfloat16)
        for e in range(experts):
            high, low = split(inverse_ref[e])
            left = jnp.concatenate([high, zeros, low, zeros], axis=0)
            right = jnp.concatenate([zeros, high, zeros, low], axis=0)
            factor_ref[e] = jnp.concatenate([left, right], axis=1)

    spread_ref[...] = query_ref[...].astype(jnp.float32).reshape(count * experts, LANES)
    for e in range(experts):
        query = spread_ref[pl.ds(e, count, stride=experts), :].astype(jnp.bfloat16)
        result = lax.dot_general(
            factor_ref[e], query, (((1,), (1,)), ((), ())), preferred_element_type=jnp.float32
        )
        result = result[: 2 * width] + result[2 * width :]
        slot = (e + experts // 2 * (lax.axis_index("proj") % 2)) % experts
        start = slot * (rows // experts) + 2 * step
        for tile in range(wide_ref.shape[0]):
            part = result[:, tile * LANES : (tile + 1) * LANES]
            wide_ref[tile, pl.ds(start, width, stride=pitch), :] = part[:width]
            wide_ref[tile, pl.ds(start + 1, width, stride=pitch), :] = part[width:]

    @pl.when(step == pl.num_programs(0) - 1)
    def _():
        copies = []
        for part in range(sems.shape[0]):
            first = part * (width // sems.shape[0])
            for j in range(first, first + width // sems.shape[0]):
                for tile in range(wide_ref.shape[0]):
                    out_ref[j * rows : (j + 1) * rows, tile * LANES : (tile + 1) * LANES] = wide_ref[
                        tile, j * pitch : j * pitch + rows, :
                    ].astype(jnp.bfloat16)
            block = pl.ds(first * rows, width // sems.shape[0] * rows)
            copies.append(pltpu.make_async_copy(out_ref.at[block], out_hbm.at[block], sems.at[part]))
            copies[-1].start()
        for copy in copies:
            copy.wait()


def condition_queries(query_grads, inverse_in):
    count, experts, flat = query_grads.shape
    width = inverse_in.shape[1]
    rows = experts * flat
    return pl.pallas_call(
        query_kernel,
        grid=(flat // LANES,),
        in_specs=[
            pl.BlockSpec((count, experts, LANES), lambda c: (0, 0, c)),
            pl.BlockSpec(inverse_in.shape, lambda c: (0, 0, 0)),
        ],
        out_specs=HBM,
        out_shape=pltpu.HBM((rows, count), jnp.bfloat16),
        scratch_shapes=[
            pltpu.VMEM((experts, 4 * width, 2 * width), jnp.bfloat16),
            pltpu.VMEM((count * experts, LANES), jnp.float32),
            pltpu.VMEM((count // LANES, rows + 8 * width, LANES), jnp.float32),
            pltpu.VMEM((rows, count), jnp.bfloat16),
            pltpu.SemaphoreType.DMA((4,)),
        ],
        compiler_params=pltpu.CompilerParams(vmem_limit_bytes=40 * MIB),
        cost_estimate=cost(10),
    )(stay(query_grads), inverse_in)


def score_kernel(
    arrived_ref, inner_ref, far_ref, out_ref, grads_ref, queries_ref, sem, *, width, doc_count, turns
):
    fetch = pltpu.make_async_copy(far_ref, queries_ref, sem)
    fetch.start()
    sources, quarter, lanes = arrived_ref.shape
    shares = lax.axis_size("proj")
    owners = sources // shares
    outer, inner, docs = [], [], []
    for entry, (owner_turn, share_turn) in enumerate(turns):
        owner = jnp.bitwise_xor(lax.axis_index("expert"), owner_turn)
        share = jnp.bitwise_xor(lax.axis_index("proj"), share_turn)
        outer.append(arrived_ref[listed(owner, owners, owners // 2) * shares + share])
        docs.append(inner_ref[entry, width:, :].astype(jnp.float32).astype(jnp.int32))
        inner.append(inner_ref[entry, :width, :])
    outer = jnp.concatenate(outer, axis=0)
    inner = jnp.concatenate(inner, axis=1)
    docs = jnp.concatenate(docs, axis=1)
    odd = lax.dot_general(
        (docs & 1).astype(jnp.float32).astype(jnp.bfloat16),
        jnp.full((DOC_ROWS, lanes), 1 / DOC_ROWS, jnp.bfloat16),
        (((0,), (0,)), ((), ())),
        preferred_element_type=jnp.float32,
    ).astype(jnp.bfloat16)
    odd_outer = outer * odd
    outer = jnp.concatenate([outer - odd_outer, odd_outer], axis=1)
    pairs = jnp.broadcast_to(docs[:1] >> 1, inner.shape)
    pair_group = min(16, doc_count // 2)
    pitch = grads_ref.shape[0] // doc_count

    def one_group(group, carry):
        masked = [
            jnp.where(pairs == group * pair_group + p, inner, jnp.zeros_like(inner)) for p in range(pair_group)
        ]
        sums = jnp.dot(jnp.concatenate(masked, axis=0), outer, preferred_element_type=jnp.float32)
        for p in range(pair_group):
            for parity in range(2):
                start = pl.multiple_of((2 * (group * pair_group + p) + parity) * pitch, 8)
                grads_ref[pl.ds(start, width), :] = sums[
                    p * width : (p + 1) * width, parity * lanes : (parity + 1) * lanes
                ]
        return carry

    groups = doc_count // (2 * pair_group)
    lax.fori_loop(0, groups, one_group, 0, unroll=groups == 1)
    high, low = [], []
    for j in range(width):
        parts = split(grads_ref[pl.ds(j, doc_count, stride=pitch), :])
        high.append(parts[0])
        low.append(parts[1])
    flat = jnp.concatenate([jnp.concatenate(high, axis=1), jnp.concatenate(low, axis=1)], axis=0)
    fetch.wait()
    result = jnp.dot(flat, queries_ref[...], preferred_element_type=jnp.float32)
    result = result[:doc_count] + result[doc_count:]
    columns = result.shape[1] // shares
    fill = jnp.zeros((DOC_DEV, LANES - columns), jnp.float32)
    for owner in range(owners):
        for share in range(shares):
            piece = result[owner * DOC_DEV : (owner + 1) * DOC_DEV, share * columns : (share + 1) * columns]
            out_ref[listed(owner, owners, owners - 1) * shares + share] = jnp.concatenate([piece, fill], axis=1)


def score(arrived, inner, queries, turns, owners):
    sources = arrived.shape[0]
    width = inner.shape[1] - DOC_ROWS
    doc_count = DOC_DEV * owners
    return pl.pallas_call(
        functools.partial(score_kernel, width=width, doc_count=doc_count, turns=turns),
        in_specs=[VMEM, VMEM, HBM],
        out_shape=jax.ShapeDtypeStruct((sources, DOC_DEV, LANES), jnp.float32),
        scratch_shapes=[
            pltpu.VMEM((doc_count * (width + 8), arrived.shape[2]), jnp.float32),
            pltpu.VMEM(queries.shape, jnp.bfloat16),
            pltpu.SemaphoreType.DMA,
        ],
        compiler_params=pltpu.CompilerParams(vmem_limit_bytes=40 * MIB),
        cost_estimate=cost(5),
    )(arrived, inner, stay(queries))


def sum_kernel(pieces_ref, out_ref):
    total = pieces_ref[0]
    for source in range(1, pieces_ref.shape[0]):
        total = total + pieces_ref[source]
    out_ref[...] = total[:, : out_ref.shape[1]]


def sum_pieces(pieces, columns):
    return pl.pallas_call(
        sum_kernel,
        in_specs=[VMEM],
        out_shape=jax.ShapeDtypeStruct((pieces.shape[1], columns), jnp.float32),
        compiler_params=pltpu.CompilerParams(vmem_limit_bytes=40 * MIB),
    )(pieces)


def exchange(block, axis, size, turn):
    return lax.ppermute(block, axis, [(i, i ^ turn) for i in range(size)])


def double(blocks, turns, axis, size, turn):
    blocks = jnp.concatenate([blocks, exchange(blocks, axis, size, turn)], axis=0)
    return blocks, turns + tuple(t ^ turn for t in turns)


def local(
    activations,
    grad_hidden,
    routes,
    doc_ids,
    query_grads,
    in_projection,
    out_projection,
    inverse_in,
    inverse_out,
):
    tokens, top = routes.shape
    experts, width, _ = inverse_in.shape
    owners = lax.axis_size("expert")
    shares = lax.axis_size("proj")
    quarter = tokens // shares
    assert quarter == LANES and 2 * width == LANES and experts * width // shares == LANES
    assert experts % 4 == 0 and experts // 4 <= DIAGONAL_ROWS
    assert shares == 4 and owners & (owners - 1) == 0
    assert DOC_DEV * owners <= 256

    flat_hidden = grad_hidden.reshape(tokens * top, grad_hidden.shape[2])
    inner_leaving, inner_own, shared, near_hidden = project_inner(
        activations, in_projection, inverse_out, flat_hidden, shares
    )
    inner_first = exchange(inner_leaving, "proj", shares, 2)
    far_shared = exchange(shared, "expert", owners, owners // 2)
    leaving, own = project_outer(near_hidden, flat_hidden, out_projection, shares, top)
    far_shared, inner_first, leaving = lax.optimization_barrier((far_shared, inner_first, leaving))
    near = exchange(leaving, "proj", shares, 1)
    shared, turns = jnp.stack([shared, far_shared]), (0, owners // 2)
    for bit in reversed(range(1, (owners // 2).bit_length() - 1)):
        shared, turns = double(shared, turns, "expert", owners, 1 << bit)
    shared = shared.reshape(-1, LANES)
    even = expand(shared, turns, width, experts, shares)
    near, even = lax.optimization_barrier((near, even))
    inner_second = exchange(combine(combine_inner_kernel, inner_own, inner_first), "proj", shares, 1)
    sent = combine(combine_outer_kernel, own, near)
    far = exchange(sent, "proj", shares, 2)
    inner = finish_inner(inner_own, inner_first, inner_second, doc_ids.reshape(shares, quarter), width)
    packet = exchange(jnp.concatenate([shared, inner], axis=0), "expert", owners, 1)
    inner, _ = lax.optimization_barrier((inner, sent))
    owner_turns = tuple(reversed(range(owners)))
    arriving = [exchange(inner, "expert", owners, turn) for turn in owner_turns if turn > 1]
    arriving.append(packet[shared.shape[0] :])
    odd = expand(packet, turns, width, experts, shares)
    far, odd = lax.optimization_barrier((far, odd))
    quarter_routes = lax.dynamic_slice_in_dim(routes, lax.axis_index("proj") * quarter, quarter, 0)
    payload = condition(own, near, far, quarter_routes, even, odd, shares, width)
    payload, arriving = lax.optimization_barrier((payload, arriving))
    arrived = send_to_all(payload, owners, shares, owners // 2)
    inner = jnp.stack(arriving + [inner])
    inner, share_turns = inner[None], (0,)
    inner, share_turns = double(inner, share_turns, "proj", shares, 1)
    inner, query_grads = lax.optimization_barrier((inner, query_grads))
    inner, share_turns = double(inner, share_turns, "proj", shares, 2)
    inner = inner.reshape(owners * shares, width + DOC_ROWS, quarter)
    all_turns = tuple((o, p) for p in share_turns for o in owner_turns)
    queries = condition_queries(query_grads, inverse_in)
    pieces = score(arrived, inner, queries, all_turns, owners)
    pieces = send_to_all(pieces, owners, shares, owners - 1)
    return sum_pieces(pieces, query_grads.shape[0] // shares).T


def solution(mesh):
    in_specs = (
        P(("groups", "expert"), "proj"),
        P(("groups", "expert"), None, "proj"),
        P(("groups", "expert"), None),
        P(("groups", "expert")),
        P(None, "expert", "proj"),
        P(None, "proj"),
        P(None, "proj"),
        P("expert", None, None),
        P("expert", None, None),
    )
    out_specs = P("proj", ("groups", "expert"))
    return jax.shard_map(local, mesh=mesh, in_specs=in_specs, out_specs=out_specs, check_vma=False)
```

```python
import functools

import jax
import jax.numpy as jnp
from jax import lax
from jax.experimental import pallas as pl
from jax.experimental.pallas import tpu as pltpu
from jax.sharding import PartitionSpec as P

DOC_DEV = 8
LANES = 128
DOC_ROWS = 16
DIAGONAL_ROWS = 16
MIB = 1024 * 1024
VMEM = pl.BlockSpec(memory_space=pltpu.VMEM)
HBM = pl.BlockSpec(memory_space=pltpu.HBM)


def low_lanes(rows, width):
    return lax.broadcasted_iota(jnp.int32, (rows, LANES), 1) < width


def stay(array):
    return pltpu.with_memory_space_constraint(array, pltpu.HBM)


def listed(owner, owners, first):
    return (owner + owners - first) % owners


def send_to_all(blocks, owners, shares, first):
    members = [(i + first * shares) % (owners * shares) for i in range(owners * shares)]
    return lax.all_to_all(blocks, ("expert", "proj"), 0, 0, tiled=True, axis_index_groups=[members])


def split(value):
    high = value.astype(jnp.bfloat16)
    return high, (value - high.astype(jnp.float32)).astype(jnp.bfloat16)


def cost(microseconds):
    return pl.CostEstimate(flops=0, bytes_accessed=int(microseconds * 3.3e6), transcendentals=0)


def in_order(copies, ahead):
    for copy in copies[:ahead]:
        copy.start()
    state = [0]

    def take():
        copies[state[0]].wait()
        if state[0] + ahead < len(copies):
            copies[state[0] + ahead].start()
        state[0] += 1

    return take


def twice_transposed(projection):
    once = jnp.transpose(projection.astype(jnp.float32))
    return jnp.concatenate([once, once], axis=1).astype(jnp.bfloat16)


def triangles(width):
    row = lax.broadcasted_iota(jnp.int32, (width, LANES), 0)
    column = lax.broadcasted_iota(jnp.int32, (width, LANES), 1) % width
    return row, column


def pack_factors(inverse_ref, shared_ref):
    experts, width, _ = inverse_ref.shape
    quarter = experts // 4
    row, column = triangles(width)
    diagonals = []
    for e in range(quarter):
        lower, upper = (
            jnp.concatenate([inverse_ref[first], inverse_ref[first + 2 * quarter]], axis=1) for first in (e, e + quarter)
        )
        shared_ref[e * width : (e + 1) * width, :] = jnp.where(row >= column, lower, upper).astype(jnp.bfloat16)
        diagonals.append(jnp.sum(jnp.where(row == column, upper, 0.0), axis=0, keepdims=True))
    fill = jnp.zeros((DIAGONAL_ROWS - quarter, LANES), jnp.float32)
    shared_ref[quarter * width :, :] = jnp.concatenate(diagonals + [fill], axis=0).astype(jnp.bfloat16)


def unpack_factors(packed, width, quarter):
    row, column = triangles(width)
    packed = packed.astype(jnp.float32)
    lower, upper = [], []
    for e in range(quarter):
        square = packed[e * width : (e + 1) * width]
        turned = jnp.transpose(square)
        turned = jnp.concatenate([turned[:width], turned[width:]], axis=1)
        diagonal = packed[quarter * width + e : quarter * width + e + 1]
        lower.append(jnp.where(row >= column, square, turned))
        upper.append(jnp.where(row == column, diagonal, jnp.where(row < column, square, turned)))
    return jnp.concatenate(lower + upper, axis=0).astype(jnp.bfloat16)


OUTER_TURNS = (1, 3, 2, 0)


def quarter_rows(place, turn, rows):
    return pl.ds(pl.multiple_of(jnp.bitwise_xor(place, turn) * rows, rows), rows)


def inner_kernel(
    act_hbm,
    in_proj_hbm,
    inverse_hbm,
    hidden_hbm,
    leaving_ref,
    own_ref,
    shared_ref,
    hidden_ref,
    act_ref,
    in_proj_ref,
    inverse_ref,
    sems,
):
    turns = (2, 3, 1, 0)
    quarter = act_ref.shape[1]
    width = in_proj_ref.shape[0]
    half = quarter // 2
    place = lax.axis_index("proj")
    pairs = [(in_proj_hbm, in_proj_ref)]
    for g, turn in enumerate(turns):
        rows = pl.ds(pl.multiple_of(jnp.bitwise_xor(place, turn) * quarter, quarter), quarter)
        pairs.append((act_hbm.at[rows], act_ref.at[g]))
        if g == 0:
            pairs.append((inverse_hbm, inverse_ref))
    for g in range(hidden_ref.shape[0]):
        pairs.append((hidden_hbm.at[quarter_rows(place, OUTER_TURNS[g], hidden_ref.shape[1])], hidden_ref.at[g]))
    take = in_order([pltpu.make_async_copy(*pair, sems.at[i]) for i, pair in enumerate(pairs)], 4)
    take()
    first = low_lanes(half, width)
    weights = twice_transposed(in_proj_ref[...])
    for wire_ref in (leaving_ref, own_ref):
        take()
        if wire_ref is leaving_ref:
            take()
            pack_factors(inverse_ref, shared_ref)
        take()
        g = 0 if wire_ref is leaving_ref else 2
        rows = act_ref[g : g + 2].reshape(2 * quarter, act_ref.shape[2])
        inner = jnp.dot(rows, weights, preferred_element_type=jnp.float32)
        for i in range(2):
            start = i * quarter
            high, low = split(jnp.where(first, inner[start : start + half], inner[start + half : start + quarter]))
            wire_ref[i, :half, :] = high
            wire_ref[i, half:, :] = low
    for _ in range(hidden_ref.shape[0]):
        take()


def project_inner(activations, in_projection, inverse_out, flat_hidden, quarters):
    tokens, model = activations.shape
    quarter = tokens // quarters
    experts, width, _ = inverse_out.shape
    wire = jax.ShapeDtypeStruct((quarters // 2, quarter, LANES), jnp.bfloat16)
    fixed = (in_projection, inverse_out)
    return pl.pallas_call(
        inner_kernel,
        in_specs=[HBM] * 4,
        out_specs=[VMEM] * 4,
        out_shape=[
            wire,
            wire,
            jax.ShapeDtypeStruct((experts // 4 * width + DIAGONAL_ROWS, LANES), jnp.bfloat16),
            jax.ShapeDtypeStruct((quarters // 2, flat_hidden.shape[0] // quarters, flat_hidden.shape[1]), jnp.bfloat16),
        ],
        scratch_shapes=[pltpu.VMEM((quarters, quarter, model), jnp.bfloat16)]
        + [pltpu.VMEM(array.shape, array.dtype) for array in fixed]
        + [pltpu.SemaphoreType.DMA((quarters + len(fixed) + quarters // 2,))],
        compiler_params=pltpu.CompilerParams(vmem_limit_bytes=40 * MIB),
        cost_estimate=cost(2.5),
    )(*[stay(array) for array in (activations, *fixed, flat_hidden)])


def outer_kernel(near_ref, hidden_hbm, out_proj_hbm, leaving_ref, own_ref, hidden_ref, out_proj_ref, rows_ref, sems, *, top):
    ready, rows, _ = near_ref.shape
    quarter = rows // top
    width = out_proj_ref.shape[0]
    place = lax.axis_index("proj")
    pairs = [(out_proj_hbm, out_proj_ref)]
    for i, turn in enumerate(OUTER_TURNS[ready:]):
        pairs.append((hidden_hbm.at[quarter_rows(place, turn, rows)], hidden_ref.at[i]))
    take = in_order([pltpu.make_async_copy(*pair, sems.at[i]) for i, pair in enumerate(pairs)], len(pairs))
    take()
    first = low_lanes(quarter, width)
    weights = twice_transposed(out_proj_ref[...])

    def pack_rows(g):
        wire_ref = leaving_ref.at[g] if g < 2 else own_ref.at[g - 2]
        for pair in range(top // 2):
            even = rows_ref[g % 2, pl.ds(2 * pair, quarter, stride=top), :]
            odd = rows_ref[g % 2, pl.ds(2 * pair + 1, quarter, stride=top), :]
            wire_ref[pair * quarter : (pair + 1) * quarter, :] = jnp.where(first, even, odd).astype(jnp.bfloat16)

    for g in range(len(OUTER_TURNS)):
        if g >= ready:
            take()
        hidden = near_ref[g] if g < ready else hidden_ref[g - ready]
        rows_ref[g % 2] = jnp.dot(hidden, weights, preferred_element_type=jnp.float32)
        if g:
            pack_rows(g - 1)
    pack_rows(len(OUTER_TURNS) - 1)


def project_outer(near_hidden, flat_hidden, out_projection, quarters, top):
    rows, hidden = flat_hidden.shape
    wire = jax.ShapeDtypeStruct((quarters // 2, rows // quarters // 2, LANES), jnp.bfloat16)
    return pl.pallas_call(
        functools.partial(outer_kernel, top=top),
        in_specs=[VMEM, HBM, HBM],
        out_specs=[VMEM] * 2,
        out_shape=[wire, wire],
        scratch_shapes=[
            pltpu.VMEM((quarters // 2, rows // quarters, hidden), jnp.bfloat16),
            pltpu.VMEM(out_projection.shape, out_projection.dtype),
            pltpu.VMEM((2, rows // quarters, LANES), jnp.float32),
            pltpu.SemaphoreType.DMA((quarters // 2 + 1,)),
        ],
        compiler_params=pltpu.CompilerParams(vmem_limit_bytes=40 * MIB),
        cost_estimate=cost(4),
    )(near_hidden, stay(flat_hidden), stay(out_projection))


def exact_rows(rows):
    half = rows.shape[0] // 2
    return rows[:half].astype(jnp.float32) + rows[half:].astype(jnp.float32)


def combine_inner_kernel(own_ref, near_ref, out_ref):
    high, low = split(exact_rows(own_ref[0]) + exact_rows(near_ref[1]))
    out_ref[: high.shape[0], :] = high
    out_ref[high.shape[0] :, :] = low


def combine_outer_kernel(own_ref, near_ref, out_ref):
    out_ref[...] = (own_ref[0].astype(jnp.float32) + near_ref[1].astype(jnp.float32)).astype(jnp.bfloat16)


def combine(kernel, own, near):
    return pl.pallas_call(
        kernel,
        in_specs=[VMEM, VMEM],
        out_shape=jax.ShapeDtypeStruct(own.shape[1:], jnp.bfloat16),
        compiler_params=pltpu.CompilerParams(vmem_limit_bytes=40 * MIB),
        cost_estimate=cost(0.5),
    )(own, near)


def finish_inner_kernel(own_ref, first_ref, second_ref, docs_ref, out_ref):
    total = exact_rows(own_ref[1]) + exact_rows(first_ref[0]) + exact_rows(second_ref[...])
    width = out_ref.shape[0] - DOC_ROWS
    total = jnp.concatenate([total[:, :width], total[:, width:]], axis=0)
    out_ref[:width, :] = jnp.transpose(total).astype(jnp.bfloat16)
    docs = docs_ref[pl.ds(lax.axis_index("proj"), 1), :].astype(jnp.float32)
    out_ref[width:, :] = jnp.broadcast_to(docs, (DOC_ROWS, LANES)).astype(jnp.bfloat16)


def finish_inner(own, first, second, doc_rows, width):
    return pl.pallas_call(
        finish_inner_kernel,
        in_specs=[VMEM] * 4,
        out_shape=jax.ShapeDtypeStruct((width + DOC_ROWS, own.shape[1]), jnp.bfloat16),
        compiler_params=pltpu.CompilerParams(vmem_limit_bytes=40 * MIB),
        cost_estimate=cost(0.5),
    )(own, first, second, doc_rows)


def expand_kernel(shared_ref, weights_ref, *, width, experts, shares, turns):
    half = experts // 2
    share_rows = width // shares
    columns = shares * half * share_rows
    lane = lax.broadcasted_iota(jnp.int32, (LANES, columns), 1)
    row = lax.broadcasted_iota(jnp.int32, (LANES, columns), 0)
    expert_lane = lax.broadcasted_iota(jnp.int32, (half * width, columns), 1) // share_rows % half
    expert_row = lax.broadcasted_iota(jnp.int32, (half * width, columns), 0) // width
    own = expert_lane == expert_row
    rows = half // 2 * width + DIAGONAL_ROWS
    factors = [
        unpack_factors(shared_ref[entry * rows : (entry + 1) * rows], width, half // 2) for entry in range(len(turns))
    ]
    for side in range(2):
        share = jnp.bitwise_xor(lane // (half * share_rows), side)
        source = share * share_rows + lane % share_rows
        spread = (row == source + side * width).astype(jnp.float32).astype(jnp.bfloat16)
        for entry, turn in enumerate(turns):
            placed = jnp.dot(factors[entry], spread, preferred_element_type=jnp.float32)
            weights_ref[turn // 2, side] = jnp.where(own, placed, 0.0).astype(jnp.bfloat16)


def expand(shared, turns, width, experts, shares):
    owners = len(turns)
    return pl.pallas_call(
        functools.partial(expand_kernel, width=width, experts=experts, shares=shares, turns=turns),
        in_specs=[VMEM],
        out_shape=jax.ShapeDtypeStruct((owners, 2, experts // 2 * width, experts // 2 * width), jnp.bfloat16),
        compiler_params=pltpu.CompilerParams(vmem_limit_bytes=40 * MIB),
        cost_estimate=cost(1),
    )(shared)


def condition_kernel(
    own_ref, near_ref, far_ref, routes_ref, even_ref, odd_ref, payload_ref, value_ref, name_ref, *, top, width
):
    quarter = routes_ref.shape[0]
    pairs, sides, dense_width, _ = even_ref.shape
    groups = 2 * pairs
    shares = payload_ref.shape[0] // groups
    experts = sides * dense_width // width
    first = low_lanes(quarter, width)
    second = 1 - first.astype(jnp.int32)

    def summed(start, size):
        rows = slice(start, start + size)
        total = own_ref[1, rows, :].astype(jnp.float32) + near_ref[0, rows, :].astype(jnp.float32)
        return total + far_ref[rows, :].astype(jnp.float32)

    for pair in range(top // 2):
        both = summed(pair * quarter, quarter)
        swapped = pltpu.roll(both, width, 1)
        value_ref[2 * pair] = jnp.where(first, both, swapped)
        value_ref[2 * pair + 1] = jnp.where(first, swapped, both)
    for k in range(top):
        name_ref[k] = jnp.broadcast_to(routes_ref[:, k : k + 1], (quarter, LANES)) - second

    def one_group(step, carry, parity):
        weights_ref = odd_ref if parity else even_ref
        group = jnp.bitwise_xor(lax.axis_index("expert"), 2 * step + parity)
        dense = []
        for pair in range(experts // 2):
            base = group * experts + 2 * pair
            chosen = jnp.zeros((quarter, LANES), jnp.float32)
            for k in range(top):
                chosen = jnp.where(name_ref[k] == base, value_ref[k], chosen)
            dense.append(chosen.astype(jnp.bfloat16))
        per_side = len(dense) // sides
        results = [
            jnp.dot(
                jnp.concatenate(dense[side * per_side : (side + 1) * per_side], axis=1),
                weights_ref[step, side],
                preferred_element_type=jnp.float32,
            )
            for side in range(sides)
        ]
        for share in range(shares):
            lanes = slice(share // 2 * LANES, (share // 2 + 1) * LANES)
            low, high = (results[side][:, lanes] for side in ((0, 1) if share % 2 == 0 else (1, 0)))
            place = listed(group, groups, groups // 2) * shares + share
            payload_ref[place] = jnp.where(first, low, high).astype(jnp.bfloat16)
        return carry

    for parity in range(2):
        lax.fori_loop(0, pairs, functools.partial(one_group, parity=parity), 0, unroll=pairs <= 2)


def condition(own, near, far, quarter_routes, even, odd, shares, width):
    quarter, top = quarter_routes.shape
    groups = 2 * even.shape[0]
    return pl.pallas_call(
        functools.partial(condition_kernel, top=top, width=width),
        in_specs=[VMEM] * 6,
        out_shape=jax.ShapeDtypeStruct((groups * shares, quarter, LANES), jnp.bfloat16),
        scratch_shapes=[
            pltpu.VMEM((top, quarter, LANES), jnp.float32),
            pltpu.VMEM((top, quarter, LANES), jnp.int32),
        ],
        compiler_params=pltpu.CompilerParams(vmem_limit_bytes=40 * MIB),
        cost_estimate=cost(2),
    )(own, near, far, quarter_routes, even, odd)


def query_kernel(query_ref, inverse_ref, out_hbm, factor_ref, spread_ref, wide_ref, out_ref, sems):
    count, experts, _ = query_ref.shape
    width = inverse_ref.shape[1]
    step = pl.program_id(0)
    rows = out_ref.shape[0] // width
    pitch = wide_ref.shape[1] // width

    @pl.when(step == 0)
    def _():
        zeros = jnp.zeros((width, width), jnp.bfloat16)
        for e in range(experts):
            high, low = split(inverse_ref[e])
            left = jnp.concatenate([high, zeros, low, zeros], axis=0)
            right = jnp.concatenate([zeros, high, zeros, low], axis=0)
            factor_ref[e] = jnp.concatenate([left, right], axis=1)

    spread_ref[...] = query_ref[...].astype(jnp.float32).reshape(count * experts, LANES)
    for e in range(experts):
        query = spread_ref[pl.ds(e, count, stride=experts), :].astype(jnp.bfloat16)
        result = lax.dot_general(
            factor_ref[e], query, (((1,), (1,)), ((), ())), preferred_element_type=jnp.float32
        )
        result = result[: 2 * width] + result[2 * width :]
        slot = (e + experts // 2 * (lax.axis_index("proj") % 2)) % experts
        start = slot * (rows // experts) + 2 * step
        for tile in range(wide_ref.shape[0]):
            part = result[:, tile * LANES : (tile + 1) * LANES]
            wide_ref[tile, pl.ds(start, width, stride=pitch), :] = part[:width]
            wide_ref[tile, pl.ds(start + 1, width, stride=pitch), :] = part[width:]

    @pl.when(step == pl.num_programs(0) - 1)
    def _():
        copies = []
        for part in range(sems.shape[0]):
            first = part * (width // sems.shape[0])
            for j in range(first, first + width // sems.shape[0]):
                for tile in range(wide_ref.shape[0]):
                    out_ref[j * rows : (j + 1) * rows, tile * LANES : (tile + 1) * LANES] = wide_ref[
                        tile, j * pitch : j * pitch + rows, :
                    ].astype(jnp.bfloat16)
            block = pl.ds(first * rows, width // sems.shape[0] * rows)
            copies.append(pltpu.make_async_copy(out_ref.at[block], out_hbm.at[block], sems.at[part]))
            copies[-1].start()
        for copy in copies:
            copy.wait()


def condition_queries(query_grads, inverse_in):
    count, experts, flat = query_grads.shape
    width = inverse_in.shape[1]
    rows = experts * flat
    return pl.pallas_call(
        query_kernel,
        grid=(flat // LANES,),
        in_specs=[
            pl.BlockSpec((count, experts, LANES), lambda c: (0, 0, c)),
            pl.BlockSpec(inverse_in.shape, lambda c: (0, 0, 0)),
        ],
        out_specs=HBM,
        out_shape=pltpu.HBM((rows, count), jnp.bfloat16),
        scratch_shapes=[
            pltpu.VMEM((experts, 4 * width, 2 * width), jnp.bfloat16),
            pltpu.VMEM((count * experts, LANES), jnp.float32),
            pltpu.VMEM((count // LANES, rows + 8 * width, LANES), jnp.float32),
            pltpu.VMEM((rows, count), jnp.bfloat16),
            pltpu.SemaphoreType.DMA((8,)),
        ],
        compiler_params=pltpu.CompilerParams(vmem_limit_bytes=40 * MIB),
        cost_estimate=cost(10),
    )(stay(query_grads), inverse_in)


def score_kernel(
    arrived_ref, inner_ref, far_ref, out_ref, grads_ref, queries_ref, sem, *, width, doc_count, turns
):
    fetch = pltpu.make_async_copy(far_ref, queries_ref, sem)
    fetch.start()
    sources, quarter, lanes = arrived_ref.shape
    shares = lax.axis_size("proj")
    owners = sources // shares
    outer, inner, docs = [], [], []
    for entry, (owner_turn, share_turn) in enumerate(turns):
        owner = jnp.bitwise_xor(lax.axis_index("expert"), owner_turn)
        share = jnp.bitwise_xor(lax.axis_index("proj"), share_turn)
        outer.append(arrived_ref[listed(owner, owners, owners // 2) * shares + share])
        docs.append(inner_ref[entry, width:, :].astype(jnp.float32).astype(jnp.int32))
        inner.append(inner_ref[entry, :width, :])
    outer = jnp.concatenate(outer, axis=0)
    inner = jnp.concatenate(inner, axis=1)
    docs = jnp.concatenate(docs, axis=1)
    odd = lax.dot_general(
        (docs & 1).astype(jnp.float32).astype(jnp.bfloat16),
        jnp.full((DOC_ROWS, lanes), 1 / DOC_ROWS, jnp.bfloat16),
        (((0,), (0,)), ((), ())),
        preferred_element_type=jnp.float32,
    ).astype(jnp.bfloat16)
    odd_outer = outer * odd
    outer = jnp.concatenate([outer - odd_outer, odd_outer], axis=1)
    pairs = jnp.broadcast_to(docs[:1] >> 1, inner.shape)
    pair_group = min(16, doc_count // 2)
    pitch = grads_ref.shape[0] // doc_count

    def one_group(group, carry):
        masked = [
            jnp.where(pairs == group * pair_group + p, inner, jnp.zeros_like(inner)) for p in range(pair_group)
        ]
        sums = jnp.dot(jnp.concatenate(masked, axis=0), outer, preferred_element_type=jnp.float32)
        for p in range(pair_group):
            for parity in range(2):
                start = pl.multiple_of((2 * (group * pair_group + p) + parity) * pitch, 8)
                grads_ref[pl.ds(start, width), :] = sums[
                    p * width : (p + 1) * width, parity * lanes : (parity + 1) * lanes
                ]
        return carry

    groups = doc_count // (2 * pair_group)
    lax.fori_loop(0, groups, one_group, 0, unroll=groups == 1)
    flat = jnp.concatenate(
        [grads_ref[pl.ds(j, doc_count, stride=pitch), :].astype(jnp.bfloat16) for j in range(width)], axis=1
    )
    fetch.wait()
    result = jnp.dot(flat, queries_ref[...], preferred_element_type=jnp.float32)
    columns = result.shape[1] // shares
    fill = jnp.zeros((DOC_DEV, LANES - columns), jnp.float32)
    for owner in range(owners):
        for share in range(shares):
            piece = result[owner * DOC_DEV : (owner + 1) * DOC_DEV, share * columns : (share + 1) * columns]
            out_ref[listed(owner, owners, owners - 1) * shares + share] = jnp.concatenate([piece, fill], axis=1)


def score(arrived, inner, queries, turns, owners):
    sources = arrived.shape[0]
    width = inner.shape[1] - DOC_ROWS
    doc_count = DOC_DEV * owners
    return pl.pallas_call(
        functools.partial(score_kernel, width=width, doc_count=doc_count, turns=turns),
        in_specs=[VMEM, VMEM, HBM],
        out_shape=jax.ShapeDtypeStruct((sources, DOC_DEV, LANES), jnp.float32),
        scratch_shapes=[
            pltpu.VMEM((doc_count * (width + 8), arrived.shape[2]), jnp.float32),
            pltpu.VMEM(queries.shape, jnp.bfloat16),
            pltpu.SemaphoreType.DMA,
        ],
        compiler_params=pltpu.CompilerParams(vmem_limit_bytes=40 * MIB),
        cost_estimate=cost(5),
    )(arrived, inner, stay(queries))


def sum_kernel(pieces_ref, out_ref):
    total = pieces_ref[0]
    for source in range(1, pieces_ref.shape[0]):
        total = total + pieces_ref[source]
    out_ref[...] = total[:, : out_ref.shape[1]]


def sum_pieces(pieces, columns):
    return pl.pallas_call(
        sum_kernel,
        in_specs=[VMEM],
        out_shape=jax.ShapeDtypeStruct((pieces.shape[1], columns), jnp.float32),
        compiler_params=pltpu.CompilerParams(vmem_limit_bytes=40 * MIB),
    )(pieces)


def exchange(block, axis, size, turn):
    return lax.ppermute(block, axis, [(i, i ^ turn) for i in range(size)])


def double(blocks, turns, axis, size, turn):
    blocks = jnp.concatenate([blocks, exchange(blocks, axis, size, turn)], axis=0)
    return blocks, turns + tuple(t ^ turn for t in turns)


def local(
    activations,
    grad_hidden,
    routes,
    doc_ids,
    query_grads,
    in_projection,
    out_projection,
    inverse_in,
    inverse_out,
):
    tokens, top = routes.shape
    experts, width, _ = inverse_in.shape
    owners = lax.axis_size("expert")
    shares = lax.axis_size("proj")
    quarter = tokens // shares
    assert quarter == LANES and 2 * width == LANES and experts * width // shares == LANES
    assert experts % 4 == 0 and experts // 4 <= DIAGONAL_ROWS
    assert shares == 4 and owners & (owners - 1) == 0
    assert DOC_DEV * owners <= 256

    flat_hidden = grad_hidden.reshape(tokens * top, grad_hidden.shape[2])
    inner_leaving, inner_own, shared, near_hidden = project_inner(
        activations, in_projection, inverse_out, flat_hidden, shares
    )
    inner_first = exchange(inner_leaving, "proj", shares, 2)
    far_shared = exchange(shared, "expert", owners, owners // 2)
    leaving, own = project_outer(near_hidden, flat_hidden, out_projection, shares, top)
    far_shared, inner_first, leaving = lax.optimization_barrier((far_shared, inner_first, leaving))
    near = exchange(leaving, "proj", shares, 1)
    shared, turns = jnp.stack([shared, far_shared]), (0, owners // 2)
    for bit in reversed(range(1, (owners // 2).bit_length() - 1)):
        shared, turns = double(shared, turns, "expert", owners, 1 << bit)
    shared = shared.reshape(-1, LANES)
    even = expand(shared, turns, width, experts, shares)
    near, even = lax.optimization_barrier((near, even))
    inner_second = exchange(combine(combine_inner_kernel, inner_own, inner_first), "proj", shares, 1)
    sent = combine(combine_outer_kernel, own, near)
    far = exchange(sent, "proj", shares, 2)
    inner = finish_inner(inner_own, inner_first, inner_second, doc_ids.reshape(shares, quarter), width)
    packet = exchange(jnp.concatenate([shared, inner], axis=0), "expert", owners, 1)
    inner, _ = lax.optimization_barrier((inner, sent))
    owner_turns = (*range(2, owners), 1, 0)
    arriving = [exchange(inner, "expert", owners, turn) for turn in owner_turns if turn > 1]
    arriving.append(packet[shared.shape[0] :])
    odd = expand(packet, turns, width, experts, shares)
    far, odd = lax.optimization_barrier((far, odd))
    quarter_routes = lax.dynamic_slice_in_dim(routes, lax.axis_index("proj") * quarter, quarter, 0)
    payload = condition(own, near, far, quarter_routes, even, odd, shares, width)
    payload, arriving = lax.optimization_barrier((payload, arriving))
    arrived = send_to_all(payload, owners, shares, owners // 2)
    inner = jnp.stack(arriving + [inner])
    inner, share_turns = inner[None], (0,)
    inner, share_turns = double(inner, share_turns, "proj", shares, 1)
    inner, query_grads = lax.optimization_barrier((inner, query_grads))
    inner, share_turns = double(inner, share_turns, "proj", shares, 2)
    inner = inner.reshape(owners * shares, width + DOC_ROWS, quarter)
    all_turns = tuple((o, p) for p in share_turns for o in owner_turns)
    queries = condition_queries(query_grads, inverse_in)
    pieces = score(arrived, inner, queries, all_turns, owners)
    pieces = send_to_all(pieces, owners, shares, owners - 1)
    return sum_pieces(pieces, query_grads.shape[0] // shares).T


def solution(mesh):
    in_specs = (
        P(("groups", "expert"), "proj"),
        P(("groups", "expert"), None, "proj"),
        P(("groups", "expert"), None),
        P(("groups", "expert")),
        P(None, "expert", "proj"),
        P(None, "proj"),
        P(None, "proj"),
        P("expert", None, None),
        P("expert", None, None),
    )
    out_specs = P("proj", ("groups", "expert"))
    return jax.shard_map(local, mesh=mesh, in_specs=in_specs, out_specs=out_specs, check_vma=False)
```

```python
import functools

import jax
import jax.numpy as jnp
from jax import lax
from jax.experimental import pallas as pl
from jax.experimental.pallas import tpu as pltpu
from jax.sharding import PartitionSpec as P

DOC_DEV = 8
LANES = 128
DOC_ROWS = 16
DIAGONAL_ROWS = 16
MIB = 1024 * 1024
VMEM = pl.BlockSpec(memory_space=pltpu.VMEM)
HBM = pl.BlockSpec(memory_space=pltpu.HBM)


def low_lanes(rows, width):
    return lax.broadcasted_iota(jnp.int32, (rows, LANES), 1) < width


def stay(array):
    return pltpu.with_memory_space_constraint(array, pltpu.HBM)


def listed(owner, owners, first):
    return (owner + owners - first) % owners


def send_to_all(blocks, owners, shares, first):
    members = [(i + first * shares) % (owners * shares) for i in range(owners * shares)]
    return lax.all_to_all(blocks, ("expert", "proj"), 0, 0, tiled=True, axis_index_groups=[members])


def split(value):
    high = value.astype(jnp.bfloat16)
    return high, (value - high.astype(jnp.float32)).astype(jnp.bfloat16)


def cost(microseconds):
    return pl.CostEstimate(flops=0, bytes_accessed=int(microseconds * 3.3e6), transcendentals=0)


def in_order(copies, ahead):
    for copy in copies[:ahead]:
        copy.start()
    state = [0]

    def take():
        copies[state[0]].wait()
        if state[0] + ahead < len(copies):
            copies[state[0] + ahead].start()
        state[0] += 1

    return take


def twice_transposed(projection):
    once = jnp.transpose(projection.astype(jnp.float32))
    return jnp.concatenate([once, once], axis=1).astype(jnp.bfloat16)


def triangles(width):
    row = lax.broadcasted_iota(jnp.int32, (width, LANES), 0)
    column = lax.broadcasted_iota(jnp.int32, (width, LANES), 1) % width
    return row, column


def pack_factors(inverse_ref, shared_ref):
    experts, width, _ = inverse_ref.shape
    quarter = experts // 4
    row, column = triangles(width)
    diagonals = []
    for e in range(quarter):
        lower, upper = (
            jnp.concatenate([inverse_ref[first], inverse_ref[first + 2 * quarter]], axis=1) for first in (e, e + quarter)
        )
        shared_ref[e * width : (e + 1) * width, :] = jnp.where(row >= column, lower, upper).astype(jnp.bfloat16)
        diagonals.append(jnp.sum(jnp.where(row == column, upper, 0.0), axis=0, keepdims=True))
    fill = jnp.zeros((DIAGONAL_ROWS - quarter, LANES), jnp.float32)
    shared_ref[quarter * width :, :] = jnp.concatenate(diagonals + [fill], axis=0).astype(jnp.bfloat16)


def unpack_factors(packed, width, quarter):
    row, column = triangles(width)
    packed = packed.astype(jnp.float32)
    lower, upper = [], []
    for e in range(quarter):
        square = packed[e * width : (e + 1) * width]
        turned = jnp.transpose(square)
        turned = jnp.concatenate([turned[:width], turned[width:]], axis=1)
        diagonal = packed[quarter * width + e : quarter * width + e + 1]
        lower.append(jnp.where(row >= column, square, turned))
        upper.append(jnp.where(row == column, diagonal, jnp.where(row < column, square, turned)))
    return jnp.concatenate(lower + upper, axis=0).astype(jnp.bfloat16)


OUTER_TURNS = (1, 3, 2, 0)


def quarter_rows(place, turn, rows):
    return pl.ds(pl.multiple_of(jnp.bitwise_xor(place, turn) * rows, rows), rows)


def inner_kernel(
    act_hbm,
    in_proj_hbm,
    inverse_hbm,
    hidden_hbm,
    leaving_ref,
    own_ref,
    shared_ref,
    hidden_ref,
    act_ref,
    in_proj_ref,
    inverse_ref,
    sems,
):
    turns = (2, 3, 1, 0)
    quarter = act_ref.shape[1]
    width = in_proj_ref.shape[0]
    half = quarter // 2
    place = lax.axis_index("proj")
    pairs = [(in_proj_hbm, in_proj_ref)]
    for g, turn in enumerate(turns):
        rows = pl.ds(pl.multiple_of(jnp.bitwise_xor(place, turn) * quarter, quarter), quarter)
        pairs.append((act_hbm.at[rows], act_ref.at[g]))
        if g == 0:
            pairs.append((inverse_hbm, inverse_ref))
    for g in range(hidden_ref.shape[0]):
        pairs.append((hidden_hbm.at[quarter_rows(place, OUTER_TURNS[g], hidden_ref.shape[1])], hidden_ref.at[g]))
    take = in_order([pltpu.make_async_copy(*pair, sems.at[i]) for i, pair in enumerate(pairs)], 4)
    take()
    first = low_lanes(half, width)
    weights = twice_transposed(in_proj_ref[...])
    for wire_ref in (leaving_ref, own_ref):
        take()
        if wire_ref is leaving_ref:
            take()
            pack_factors(inverse_ref, shared_ref)
        take()
        g = 0 if wire_ref is leaving_ref else 2
        rows = act_ref[g : g + 2].reshape(2 * quarter, act_ref.shape[2])
        inner = jnp.dot(rows, weights, preferred_element_type=jnp.float32)
        for i in range(2):
            start = i * quarter
            high, low = split(jnp.where(first, inner[start : start + half], inner[start + half : start + quarter]))
            wire_ref[i, :half, :] = high
            wire_ref[i, half:, :] = low
    for _ in range(hidden_ref.shape[0]):
        take()


def project_inner(activations, in_projection, inverse_out, flat_hidden, quarters):
    tokens, model = activations.shape
    quarter = tokens // quarters
    experts, width, _ = inverse_out.shape
    wire = jax.ShapeDtypeStruct((quarters // 2, quarter, LANES), jnp.bfloat16)
    fixed = (in_projection, inverse_out)
    return pl.pallas_call(
        inner_kernel,
        in_specs=[HBM] * 4,
        out_specs=[VMEM] * 4,
        out_shape=[
            wire,
            wire,
            jax.ShapeDtypeStruct((experts // 4 * width + DIAGONAL_ROWS, LANES), jnp.bfloat16),
            jax.ShapeDtypeStruct((quarters // 2, flat_hidden.shape[0] // quarters, flat_hidden.shape[1]), jnp.bfloat16),
        ],
        scratch_shapes=[pltpu.VMEM((quarters, quarter, model), jnp.bfloat16)]
        + [pltpu.VMEM(array.shape, array.dtype) for array in fixed]
        + [pltpu.SemaphoreType.DMA((quarters + len(fixed) + quarters // 2,))],
        compiler_params=pltpu.CompilerParams(vmem_limit_bytes=40 * MIB),
        cost_estimate=cost(2.5),
    )(*[stay(array) for array in (activations, *fixed, flat_hidden)])


def outer_kernel(near_ref, hidden_hbm, out_proj_hbm, leaving_ref, own_ref, hidden_ref, out_proj_ref, rows_ref, sems, *, top):
    ready, rows, _ = near_ref.shape
    quarter = rows // top
    width = out_proj_ref.shape[0]
    place = lax.axis_index("proj")
    pairs = [(out_proj_hbm, out_proj_ref)]
    for i, turn in enumerate(OUTER_TURNS[ready:]):
        pairs.append((hidden_hbm.at[quarter_rows(place, turn, rows)], hidden_ref.at[i]))
    take = in_order([pltpu.make_async_copy(*pair, sems.at[i]) for i, pair in enumerate(pairs)], len(pairs))
    take()
    first = low_lanes(quarter, width)
    weights = twice_transposed(out_proj_ref[...])

    def pack_rows(g):
        wire_ref = leaving_ref.at[g] if g < 2 else own_ref.at[g - 2]
        for pair in range(top // 2):
            even = rows_ref[g % 2, pl.ds(2 * pair, quarter, stride=top), :]
            odd = rows_ref[g % 2, pl.ds(2 * pair + 1, quarter, stride=top), :]
            wire_ref[pair * quarter : (pair + 1) * quarter, :] = jnp.where(first, even, odd).astype(jnp.bfloat16)

    for g in range(len(OUTER_TURNS)):
        if g >= ready:
            take()
        hidden = near_ref[g] if g < ready else hidden_ref[g - ready]
        rows_ref[g % 2] = jnp.dot(hidden, weights, preferred_element_type=jnp.float32)
        if g:
            pack_rows(g - 1)
    pack_rows(len(OUTER_TURNS) - 1)


def project_outer(near_hidden, flat_hidden, out_projection, quarters, top):
    rows, hidden = flat_hidden.shape
    wire = jax.ShapeDtypeStruct((quarters // 2, rows // quarters // 2, LANES), jnp.bfloat16)
    return pl.pallas_call(
        functools.partial(outer_kernel, top=top),
        in_specs=[VMEM, HBM, HBM],
        out_specs=[VMEM] * 2,
        out_shape=[wire, wire],
        scratch_shapes=[
            pltpu.VMEM((quarters // 2, rows // quarters, hidden), jnp.bfloat16),
            pltpu.VMEM(out_projection.shape, out_projection.dtype),
            pltpu.VMEM((2, rows // quarters, LANES), jnp.float32),
            pltpu.SemaphoreType.DMA((quarters // 2 + 1,)),
        ],
        compiler_params=pltpu.CompilerParams(vmem_limit_bytes=40 * MIB),
        cost_estimate=cost(4),
    )(near_hidden, stay(flat_hidden), stay(out_projection))


def exact_rows(rows):
    half = rows.shape[0] // 2
    return rows[:half].astype(jnp.float32) + rows[half:].astype(jnp.float32)


def combine_inner_kernel(own_ref, near_ref, out_ref):
    high, low = split(exact_rows(own_ref[0]) + exact_rows(near_ref[1]))
    out_ref[: high.shape[0], :] = high
    out_ref[high.shape[0] :, :] = low


def combine_outer_kernel(own_ref, near_ref, out_ref):
    out_ref[...] = (own_ref[0].astype(jnp.float32) + near_ref[1].astype(jnp.float32)).astype(jnp.bfloat16)


def combine(kernel, own, near):
    return pl.pallas_call(
        kernel,
        in_specs=[VMEM, VMEM],
        out_shape=jax.ShapeDtypeStruct(own.shape[1:], jnp.bfloat16),
        compiler_params=pltpu.CompilerParams(vmem_limit_bytes=40 * MIB),
        cost_estimate=cost(0.5),
    )(own, near)


def finish_inner_kernel(own_ref, first_ref, second_ref, docs_ref, out_ref):
    total = exact_rows(own_ref[1]) + exact_rows(first_ref[0]) + exact_rows(second_ref[...])
    width = out_ref.shape[0] - DOC_ROWS
    total = jnp.concatenate([total[:, :width], total[:, width:]], axis=0)
    out_ref[:width, :] = jnp.transpose(total).astype(jnp.bfloat16)
    docs = docs_ref[pl.ds(lax.axis_index("proj"), 1), :].astype(jnp.float32)
    out_ref[width:, :] = jnp.broadcast_to(docs, (DOC_ROWS, LANES)).astype(jnp.bfloat16)


def finish_inner(own, first, second, doc_rows, width):
    return pl.pallas_call(
        finish_inner_kernel,
        in_specs=[VMEM] * 4,
        out_shape=jax.ShapeDtypeStruct((width + DOC_ROWS, own.shape[1]), jnp.bfloat16),
        compiler_params=pltpu.CompilerParams(vmem_limit_bytes=40 * MIB),
        cost_estimate=cost(0.5),
    )(own, first, second, doc_rows)


def expand_kernel(shared_ref, weights_ref, *, width, experts, shares, turns):
    half = experts // 2
    share_rows = width // shares
    columns = shares * half * share_rows
    lane = lax.broadcasted_iota(jnp.int32, (LANES, columns), 1)
    row = lax.broadcasted_iota(jnp.int32, (LANES, columns), 0)
    expert_lane = lax.broadcasted_iota(jnp.int32, (half * width, columns), 1) // share_rows % half
    expert_row = lax.broadcasted_iota(jnp.int32, (half * width, columns), 0) // width
    own = expert_lane == expert_row
    rows = half // 2 * width + DIAGONAL_ROWS
    factors = [
        unpack_factors(shared_ref[entry * rows : (entry + 1) * rows], width, half // 2) for entry in range(len(turns))
    ]
    for side in range(2):
        share = jnp.bitwise_xor(lane // (half * share_rows), side)
        source = share * share_rows + lane % share_rows
        spread = (row == source + side * width).astype(jnp.float32).astype(jnp.bfloat16)
        for entry, turn in enumerate(turns):
            placed = jnp.dot(factors[entry], spread, preferred_element_type=jnp.float32)
            weights_ref[turn // 2, side] = jnp.where(own, placed, 0.0).astype(jnp.bfloat16)


def expand(shared, turns, width, experts, shares):
    owners = len(turns)
    return pl.pallas_call(
        functools.partial(expand_kernel, width=width, experts=experts, shares=shares, turns=turns),
        in_specs=[VMEM],
        out_shape=jax.ShapeDtypeStruct((owners, 2, experts // 2 * width, experts // 2 * width), jnp.bfloat16),
        compiler_params=pltpu.CompilerParams(vmem_limit_bytes=40 * MIB),
        cost_estimate=cost(1),
    )(shared)


def condition_kernel(
    own_ref, near_ref, far_ref, routes_ref, even_ref, odd_ref, payload_ref, value_ref, name_ref, *, top, width
):
    quarter = routes_ref.shape[0]
    pairs, sides, dense_width, _ = even_ref.shape
    groups = 2 * pairs
    shares = payload_ref.shape[0] // groups
    experts = sides * dense_width // width
    first = low_lanes(quarter, width)
    second = 1 - first.astype(jnp.int32)

    def summed(start, size):
        rows = slice(start, start + size)
        total = own_ref[1, rows, :].astype(jnp.float32) + near_ref[0, rows, :].astype(jnp.float32)
        return total + far_ref[rows, :].astype(jnp.float32)

    for pair in range(top // 2):
        both = summed(pair * quarter, quarter)
        swapped = pltpu.roll(both, width, 1)
        value_ref[2 * pair] = jnp.where(first, both, swapped)
        value_ref[2 * pair + 1] = jnp.where(first, swapped, both)
    for k in range(top):
        name_ref[k] = jnp.broadcast_to(routes_ref[:, k : k + 1], (quarter, LANES)) - second

    def one_group(step, carry, parity):
        weights_ref = odd_ref if parity else even_ref
        group = jnp.bitwise_xor(lax.axis_index("expert"), 2 * step + parity)
        dense = []
        for pair in range(experts // 2):
            base = group * experts + 2 * pair
            chosen = jnp.zeros((quarter, LANES), jnp.float32)
            for k in range(top):
                chosen = jnp.where(name_ref[k] == base, value_ref[k], chosen)
            dense.append(chosen.astype(jnp.bfloat16))
        per_side = len(dense) // sides
        results = [
            jnp.dot(
                jnp.concatenate(dense[side * per_side : (side + 1) * per_side], axis=1),
                weights_ref[step, side],
                preferred_element_type=jnp.float32,
            )
            for side in range(sides)
        ]
        for share in range(shares):
            lanes = slice(share // 2 * LANES, (share // 2 + 1) * LANES)
            low, high = (results[side][:, lanes] for side in ((0, 1) if share % 2 == 0 else (1, 0)))
            place = listed(group, groups, groups // 2) * shares + share
            payload_ref[place] = jnp.where(first, low, high).astype(jnp.bfloat16)
        return carry

    for parity in range(2):
        lax.fori_loop(0, pairs, functools.partial(one_group, parity=parity), 0, unroll=pairs <= 2)


def condition(own, near, far, quarter_routes, even, odd, shares, width):
    quarter, top = quarter_routes.shape
    groups = 2 * even.shape[0]
    return pl.pallas_call(
        functools.partial(condition_kernel, top=top, width=width),
        in_specs=[VMEM] * 6,
        out_shape=jax.ShapeDtypeStruct((groups * shares, quarter, LANES), jnp.bfloat16),
        scratch_shapes=[
            pltpu.VMEM((top, quarter, LANES), jnp.float32),
            pltpu.VMEM((top, quarter, LANES), jnp.int32),
        ],
        compiler_params=pltpu.CompilerParams(vmem_limit_bytes=40 * MIB),
        cost_estimate=cost(2),
    )(own, near, far, quarter_routes, even, odd)


def query_kernel(query_ref, inverse_ref, out_hbm, factor_ref, spread_ref, wide_ref, out_ref, sems):
    count, experts, _ = query_ref.shape
    width = inverse_ref.shape[1]
    step = pl.program_id(0)
    rows = out_ref.shape[0] // width
    pitch = wide_ref.shape[1] // width

    @pl.when(step == 0)
    def _():
        zeros = jnp.zeros((width, width), jnp.bfloat16)
        for e in range(experts):
            high, low = split(inverse_ref[e])
            left = jnp.concatenate([high, zeros, low, zeros], axis=0)
            right = jnp.concatenate([zeros, high, zeros, low], axis=0)
            factor_ref[e] = jnp.concatenate([left, right], axis=1)

    spread_ref[...] = query_ref[...].astype(jnp.float32).reshape(count * experts, LANES)
    for e in range(experts):
        query = spread_ref[pl.ds(e, count, stride=experts), :].astype(jnp.bfloat16)
        result = lax.dot_general(
            factor_ref[e], query, (((1,), (1,)), ((), ())), preferred_element_type=jnp.float32
        )
        result = result[: 2 * width] + result[2 * width :]
        slot = (e + experts // 2 * (lax.axis_index("proj") % 2)) % experts
        start = slot * (rows // experts) + 2 * step
        for tile in range(wide_ref.shape[0]):
            part = result[:, tile * LANES : (tile + 1) * LANES]
            wide_ref[tile, pl.ds(start, width, stride=pitch), :] = part[:width]
            wide_ref[tile, pl.ds(start + 1, width, stride=pitch), :] = part[width:]

    @pl.when(step == pl.num_programs(0) - 1)
    def _():
        copies = []
        for part in range(sems.shape[0]):
            first = part * (width // sems.shape[0])
            for j in range(first, first + width // sems.shape[0]):
                for tile in range(wide_ref.shape[0]):
                    out_ref[j * rows : (j + 1) * rows, tile * LANES : (tile + 1) * LANES] = wide_ref[
                        tile, j * pitch : j * pitch + rows, :
                    ].astype(jnp.bfloat16)
            block = pl.ds(first * rows, width // sems.shape[0] * rows)
            copies.append(pltpu.make_async_copy(out_ref.at[block], out_hbm.at[block], sems.at[part]))
            copies[-1].start()
        for copy in copies:
            copy.wait()


def condition_queries(query_grads, inverse_in):
    count, experts, flat = query_grads.shape
    width = inverse_in.shape[1]
    rows = experts * flat
    return pl.pallas_call(
        query_kernel,
        grid=(flat // LANES,),
        in_specs=[
            pl.BlockSpec((count, experts, LANES), lambda c: (0, 0, c)),
            pl.BlockSpec(inverse_in.shape, lambda c: (0, 0, 0)),
        ],
        out_specs=HBM,
        out_shape=pltpu.HBM((rows, count), jnp.bfloat16),
        scratch_shapes=[
            pltpu.VMEM((experts, 4 * width, 2 * width), jnp.bfloat16),
            pltpu.VMEM((count * experts, LANES), jnp.float32),
            pltpu.VMEM((count // LANES, rows + 8 * width, LANES), jnp.float32),
            pltpu.VMEM((rows, count), jnp.bfloat16),
            pltpu.SemaphoreType.DMA((8,)),
        ],
        compiler_params=pltpu.CompilerParams(vmem_limit_bytes=40 * MIB),
        cost_estimate=cost(10),
    )(stay(query_grads), inverse_in)


def score_kernel(
    arrived_ref, inner_ref, far_ref, out_ref, grads_ref, queries_ref, sems, *, width, doc_count, turns
):
    parts = sems.shape[0]
    part_rows = queries_ref.shape[0] // parts
    fetches = []
    for part in range(parts):
        rows = pl.ds(part * part_rows, part_rows)
        fetches.append(pltpu.make_async_copy(far_ref.at[rows], queries_ref.at[rows], sems.at[part]))
        fetches[-1].start()
    sources, quarter, lanes = arrived_ref.shape
    shares = lax.axis_size("proj")
    owners = sources // shares
    outer, inner, docs = [], [], []
    for entry, (owner_turn, share_turn) in enumerate(turns):
        owner = jnp.bitwise_xor(lax.axis_index("expert"), owner_turn)
        share = jnp.bitwise_xor(lax.axis_index("proj"), share_turn)
        outer.append(arrived_ref[listed(owner, owners, owners // 2) * shares + share])
        docs.append(inner_ref[entry, width:, :].astype(jnp.float32).astype(jnp.int32))
        inner.append(inner_ref[entry, :width, :])
    outer = jnp.concatenate(outer, axis=0)
    inner = jnp.concatenate(inner, axis=1)
    docs = jnp.concatenate(docs, axis=1)
    odd = lax.dot_general(
        (docs & 1).astype(jnp.float32).astype(jnp.bfloat16),
        jnp.full((DOC_ROWS, lanes), 1 / DOC_ROWS, jnp.bfloat16),
        (((0,), (0,)), ((), ())),
        preferred_element_type=jnp.float32,
    ).astype(jnp.bfloat16)
    odd_outer = outer * odd
    outer = jnp.concatenate([outer - odd_outer, odd_outer], axis=1)
    pairs = jnp.broadcast_to(docs[:1] >> 1, inner.shape)
    pair_group = min(16, doc_count // 2)
    pitch = grads_ref.shape[0] // doc_count

    def one_group(group, carry):
        masked = [
            jnp.where(pairs == group * pair_group + p, inner, jnp.zeros_like(inner)) for p in range(pair_group)
        ]
        sums = jnp.dot(jnp.concatenate(masked, axis=0), outer, preferred_element_type=jnp.float32)
        for p in range(pair_group):
            for parity in range(2):
                start = pl.multiple_of((2 * (group * pair_group + p) + parity) * pitch, 8)
                grads_ref[pl.ds(start, width), :] = sums[
                    p * width : (p + 1) * width, parity * lanes : (parity + 1) * lanes
                ]
        return carry

    groups = doc_count // (2 * pair_group)
    lax.fori_loop(0, groups, one_group, 0, unroll=groups == 1)
    result = 0
    for part in range(parts):
        high, low = [], []
        for j in range(part * width // parts, (part + 1) * width // parts):
            pieces = split(grads_ref[pl.ds(j, doc_count, stride=pitch), :])
            high.append(pieces[0])
            low.append(pieces[1])
        flat = jnp.concatenate([jnp.concatenate(high, axis=1), jnp.concatenate(low, axis=1)], axis=0)
        fetches[part].wait()
        rows = slice(part * part_rows, (part + 1) * part_rows)
        result = result + jnp.dot(flat, queries_ref[rows, :], preferred_element_type=jnp.float32)
    result = result[:doc_count] + result[doc_count:]
    columns = result.shape[1] // shares
    fill = jnp.zeros((DOC_DEV, LANES - columns), jnp.float32)
    for owner in range(owners):
        for share in range(shares):
            piece = result[owner * DOC_DEV : (owner + 1) * DOC_DEV, share * columns : (share + 1) * columns]
            out_ref[listed(owner, owners, owners - 1) * shares + share] = jnp.concatenate([piece, fill], axis=1)


def score(arrived, inner, queries, turns, owners):
    sources = arrived.shape[0]
    width = inner.shape[1] - DOC_ROWS
    doc_count = DOC_DEV * owners
    return pl.pallas_call(
        functools.partial(score_kernel, width=width, doc_count=doc_count, turns=turns),
        in_specs=[VMEM, VMEM, HBM],
        out_shape=jax.ShapeDtypeStruct((sources, DOC_DEV, LANES), jnp.float32),
        scratch_shapes=[
            pltpu.VMEM((doc_count * (width + 8), arrived.shape[2]), jnp.float32),
            pltpu.VMEM(queries.shape, jnp.bfloat16),
            pltpu.SemaphoreType.DMA((8,)),
        ],
        compiler_params=pltpu.CompilerParams(vmem_limit_bytes=40 * MIB),
        cost_estimate=cost(5),
    )(arrived, inner, stay(queries))


def sum_kernel(pieces_ref, out_ref):
    total = pieces_ref[0]
    for source in range(1, pieces_ref.shape[0]):
        total = total + pieces_ref[source]
    out_ref[...] = total[:, : out_ref.shape[1]]


def sum_pieces(pieces, columns):
    return pl.pallas_call(
        sum_kernel,
        in_specs=[VMEM],
        out_shape=jax.ShapeDtypeStruct((pieces.shape[1], columns), jnp.float32),
        compiler_params=pltpu.CompilerParams(vmem_limit_bytes=40 * MIB),
    )(pieces)


def exchange(block, axis, size, turn):
    return lax.ppermute(block, axis, [(i, i ^ turn) for i in range(size)])


def double(blocks, turns, axis, size, turn):
    blocks = jnp.concatenate([blocks, exchange(blocks, axis, size, turn)], axis=0)
    return blocks, turns + tuple(t ^ turn for t in turns)


def local(
    activations,
    grad_hidden,
    routes,
    doc_ids,
    query_grads,
    in_projection,
    out_projection,
    inverse_in,
    inverse_out,
):
    tokens, top = routes.shape
    experts, width, _ = inverse_in.shape
    owners = lax.axis_size("expert")
    shares = lax.axis_size("proj")
    quarter = tokens // shares
    assert quarter == LANES and 2 * width == LANES and experts * width // shares == LANES
    assert experts % 4 == 0 and experts // 4 <= DIAGONAL_ROWS
    assert shares == 4 and owners & (owners - 1) == 0
    assert DOC_DEV * owners <= 256

    flat_hidden = grad_hidden.reshape(tokens * top, grad_hidden.shape[2])
    inner_leaving, inner_own, shared, near_hidden = project_inner(
        activations, in_projection, inverse_out, flat_hidden, shares
    )
    inner_first = exchange(inner_leaving, "proj", shares, 2)
    far_shared = exchange(shared, "expert", owners, owners // 2)
    leaving, own = project_outer(near_hidden, flat_hidden, out_projection, shares, top)
    far_shared, inner_first, leaving = lax.optimization_barrier((far_shared, inner_first, leaving))
    near = exchange(leaving, "proj", shares, 1)
    shared, turns = jnp.stack([shared, far_shared]), (0, owners // 2)
    for bit in reversed(range(1, (owners // 2).bit_length() - 1)):
        shared, turns = double(shared, turns, "expert", owners, 1 << bit)
    shared = shared.reshape(-1, LANES)
    even = expand(shared, turns, width, experts, shares)
    near, even = lax.optimization_barrier((near, even))
    inner_second = exchange(combine(combine_inner_kernel, inner_own, inner_first), "proj", shares, 1)
    sent = combine(combine_outer_kernel, own, near)
    far = exchange(sent, "proj", shares, 2)
    inner = finish_inner(inner_own, inner_first, inner_second, doc_ids.reshape(shares, quarter), width)
    packet = exchange(jnp.concatenate([shared, inner], axis=0), "expert", owners, 1)
    inner, _ = lax.optimization_barrier((inner, sent))
    owner_turns = (*range(2, owners), 1, 0)
    arriving = [exchange(inner, "expert", owners, turn) for turn in owner_turns if turn > 1]
    arriving.append(packet[shared.shape[0] :])
    odd = expand(packet, turns, width, experts, shares)
    far, odd = lax.optimization_barrier((far, odd))
    quarter_routes = lax.dynamic_slice_in_dim(routes, lax.axis_index("proj") * quarter, quarter, 0)
    payload = condition(own, near, far, quarter_routes, even, odd, shares, width)
    payload, arriving = lax.optimization_barrier((payload, arriving))
    arrived = send_to_all(payload, owners, shares, owners // 2)
    inner = jnp.stack(arriving + [inner])
    inner, share_turns = inner[None], (0,)
    inner, share_turns = double(inner, share_turns, "proj", shares, 1)
    inner, query_grads = lax.optimization_barrier((inner, query_grads))
    inner, share_turns = double(inner, share_turns, "proj", shares, 2)
    inner = inner.reshape(owners * shares, width + DOC_ROWS, quarter)
    all_turns = tuple((o, p) for p in share_turns for o in owner_turns)
    queries = condition_queries(query_grads, inverse_in)
    pieces = score(arrived, inner, queries, all_turns, owners)
    pieces = send_to_all(pieces, owners, shares, owners - 1)
    return sum_pieces(pieces, query_grads.shape[0] // shares).T


def solution(mesh):
    in_specs = (
        P(("groups", "expert"), "proj"),
        P(("groups", "expert"), None, "proj"),
        P(("groups", "expert"), None),
        P(("groups", "expert")),
        P(None, "expert", "proj"),
        P(None, "proj"),
        P(None, "proj"),
        P("expert", None, None),
        P("expert", None, None),
    )
    out_specs = P("proj", ("groups", "expert"))
    return jax.shard_map(local, mesh=mesh, in_specs=in_specs, out_specs=out_specs, check_vma=False)
```

```python
import functools

import jax
import jax.numpy as jnp
from jax import lax
from jax.experimental import pallas as pl
from jax.experimental.pallas import tpu as pltpu
from jax.sharding import PartitionSpec as P

DOC_DEV = 8
LANES = 128
DOC_ROWS = 16
DIAGONAL_ROWS = 16
QUERY_PARTS = 4
MIB = 1024 * 1024
VMEM = pl.BlockSpec(memory_space=pltpu.VMEM)
HBM = pl.BlockSpec(memory_space=pltpu.HBM)


def low_lanes(rows, width):
    return lax.broadcasted_iota(jnp.int32, (rows, LANES), 1) < width


def stay(array):
    return pltpu.with_memory_space_constraint(array, pltpu.HBM)


def listed(owner, owners, first):
    return (owner + owners - first) % owners


def send_to_all(blocks, owners, shares, first):
    members = [(i + first * shares) % (owners * shares) for i in range(owners * shares)]
    return lax.all_to_all(blocks, ("expert", "proj"), 0, 0, tiled=True, axis_index_groups=[members])


def split(value):
    high = value.astype(jnp.bfloat16)
    return high, (value - high.astype(jnp.float32)).astype(jnp.bfloat16)


def cost(microseconds):
    return pl.CostEstimate(flops=0, bytes_accessed=int(microseconds * 3.3e6), transcendentals=0)


def in_order(copies, ahead):
    for copy in copies[:ahead]:
        copy.start()
    state = [0]

    def take():
        copies[state[0]].wait()
        if state[0] + ahead < len(copies):
            copies[state[0] + ahead].start()
        state[0] += 1

    return take


def twice_transposed(projection):
    once = jnp.transpose(projection.astype(jnp.float32))
    return jnp.concatenate([once, once], axis=1).astype(jnp.bfloat16)


def triangles(width):
    row = lax.broadcasted_iota(jnp.int32, (width, LANES), 0)
    column = lax.broadcasted_iota(jnp.int32, (width, LANES), 1) % width
    return row, column


def pack_factors(inverse_ref, shared_ref):
    experts, width, _ = inverse_ref.shape
    quarter = experts // 4
    row, column = triangles(width)
    diagonals = []
    for e in range(quarter):
        lower, upper = (
            jnp.concatenate([inverse_ref[first], inverse_ref[first + 2 * quarter]], axis=1) for first in (e, e + quarter)
        )
        shared_ref[e * width : (e + 1) * width, :] = jnp.where(row >= column, lower, upper).astype(jnp.bfloat16)
        diagonals.append(jnp.sum(jnp.where(row == column, upper, 0.0), axis=0, keepdims=True))
    fill = jnp.zeros((DIAGONAL_ROWS - quarter, LANES), jnp.float32)
    shared_ref[quarter * width :, :] = jnp.concatenate(diagonals + [fill], axis=0).astype(jnp.bfloat16)


def unpack_factors(packed, width, quarter):
    row, column = triangles(width)
    packed = packed.astype(jnp.float32)
    lower, upper = [], []
    for e in range(quarter):
        square = packed[e * width : (e + 1) * width]
        turned = jnp.transpose(square)
        turned = jnp.concatenate([turned[:width], turned[width:]], axis=1)
        diagonal = packed[quarter * width + e : quarter * width + e + 1]
        lower.append(jnp.where(row >= column, square, turned))
        upper.append(jnp.where(row == column, diagonal, jnp.where(row < column, square, turned)))
    return jnp.concatenate(lower + upper, axis=0).astype(jnp.bfloat16)


OUTER_TURNS = (1, 3, 2, 0)


def quarter_rows(place, turn, rows):
    return pl.ds(pl.multiple_of(jnp.bitwise_xor(place, turn) * rows, rows), rows)


def inner_kernel(
    act_hbm,
    in_proj_hbm,
    inverse_hbm,
    hidden_hbm,
    leaving_ref,
    own_ref,
    shared_ref,
    hidden_ref,
    act_ref,
    in_proj_ref,
    inverse_ref,
    sems,
):
    turns = (2, 3, 1, 0)
    quarter = act_ref.shape[1]
    width = in_proj_ref.shape[0]
    half = quarter // 2
    place = lax.axis_index("proj")
    pairs = [(in_proj_hbm, in_proj_ref)]
    for g, turn in enumerate(turns):
        rows = pl.ds(pl.multiple_of(jnp.bitwise_xor(place, turn) * quarter, quarter), quarter)
        pairs.append((act_hbm.at[rows], act_ref.at[g]))
        if g == 0:
            pairs.append((inverse_hbm, inverse_ref))
    for g in range(hidden_ref.shape[0]):
        pairs.append((hidden_hbm.at[quarter_rows(place, OUTER_TURNS[g], hidden_ref.shape[1])], hidden_ref.at[g]))
    take = in_order([pltpu.make_async_copy(*pair, sems.at[i]) for i, pair in enumerate(pairs)], 4)
    take()
    first = low_lanes(half, width)
    weights = twice_transposed(in_proj_ref[...])
    for wire_ref in (leaving_ref, own_ref):
        take()
        if wire_ref is leaving_ref:
            take()
            pack_factors(inverse_ref, shared_ref)
        take()
        g = 0 if wire_ref is leaving_ref else 2
        rows = act_ref[g : g + 2].reshape(2 * quarter, act_ref.shape[2])
        inner = jnp.dot(rows, weights, preferred_element_type=jnp.float32)
        for i in range(2):
            start = i * quarter
            high, low = split(jnp.where(first, inner[start : start + half], inner[start + half : start + quarter]))
            wire_ref[i, :half, :] = high
            wire_ref[i, half:, :] = low
    for _ in range(hidden_ref.shape[0]):
        take()


def project_inner(activations, in_projection, inverse_out, flat_hidden, quarters):
    tokens, model = activations.shape
    quarter = tokens // quarters
    experts, width, _ = inverse_out.shape
    wire = jax.ShapeDtypeStruct((quarters // 2, quarter, LANES), jnp.bfloat16)
    fixed = (in_projection, inverse_out)
    return pl.pallas_call(
        inner_kernel,
        in_specs=[HBM] * 4,
        out_specs=[VMEM] * 4,
        out_shape=[
            wire,
            wire,
            jax.ShapeDtypeStruct((experts // 4 * width + DIAGONAL_ROWS, LANES), jnp.bfloat16),
            jax.ShapeDtypeStruct((quarters // 2, flat_hidden.shape[0] // quarters, flat_hidden.shape[1]), jnp.bfloat16),
        ],
        scratch_shapes=[pltpu.VMEM((quarters, quarter, model), jnp.bfloat16)]
        + [pltpu.VMEM(array.shape, array.dtype) for array in fixed]
        + [pltpu.SemaphoreType.DMA((quarters + len(fixed) + quarters // 2,))],
        compiler_params=pltpu.CompilerParams(vmem_limit_bytes=40 * MIB),
        cost_estimate=cost(2.5),
    )(*[stay(array) for array in (activations, *fixed, flat_hidden)])


def outer_kernel(near_ref, hidden_hbm, out_proj_hbm, leaving_ref, own_ref, hidden_ref, out_proj_ref, rows_ref, sems, *, top):
    ready, rows, _ = near_ref.shape
    quarter = rows // top
    width = out_proj_ref.shape[0]
    place = lax.axis_index("proj")
    pairs = [(out_proj_hbm, out_proj_ref)]
    for i, turn in enumerate(OUTER_TURNS[ready:]):
        pairs.append((hidden_hbm.at[quarter_rows(place, turn, rows)], hidden_ref.at[i]))
    take = in_order([pltpu.make_async_copy(*pair, sems.at[i]) for i, pair in enumerate(pairs)], len(pairs))
    take()
    first = low_lanes(quarter, width)
    weights = twice_transposed(out_proj_ref[...])

    def pack_rows(g):
        wire_ref = leaving_ref.at[g] if g < 2 else own_ref.at[g - 2]
        for pair in range(top // 2):
            even = rows_ref[g % 2, pl.ds(2 * pair, quarter, stride=top), :]
            odd = rows_ref[g % 2, pl.ds(2 * pair + 1, quarter, stride=top), :]
            wire_ref[pair * quarter : (pair + 1) * quarter, :] = jnp.where(first, even, odd).astype(jnp.bfloat16)

    for g in range(len(OUTER_TURNS)):
        if g >= ready:
            take()
        hidden = near_ref[g] if g < ready else hidden_ref[g - ready]
        rows_ref[g % 2] = jnp.dot(hidden, weights, preferred_element_type=jnp.float32)
        if g:
            pack_rows(g - 1)
    pack_rows(len(OUTER_TURNS) - 1)


def project_outer(near_hidden, flat_hidden, out_projection, quarters, top):
    rows, hidden = flat_hidden.shape
    wire = jax.ShapeDtypeStruct((quarters // 2, rows // quarters // 2, LANES), jnp.bfloat16)
    return pl.pallas_call(
        functools.partial(outer_kernel, top=top),
        in_specs=[VMEM, HBM, HBM],
        out_specs=[VMEM] * 2,
        out_shape=[wire, wire],
        scratch_shapes=[
            pltpu.VMEM((quarters // 2, rows // quarters, hidden), jnp.bfloat16),
            pltpu.VMEM(out_projection.shape, out_projection.dtype),
            pltpu.VMEM((2, rows // quarters, LANES), jnp.float32),
            pltpu.SemaphoreType.DMA((quarters // 2 + 1,)),
        ],
        compiler_params=pltpu.CompilerParams(vmem_limit_bytes=40 * MIB),
        cost_estimate=cost(4),
    )(near_hidden, stay(flat_hidden), stay(out_projection))


def exact_rows(rows):
    half = rows.shape[0] // 2
    return rows[:half].astype(jnp.float32) + rows[half:].astype(jnp.float32)


def combine_inner_kernel(own_ref, near_ref, out_ref):
    high, low = split(exact_rows(own_ref[0]) + exact_rows(near_ref[1]))
    out_ref[: high.shape[0], :] = high
    out_ref[high.shape[0] :, :] = low


def combine_outer_kernel(own_ref, near_ref, out_ref):
    out_ref[...] = (own_ref[0].astype(jnp.float32) + near_ref[1].astype(jnp.float32)).astype(jnp.bfloat16)


def combine(kernel, own, near):
    return pl.pallas_call(
        kernel,
        in_specs=[VMEM, VMEM],
        out_shape=jax.ShapeDtypeStruct(own.shape[1:], jnp.bfloat16),
        compiler_params=pltpu.CompilerParams(vmem_limit_bytes=40 * MIB),
        cost_estimate=cost(0.5),
    )(own, near)


def finish_inner_kernel(own_ref, first_ref, second_ref, docs_ref, out_ref):
    total = exact_rows(own_ref[1]) + exact_rows(first_ref[0]) + exact_rows(second_ref[...])
    width = out_ref.shape[0] - DOC_ROWS
    total = jnp.concatenate([total[:, :width], total[:, width:]], axis=0)
    out_ref[:width, :] = jnp.transpose(total).astype(jnp.bfloat16)
    docs = docs_ref[pl.ds(lax.axis_index("proj"), 1), :].astype(jnp.float32)
    out_ref[width:, :] = jnp.broadcast_to(docs, (DOC_ROWS, LANES)).astype(jnp.bfloat16)


def finish_inner(own, first, second, doc_rows, width):
    return pl.pallas_call(
        finish_inner_kernel,
        in_specs=[VMEM] * 4,
        out_shape=jax.ShapeDtypeStruct((width + DOC_ROWS, own.shape[1]), jnp.bfloat16),
        compiler_params=pltpu.CompilerParams(vmem_limit_bytes=40 * MIB),
        cost_estimate=cost(0.5),
    )(own, first, second, doc_rows)


def expand_kernel(shared_ref, weights_ref, *, width, experts, shares, turns):
    half = experts // 2
    share_rows = width // shares
    columns = shares * half * share_rows
    lane = lax.broadcasted_iota(jnp.int32, (LANES, columns), 1)
    row = lax.broadcasted_iota(jnp.int32, (LANES, columns), 0)
    expert_lane = lax.broadcasted_iota(jnp.int32, (half * width, columns), 1) // share_rows % half
    expert_row = lax.broadcasted_iota(jnp.int32, (half * width, columns), 0) // width
    own = expert_lane == expert_row
    rows = half // 2 * width + DIAGONAL_ROWS
    factors = [
        unpack_factors(shared_ref[entry * rows : (entry + 1) * rows], width, half // 2) for entry in range(len(turns))
    ]
    for side in range(2):
        share = jnp.bitwise_xor(lane // (half * share_rows), side)
        source = share * share_rows + lane % share_rows
        spread = (row == source + side * width).astype(jnp.float32).astype(jnp.bfloat16)
        for entry, turn in enumerate(turns):
            placed = jnp.dot(factors[entry], spread, preferred_element_type=jnp.float32)
            weights_ref[turn // 2, side] = jnp.where(own, placed, 0.0).astype(jnp.bfloat16)


def expand(shared, turns, width, experts, shares):
    owners = len(turns)
    return pl.pallas_call(
        functools.partial(expand_kernel, width=width, experts=experts, shares=shares, turns=turns),
        in_specs=[VMEM],
        out_shape=jax.ShapeDtypeStruct((owners, 2, experts // 2 * width, experts // 2 * width), jnp.bfloat16),
        compiler_params=pltpu.CompilerParams(vmem_limit_bytes=40 * MIB),
        cost_estimate=cost(1),
    )(shared)


def condition_kernel(
    own_ref, near_ref, far_ref, routes_ref, even_ref, odd_ref, payload_ref, value_ref, name_ref, *, top, width
):
    quarter = routes_ref.shape[0]
    pairs, sides, dense_width, _ = even_ref.shape
    groups = 2 * pairs
    shares = payload_ref.shape[0] // groups
    experts = sides * dense_width // width
    first = low_lanes(quarter, width)
    second = 1 - first.astype(jnp.int32)

    def summed(start, size):
        rows = slice(start, start + size)
        total = own_ref[1, rows, :].astype(jnp.float32) + near_ref[0, rows, :].astype(jnp.float32)
        return total + far_ref[rows, :].astype(jnp.float32)

    for pair in range(top // 2):
        both = summed(pair * quarter, quarter)
        swapped = pltpu.roll(both, width, 1)
        value_ref[2 * pair] = jnp.where(first, both, swapped)
        value_ref[2 * pair + 1] = jnp.where(first, swapped, both)
    for k in range(top):
        name_ref[k] = jnp.broadcast_to(routes_ref[:, k : k + 1], (quarter, LANES)) - second

    def one_group(step, carry, parity):
        weights_ref = odd_ref if parity else even_ref
        group = jnp.bitwise_xor(lax.axis_index("expert"), 2 * step + parity)
        dense = []
        for pair in range(experts // 2):
            base = group * experts + 2 * pair
            chosen = jnp.zeros((quarter, LANES), jnp.float32)
            for k in range(top):
                chosen = jnp.where(name_ref[k] == base, value_ref[k], chosen)
            dense.append(chosen.astype(jnp.bfloat16))
        per_side = len(dense) // sides
        results = [
            jnp.dot(
                jnp.concatenate(dense[side * per_side : (side + 1) * per_side], axis=1),
                weights_ref[step, side],
                preferred_element_type=jnp.float32,
            )
            for side in range(sides)
        ]
        for share in range(shares):
            lanes = slice(share // 2 * LANES, (share // 2 + 1) * LANES)
            low, high = (results[side][:, lanes] for side in ((0, 1) if share % 2 == 0 else (1, 0)))
            place = listed(group, groups, groups // 2) * shares + share
            payload_ref[place] = jnp.where(first, low, high).astype(jnp.bfloat16)
        return carry

    for parity in range(2):
        lax.fori_loop(0, pairs, functools.partial(one_group, parity=parity), 0, unroll=pairs <= 2)


def condition(own, near, far, quarter_routes, even, odd, shares, width):
    quarter, top = quarter_routes.shape
    groups = 2 * even.shape[0]
    return pl.pallas_call(
        functools.partial(condition_kernel, top=top, width=width),
        in_specs=[VMEM] * 6,
        out_shape=jax.ShapeDtypeStruct((groups * shares, quarter, LANES), jnp.bfloat16),
        scratch_shapes=[
            pltpu.VMEM((top, quarter, LANES), jnp.float32),
            pltpu.VMEM((top, quarter, LANES), jnp.int32),
        ],
        compiler_params=pltpu.CompilerParams(vmem_limit_bytes=40 * MIB),
        cost_estimate=cost(2),
    )(own, near, far, quarter_routes, even, odd)


def query_kernel(*refs):
    *query_refs, inverse_ref, out_hbm, factor_ref, spread_ref, wide_ref, out_ref, sems = refs
    part_count, experts, _ = query_refs[0].shape
    count = part_count * len(query_refs)
    width = inverse_ref.shape[1]
    step = pl.program_id(0)
    rows = out_ref.shape[0] // width
    pitch = wide_ref.shape[1] // width

    @pl.when(step == 0)
    def _():
        zeros = jnp.zeros((width, width), jnp.bfloat16)
        for e in range(experts):
            high, low = split(inverse_ref[e])
            left = jnp.concatenate([high, zeros, low, zeros], axis=0)
            right = jnp.concatenate([zeros, high, zeros, low], axis=0)
            factor_ref[e] = jnp.concatenate([left, right], axis=1)

    part_rows = part_count * experts
    for r, query_ref in enumerate(query_refs):
        spread_ref[r * part_rows : (r + 1) * part_rows, :] = (
            query_ref[...].astype(jnp.float32).reshape(part_rows, LANES)
        )
    for e in range(experts):
        query = spread_ref[pl.ds(e, count, stride=experts), :].astype(jnp.bfloat16)
        result = lax.dot_general(
            factor_ref[e], query, (((1,), (1,)), ((), ())), preferred_element_type=jnp.float32
        )
        result = result[: 2 * width] + result[2 * width :]
        slot = (e + experts // 2 * (lax.axis_index("proj") % 2)) % experts
        start = slot * (rows // experts) + 2 * step
        for tile in range(wide_ref.shape[0]):
            part = result[:, tile * LANES : (tile + 1) * LANES]
            wide_ref[tile, pl.ds(start, width, stride=pitch), :] = part[:width]
            wide_ref[tile, pl.ds(start + 1, width, stride=pitch), :] = part[width:]

    @pl.when(step == pl.num_programs(0) - 1)
    def _():
        copies = []
        for part in range(sems.shape[0]):
            first = part * (width // sems.shape[0])
            for j in range(first, first + width // sems.shape[0]):
                for tile in range(wide_ref.shape[0]):
                    out_ref[j * rows : (j + 1) * rows, tile * LANES : (tile + 1) * LANES] = wide_ref[
                        tile, j * pitch : j * pitch + rows, :
                    ].astype(jnp.bfloat16)
            block = pl.ds(first * rows, width // sems.shape[0] * rows)
            copies.append(pltpu.make_async_copy(out_ref.at[block], out_hbm.at[block], sems.at[part]))
            copies[-1].start()
        for copy in copies:
            copy.wait()


def condition_queries(query_grads, inverse_in):
    count, experts, flat = query_grads.shape
    width = inverse_in.shape[1]
    rows = experts * flat
    return pl.pallas_call(
        query_kernel,
        grid=(flat // LANES,),
        in_specs=[
            pl.BlockSpec((count // QUERY_PARTS, experts, LANES), functools.partial(lambda r, c: (r, 0, c), r))
            for r in range(QUERY_PARTS)
        ]
        + [pl.BlockSpec(inverse_in.shape, lambda c: (0, 0, 0))],
        out_specs=HBM,
        out_shape=pltpu.HBM((rows, count), jnp.bfloat16),
        scratch_shapes=[
            pltpu.VMEM((experts, 4 * width, 2 * width), jnp.bfloat16),
            pltpu.VMEM((count * experts, LANES), jnp.float32),
            pltpu.VMEM((count // LANES, rows + 8 * width, LANES), jnp.float32),
            pltpu.VMEM((rows, count), jnp.bfloat16),
            pltpu.SemaphoreType.DMA((8,)),
        ],
        compiler_params=pltpu.CompilerParams(vmem_limit_bytes=40 * MIB),
        cost_estimate=cost(10),
    )(*[stay(query_grads)] * QUERY_PARTS, inverse_in)


def score_kernel(
    arrived_ref, inner_ref, far_ref, out_ref, grads_ref, queries_ref, sems, *, width, doc_count, turns
):
    parts = sems.shape[0]
    part_rows = queries_ref.shape[0] // parts
    fetches = []
    for part in range(parts):
        rows = pl.ds(part * part_rows, part_rows)
        fetches.append(pltpu.make_async_copy(far_ref.at[rows], queries_ref.at[rows], sems.at[part]))
        fetches[-1].start()
    sources, quarter, lanes = arrived_ref.shape
    shares = lax.axis_size("proj")
    owners = sources // shares
    outer, inner, docs = [], [], []
    for entry, (owner_turn, share_turn) in enumerate(turns):
        owner = jnp.bitwise_xor(lax.axis_index("expert"), owner_turn)
        share = jnp.bitwise_xor(lax.axis_index("proj"), share_turn)
        outer.append(arrived_ref[listed(owner, owners, owners // 2) * shares + share])
        docs.append(inner_ref[entry, width:, :].astype(jnp.float32).astype(jnp.int32))
        inner.append(inner_ref[entry, :width, :])
    outer = jnp.concatenate(outer, axis=0)
    inner = jnp.concatenate(inner, axis=1)
    docs = jnp.concatenate(docs, axis=1)
    odd = lax.dot_general(
        (docs & 1).astype(jnp.float32).astype(jnp.bfloat16),
        jnp.full((DOC_ROWS, lanes), 1 / DOC_ROWS, jnp.bfloat16),
        (((0,), (0,)), ((), ())),
        preferred_element_type=jnp.float32,
    ).astype(jnp.bfloat16)
    odd_outer = outer * odd
    outer = jnp.concatenate([outer - odd_outer, odd_outer], axis=1)
    pairs = jnp.broadcast_to(docs[:1] >> 1, inner.shape)
    pair_group = min(16, doc_count // 2)
    pitch = grads_ref.shape[0] // doc_count

    def one_group(group, carry):
        masked = [
            jnp.where(pairs == group * pair_group + p, inner, jnp.zeros_like(inner)) for p in range(pair_group)
        ]
        sums = jnp.dot(jnp.concatenate(masked, axis=0), outer, preferred_element_type=jnp.float32)
        for p in range(pair_group):
            for parity in range(2):
                start = pl.multiple_of((2 * (group * pair_group + p) + parity) * pitch, 8)
                grads_ref[pl.ds(start, width), :] = sums[
                    p * width : (p + 1) * width, parity * lanes : (parity + 1) * lanes
                ]
        return carry

    groups = doc_count // (2 * pair_group)
    lax.fori_loop(0, groups, one_group, 0, unroll=groups == 1)
    result = 0
    for part in range(parts):
        high, low = [], []
        for j in range(part * width // parts, (part + 1) * width // parts):
            pieces = split(grads_ref[pl.ds(j, doc_count, stride=pitch), :])
            high.append(pieces[0])
            low.append(pieces[1])
        flat = jnp.concatenate([jnp.concatenate(high, axis=1), jnp.concatenate(low, axis=1)], axis=0)
        fetches[part].wait()
        rows = slice(part * part_rows, (part + 1) * part_rows)
        result = result + jnp.dot(flat, queries_ref[rows, :], preferred_element_type=jnp.float32)
    result = result[:doc_count] + result[doc_count:]
    columns = result.shape[1] // shares
    fill = jnp.zeros((DOC_DEV, LANES - columns), jnp.float32)
    for owner in range(owners):
        for share in range(shares):
            piece = result[owner * DOC_DEV : (owner + 1) * DOC_DEV, share * columns : (share + 1) * columns]
            out_ref[listed(owner, owners, owners - 1) * shares + share] = jnp.concatenate([piece, fill], axis=1)


def score(arrived, inner, queries, turns, owners):
    sources = arrived.shape[0]
    width = inner.shape[1] - DOC_ROWS
    doc_count = DOC_DEV * owners
    return pl.pallas_call(
        functools.partial(score_kernel, width=width, doc_count=doc_count, turns=turns),
        in_specs=[VMEM, VMEM, HBM],
        out_shape=jax.ShapeDtypeStruct((sources, DOC_DEV, LANES), jnp.float32),
        scratch_shapes=[
            pltpu.VMEM((doc_count * (width + 8), arrived.shape[2]), jnp.float32),
            pltpu.VMEM(queries.shape, jnp.bfloat16),
            pltpu.SemaphoreType.DMA((8,)),
        ],
        compiler_params=pltpu.CompilerParams(vmem_limit_bytes=40 * MIB),
        cost_estimate=cost(5),
    )(arrived, inner, stay(queries))


def sum_kernel(pieces_ref, out_ref):
    total = pieces_ref[0]
    for source in range(1, pieces_ref.shape[0]):
        total = total + pieces_ref[source]
    out_ref[...] = total[:, : out_ref.shape[1]]


def sum_pieces(pieces, columns):
    return pl.pallas_call(
        sum_kernel,
        in_specs=[VMEM],
        out_shape=jax.ShapeDtypeStruct((pieces.shape[1], columns), jnp.float32),
        compiler_params=pltpu.CompilerParams(vmem_limit_bytes=40 * MIB),
    )(pieces)


def exchange(block, axis, size, turn):
    return lax.ppermute(block, axis, [(i, i ^ turn) for i in range(size)])


def double(blocks, turns, axis, size, turn):
    blocks = jnp.concatenate([blocks, exchange(blocks, axis, size, turn)], axis=0)
    return blocks, turns + tuple(t ^ turn for t in turns)


def local(
    activations,
    grad_hidden,
    routes,
    doc_ids,
    query_grads,
    in_projection,
    out_projection,
    inverse_in,
    inverse_out,
):
    tokens, top = routes.shape
    experts, width, _ = inverse_in.shape
    owners = lax.axis_size("expert")
    shares = lax.axis_size("proj")
    quarter = tokens // shares
    assert quarter == LANES and 2 * width == LANES and experts * width // shares == LANES
    assert experts % 4 == 0 and experts // 4 <= DIAGONAL_ROWS
    assert shares == 4 and owners & (owners - 1) == 0
    assert DOC_DEV * owners <= 256

    flat_hidden = grad_hidden.reshape(tokens * top, grad_hidden.shape[2])
    inner_leaving, inner_own, shared, near_hidden = project_inner(
        activations, in_projection, inverse_out, flat_hidden, shares
    )
    inner_first = exchange(inner_leaving, "proj", shares, 2)
    far_shared = exchange(shared, "expert", owners, owners // 2)
    leaving, own = project_outer(near_hidden, flat_hidden, out_projection, shares, top)
    far_shared, inner_first, leaving = lax.optimization_barrier((far_shared, inner_first, leaving))
    near = exchange(leaving, "proj", shares, 1)
    shared, turns = jnp.stack([shared, far_shared]), (0, owners // 2)
    for bit in reversed(range(1, (owners // 2).bit_length() - 1)):
        shared, turns = double(shared, turns, "expert", owners, 1 << bit)
    shared = shared.reshape(-1, LANES)
    even = expand(shared, turns, width, experts, shares)
    near, even = lax.optimization_barrier((near, even))
    inner_second = exchange(combine(combine_inner_kernel, inner_own, inner_first), "proj", shares, 1)
    sent = combine(combine_outer_kernel, own, near)
    far = exchange(sent, "proj", shares, 2)
    inner = finish_inner(inner_own, inner_first, inner_second, doc_ids.reshape(shares, quarter), width)
    packet = exchange(jnp.concatenate([shared, inner], axis=0), "expert", owners, 1)
    inner, _ = lax.optimization_barrier((inner, sent))
    owner_turns = (*range(2, owners), 1, 0)
    arriving = [exchange(inner, "expert", owners, turn) for turn in owner_turns if turn > 1]
    arriving.append(packet[shared.shape[0] :])
    odd = expand(packet, turns, width, experts, shares)
    far, odd = lax.optimization_barrier((far, odd))
    quarter_routes = lax.dynamic_slice_in_dim(routes, lax.axis_index("proj") * quarter, quarter, 0)
    payload = condition(own, near, far, quarter_routes, even, odd, shares, width)
    payload, arriving = lax.optimization_barrier((payload, arriving))
    arrived = send_to_all(payload, owners, shares, owners // 2)
    inner = jnp.stack(arriving + [inner])
    inner, share_turns = inner[None], (0,)
    inner, share_turns = double(inner, share_turns, "proj", shares, 1)
    inner, query_grads = lax.optimization_barrier((inner, query_grads))
    inner, share_turns = double(inner, share_turns, "proj", shares, 2)
    inner = inner.reshape(owners * shares, width + DOC_ROWS, quarter)
    all_turns = tuple((o, p) for p in share_turns for o in owner_turns)
    queries = condition_queries(query_grads, inverse_in)
    pieces = score(arrived, inner, queries, all_turns, owners)
    pieces = send_to_all(pieces, owners, shares, owners - 1)
    return sum_pieces(pieces, query_grads.shape[0] // shares).T


def solution(mesh):
    in_specs = (
        P(("groups", "expert"), "proj"),
        P(("groups", "expert"), None, "proj"),
        P(("groups", "expert"), None),
        P(("groups", "expert")),
        P(None, "expert", "proj"),
        P(None, "proj"),
        P(None, "proj"),
        P("expert", None, None),
        P("expert", None, None),
    )
    out_specs = P("proj", ("groups", "expert"))
    return jax.shard_map(local, mesh=mesh, in_specs=in_specs, out_specs=out_specs, check_vma=False)
```

```python
import functools

import jax
import jax.numpy as jnp
from jax import lax
from jax.experimental import pallas as pl
from jax.experimental.pallas import tpu as pltpu
from jax.sharding import PartitionSpec as P

DOC_DEV = 8
LANES = 128
DOC_ROWS = 16
DIAGONAL_ROWS = 16
QUERY_PARTS = 1
MIB = 1024 * 1024
VMEM = pl.BlockSpec(memory_space=pltpu.VMEM)
HBM = pl.BlockSpec(memory_space=pltpu.HBM)


def low_lanes(rows, width):
    return lax.broadcasted_iota(jnp.int32, (rows, LANES), 1) < width


def stay(array):
    return pltpu.with_memory_space_constraint(array, pltpu.HBM)


def listed(owner, owners, first):
    return (owner + owners - first) % owners


def send_to_all(blocks, owners, shares, first):
    members = [(i + first * shares) % (owners * shares) for i in range(owners * shares)]
    return lax.all_to_all(blocks, ("expert", "proj"), 0, 0, tiled=True, axis_index_groups=[members])


def split(value):
    high = value.astype(jnp.bfloat16)
    return high, (value - high.astype(jnp.float32)).astype(jnp.bfloat16)


def cost(microseconds):
    return pl.CostEstimate(flops=0, bytes_accessed=int(microseconds * 3.3e6), transcendentals=0)


def in_order(copies, ahead):
    for copy in copies[:ahead]:
        copy.start()
    state = [0]

    def take():
        copies[state[0]].wait()
        if state[0] + ahead < len(copies):
            copies[state[0] + ahead].start()
        state[0] += 1

    return take


def twice_transposed(projection):
    once = jnp.transpose(projection.astype(jnp.float32))
    return jnp.concatenate([once, once], axis=1).astype(jnp.bfloat16)


def triangles(width):
    row = lax.broadcasted_iota(jnp.int32, (width, LANES), 0)
    column = lax.broadcasted_iota(jnp.int32, (width, LANES), 1) % width
    return row, column


def pack_factors(inverse_ref, shared_ref):
    experts, width, _ = inverse_ref.shape
    quarter = experts // 4
    row, column = triangles(width)
    diagonals = []
    for e in range(quarter):
        lower, upper = (
            jnp.concatenate([inverse_ref[first], inverse_ref[first + 2 * quarter]], axis=1) for first in (e, e + quarter)
        )
        shared_ref[e * width : (e + 1) * width, :] = jnp.where(row >= column, lower, upper).astype(jnp.bfloat16)
        diagonals.append(jnp.sum(jnp.where(row == column, upper, 0.0), axis=0, keepdims=True))
    fill = jnp.zeros((DIAGONAL_ROWS - quarter, LANES), jnp.float32)
    shared_ref[quarter * width :, :] = jnp.concatenate(diagonals + [fill], axis=0).astype(jnp.bfloat16)


def unpack_factors(packed, width, quarter):
    row, column = triangles(width)
    packed = packed.astype(jnp.float32)
    lower, upper = [], []
    for e in range(quarter):
        square = packed[e * width : (e + 1) * width]
        turned = jnp.transpose(square)
        turned = jnp.concatenate([turned[:width], turned[width:]], axis=1)
        diagonal = packed[quarter * width + e : quarter * width + e + 1]
        lower.append(jnp.where(row >= column, square, turned))
        upper.append(jnp.where(row == column, diagonal, jnp.where(row < column, square, turned)))
    return jnp.concatenate(lower + upper, axis=0).astype(jnp.bfloat16)


OUTER_TURNS = (1, 3, 2, 0)


def quarter_rows(place, turn, rows):
    return pl.ds(pl.multiple_of(jnp.bitwise_xor(place, turn) * rows, rows), rows)


def inner_kernel(
    act_hbm,
    in_proj_hbm,
    inverse_hbm,
    hidden_hbm,
    leaving_ref,
    own_ref,
    shared_ref,
    hidden_ref,
    act_ref,
    in_proj_ref,
    inverse_ref,
    sems,
):
    turns = (2, 3, 1, 0)
    quarter = act_ref.shape[1]
    width = in_proj_ref.shape[0]
    half = quarter // 2
    place = lax.axis_index("proj")
    pairs = [(in_proj_hbm, in_proj_ref)]
    for g, turn in enumerate(turns):
        rows = pl.ds(pl.multiple_of(jnp.bitwise_xor(place, turn) * quarter, quarter), quarter)
        pairs.append((act_hbm.at[rows], act_ref.at[g]))
        if g == 0:
            pairs.append((inverse_hbm, inverse_ref))
    for g in range(hidden_ref.shape[0]):
        pairs.append((hidden_hbm.at[quarter_rows(place, OUTER_TURNS[g], hidden_ref.shape[1])], hidden_ref.at[g]))
    take = in_order([pltpu.make_async_copy(*pair, sems.at[i]) for i, pair in enumerate(pairs)], 4)
    take()
    first = low_lanes(half, width)
    weights = twice_transposed(in_proj_ref[...])
    for wire_ref in (leaving_ref, own_ref):
        take()
        if wire_ref is leaving_ref:
            take()
            pack_factors(inverse_ref, shared_ref)
        take()
        g = 0 if wire_ref is leaving_ref else 2
        rows = act_ref[g : g + 2].reshape(2 * quarter, act_ref.shape[2])
        inner = jnp.dot(rows, weights, preferred_element_type=jnp.float32)
        for i in range(2):
            start = i * quarter
            high, low = split(jnp.where(first, inner[start : start + half], inner[start + half : start + quarter]))
            wire_ref[i, :half, :] = high
            wire_ref[i, half:, :] = low
    for _ in range(hidden_ref.shape[0]):
        take()


def project_inner(activations, in_projection, inverse_out, flat_hidden, quarters):
    tokens, model = activations.shape
    quarter = tokens // quarters
    experts, width, _ = inverse_out.shape
    wire = jax.ShapeDtypeStruct((quarters // 2, quarter, LANES), jnp.bfloat16)
    fixed = (in_projection, inverse_out)
    return pl.pallas_call(
        inner_kernel,
        in_specs=[HBM] * 4,
        out_specs=[VMEM] * 4,
        out_shape=[
            wire,
            wire,
            jax.ShapeDtypeStruct((experts // 4 * width + DIAGONAL_ROWS, LANES), jnp.bfloat16),
            jax.ShapeDtypeStruct((quarters // 2, flat_hidden.shape[0] // quarters, flat_hidden.shape[1]), jnp.bfloat16),
        ],
        scratch_shapes=[pltpu.VMEM((quarters, quarter, model), jnp.bfloat16)]
        + [pltpu.VMEM(array.shape, array.dtype) for array in fixed]
        + [pltpu.SemaphoreType.DMA((quarters + len(fixed) + quarters // 2,))],
        compiler_params=pltpu.CompilerParams(vmem_limit_bytes=40 * MIB),
        cost_estimate=cost(2.5),
    )(*[stay(array) for array in (activations, *fixed, flat_hidden)])


def outer_kernel(near_ref, hidden_hbm, out_proj_hbm, leaving_ref, own_ref, hidden_ref, out_proj_ref, rows_ref, sems, *, top):
    ready, rows, _ = near_ref.shape
    quarter = rows // top
    width = out_proj_ref.shape[0]
    place = lax.axis_index("proj")
    pairs = [(out_proj_hbm, out_proj_ref)]
    for i, turn in enumerate(OUTER_TURNS[ready:]):
        pairs.append((hidden_hbm.at[quarter_rows(place, turn, rows)], hidden_ref.at[i]))
    take = in_order([pltpu.make_async_copy(*pair, sems.at[i]) for i, pair in enumerate(pairs)], len(pairs))
    take()
    first = low_lanes(quarter, width)
    weights = twice_transposed(out_proj_ref[...])

    def pack_rows(g):
        wire_ref = leaving_ref.at[g] if g < 2 else own_ref.at[g - 2]
        for pair in range(top // 2):
            even = rows_ref[g % 2, pl.ds(2 * pair, quarter, stride=top), :]
            odd = rows_ref[g % 2, pl.ds(2 * pair + 1, quarter, stride=top), :]
            wire_ref[pair * quarter : (pair + 1) * quarter, :] = jnp.where(first, even, odd).astype(jnp.bfloat16)

    for g in range(len(OUTER_TURNS)):
        if g >= ready:
            take()
        hidden = near_ref[g] if g < ready else hidden_ref[g - ready]
        rows_ref[g % 2] = jnp.dot(hidden, weights, preferred_element_type=jnp.float32)
        if g:
            pack_rows(g - 1)
    pack_rows(len(OUTER_TURNS) - 1)


def project_outer(near_hidden, flat_hidden, out_projection, quarters, top):
    rows, hidden = flat_hidden.shape
    wire = jax.ShapeDtypeStruct((quarters // 2, rows // quarters // 2, LANES), jnp.bfloat16)
    return pl.pallas_call(
        functools.partial(outer_kernel, top=top),
        in_specs=[VMEM, HBM, HBM],
        out_specs=[VMEM] * 2,
        out_shape=[wire, wire],
        scratch_shapes=[
            pltpu.VMEM((quarters // 2, rows // quarters, hidden), jnp.bfloat16),
            pltpu.VMEM(out_projection.shape, out_projection.dtype),
            pltpu.VMEM((2, rows // quarters, LANES), jnp.float32),
            pltpu.SemaphoreType.DMA((quarters // 2 + 1,)),
        ],
        compiler_params=pltpu.CompilerParams(vmem_limit_bytes=40 * MIB),
        cost_estimate=cost(4),
    )(near_hidden, stay(flat_hidden), stay(out_projection))


def exact_rows(rows):
    half = rows.shape[0] // 2
    return rows[:half].astype(jnp.float32) + rows[half:].astype(jnp.float32)


def combine_inner_kernel(own_ref, near_ref, out_ref):
    high, low = split(exact_rows(own_ref[0]) + exact_rows(near_ref[1]))
    out_ref[: high.shape[0], :] = high
    out_ref[high.shape[0] :, :] = low


def combine_outer_kernel(own_ref, near_ref, out_ref):
    out_ref[...] = (own_ref[0].astype(jnp.float32) + near_ref[1].astype(jnp.float32)).astype(jnp.bfloat16)


def combine(kernel, own, near):
    return pl.pallas_call(
        kernel,
        in_specs=[VMEM, VMEM],
        out_shape=jax.ShapeDtypeStruct(own.shape[1:], jnp.bfloat16),
        compiler_params=pltpu.CompilerParams(vmem_limit_bytes=40 * MIB),
        cost_estimate=cost(0.5),
    )(own, near)


def finish_inner_kernel(own_ref, first_ref, second_ref, docs_ref, out_ref):
    total = exact_rows(own_ref[1]) + exact_rows(first_ref[0]) + exact_rows(second_ref[...])
    width = out_ref.shape[0] - DOC_ROWS
    total = jnp.concatenate([total[:, :width], total[:, width:]], axis=0)
    out_ref[:width, :] = jnp.transpose(total).astype(jnp.bfloat16)
    docs = docs_ref[pl.ds(lax.axis_index("proj"), 1), :].astype(jnp.float32)
    out_ref[width:, :] = jnp.broadcast_to(docs, (DOC_ROWS, LANES)).astype(jnp.bfloat16)


def finish_inner(own, first, second, doc_rows, width):
    return pl.pallas_call(
        finish_inner_kernel,
        in_specs=[VMEM] * 4,
        out_shape=jax.ShapeDtypeStruct((width + DOC_ROWS, own.shape[1]), jnp.bfloat16),
        compiler_params=pltpu.CompilerParams(vmem_limit_bytes=40 * MIB),
        cost_estimate=cost(0.5),
    )(own, first, second, doc_rows)


def expand_kernel(shared_ref, weights_ref, *, width, experts, shares, turns):
    half = experts // 2
    share_rows = width // shares
    columns = shares * half * share_rows
    lane = lax.broadcasted_iota(jnp.int32, (LANES, columns), 1)
    row = lax.broadcasted_iota(jnp.int32, (LANES, columns), 0)
    expert_lane = lax.broadcasted_iota(jnp.int32, (half * width, columns), 1) // share_rows % half
    expert_row = lax.broadcasted_iota(jnp.int32, (half * width, columns), 0) // width
    own = expert_lane == expert_row
    rows = half // 2 * width + DIAGONAL_ROWS
    factors = [
        unpack_factors(shared_ref[entry * rows : (entry + 1) * rows], width, half // 2) for entry in range(len(turns))
    ]
    for side in range(2):
        share = jnp.bitwise_xor(lane // (half * share_rows), side)
        source = share * share_rows + lane % share_rows
        spread = (row == source + side * width).astype(jnp.float32).astype(jnp.bfloat16)
        for entry, turn in enumerate(turns):
            placed = jnp.dot(factors[entry], spread, preferred_element_type=jnp.float32)
            weights_ref[turn // 2, side] = jnp.where(own, placed, 0.0).astype(jnp.bfloat16)


def expand(shared, turns, width, experts, shares):
    owners = len(turns)
    return pl.pallas_call(
        functools.partial(expand_kernel, width=width, experts=experts, shares=shares, turns=turns),
        in_specs=[VMEM],
        out_shape=jax.ShapeDtypeStruct((owners, 2, experts // 2 * width, experts // 2 * width), jnp.bfloat16),
        compiler_params=pltpu.CompilerParams(vmem_limit_bytes=40 * MIB),
        cost_estimate=cost(1),
    )(shared)


def condition_kernel(
    own_ref, near_ref, far_ref, routes_ref, even_ref, odd_ref, payload_ref, value_ref, name_ref, *, top, width
):
    quarter = routes_ref.shape[0]
    pairs, sides, dense_width, _ = even_ref.shape
    groups = 2 * pairs
    shares = payload_ref.shape[0] // groups
    experts = sides * dense_width // width
    first = low_lanes(quarter, width)
    second = 1 - first.astype(jnp.int32)

    def summed(start, size):
        rows = slice(start, start + size)
        total = own_ref[1, rows, :].astype(jnp.float32) + near_ref[0, rows, :].astype(jnp.float32)
        return total + far_ref[rows, :].astype(jnp.float32)

    for pair in range(top // 2):
        both = summed(pair * quarter, quarter)
        swapped = pltpu.roll(both, width, 1)
        value_ref[2 * pair] = jnp.where(first, both, swapped)
        value_ref[2 * pair + 1] = jnp.where(first, swapped, both)
    for k in range(top):
        name_ref[k] = jnp.broadcast_to(routes_ref[:, k : k + 1], (quarter, LANES)) - second

    def one_group(step, carry, parity):
        weights_ref = odd_ref if parity else even_ref
        group = jnp.bitwise_xor(lax.axis_index("expert"), 2 * step + parity)
        dense = []
        for pair in range(experts // 2):
            base = group * experts + 2 * pair
            chosen = jnp.zeros((quarter, LANES), jnp.float32)
            for k in range(top):
                chosen = jnp.where(name_ref[k] == base, value_ref[k], chosen)
            dense.append(chosen.astype(jnp.bfloat16))
        per_side = len(dense) // sides
        results = [
            jnp.dot(
                jnp.concatenate(dense[side * per_side : (side + 1) * per_side], axis=1),
                weights_ref[step, side],
                preferred_element_type=jnp.float32,
            )
            for side in range(sides)
        ]
        for share in range(shares):
            lanes = slice(share // 2 * LANES, (share // 2 + 1) * LANES)
            low, high = (results[side][:, lanes] for side in ((0, 1) if share % 2 == 0 else (1, 0)))
            place = listed(group, groups, groups // 2) * shares + share
            payload_ref[place] = jnp.where(first, low, high).astype(jnp.bfloat16)
        return carry

    for parity in range(2):
        lax.fori_loop(0, pairs, functools.partial(one_group, parity=parity), 0, unroll=pairs <= 2)


def condition(own, near, far, quarter_routes, even, odd, shares, width):
    quarter, top = quarter_routes.shape
    groups = 2 * even.shape[0]
    return pl.pallas_call(
        functools.partial(condition_kernel, top=top, width=width),
        in_specs=[VMEM] * 6,
        out_shape=jax.ShapeDtypeStruct((groups * shares, quarter, LANES), jnp.bfloat16),
        scratch_shapes=[
            pltpu.VMEM((top, quarter, LANES), jnp.float32),
            pltpu.VMEM((top, quarter, LANES), jnp.int32),
        ],
        compiler_params=pltpu.CompilerParams(vmem_limit_bytes=40 * MIB),
        cost_estimate=cost(2),
    )(own, near, far, quarter_routes, even, odd)


def query_kernel(*refs):
    *query_refs, inverse_ref, out_hbm, factor_ref, spread_ref, wide_ref, out_ref, sems = refs
    part_count, experts, _ = query_refs[0].shape
    count = part_count * len(query_refs)
    width = inverse_ref.shape[1]
    step = pl.program_id(0)
    rows = out_ref.shape[0] // width
    pitch = wide_ref.shape[1] // width

    @pl.when(step == 0)
    def _():
        zeros = jnp.zeros((width, width), jnp.bfloat16)
        for e in range(experts):
            high, low = split(inverse_ref[e])
            left = jnp.concatenate([high, zeros, low, zeros], axis=0)
            right = jnp.concatenate([zeros, high, zeros, low], axis=0)
            factor_ref[e] = jnp.concatenate([left, right], axis=1)

    part_rows = part_count * experts
    for r, query_ref in enumerate(query_refs):
        spread_ref[r * part_rows : (r + 1) * part_rows, :] = (
            query_ref[...].astype(jnp.float32).reshape(part_rows, LANES)
        )
    for e in range(experts):
        query = spread_ref[pl.ds(e, count, stride=experts), :].astype(jnp.bfloat16)
        result = lax.dot_general(
            factor_ref[e], query, (((1,), (1,)), ((), ())), preferred_element_type=jnp.float32
        )
        result = result[: 2 * width] + result[2 * width :]
        slot = (e + experts // 2 * (lax.axis_index("proj") % 2)) % experts
        start = slot * (rows // experts) + 2 * step
        for tile in range(wide_ref.shape[0]):
            part = result[:, tile * LANES : (tile + 1) * LANES]
            wide_ref[tile, pl.ds(start, width, stride=pitch), :] = part[:width]
            wide_ref[tile, pl.ds(start + 1, width, stride=pitch), :] = part[width:]

    @pl.when(step == pl.num_programs(0) - 1)
    def _():
        copies = []
        for part in range(sems.shape[0]):
            first = part * (width // sems.shape[0])
            for j in range(first, first + width // sems.shape[0]):
                for tile in range(wide_ref.shape[0]):
                    out_ref[j * rows : (j + 1) * rows, tile * LANES : (tile + 1) * LANES] = wide_ref[
                        tile, j * pitch : j * pitch + rows, :
                    ].astype(jnp.bfloat16)
            block = pl.ds(first * rows, width // sems.shape[0] * rows)
            copies.append(pltpu.make_async_copy(out_ref.at[block], out_hbm.at[block], sems.at[part]))
            copies[-1].start()
        for copy in copies:
            copy.wait()


def condition_queries(query_grads, inverse_in):
    count, experts, flat = query_grads.shape
    width = inverse_in.shape[1]
    rows = experts * flat
    return pl.pallas_call(
        query_kernel,
        grid=(flat // LANES,),
        in_specs=[
            pl.BlockSpec((count // QUERY_PARTS, experts, LANES), functools.partial(lambda r, c: (r, 0, c), r))
            for r in range(QUERY_PARTS)
        ]
        + [pl.BlockSpec(inverse_in.shape, lambda c: (0, 0, 0))],
        out_specs=HBM,
        out_shape=pltpu.HBM((rows, count), jnp.bfloat16),
        scratch_shapes=[
            pltpu.VMEM((experts, 4 * width, 2 * width), jnp.bfloat16),
            pltpu.VMEM((count * experts, LANES), jnp.float32),
            pltpu.VMEM((count // LANES, rows + 8 * width, LANES), jnp.float32),
            pltpu.VMEM((rows, count), jnp.bfloat16),
            pltpu.SemaphoreType.DMA((8,)),
        ],
        compiler_params=pltpu.CompilerParams(vmem_limit_bytes=40 * MIB),
        cost_estimate=cost(10),
    )(*[stay(query_grads)] * QUERY_PARTS, inverse_in)


def score_kernel(
    arrived_ref, inner_ref, far_ref, out_ref, grads_ref, queries_ref, sems, *, width, doc_count, turns
):
    parts = sems.shape[0]
    part_rows = queries_ref.shape[0] // parts
    fetches = []
    for part in range(parts):
        rows = pl.ds(part * part_rows, part_rows)
        fetches.append(pltpu.make_async_copy(far_ref.at[rows], queries_ref.at[rows], sems.at[part]))
        fetches[-1].start()
    sources, quarter, lanes = arrived_ref.shape
    shares = lax.axis_size("proj")
    owners = sources // shares
    outer, inner, docs = [], [], []
    for entry, (owner_turn, share_turn) in enumerate(turns):
        owner = jnp.bitwise_xor(lax.axis_index("expert"), owner_turn)
        share = jnp.bitwise_xor(lax.axis_index("proj"), share_turn)
        outer.append(arrived_ref[listed(owner, owners, owners // 2) * shares + share])
        docs.append(inner_ref[entry, width:, :].astype(jnp.float32).astype(jnp.int32))
        inner.append(inner_ref[entry, :width, :])
    outer = jnp.concatenate(outer, axis=0)
    inner = jnp.concatenate(inner, axis=1)
    docs = jnp.concatenate(docs, axis=1)
    odd = lax.dot_general(
        (docs & 1).astype(jnp.float32).astype(jnp.bfloat16),
        jnp.full((DOC_ROWS, lanes), 1 / DOC_ROWS, jnp.bfloat16),
        (((0,), (0,)), ((), ())),
        preferred_element_type=jnp.float32,
    ).astype(jnp.bfloat16)
    odd_outer = outer * odd
    outer = jnp.concatenate([outer - odd_outer, odd_outer], axis=1)
    pairs = jnp.broadcast_to(docs[:1] >> 1, inner.shape)
    pair_group = min(16, doc_count // 2)
    pitch = grads_ref.shape[0] // doc_count

    def one_group(group, carry):
        masked = [
            jnp.where(pairs == group * pair_group + p, inner, jnp.zeros_like(inner)) for p in range(pair_group)
        ]
        sums = jnp.dot(jnp.concatenate(masked, axis=0), outer, preferred_element_type=jnp.float32)
        for p in range(pair_group):
            for parity in range(2):
                start = pl.multiple_of((2 * (group * pair_group + p) + parity) * pitch, 8)
                grads_ref[pl.ds(start, width), :] = sums[
                    p * width : (p + 1) * width, parity * lanes : (parity + 1) * lanes
                ]
        return carry

    groups = doc_count // (2 * pair_group)
    lax.fori_loop(0, groups, one_group, 0, unroll=groups == 1)
    result = 0
    for part in range(parts):
        high, low = [], []
        for j in range(part * width // parts, (part + 1) * width // parts):
            pieces = split(grads_ref[pl.ds(j, doc_count, stride=pitch), :])
            high.append(pieces[0])
            low.append(pieces[1])
        flat = jnp.concatenate([jnp.concatenate(high, axis=1), jnp.concatenate(low, axis=1)], axis=0)
        fetches[part].wait()
        rows = slice(part * part_rows, (part + 1) * part_rows)
        result = result + jnp.dot(flat, queries_ref[rows, :], preferred_element_type=jnp.float32)
    result = result[:doc_count] + result[doc_count:]
    columns = result.shape[1] // shares
    fill = jnp.zeros((DOC_DEV, LANES - columns), jnp.float32)
    for owner in range(owners):
        for share in range(shares):
            piece = result[owner * DOC_DEV : (owner + 1) * DOC_DEV, share * columns : (share + 1) * columns]
            out_ref[listed(owner, owners, owners - 1) * shares + share] = jnp.concatenate([piece, fill], axis=1)


def score(arrived, inner, queries, turns, owners):
    sources = arrived.shape[0]
    width = inner.shape[1] - DOC_ROWS
    doc_count = DOC_DEV * owners
    return pl.pallas_call(
        functools.partial(score_kernel, width=width, doc_count=doc_count, turns=turns),
        in_specs=[VMEM, VMEM, HBM],
        out_shape=jax.ShapeDtypeStruct((sources, DOC_DEV, LANES), jnp.float32),
        scratch_shapes=[
            pltpu.VMEM((doc_count * (width + 8), arrived.shape[2]), jnp.float32),
            pltpu.VMEM(queries.shape, jnp.bfloat16),
            pltpu.SemaphoreType.DMA((8,)),
        ],
        compiler_params=pltpu.CompilerParams(vmem_limit_bytes=40 * MIB),
        cost_estimate=cost(5),
    )(arrived, inner, stay(queries))


def sum_kernel(pieces_ref, out_ref):
    total = pieces_ref[0]
    for source in range(1, pieces_ref.shape[0]):
        total = total + pieces_ref[source]
    out_ref[...] = total[:, : out_ref.shape[1]]


def sum_pieces(pieces, columns):
    return pl.pallas_call(
        sum_kernel,
        in_specs=[VMEM],
        out_shape=jax.ShapeDtypeStruct((pieces.shape[1], columns), jnp.float32),
        compiler_params=pltpu.CompilerParams(vmem_limit_bytes=40 * MIB),
    )(pieces)


def exchange(block, axis, size, turn):
    return lax.ppermute(block, axis, [(i, i ^ turn) for i in range(size)])


def double(blocks, turns, axis, size, turn):
    blocks = jnp.concatenate([blocks, exchange(blocks, axis, size, turn)], axis=0)
    return blocks, turns + tuple(t ^ turn for t in turns)


def local(
    activations,
    grad_hidden,
    routes,
    doc_ids,
    query_grads,
    in_projection,
    out_projection,
    inverse_in,
    inverse_out,
):
    tokens, top = routes.shape
    experts, width, _ = inverse_in.shape
    owners = lax.axis_size("expert")
    shares = lax.axis_size("proj")
    quarter = tokens // shares
    assert quarter == LANES and 2 * width == LANES and experts * width // shares == LANES
    assert experts % 4 == 0 and experts // 4 <= DIAGONAL_ROWS
    assert shares == 4 and owners & (owners - 1) == 0
    assert DOC_DEV * owners <= 256

    flat_hidden = grad_hidden.reshape(tokens * top, grad_hidden.shape[2])
    inner_leaving, inner_own, shared, near_hidden = project_inner(
        activations, in_projection, inverse_out, flat_hidden, shares
    )
    inner_first = exchange(inner_leaving, "proj", shares, 2)
    far_shared = exchange(shared, "expert", owners, owners // 2)
    leaving, own = project_outer(near_hidden, flat_hidden, out_projection, shares, top)
    far_shared, inner_first, leaving = lax.optimization_barrier((far_shared, inner_first, leaving))
    near = exchange(leaving, "proj", shares, 1)
    shared, turns = jnp.stack([shared, far_shared]), (0, owners // 2)
    for bit in reversed(range(1, (owners // 2).bit_length() - 1)):
        shared, turns = double(shared, turns, "expert", owners, 1 << bit)
    shared = shared.reshape(-1, LANES)
    even = expand(shared, turns, width, experts, shares)
    near, even = lax.optimization_barrier((near, even))
    inner_second = exchange(combine(combine_inner_kernel, inner_own, inner_first), "proj", shares, 1)
    sent = combine(combine_outer_kernel, own, near)
    far = exchange(sent, "proj", shares, 2)
    inner = finish_inner(inner_own, inner_first, inner_second, doc_ids.reshape(shares, quarter), width)
    packet = exchange(jnp.concatenate([shared, inner], axis=0), "expert", owners, 1)
    inner, _ = lax.optimization_barrier((inner, sent))
    owner_turns = (*range(2, owners), 1, 0)
    arriving = [exchange(inner, "expert", owners, turn) for turn in owner_turns if turn > 1]
    arriving.append(packet[shared.shape[0] :])
    odd = expand(packet, turns, width, experts, shares)
    far, odd = lax.optimization_barrier((far, odd))
    quarter_routes = lax.dynamic_slice_in_dim(routes, lax.axis_index("proj") * quarter, quarter, 0)
    payload = condition(own, near, far, quarter_routes, even, odd, shares, width)
    payload, arriving, query_grads = lax.optimization_barrier((payload, arriving, query_grads))
    arrived = send_to_all(payload, owners, shares, owners // 2)
    inner = jnp.stack(arriving + [inner])
    share_turns = tuple(range(shares))
    inner = jnp.stack([exchange(inner, "proj", shares, turn) if turn else inner for turn in share_turns])
    inner = inner.reshape(owners * shares, width + DOC_ROWS, quarter)
    all_turns = tuple((o, p) for p in share_turns for o in owner_turns)
    queries = condition_queries(query_grads, inverse_in)
    pieces = score(arrived, inner, queries, all_turns, owners)
    pieces = send_to_all(pieces, owners, shares, owners - 1)
    return sum_pieces(pieces, query_grads.shape[0] // shares).T


def solution(mesh):
    in_specs = (
        P(("groups", "expert"), "proj"),
        P(("groups", "expert"), None, "proj"),
        P(("groups", "expert"), None),
        P(("groups", "expert")),
        P(None, "expert", "proj"),
        P(None, "proj"),
        P(None, "proj"),
        P("expert", None, None),
        P("expert", None, None),
    )
    out_specs = P("proj", ("groups", "expert"))
    return jax.shard_map(local, mesh=mesh, in_specs=in_specs, out_specs=out_specs, check_vma=False)
```

```python
import functools

import jax
import jax.numpy as jnp
from jax import lax
from jax.experimental import pallas as pl
from jax.experimental.pallas import tpu as pltpu
from jax.sharding import PartitionSpec as P

DOC_DEV = 8
LANES = 128
DOC_ROWS = 16
DIAGONAL_ROWS = 16
QUERY_PARTS = 1
MIB = 1024 * 1024
VMEM = pl.BlockSpec(memory_space=pltpu.VMEM)
HBM = pl.BlockSpec(memory_space=pltpu.HBM)


def low_lanes(rows, width):
    return lax.broadcasted_iota(jnp.int32, (rows, LANES), 1) < width


def stay(array):
    return pltpu.with_memory_space_constraint(array, pltpu.HBM)


def listed(owner, owners, first):
    return (owner + owners - first) % owners


def send_to_all(blocks, owners, shares, first):
    members = [(i + first * shares) % (owners * shares) for i in range(owners * shares)]
    return lax.all_to_all(blocks, ("expert", "proj"), 0, 0, tiled=True, axis_index_groups=[members])


def split(value):
    high = value.astype(jnp.bfloat16)
    return high, (value - high.astype(jnp.float32)).astype(jnp.bfloat16)


def cost(microseconds):
    return pl.CostEstimate(flops=0, bytes_accessed=int(microseconds * 3.3e6), transcendentals=0)


def in_order(copies, ahead):
    for copy in copies[:ahead]:
        copy.start()
    state = [0]

    def take():
        copies[state[0]].wait()
        if state[0] + ahead < len(copies):
            copies[state[0] + ahead].start()
        state[0] += 1

    return take


def twice_transposed(projection):
    once = jnp.transpose(projection.astype(jnp.float32))
    return jnp.concatenate([once, once], axis=1).astype(jnp.bfloat16)


def triangles(width):
    row = lax.broadcasted_iota(jnp.int32, (width, LANES), 0)
    column = lax.broadcasted_iota(jnp.int32, (width, LANES), 1) % width
    return row, column


def pack_factors(inverse_ref, shared_ref):
    experts, width, _ = inverse_ref.shape
    quarter = experts // 4
    row, column = triangles(width)
    diagonals = []
    for e in range(quarter):
        lower, upper = (
            jnp.concatenate([inverse_ref[first], inverse_ref[first + 2 * quarter]], axis=1) for first in (e, e + quarter)
        )
        shared_ref[e * width : (e + 1) * width, :] = jnp.where(row >= column, lower, upper).astype(jnp.bfloat16)
        diagonals.append(jnp.sum(jnp.where(row == column, upper, 0.0), axis=0, keepdims=True))
    fill = jnp.zeros((DIAGONAL_ROWS - quarter, LANES), jnp.float32)
    shared_ref[quarter * width :, :] = jnp.concatenate(diagonals + [fill], axis=0).astype(jnp.bfloat16)


def unpack_factors(packed, width, quarter):
    row, column = triangles(width)
    packed = packed.astype(jnp.float32)
    lower, upper = [], []
    for e in range(quarter):
        square = packed[e * width : (e + 1) * width]
        turned = jnp.transpose(square)
        turned = jnp.concatenate([turned[:width], turned[width:]], axis=1)
        diagonal = packed[quarter * width + e : quarter * width + e + 1]
        lower.append(jnp.where(row >= column, square, turned))
        upper.append(jnp.where(row == column, diagonal, jnp.where(row < column, square, turned)))
    return jnp.concatenate(lower + upper, axis=0).astype(jnp.bfloat16)


OUTER_TURNS = (1, 3, 2, 0)


def quarter_rows(place, turn, rows):
    return pl.ds(pl.multiple_of(jnp.bitwise_xor(place, turn) * rows, rows), rows)


def inner_kernel(
    act_hbm,
    in_proj_hbm,
    inverse_hbm,
    out_proj_hbm,
    hidden_hbm,
    leaving_ref,
    own_ref,
    shared_ref,
    hidden_ref,
    out_weights_ref,
    act_ref,
    in_proj_ref,
    inverse_ref,
    out_proj_ref,
    sems,
):
    turns = (2, 3, 1, 0)
    quarter = act_ref.shape[1]
    width = in_proj_ref.shape[0]
    half = quarter // 2
    place = lax.axis_index("proj")
    pairs = [(in_proj_hbm, in_proj_ref)]
    for g, turn in enumerate(turns):
        rows = pl.ds(pl.multiple_of(jnp.bitwise_xor(place, turn) * quarter, quarter), quarter)
        pairs.append((act_hbm.at[rows], act_ref.at[g]))
        if g == 0:
            pairs += [(inverse_hbm, inverse_ref), (out_proj_hbm, out_proj_ref)]
    for g in range(hidden_ref.shape[0]):
        pairs.append((hidden_hbm.at[quarter_rows(place, OUTER_TURNS[g], hidden_ref.shape[1])], hidden_ref.at[g]))
    take = in_order([pltpu.make_async_copy(*pair, sems.at[i]) for i, pair in enumerate(pairs)], 4)
    take()
    first = low_lanes(half, width)
    weights = twice_transposed(in_proj_ref[...])
    for wire_ref in (leaving_ref, own_ref):
        take()
        if wire_ref is leaving_ref:
            take()
            pack_factors(inverse_ref, shared_ref)
            take()
            out_weights_ref[...] = twice_transposed(out_proj_ref[...])
        take()
        g = 0 if wire_ref is leaving_ref else 2
        rows = act_ref[g : g + 2].reshape(2 * quarter, act_ref.shape[2])
        inner = jnp.dot(rows, weights, preferred_element_type=jnp.float32)
        for i in range(2):
            start = i * quarter
            high, low = split(jnp.where(first, inner[start : start + half], inner[start + half : start + quarter]))
            wire_ref[i, :half, :] = high
            wire_ref[i, half:, :] = low
    for _ in range(hidden_ref.shape[0]):
        take()


def project_inner(activations, in_projection, inverse_out, out_projection, flat_hidden, quarters):
    tokens, model = activations.shape
    quarter = tokens // quarters
    experts, width, _ = inverse_out.shape
    wire = jax.ShapeDtypeStruct((quarters // 2, quarter, LANES), jnp.bfloat16)
    fixed = (in_projection, inverse_out, out_projection)
    return pl.pallas_call(
        inner_kernel,
        in_specs=[HBM] * 5,
        out_specs=[VMEM] * 5,
        out_shape=[
            wire,
            wire,
            jax.ShapeDtypeStruct((experts // 4 * width + DIAGONAL_ROWS, LANES), jnp.bfloat16),
            jax.ShapeDtypeStruct((quarters // 2, flat_hidden.shape[0] // quarters, flat_hidden.shape[1]), jnp.bfloat16),
            jax.ShapeDtypeStruct((out_projection.shape[1], 2 * width), jnp.bfloat16),
        ],
        scratch_shapes=[pltpu.VMEM((quarters, quarter, model), jnp.bfloat16)]
        + [pltpu.VMEM(array.shape, array.dtype) for array in fixed]
        + [pltpu.SemaphoreType.DMA((quarters + len(fixed) + quarters // 2,))],
        compiler_params=pltpu.CompilerParams(vmem_limit_bytes=40 * MIB),
        cost_estimate=cost(2.5),
    )(*[stay(array) for array in (activations, *fixed, flat_hidden)])


def outer_kernel(near_ref, hidden_hbm, weights_ref, leaving_ref, own_ref, hidden_ref, rows_ref, sems, *, top):
    ready, rows, _ = near_ref.shape
    quarter = rows // top
    width = weights_ref.shape[1] // 2
    place = lax.axis_index("proj")
    pairs = []
    for i, turn in enumerate(OUTER_TURNS[ready:]):
        pairs.append((hidden_hbm.at[quarter_rows(place, turn, rows)], hidden_ref.at[i]))
    take = in_order([pltpu.make_async_copy(*pair, sems.at[i]) for i, pair in enumerate(pairs)], len(pairs))
    first = low_lanes(quarter, width)
    weights = weights_ref[...]

    def pack_rows(g):
        wire_ref = leaving_ref.at[g] if g < 2 else own_ref.at[g - 2]
        for pair in range(top // 2):
            even = rows_ref[g % 2, pl.ds(2 * pair, quarter, stride=top), :]
            odd = rows_ref[g % 2, pl.ds(2 * pair + 1, quarter, stride=top), :]
            wire_ref[pair * quarter : (pair + 1) * quarter, :] = jnp.where(first, even, odd).astype(jnp.bfloat16)

    for g in range(len(OUTER_TURNS)):
        if g >= ready:
            take()
        hidden = near_ref[g] if g < ready else hidden_ref[g - ready]
        rows_ref[g % 2] = jnp.dot(hidden, weights, preferred_element_type=jnp.float32)
        if g:
            pack_rows(g - 1)
    pack_rows(len(OUTER_TURNS) - 1)


def project_outer(near_hidden, flat_hidden, weights, quarters, top):
    rows, hidden = flat_hidden.shape
    wire = jax.ShapeDtypeStruct((quarters // 2, rows // quarters // 2, LANES), jnp.bfloat16)
    return pl.pallas_call(
        functools.partial(outer_kernel, top=top),
        in_specs=[VMEM, HBM, VMEM],
        out_specs=[VMEM] * 2,
        out_shape=[wire, wire],
        scratch_shapes=[
            pltpu.VMEM((quarters // 2, rows // quarters, hidden), jnp.bfloat16),
            pltpu.VMEM((2, rows // quarters, LANES), jnp.float32),
            pltpu.SemaphoreType.DMA((quarters // 2,)),
        ],
        compiler_params=pltpu.CompilerParams(vmem_limit_bytes=40 * MIB),
        cost_estimate=cost(4),
    )(near_hidden, stay(flat_hidden), weights)


def exact_rows(rows):
    half = rows.shape[0] // 2
    return rows[:half].astype(jnp.float32) + rows[half:].astype(jnp.float32)


def combine_inner_kernel(own_ref, near_ref, out_ref):
    high, low = split(exact_rows(own_ref[0]) + exact_rows(near_ref[1]))
    out_ref[: high.shape[0], :] = high
    out_ref[high.shape[0] :, :] = low


def combine_outer_kernel(own_ref, near_ref, out_ref):
    out_ref[...] = (own_ref[0].astype(jnp.float32) + near_ref[1].astype(jnp.float32)).astype(jnp.bfloat16)


def combine(kernel, own, near):
    return pl.pallas_call(
        kernel,
        in_specs=[VMEM, VMEM],
        out_shape=jax.ShapeDtypeStruct(own.shape[1:], jnp.bfloat16),
        compiler_params=pltpu.CompilerParams(vmem_limit_bytes=40 * MIB),
        cost_estimate=cost(0.5),
    )(own, near)


def finish_inner_kernel(own_ref, first_ref, second_ref, docs_ref, out_ref):
    total = exact_rows(own_ref[1]) + exact_rows(first_ref[0]) + exact_rows(second_ref[...])
    width = out_ref.shape[0] - DOC_ROWS
    total = jnp.concatenate([total[:, :width], total[:, width:]], axis=0)
    out_ref[:width, :] = jnp.transpose(total).astype(jnp.bfloat16)
    docs = docs_ref[pl.ds(lax.axis_index("proj"), 1), :].astype(jnp.float32)
    out_ref[width:, :] = jnp.broadcast_to(docs, (DOC_ROWS, LANES)).astype(jnp.bfloat16)


def finish_inner(own, first, second, doc_rows, width):
    return pl.pallas_call(
        finish_inner_kernel,
        in_specs=[VMEM] * 4,
        out_shape=jax.ShapeDtypeStruct((width + DOC_ROWS, own.shape[1]), jnp.bfloat16),
        compiler_params=pltpu.CompilerParams(vmem_limit_bytes=40 * MIB),
        cost_estimate=cost(0.5),
    )(own, first, second, doc_rows)


def expand_kernel(shared_ref, weights_ref, *, width, experts, shares, turns):
    half = experts // 2
    share_rows = width // shares
    columns = shares * half * share_rows
    lane = lax.broadcasted_iota(jnp.int32, (LANES, columns), 1)
    row = lax.broadcasted_iota(jnp.int32, (LANES, columns), 0)
    expert_lane = lax.broadcasted_iota(jnp.int32, (half * width, columns), 1) // share_rows % half
    expert_row = lax.broadcasted_iota(jnp.int32, (half * width, columns), 0) // width
    own = expert_lane == expert_row
    rows = half // 2 * width + DIAGONAL_ROWS
    factors = [
        unpack_factors(shared_ref[entry * rows : (entry + 1) * rows], width, half // 2) for entry in range(len(turns))
    ]
    for side in range(2):
        share = jnp.bitwise_xor(lane // (half * share_rows), side)
        source = share * share_rows + lane % share_rows
        spread = (row == source + side * width).astype(jnp.float32).astype(jnp.bfloat16)
        for entry, turn in enumerate(turns):
            placed = jnp.dot(factors[entry], spread, preferred_element_type=jnp.float32)
            weights_ref[turn // 2, side] = jnp.where(own, placed, 0.0).astype(jnp.bfloat16)


def expand(shared, turns, width, experts, shares):
    owners = len(turns)
    return pl.pallas_call(
        functools.partial(expand_kernel, width=width, experts=experts, shares=shares, turns=turns),
        in_specs=[VMEM],
        out_shape=jax.ShapeDtypeStruct((owners, 2, experts // 2 * width, experts // 2 * width), jnp.bfloat16),
        compiler_params=pltpu.CompilerParams(vmem_limit_bytes=40 * MIB),
        cost_estimate=cost(1),
    )(shared)


def condition_kernel(
    own_ref, near_ref, far_ref, routes_ref, even_ref, odd_ref, payload_ref, value_ref, name_ref, *, top, width
):
    quarter = routes_ref.shape[0]
    pairs, sides, dense_width, _ = even_ref.shape
    groups = 2 * pairs
    shares = payload_ref.shape[0] // groups
    experts = sides * dense_width // width
    first = low_lanes(quarter, width)
    second = 1 - first.astype(jnp.int32)

    def summed(start, size):
        rows = slice(start, start + size)
        total = own_ref[1, rows, :].astype(jnp.float32) + near_ref[0, rows, :].astype(jnp.float32)
        return total + far_ref[rows, :].astype(jnp.float32)

    for pair in range(top // 2):
        both = summed(pair * quarter, quarter)
        swapped = pltpu.roll(both, width, 1)
        value_ref[2 * pair] = jnp.where(first, both, swapped)
        value_ref[2 * pair + 1] = jnp.where(first, swapped, both)
    for k in range(top):
        name_ref[k] = jnp.broadcast_to(routes_ref[:, k : k + 1], (quarter, LANES)) - second

    def one_group(step, carry, parity):
        weights_ref = odd_ref if parity else even_ref
        group = jnp.bitwise_xor(lax.axis_index("expert"), 2 * step + parity)
        dense = []
        for pair in range(experts // 2):
            base = group * experts + 2 * pair
            chosen = jnp.zeros((quarter, LANES), jnp.float32)
            for k in range(top):
                chosen = jnp.where(name_ref[k] == base, value_ref[k], chosen)
            dense.append(chosen.astype(jnp.bfloat16))
        per_side = len(dense) // sides
        results = [
            jnp.dot(
                jnp.concatenate(dense[side * per_side : (side + 1) * per_side], axis=1),
                weights_ref[step, side],
                preferred_element_type=jnp.float32,
            )
            for side in range(sides)
        ]
        for share in range(shares):
            lanes = slice(share // 2 * LANES, (share // 2 + 1) * LANES)
            low, high = (results[side][:, lanes] for side in ((0, 1) if share % 2 == 0 else (1, 0)))
            place = listed(group, groups, groups // 2) * shares + share
            payload_ref[place] = jnp.where(first, low, high).astype(jnp.bfloat16)
        return carry

    for parity in range(2):
        lax.fori_loop(0, pairs, functools.partial(one_group, parity=parity), 0, unroll=pairs <= 2)


def condition(own, near, far, quarter_routes, even, odd, shares, width):
    quarter, top = quarter_routes.shape
    groups = 2 * even.shape[0]
    return pl.pallas_call(
        functools.partial(condition_kernel, top=top, width=width),
        in_specs=[VMEM] * 6,
        out_shape=jax.ShapeDtypeStruct((groups * shares, quarter, LANES), jnp.bfloat16),
        scratch_shapes=[
            pltpu.VMEM((top, quarter, LANES), jnp.float32),
            pltpu.VMEM((top, quarter, LANES), jnp.int32),
        ],
        compiler_params=pltpu.CompilerParams(vmem_limit_bytes=40 * MIB),
        cost_estimate=cost(2),
    )(own, near, far, quarter_routes, even, odd)


def query_kernel(*refs):
    *query_refs, inverse_ref, out_hbm, factor_ref, spread_ref, wide_ref, out_ref, sems = refs
    part_count, experts, _ = query_refs[0].shape
    count = part_count * len(query_refs)
    width = inverse_ref.shape[1]
    step = pl.program_id(0)
    rows = out_ref.shape[0] // width
    pitch = wide_ref.shape[1] // width

    @pl.when(step == 0)
    def _():
        zeros = jnp.zeros((width, width), jnp.bfloat16)
        for e in range(experts):
            high, low = split(inverse_ref[e])
            left = jnp.concatenate([high, zeros, low, zeros], axis=0)
            right = jnp.concatenate([zeros, high, zeros, low], axis=0)
            factor_ref[e] = jnp.concatenate([left, right], axis=1)

    part_rows = part_count * experts
    for r, query_ref in enumerate(query_refs):
        spread_ref[r * part_rows : (r + 1) * part_rows, :] = (
            query_ref[...].astype(jnp.float32).reshape(part_rows, LANES)
        )
    for e in range(experts):
        query = spread_ref[pl.ds(e, count, stride=experts), :].astype(jnp.bfloat16)
        result = lax.dot_general(
            factor_ref[e], query, (((1,), (1,)), ((), ())), preferred_element_type=jnp.float32
        )
        result = result[: 2 * width] + result[2 * width :]
        slot = (e + experts // 2 * (lax.axis_index("proj") % 2)) % experts
        start = slot * (rows // experts) + 2 * step
        for tile in range(wide_ref.shape[0]):
            part = result[:, tile * LANES : (tile + 1) * LANES]
            wide_ref[tile, pl.ds(start, width, stride=pitch), :] = part[:width]
            wide_ref[tile, pl.ds(start + 1, width, stride=pitch), :] = part[width:]

    @pl.when(step == pl.num_programs(0) - 1)
    def _():
        copies = []
        for part in range(sems.shape[0]):
            first = part * (width // sems.shape[0])
            for j in range(first, first + width // sems.shape[0]):
                for tile in range(wide_ref.shape[0]):
                    out_ref[j * rows : (j + 1) * rows, tile * LANES : (tile + 1) * LANES] = wide_ref[
                        tile, j * pitch : j * pitch + rows, :
                    ].astype(jnp.bfloat16)
            block = pl.ds(first * rows, width // sems.shape[0] * rows)
            copies.append(pltpu.make_async_copy(out_ref.at[block], out_hbm.at[block], sems.at[part]))
            copies[-1].start()
        for copy in copies:
            copy.wait()


def condition_queries(query_grads, inverse_in):
    count, experts, flat = query_grads.shape
    width = inverse_in.shape[1]
    rows = experts * flat
    return pl.pallas_call(
        query_kernel,
        grid=(flat // LANES,),
        in_specs=[
            pl.BlockSpec((count // QUERY_PARTS, experts, LANES), functools.partial(lambda r, c: (r, 0, c), r))
            for r in range(QUERY_PARTS)
        ]
        + [pl.BlockSpec(inverse_in.shape, lambda c: (0, 0, 0))],
        out_specs=HBM,
        out_shape=pltpu.HBM((rows, count), jnp.bfloat16),
        scratch_shapes=[
            pltpu.VMEM((experts, 4 * width, 2 * width), jnp.bfloat16),
            pltpu.VMEM((count * experts, LANES), jnp.float32),
            pltpu.VMEM((count // LANES, rows + 8 * width, LANES), jnp.float32),
            pltpu.VMEM((rows, count), jnp.bfloat16),
            pltpu.SemaphoreType.DMA((8,)),
        ],
        compiler_params=pltpu.CompilerParams(vmem_limit_bytes=40 * MIB),
        cost_estimate=cost(10),
    )(*[stay(query_grads)] * QUERY_PARTS, inverse_in)


def score_kernel(
    arrived_ref, inner_ref, far_ref, out_ref, grads_ref, queries_ref, sems, *, width, doc_count, turns
):
    parts = sems.shape[0]
    part_rows = queries_ref.shape[0] // parts
    fetches = []
    for part in range(parts):
        rows = pl.ds(part * part_rows, part_rows)
        fetches.append(pltpu.make_async_copy(far_ref.at[rows], queries_ref.at[rows], sems.at[part]))
        fetches[-1].start()
    sources, quarter, lanes = arrived_ref.shape
    shares = lax.axis_size("proj")
    owners = sources // shares
    outer, inner, docs = [], [], []
    for entry, (owner_turn, share_turn) in enumerate(turns):
        owner = jnp.bitwise_xor(lax.axis_index("expert"), owner_turn)
        share = jnp.bitwise_xor(lax.axis_index("proj"), share_turn)
        outer.append(arrived_ref[listed(owner, owners, owners // 2) * shares + share])
        docs.append(inner_ref[entry, width:, :].astype(jnp.float32).astype(jnp.int32))
        inner.append(inner_ref[entry, :width, :])
    outer = jnp.concatenate(outer, axis=0)
    inner = jnp.concatenate(inner, axis=1)
    docs = jnp.concatenate(docs, axis=1)
    odd = lax.dot_general(
        (docs & 1).astype(jnp.float32).astype(jnp.bfloat16),
        jnp.full((DOC_ROWS, lanes), 1 / DOC_ROWS, jnp.bfloat16),
        (((0,), (0,)), ((), ())),
        preferred_element_type=jnp.float32,
    ).astype(jnp.bfloat16)
    odd_outer = outer * odd
    outer = jnp.concatenate([outer - odd_outer, odd_outer], axis=1)
    pairs = jnp.broadcast_to(docs[:1] >> 1, inner.shape)
    pair_group = min(16, doc_count // 2)
    pitch = grads_ref.shape[0] // doc_count

    def one_group(group, carry):
        masked = [
            jnp.where(pairs == group * pair_group + p, inner, jnp.zeros_like(inner)) for p in range(pair_group)
        ]
        sums = jnp.dot(jnp.concatenate(masked, axis=0), outer, preferred_element_type=jnp.float32)
        for p in range(pair_group):
            for parity in range(2):
                start = pl.multiple_of((2 * (group * pair_group + p) + parity) * pitch, 8)
                grads_ref[pl.ds(start, width), :] = sums[
                    p * width : (p + 1) * width, parity * lanes : (parity + 1) * lanes
                ]
        return carry

    groups = doc_count // (2 * pair_group)
    lax.fori_loop(0, groups, one_group, 0, unroll=groups == 1)
    result = 0
    for part in range(parts):
        high, low = [], []
        for j in range(part * width // parts, (part + 1) * width // parts):
            pieces = split(grads_ref[pl.ds(j, doc_count, stride=pitch), :])
            high.append(pieces[0])
            low.append(pieces[1])
        flat = jnp.concatenate([jnp.concatenate(high, axis=1), jnp.concatenate(low, axis=1)], axis=0)
        fetches[part].wait()
        rows = slice(part * part_rows, (part + 1) * part_rows)
        result = result + jnp.dot(flat, queries_ref[rows, :], preferred_element_type=jnp.float32)
    result = result[:doc_count] + result[doc_count:]
    columns = result.shape[1] // shares
    fill = jnp.zeros((DOC_DEV, LANES - columns), jnp.float32)
    for owner in range(owners):
        for share in range(shares):
            piece = result[owner * DOC_DEV : (owner + 1) * DOC_DEV, share * columns : (share + 1) * columns]
            out_ref[listed(owner, owners, owners - 1) * shares + share] = jnp.concatenate([piece, fill], axis=1)


def score(arrived, inner, queries, turns, owners):
    sources = arrived.shape[0]
    width = inner.shape[1] - DOC_ROWS
    doc_count = DOC_DEV * owners
    return pl.pallas_call(
        functools.partial(score_kernel, width=width, doc_count=doc_count, turns=turns),
        in_specs=[VMEM, VMEM, HBM],
        out_shape=jax.ShapeDtypeStruct((sources, DOC_DEV, LANES), jnp.float32),
        scratch_shapes=[
            pltpu.VMEM((doc_count * (width + 8), arrived.shape[2]), jnp.float32),
            pltpu.VMEM(queries.shape, jnp.bfloat16),
            pltpu.SemaphoreType.DMA((8,)),
        ],
        compiler_params=pltpu.CompilerParams(vmem_limit_bytes=40 * MIB),
        cost_estimate=cost(5),
    )(arrived, inner, stay(queries))


def sum_kernel(pieces_ref, out_ref):
    total = pieces_ref[0]
    for source in range(1, pieces_ref.shape[0]):
        total = total + pieces_ref[source]
    out_ref[...] = total[:, : out_ref.shape[1]]


def sum_pieces(pieces, columns):
    return pl.pallas_call(
        sum_kernel,
        in_specs=[VMEM],
        out_shape=jax.ShapeDtypeStruct((pieces.shape[1], columns), jnp.float32),
        compiler_params=pltpu.CompilerParams(vmem_limit_bytes=40 * MIB),
    )(pieces)


def exchange(block, axis, size, turn):
    return lax.ppermute(block, axis, [(i, i ^ turn) for i in range(size)])


def double(blocks, turns, axis, size, turn):
    blocks = jnp.concatenate([blocks, exchange(blocks, axis, size, turn)], axis=0)
    return blocks, turns + tuple(t ^ turn for t in turns)


def local(
    activations,
    grad_hidden,
    routes,
    doc_ids,
    query_grads,
    in_projection,
    out_projection,
    inverse_in,
    inverse_out,
):
    tokens, top = routes.shape
    experts, width, _ = inverse_in.shape
    owners = lax.axis_size("expert")
    shares = lax.axis_size("proj")
    quarter = tokens // shares
    assert quarter == LANES and 2 * width == LANES and experts * width // shares == LANES
    assert experts % 4 == 0 and experts // 4 <= DIAGONAL_ROWS
    assert shares == 4 and owners & (owners - 1) == 0
    assert DOC_DEV * owners <= 256

    flat_hidden = grad_hidden.reshape(tokens * top, grad_hidden.shape[2])
    inner_leaving, inner_own, shared, near_hidden, out_weights = project_inner(
        activations, in_projection, inverse_out, out_projection, flat_hidden, shares
    )
    inner_first = exchange(inner_leaving, "proj", shares, 2)
    far_shared = exchange(shared, "expert", owners, owners // 2)
    leaving, own = project_outer(near_hidden, flat_hidden, out_weights, shares, top)
    far_shared, inner_first, leaving = lax.optimization_barrier((far_shared, inner_first, leaving))
    near = exchange(leaving, "proj", shares, 1)
    shared, turns = jnp.stack([shared, far_shared]), (0, owners // 2)
    for bit in reversed(range(1, (owners // 2).bit_length() - 1)):
        shared, turns = double(shared, turns, "expert", owners, 1 << bit)
    shared = shared.reshape(-1, LANES)
    even = expand(shared, turns, width, experts, shares)
    near, even = lax.optimization_barrier((near, even))
    inner_second = exchange(combine(combine_inner_kernel, inner_own, inner_first), "proj", shares, 1)
    sent = combine(combine_outer_kernel, own, near)
    far = exchange(sent, "proj", shares, 2)
    inner = finish_inner(inner_own, inner_first, inner_second, doc_ids.reshape(shares, quarter), width)
    packet = exchange(jnp.concatenate([shared, inner], axis=0), "expert", owners, 1)
    inner, _ = lax.optimization_barrier((inner, sent))
    owner_turns = (*range(2, owners), 1, 0)
    arriving = [exchange(inner, "expert", owners, turn) for turn in owner_turns if turn > 1]
    arriving.append(packet[shared.shape[0] :])
    odd = expand(packet, turns, width, experts, shares)
    far, odd = lax.optimization_barrier((far, odd))
    quarter_routes = lax.dynamic_slice_in_dim(routes, lax.axis_index("proj") * quarter, quarter, 0)
    payload = condition(own, near, far, quarter_routes, even, odd, shares, width)
    payload, arriving, query_grads = lax.optimization_barrier((payload, arriving, query_grads))
    arrived = send_to_all(payload, owners, shares, owners // 2)
    inner = jnp.stack(arriving + [inner])
    share_turns = tuple(range(shares))
    inner = jnp.stack([exchange(inner, "proj", shares, turn) if turn else inner for turn in share_turns])
    inner = inner.reshape(owners * shares, width + DOC_ROWS, quarter)
    all_turns = tuple((o, p) for p in share_turns for o in owner_turns)
    queries = condition_queries(query_grads, inverse_in)
    pieces = score(arrived, inner, queries, all_turns, owners)
    pieces = send_to_all(pieces, owners, shares, owners - 1)
    return sum_pieces(pieces, query_grads.shape[0] // shares).T


def solution(mesh):
    in_specs = (
        P(("groups", "expert"), "proj"),
        P(("groups", "expert"), None, "proj"),
        P(("groups", "expert"), None),
        P(("groups", "expert")),
        P(None, "expert", "proj"),
        P(None, "proj"),
        P(None, "proj"),
        P("expert", None, None),
        P("expert", None, None),
    )
    out_specs = P("proj", ("groups", "expert"))
    return jax.shard_map(local, mesh=mesh, in_specs=in_specs, out_specs=out_specs, check_vma=False)
```

```python
import functools

import jax
import jax.numpy as jnp
from jax import lax
from jax.experimental import pallas as pl
from jax.experimental.pallas import tpu as pltpu
from jax.sharding import PartitionSpec as P

DOC_DEV = 8
LANES = 128
DOC_ROWS = 16
DIAGONAL_ROWS = 16
QUERY_PARTS = 1
MIB = 1024 * 1024
VMEM = pl.BlockSpec(memory_space=pltpu.VMEM)
HBM = pl.BlockSpec(memory_space=pltpu.HBM)


def low_lanes(rows, width):
    return lax.broadcasted_iota(jnp.int32, (rows, LANES), 1) < width


def stay(array):
    return pltpu.with_memory_space_constraint(array, pltpu.HBM)


def listed(owner, owners, first):
    return (owner + owners - first) % owners


def send_to_all(blocks, owners, shares, first):
    members = [(i + first * shares) % (owners * shares) for i in range(owners * shares)]
    return lax.all_to_all(blocks, ("expert", "proj"), 0, 0, tiled=True, axis_index_groups=[members])


def split(value):
    high = value.astype(jnp.bfloat16)
    return high, (value - high.astype(jnp.float32)).astype(jnp.bfloat16)


def cost(microseconds):
    return pl.CostEstimate(flops=0, bytes_accessed=int(microseconds * 3.3e6), transcendentals=0)


def in_order(copies, ahead):
    for copy in copies[:ahead]:
        copy.start()
    state = [0]

    def take():
        copies[state[0]].wait()
        if state[0] + ahead < len(copies):
            copies[state[0] + ahead].start()
        state[0] += 1

    return take


def twice_transposed(projection):
    once = jnp.transpose(projection.astype(jnp.float32))
    return jnp.concatenate([once, once], axis=1).astype(jnp.bfloat16)


def triangles(width):
    row = lax.broadcasted_iota(jnp.int32, (width, LANES), 0)
    column = lax.broadcasted_iota(jnp.int32, (width, LANES), 1) % width
    return row, column


def pack_factors(inverse_ref, shared_ref):
    experts, width, _ = inverse_ref.shape
    quarter = experts // 4
    row, column = triangles(width)
    diagonals = []
    for e in range(quarter):
        lower, upper = (
            jnp.concatenate([inverse_ref[first], inverse_ref[first + 2 * quarter]], axis=1) for first in (e, e + quarter)
        )
        shared_ref[e * width : (e + 1) * width, :] = jnp.where(row >= column, lower, upper).astype(jnp.bfloat16)
        diagonals.append(jnp.sum(jnp.where(row == column, upper, 0.0), axis=0, keepdims=True))
    fill = jnp.zeros((DIAGONAL_ROWS - quarter, LANES), jnp.float32)
    shared_ref[quarter * width :, :] = jnp.concatenate(diagonals + [fill], axis=0).astype(jnp.bfloat16)


def unpack_factors(packed, width, quarter):
    row, column = triangles(width)
    packed = packed.astype(jnp.float32)
    lower, upper = [], []
    for e in range(quarter):
        square = packed[e * width : (e + 1) * width]
        turned = jnp.transpose(square)
        turned = jnp.concatenate([turned[:width], turned[width:]], axis=1)
        diagonal = packed[quarter * width + e : quarter * width + e + 1]
        lower.append(jnp.where(row >= column, square, turned))
        upper.append(jnp.where(row == column, diagonal, jnp.where(row < column, square, turned)))
    return jnp.concatenate(lower + upper, axis=0).astype(jnp.bfloat16)


OUTER_TURNS = (1, 3, 2, 0)


def quarter_rows(place, turn, rows):
    return pl.ds(pl.multiple_of(jnp.bitwise_xor(place, turn) * rows, rows), rows)


def inner_kernel(
    act_hbm,
    in_proj_hbm,
    inverse_hbm,
    hidden_hbm,
    leaving_ref,
    own_ref,
    shared_ref,
    hidden_ref,
    act_ref,
    in_proj_ref,
    inverse_ref,
    sems,
):
    turns = (2, 3, 1, 0)
    quarter = act_ref.shape[1]
    width = in_proj_ref.shape[0]
    half = quarter // 2
    place = lax.axis_index("proj")
    pairs = [(in_proj_hbm, in_proj_ref)]
    for g, turn in enumerate(turns):
        rows = pl.ds(pl.multiple_of(jnp.bitwise_xor(place, turn) * quarter, quarter), quarter)
        pairs.append((act_hbm.at[rows], act_ref.at[g]))
        if g == 0:
            pairs.append((inverse_hbm, inverse_ref))
    for g in range(hidden_ref.shape[0]):
        pairs.append((hidden_hbm.at[quarter_rows(place, OUTER_TURNS[g], hidden_ref.shape[1])], hidden_ref.at[g]))
    take = in_order([pltpu.make_async_copy(*pair, sems.at[i]) for i, pair in enumerate(pairs)], 4)
    take()
    first = low_lanes(half, width)
    weights = twice_transposed(in_proj_ref[...])
    for wire_ref in (leaving_ref, own_ref):
        take()
        if wire_ref is leaving_ref:
            take()
            pack_factors(inverse_ref, shared_ref)
        take()
        g = 0 if wire_ref is leaving_ref else 2
        rows = act_ref[g : g + 2].reshape(2 * quarter, act_ref.shape[2])
        inner = jnp.dot(rows, weights, preferred_element_type=jnp.float32)
        for i in range(2):
            start = i * quarter
            high, low = split(jnp.where(first, inner[start : start + half], inner[start + half : start + quarter]))
            wire_ref[i, :half, :] = high
            wire_ref[i, half:, :] = low
    for _ in range(hidden_ref.shape[0]):
        take()


def project_inner(activations, in_projection, inverse_out, flat_hidden, quarters):
    tokens, model = activations.shape
    quarter = tokens // quarters
    experts, width, _ = inverse_out.shape
    wire = jax.ShapeDtypeStruct((quarters // 2, quarter, LANES), jnp.bfloat16)
    fixed = (in_projection, inverse_out)
    return pl.pallas_call(
        inner_kernel,
        in_specs=[HBM] * 4,
        out_specs=[VMEM] * 4,
        out_shape=[
            wire,
            wire,
            jax.ShapeDtypeStruct((experts // 4 * width + DIAGONAL_ROWS, LANES), jnp.bfloat16),
            jax.ShapeDtypeStruct((1, flat_hidden.shape[0] // quarters, flat_hidden.shape[1]), jnp.bfloat16),
        ],
        scratch_shapes=[pltpu.VMEM((quarters, quarter, model), jnp.bfloat16)]
        + [pltpu.VMEM(array.shape, array.dtype) for array in fixed]
        + [pltpu.SemaphoreType.DMA((quarters + len(fixed) + 1,))],
        compiler_params=pltpu.CompilerParams(vmem_limit_bytes=40 * MIB),
        cost_estimate=cost(2.5),
    )(*[stay(array) for array in (activations, *fixed, flat_hidden)])


def outer_kernel(near_ref, hidden_hbm, out_proj_hbm, leaving_ref, own_ref, hidden_ref, out_proj_ref, rows_ref, sems, *, top):
    ready, rows, _ = near_ref.shape
    quarter = rows // top
    width = out_proj_ref.shape[0]
    place = lax.axis_index("proj")
    pairs = [(out_proj_hbm, out_proj_ref)]
    for i, turn in enumerate(OUTER_TURNS[ready:]):
        pairs.append((hidden_hbm.at[quarter_rows(place, turn, rows)], hidden_ref.at[i]))
    take = in_order([pltpu.make_async_copy(*pair, sems.at[i]) for i, pair in enumerate(pairs)], len(pairs))
    take()
    first = low_lanes(quarter, width)
    weights = twice_transposed(out_proj_ref[...])

    def pack_rows(g):
        wire_ref = leaving_ref.at[g] if g < 2 else own_ref.at[g - 2]
        for pair in range(top // 2):
            even = rows_ref[g % 2, pl.ds(2 * pair, quarter, stride=top), :]
            odd = rows_ref[g % 2, pl.ds(2 * pair + 1, quarter, stride=top), :]
            wire_ref[pair * quarter : (pair + 1) * quarter, :] = jnp.where(first, even, odd).astype(jnp.bfloat16)

    for g in range(len(OUTER_TURNS)):
        if g >= ready:
            take()
        hidden = near_ref[g] if g < ready else hidden_ref[g - ready]
        rows_ref[g % 2] = jnp.dot(hidden, weights, preferred_element_type=jnp.float32)
        if g:
            pack_rows(g - 1)
    pack_rows(len(OUTER_TURNS) - 1)


def project_outer(near_hidden, flat_hidden, out_projection, quarters, top):
    rows, hidden = flat_hidden.shape
    wire = jax.ShapeDtypeStruct((quarters // 2, rows // quarters // 2, LANES), jnp.bfloat16)
    return pl.pallas_call(
        functools.partial(outer_kernel, top=top),
        in_specs=[VMEM, HBM, HBM],
        out_specs=[VMEM] * 2,
        out_shape=[wire, wire],
        scratch_shapes=[
            pltpu.VMEM((quarters - 1, rows // quarters, hidden), jnp.bfloat16),
            pltpu.VMEM(out_projection.shape, out_projection.dtype),
            pltpu.VMEM((2, rows // quarters, LANES), jnp.float32),
            pltpu.SemaphoreType.DMA((quarters,)),
        ],
        compiler_params=pltpu.CompilerParams(vmem_limit_bytes=40 * MIB),
        cost_estimate=cost(4),
    )(near_hidden, stay(flat_hidden), stay(out_projection))


def exact_rows(rows):
    half = rows.shape[0] // 2
    return rows[:half].astype(jnp.float32) + rows[half:].astype(jnp.float32)


def combine_inner_kernel(own_ref, near_ref, out_ref):
    high, low = split(exact_rows(own_ref[0]) + exact_rows(near_ref[1]))
    out_ref[: high.shape[0], :] = high
    out_ref[high.shape[0] :, :] = low


def combine_outer_kernel(own_ref, near_ref, out_ref):
    out_ref[...] = (own_ref[0].astype(jnp.float32) + near_ref[1].astype(jnp.float32)).astype(jnp.bfloat16)


def combine(kernel, own, near):
    return pl.pallas_call(
        kernel,
        in_specs=[VMEM, VMEM],
        out_shape=jax.ShapeDtypeStruct(own.shape[1:], jnp.bfloat16),
        compiler_params=pltpu.CompilerParams(vmem_limit_bytes=40 * MIB),
        cost_estimate=cost(0.5),
    )(own, near)


def finish_inner_kernel(own_ref, first_ref, second_ref, docs_ref, out_ref):
    total = exact_rows(own_ref[1]) + exact_rows(first_ref[0]) + exact_rows(second_ref[...])
    width = out_ref.shape[0] - DOC_ROWS
    total = jnp.concatenate([total[:, :width], total[:, width:]], axis=0)
    out_ref[:width, :] = jnp.transpose(total).astype(jnp.bfloat16)
    docs = docs_ref[pl.ds(lax.axis_index("proj"), 1), :].astype(jnp.float32)
    out_ref[width:, :] = jnp.broadcast_to(docs, (DOC_ROWS, LANES)).astype(jnp.bfloat16)


def finish_inner(own, first, second, doc_rows, width):
    return pl.pallas_call(
        finish_inner_kernel,
        in_specs=[VMEM] * 4,
        out_shape=jax.ShapeDtypeStruct((width + DOC_ROWS, own.shape[1]), jnp.bfloat16),
        compiler_params=pltpu.CompilerParams(vmem_limit_bytes=40 * MIB),
        cost_estimate=cost(0.5),
    )(own, first, second, doc_rows)


def expand_kernel(shared_ref, weights_ref, *, width, experts, shares, turns):
    half = experts // 2
    share_rows = width // shares
    columns = shares * half * share_rows
    lane = lax.broadcasted_iota(jnp.int32, (LANES, columns), 1)
    row = lax.broadcasted_iota(jnp.int32, (LANES, columns), 0)
    expert_lane = lax.broadcasted_iota(jnp.int32, (half * width, columns), 1) // share_rows % half
    expert_row = lax.broadcasted_iota(jnp.int32, (half * width, columns), 0) // width
    own = expert_lane == expert_row
    rows = half // 2 * width + DIAGONAL_ROWS
    factors = [
        unpack_factors(shared_ref[entry * rows : (entry + 1) * rows], width, half // 2) for entry in range(len(turns))
    ]
    for side in range(2):
        share = jnp.bitwise_xor(lane // (half * share_rows), side)
        source = share * share_rows + lane % share_rows
        spread = (row == source + side * width).astype(jnp.float32).astype(jnp.bfloat16)
        for entry, turn in enumerate(turns):
            placed = jnp.dot(factors[entry], spread, preferred_element_type=jnp.float32)
            weights_ref[turn // 2, side] = jnp.where(own, placed, 0.0).astype(jnp.bfloat16)


def expand(shared, turns, width, experts, shares):
    owners = len(turns)
    return pl.pallas_call(
        functools.partial(expand_kernel, width=width, experts=experts, shares=shares, turns=turns),
        in_specs=[VMEM],
        out_shape=jax.ShapeDtypeStruct((owners, 2, experts // 2 * width, experts // 2 * width), jnp.bfloat16),
        compiler_params=pltpu.CompilerParams(vmem_limit_bytes=40 * MIB),
        cost_estimate=cost(1),
    )(shared)


def condition_kernel(
    own_ref, near_ref, far_ref, routes_ref, even_ref, odd_ref, payload_ref, value_ref, name_ref, *, top, width
):
    quarter = routes_ref.shape[0]
    pairs, sides, dense_width, _ = even_ref.shape
    groups = 2 * pairs
    shares = payload_ref.shape[0] // groups
    experts = sides * dense_width // width
    first = low_lanes(quarter, width)
    second = 1 - first.astype(jnp.int32)

    def summed(start, size):
        rows = slice(start, start + size)
        total = own_ref[1, rows, :].astype(jnp.float32) + near_ref[0, rows, :].astype(jnp.float32)
        return total + far_ref[rows, :].astype(jnp.float32)

    for pair in range(top // 2):
        both = summed(pair * quarter, quarter)
        swapped = pltpu.roll(both, width, 1)
        value_ref[2 * pair] = jnp.where(first, both, swapped)
        value_ref[2 * pair + 1] = jnp.where(first, swapped, both)
    for k in range(top):
        name_ref[k] = jnp.broadcast_to(routes_ref[:, k : k + 1], (quarter, LANES)) - second

    def one_group(step, carry, parity):
        weights_ref = odd_ref if parity else even_ref
        group = jnp.bitwise_xor(lax.axis_index("expert"), 2 * step + parity)
        dense = []
        for pair in range(experts // 2):
            base = group * experts + 2 * pair
            chosen = jnp.zeros((quarter, LANES), jnp.float32)
            for k in range(top):
                chosen = jnp.where(name_ref[k] == base, value_ref[k], chosen)
            dense.append(chosen.astype(jnp.bfloat16))
        per_side = len(dense) // sides
        results = [
            jnp.dot(
                jnp.concatenate(dense[side * per_side : (side + 1) * per_side], axis=1),
                weights_ref[step, side],
                preferred_element_type=jnp.float32,
            )
            for side in range(sides)
        ]
        for share in range(shares):
            lanes = slice(share // 2 * LANES, (share // 2 + 1) * LANES)
            low, high = (results[side][:, lanes] for side in ((0, 1) if share % 2 == 0 else (1, 0)))
            place = listed(group, groups, groups // 2) * shares + share
            payload_ref[place] = jnp.where(first, low, high).astype(jnp.bfloat16)
        return carry

    for parity in range(2):
        lax.fori_loop(0, pairs, functools.partial(one_group, parity=parity), 0, unroll=pairs <= 2)


def condition(own, near, far, quarter_routes, even, odd, shares, width):
    quarter, top = quarter_routes.shape
    groups = 2 * even.shape[0]
    return pl.pallas_call(
        functools.partial(condition_kernel, top=top, width=width),
        in_specs=[VMEM] * 6,
        out_shape=jax.ShapeDtypeStruct((groups * shares, quarter, LANES), jnp.bfloat16),
        scratch_shapes=[
            pltpu.VMEM((top, quarter, LANES), jnp.float32),
            pltpu.VMEM((top, quarter, LANES), jnp.int32),
        ],
        compiler_params=pltpu.CompilerParams(vmem_limit_bytes=40 * MIB),
        cost_estimate=cost(2),
    )(own, near, far, quarter_routes, even, odd)


def query_kernel(*refs):
    *query_refs, inverse_ref, out_hbm, factor_ref, spread_ref, wide_ref, out_ref, sems = refs
    part_count, experts, _ = query_refs[0].shape
    count = part_count * len(query_refs)
    width = inverse_ref.shape[1]
    step = pl.program_id(0)
    rows = out_ref.shape[0] // width
    pitch = wide_ref.shape[1] // width

    @pl.when(step == 0)
    def _():
        zeros = jnp.zeros((width, width), jnp.bfloat16)
        for e in range(experts):
            high, low = split(inverse_ref[e])
            left = jnp.concatenate([high, zeros, low, zeros], axis=0)
            right = jnp.concatenate([zeros, high, zeros, low], axis=0)
            factor_ref[e] = jnp.concatenate([left, right], axis=1)

    part_rows = part_count * experts
    for r, query_ref in enumerate(query_refs):
        spread_ref[r * part_rows : (r + 1) * part_rows, :] = (
            query_ref[...].astype(jnp.float32).reshape(part_rows, LANES)
        )
    for e in range(experts):
        query = spread_ref[pl.ds(e, count, stride=experts), :].astype(jnp.bfloat16)
        result = lax.dot_general(
            factor_ref[e], query, (((1,), (1,)), ((), ())), preferred_element_type=jnp.float32
        )
        result = result[: 2 * width] + result[2 * width :]
        slot = (e + experts // 2 * (lax.axis_index("proj") % 2)) % experts
        start = slot * (rows // experts) + 2 * step
        for tile in range(wide_ref.shape[0]):
            part = result[:, tile * LANES : (tile + 1) * LANES]
            wide_ref[tile, pl.ds(start, width, stride=pitch), :] = part[:width]
            wide_ref[tile, pl.ds(start + 1, width, stride=pitch), :] = part[width:]

    @pl.when(step == pl.num_programs(0) - 1)
    def _():
        copies = []
        for part in range(sems.shape[0]):
            first = part * (width // sems.shape[0])
            for j in range(first, first + width // sems.shape[0]):
                for tile in range(wide_ref.shape[0]):
                    out_ref[j * rows : (j + 1) * rows, tile * LANES : (tile + 1) * LANES] = wide_ref[
                        tile, j * pitch : j * pitch + rows, :
                    ].astype(jnp.bfloat16)
            block = pl.ds(first * rows, width // sems.shape[0] * rows)
            copies.append(pltpu.make_async_copy(out_ref.at[block], out_hbm.at[block], sems.at[part]))
            copies[-1].start()
        for copy in copies:
            copy.wait()


def condition_queries(query_grads, inverse_in):
    count, experts, flat = query_grads.shape
    width = inverse_in.shape[1]
    rows = experts * flat
    return pl.pallas_call(
        query_kernel,
        grid=(flat // LANES,),
        in_specs=[
            pl.BlockSpec((count // QUERY_PARTS, experts, LANES), functools.partial(lambda r, c: (r, 0, c), r))
            for r in range(QUERY_PARTS)
        ]
        + [pl.BlockSpec(inverse_in.shape, lambda c: (0, 0, 0))],
        out_specs=HBM,
        out_shape=pltpu.HBM((rows, count), jnp.bfloat16),
        scratch_shapes=[
            pltpu.VMEM((experts, 4 * width, 2 * width), jnp.bfloat16),
            pltpu.VMEM((count * experts, LANES), jnp.float32),
            pltpu.VMEM((count // LANES, rows + 8 * width, LANES), jnp.float32),
            pltpu.VMEM((rows, count), jnp.bfloat16),
            pltpu.SemaphoreType.DMA((8,)),
        ],
        compiler_params=pltpu.CompilerParams(vmem_limit_bytes=40 * MIB),
        cost_estimate=cost(10),
    )(*[stay(query_grads)] * QUERY_PARTS, inverse_in)


def score_kernel(
    arrived_ref, inner_ref, far_ref, out_ref, grads_ref, queries_ref, sems, *, width, doc_count, turns
):
    parts = sems.shape[0]
    part_rows = queries_ref.shape[0] // parts
    fetches = []
    for part in range(parts):
        rows = pl.ds(part * part_rows, part_rows)
        fetches.append(pltpu.make_async_copy(far_ref.at[rows], queries_ref.at[rows], sems.at[part]))
        fetches[-1].start()
    sources, quarter, lanes = arrived_ref.shape
    shares = lax.axis_size("proj")
    owners = sources // shares
    outer, inner, docs = [], [], []
    for entry, (owner_turn, share_turn) in enumerate(turns):
        owner = jnp.bitwise_xor(lax.axis_index("expert"), owner_turn)
        share = jnp.bitwise_xor(lax.axis_index("proj"), share_turn)
        outer.append(arrived_ref[listed(owner, owners, owners // 2) * shares + share])
        docs.append(inner_ref[entry, width:, :].astype(jnp.float32).astype(jnp.int32))
        inner.append(inner_ref[entry, :width, :])
    outer = jnp.concatenate(outer, axis=0)
    inner = jnp.concatenate(inner, axis=1)
    docs = jnp.concatenate(docs, axis=1)
    odd = lax.dot_general(
        (docs & 1).astype(jnp.float32).astype(jnp.bfloat16),
        jnp.full((DOC_ROWS, lanes), 1 / DOC_ROWS, jnp.bfloat16),
        (((0,), (0,)), ((), ())),
        preferred_element_type=jnp.float32,
    ).astype(jnp.bfloat16)
    odd_outer = outer * odd
    outer = jnp.concatenate([outer - odd_outer, odd_outer], axis=1)
    pairs = jnp.broadcast_to(docs[:1] >> 1, inner.shape)
    pair_group = min(16, doc_count // 2)
    pitch = grads_ref.shape[0] // doc_count

    def one_group(group, carry):
        masked = [
            jnp.where(pairs == group * pair_group + p, inner, jnp.zeros_like(inner)) for p in range(pair_group)
        ]
        sums = jnp.dot(jnp.concatenate(masked, axis=0), outer, preferred_element_type=jnp.float32)
        for p in range(pair_group):
            for parity in range(2):
                start = pl.multiple_of((2 * (group * pair_group + p) + parity) * pitch, 8)
                grads_ref[pl.ds(start, width), :] = sums[
                    p * width : (p + 1) * width, parity * lanes : (parity + 1) * lanes
                ]
        return carry

    groups = doc_count // (2 * pair_group)
    lax.fori_loop(0, groups, one_group, 0, unroll=groups == 1)
    result = 0
    for part in range(parts):
        high, low = [], []
        for j in range(part * width // parts, (part + 1) * width // parts):
            pieces = split(grads_ref[pl.ds(j, doc_count, stride=pitch), :])
            high.append(pieces[0])
            low.append(pieces[1])
        flat = jnp.concatenate([jnp.concatenate(high, axis=1), jnp.concatenate(low, axis=1)], axis=0)
        fetches[part].wait()
        rows = slice(part * part_rows, (part + 1) * part_rows)
        result = result + jnp.dot(flat, queries_ref[rows, :], preferred_element_type=jnp.float32)
    result = result[:doc_count] + result[doc_count:]
    columns = result.shape[1] // shares
    fill = jnp.zeros((DOC_DEV, LANES - columns), jnp.float32)
    for owner in range(owners):
        for share in range(shares):
            piece = result[owner * DOC_DEV : (owner + 1) * DOC_DEV, share * columns : (share + 1) * columns]
            out_ref[listed(owner, owners, owners - 1) * shares + share] = jnp.concatenate([piece, fill], axis=1)


def score(arrived, inner, queries, turns, owners):
    sources = arrived.shape[0]
    width = inner.shape[1] - DOC_ROWS
    doc_count = DOC_DEV * owners
    return pl.pallas_call(
        functools.partial(score_kernel, width=width, doc_count=doc_count, turns=turns),
        in_specs=[VMEM, VMEM, HBM],
        out_shape=jax.ShapeDtypeStruct((sources, DOC_DEV, LANES), jnp.float32),
        scratch_shapes=[
            pltpu.VMEM((doc_count * (width + 8), arrived.shape[2]), jnp.float32),
            pltpu.VMEM(queries.shape, jnp.bfloat16),
            pltpu.SemaphoreType.DMA((8,)),
        ],
        compiler_params=pltpu.CompilerParams(vmem_limit_bytes=40 * MIB),
        cost_estimate=cost(5),
    )(arrived, inner, stay(queries))


def sum_kernel(pieces_ref, out_ref):
    total = pieces_ref[0]
    for source in range(1, pieces_ref.shape[0]):
        total = total + pieces_ref[source]
    out_ref[...] = total[:, : out_ref.shape[1]]


def sum_pieces(pieces, columns):
    return pl.pallas_call(
        sum_kernel,
        in_specs=[VMEM],
        out_shape=jax.ShapeDtypeStruct((pieces.shape[1], columns), jnp.float32),
        compiler_params=pltpu.CompilerParams(vmem_limit_bytes=40 * MIB),
    )(pieces)


def exchange(block, axis, size, turn):
    return lax.ppermute(block, axis, [(i, i ^ turn) for i in range(size)])


def double(blocks, turns, axis, size, turn):
    blocks = jnp.concatenate([blocks, exchange(blocks, axis, size, turn)], axis=0)
    return blocks, turns + tuple(t ^ turn for t in turns)


def local(
    activations,
    grad_hidden,
    routes,
    doc_ids,
    query_grads,
    in_projection,
    out_projection,
    inverse_in,
    inverse_out,
):
    tokens, top = routes.shape
    experts, width, _ = inverse_in.shape
    owners = lax.axis_size("expert")
    shares = lax.axis_size("proj")
    quarter = tokens // shares
    assert quarter == LANES and 2 * width == LANES and experts * width // shares == LANES
    assert experts % 4 == 0 and experts // 4 <= DIAGONAL_ROWS
    assert shares == 4 and owners & (owners - 1) == 0
    assert DOC_DEV * owners <= 256

    flat_hidden = grad_hidden.reshape(tokens * top, grad_hidden.shape[2])
    inner_leaving, inner_own, shared, near_hidden = project_inner(
        activations, in_projection, inverse_out, flat_hidden, shares
    )
    inner_first = exchange(inner_leaving, "proj", shares, 2)
    far_shared = exchange(shared, "expert", owners, owners // 2)
    leaving, own = project_outer(near_hidden, flat_hidden, out_projection, shares, top)
    far_shared, inner_first, leaving = lax.optimization_barrier((far_shared, inner_first, leaving))
    near = exchange(leaving, "proj", shares, 1)
    shared, turns = jnp.stack([shared, far_shared]), (0, owners // 2)
    for bit in reversed(range(1, (owners // 2).bit_length() - 1)):
        shared, turns = double(shared, turns, "expert", owners, 1 << bit)
    shared = shared.reshape(-1, LANES)
    even = expand(shared, turns, width, experts, shares)
    near, even = lax.optimization_barrier((near, even))
    inner_second = exchange(combine(combine_inner_kernel, inner_own, inner_first), "proj", shares, 1)
    sent = combine(combine_outer_kernel, own, near)
    far = exchange(sent, "proj", shares, 2)
    inner = finish_inner(inner_own, inner_first, inner_second, doc_ids.reshape(shares, quarter), width)
    packet = exchange(jnp.concatenate([shared, inner], axis=0), "expert", owners, 1)
    inner, _ = lax.optimization_barrier((inner, sent))
    owner_turns = (*range(2, owners), 1, 0)
    arriving = [exchange(inner, "expert", owners, turn) for turn in owner_turns if turn > 1]
    arriving.append(packet[shared.shape[0] :])
    odd = expand(packet, turns, width, experts, shares)
    far, odd = lax.optimization_barrier((far, odd))
    quarter_routes = lax.dynamic_slice_in_dim(routes, lax.axis_index("proj") * quarter, quarter, 0)
    payload = condition(own, near, far, quarter_routes, even, odd, shares, width)
    payload, arriving, query_grads = lax.optimization_barrier((payload, arriving, query_grads))
    arrived = send_to_all(payload, owners, shares, owners // 2)
    inner = jnp.stack(arriving + [inner])
    share_turns = tuple(range(shares))
    inner = jnp.stack([exchange(inner, "proj", shares, turn) if turn else inner for turn in share_turns])
    inner = inner.reshape(owners * shares, width + DOC_ROWS, quarter)
    all_turns = tuple((o, p) for p in share_turns for o in owner_turns)
    queries = condition_queries(query_grads, inverse_in)
    pieces = score(arrived, inner, queries, all_turns, owners)
    pieces = send_to_all(pieces, owners, shares, owners - 1)
    return sum_pieces(pieces, query_grads.shape[0] // shares).T


def solution(mesh):
    in_specs = (
        P(("groups", "expert"), "proj"),
        P(("groups", "expert"), None, "proj"),
        P(("groups", "expert"), None),
        P(("groups", "expert")),
        P(None, "expert", "proj"),
        P(None, "proj"),
        P(None, "proj"),
        P("expert", None, None),
        P("expert", None, None),
    )
    out_specs = P("proj", ("groups", "expert"))
    return jax.shard_map(local, mesh=mesh, in_specs=in_specs, out_specs=out_specs, check_vma=False)
```
